32 devices in a mesh: section: 2 (over x), dp: 4 (over z), mp: 4 (over y, core).
Axes of the slice: x: 2, y: 2, z: 4, core: 2. Of those that a mesh axis runs over, the one named last changes fastest.
Arguments:
- frames: bfloat16 [4, 4, 1024, 512], P(None, 'dp'), may hold values from -6 to 6
- lengths: int32 [4, 4], P(None, 'dp'), may hold values from 256 to 1024, as said below
- out_grad: bfloat16 [4, 4, 1024, 512], P(None, 'dp'), may hold values from -6 to 6
- norm_gains: float32 [2, 3, 512], P('section'), may hold values from 0.1 to 1.9
- norm_biases: float32 [2, 3, 512], P('section'), may hold values from -1.75 to 1.75
- query_key_value_weight: bfloat16 [2, 3, 512, 512], P('section', None, None, 'mp'), may hold values from -0.25 to 0.25
- query_key_value_bias: float32 [2, 3, 512], P('section', None, 'mp'), may hold values from -1.75 to 1.75
- output_weight: bfloat16 [2, 512, 512], P('section', 'mp'), may hold values from -4 to 4
- upward_weight: bfloat16 [2, 2, 512, 1536], P('section', None, None, 'mp'), may hold values from -0.3314563 to 0.3314563
- upward_bias: float32 [2, 2, 1536], P('section', None, 'mp'), may hold values from -1.75 to 1.75
- gate_gain: float32 [2, 1536], P('section', 'mp'), may hold values from 0.24 to 3.6
- gate_biases: float32 [2, 2, 1536], P('section', None, 'mp'), may hold values from -1.75 to 1.75
- conv_weight: float32 [2, 31, 1536], P('section', None, 'mp'), may hold values from -1 to 1
- downward_weight: bfloat16 [2, 1536, 512], P('section', 'mp'), may hold values from -0.15625 to 0.15625
- out_biases: float32 [2, 2, 512], P('section'), may hold values from -1.75 to 1.75
- merge_logits: float32 [2, 2], P('section'), may hold values from -1 to 1
Outputs:
- layer_out: bfloat16 [2, 4, 4, 1024, 512], P('section', None, 'dp')
- input_grad: bfloat16 [2, 4, 4, 1024, 512], P('section', None, 'dp')
- grad_norm_gains: float32 [2, 3, 512], P('section')
- grad_norm_biases: float32 [2, 3, 512], P('section')
- grad_w_qkv: float32 [2, 3, 512, 512], P('section', None, None, 'mp')
- grad_b_qkv: float32 [2, 3, 512], P('section', None, 'mp')
- output_weight_gradient: float32 [2, 512, 512], P('section', 'mp')
- upward_weight_gradient: float32 [2, 2, 512, 1536], P('section', None, None, 'mp')
- grad_b_up: float32 [2, 2, 1536], P('section', None, 'mp')
- grad_gate_gain: float32 [2, 1536], P('section', 'mp')
- grad_gate_biases: float32 [2, 2, 1536], P('section', None, 'mp')
- grad_conv_weight: float32 [2, 31, 1536], P('section', None, 'mp')
- grad_w_down: float32 [2, 1536, 512], P('section', 'mp')
- grad_out_biases: float32 [2, 2, 512], P('section')
- grad_merge_logits: float32 [2, 2], P('section')
The draws below stay inside these ranges and needn't reach their ends.
Inputs may be any that keep to these rules, and one draw needn't show every extreme that they name: `lengths`: in every micro-batch at least one utterance has 1024 frames; the others have 1024 // 4 or more.
All inputs are finite; a program needn't handle non-finite values.
Results may differ from the reference program's by a relative error of at most 0.023.
The reference program's roundings to bfloat16 on the way count: a program that leaves them out, or rounds other values in their place, can miss the bound.
Values may be sent and summed in bfloat16 or wider, within the bound.
No kernel may reach another device: no remote copies, remote signals or barrier semaphores. Data moves between devices by JAX's collectives and lax.ppermute only.
A program may use at most 320 MiB of HBM per device.

```python
import math
import jax
import jax.numpy as jnp
from jax import lax

D = 512
HEADS = 8
HALF = 1536
KERNEL = 31
MB = 4
LEN = 1024
SEQS = 4
LAYERS = 2


def draw_lengths(key, part):
    key = jax.random.fold_in(key, 7)
    key_lengths, key_pick = jax.random.split(key)
    sample_lengths = jax.random.randint(key_lengths, (MB, SEQS), LEN // 4, LEN + 1)
    chosen = jax.random.randint(key_pick, (MB, 1), 0, SEQS)
    return jnp.where(jnp.arange(SEQS)[None, :] == chosen, LEN, sample_lengths).astype(jnp.int32)


def unit_ramp(count):
    return jnp.arange(count, dtype=jnp.float32) / max(count - 1, 1)


def draw_gate_gain(key, part):
    key = jax.random.fold_in(key, 13)
    low_end = 0.4
    ratio = 6.0
    base = low_end * jnp.exp(jnp.log(ratio) * unit_ramp(HALF))
    jitter = 1.0 + 0.18 * jax.random.uniform(key, (LAYERS, HALF), jnp.float32, -1.0, 1.0)
    return (base[None, :] * jitter).astype(jnp.float32)


def draw_upward_weight(key, part):
    key = jax.random.fold_in(key, 17)
    column_scale = 0.5 * jnp.exp(jnp.log(5.0) * unit_ramp(HALF)) / jnp.sqrt(jnp.float32(D))
    shape = (LAYERS, 2, D, HALF)
    noise = jax.random.truncated_normal(key, -3.0, 3.0, shape, jnp.float32)
    return (noise * column_scale).astype(jnp.bfloat16)


def steps_of(stream_key, extent, cuts, smallest, high):
    factor_of, own = 1.0, jax.random.fold_in(stream_key, 6)
    for position, blocks in cuts:
        steps = jnp.exp(jax.random.uniform(jax.random.fold_in(own, position), (blocks,), jnp.float32, smallest / len(cuts), high / len(cuts)))
        factor_of = factor_of * jnp.repeat(steps, extent[position] // blocks).reshape([-1 if axis == position else 1 for axis in range(len(extent))])
    return factor_of


def gaussian(own_key, extent, scale, reach, shards=(), held_as=jnp.bfloat16):
    array = scale * jax.random.normal(own_key, extent, jnp.float32)
    if shards:
        array = array * steps_of(own_key, extent, shards, -0.22, 0.18)
    return jnp.clip(array, -reach, reach).astype(held_as)


def setup_inputs(seed: int = 0) -> dict:
    seeds = jax.random.split(jax.random.key(seed), 17)
    frames = gaussian(seeds[0], (MB, SEQS, LEN, D), 1.0, 6.0, ((1, 4),))
    lengths = draw_lengths(jax.random.fold_in(seeds[16], 71), 0)
    out_grad = gaussian(seeds[2], (MB, SEQS, LEN, D), 1.0, 6.0, ((1, 4),))
    norm_gains = jnp.clip(1.0 + 0.18 * jax.random.normal(seeds[3], (LAYERS, 3, D), jnp.float32), 0.1, 1.9)
    norm_biases = gaussian(seeds[4], (LAYERS, 3, D), 0.3, 1.75, ((0, 2),), jnp.float32)
    query_key_value_weight = gaussian(seeds[5], (LAYERS, 3, D, D), D ** -0.5, 0.25, ((0, 2), (3, 4)))
    query_key_value_bias = gaussian(seeds[6], (LAYERS, 3, D), 0.3, 1.75, ((0, 2), (2, 4)), jnp.float32)
    output_weight = gaussian(seeds[7], (LAYERS, D, D), (max(1, D * 4 // LEN)) ** -0.5, 4.0, ((0, 2), (1, 4)))
    upward_weight = draw_upward_weight(jax.random.fold_in(seeds[16], 71), 0)
    upward_bias = gaussian(seeds[9], (LAYERS, 2, HALF), 0.3, 1.75, ((0, 2), (2, 4)), jnp.float32)
    gate_gain = draw_gate_gain(jax.random.fold_in(seeds[16], 71), 0)
    gate_biases = gaussian(seeds[11], (LAYERS, 2, HALF), 0.3, 1.75, ((0, 2), (2, 4)), jnp.float32)
    conv_weight = gaussian(seeds[12], (LAYERS, KERNEL, HALF), KERNEL ** -0.5, 1.0, ((0, 2), (2, 4)), jnp.float32)
    downward_weight = gaussian(seeds[13], (LAYERS, HALF, D), HALF ** -0.5, 0.15625, ((0, 2), (1, 4)))
    out_biases = gaussian(seeds[14], (LAYERS, 2, D), 0.3, 1.75, ((0, 2),), jnp.float32)
    merge_logits = jnp.clip(jax.random.uniform(seeds[15], (LAYERS, 2), jnp.float32, -1.0, 1.0) * steps_of(seeds[15], (LAYERS, 2), ((0, 2),), -0.4, 0.0), -1.0, 1.0)
    return {"frames": frames, "lengths": lengths, "out_grad": out_grad, "norm_gains": norm_gains, "norm_biases": norm_biases, "query_key_value_weight": query_key_value_weight, "query_key_value_bias": query_key_value_bias, "output_weight": output_weight, "upward_weight": upward_weight, "upward_bias": upward_bias, "gate_gain": gate_gain, "gate_biases": gate_biases, "conv_weight": conv_weight, "downward_weight": downward_weight, "out_biases": out_biases, "merge_logits": merge_logits}


epsilon = 1e-05
highest_precision = lax.Precision.HIGHEST

@jax.custom_vjp
def low(v):
    return lax.optimization_barrier(v.astype(jnp.bfloat16)).astype(jnp.float32)

@jax.custom_vjp
def lower_backward(v):
    return v

def low_keep(v):
    return (low(v), None)

def low_pass(kept, grad):
    return (grad,)

def back_keep(v):
    return (v, None)

def back_low(kept, grad):
    return (low(grad),)
low.defvjp(low_keep, low_pass)
lower_backward.defvjp(back_keep, back_low)

def layer_norm(values, norm_gain, norm_bias):
    center = lax.optimization_barrier(jnp.mean(values, axis=-1, keepdims=True))
    spread = lax.optimization_barrier(jnp.mean(jnp.square(values - center), axis=-1, keepdims=True))
    return (values - center) * lax.rsqrt(spread + epsilon) * norm_gain + norm_bias

def rotary_tables(length, head_width):
    halfway = head_width // 2
    frequency = jnp.exp(jnp.arange(halfway, dtype=jnp.float32) * (-math.log(10000.0) / halfway))
    angles = jnp.arange(length, dtype=jnp.float32)[:, None] * frequency[None, :]
    return (jnp.cos(angles), jnp.sin(angles))

def rotate(values, cosine, sine_table):
    halfway = values.shape[-1] // 2
    first_half = values[..., :halfway]
    second_half = values[..., halfway:]
    cos_wide = cosine[None, :, None, :]
    sin_wide = sine_table[None, :, None, :]
    return jnp.concatenate([first_half * cos_wide - second_half * sin_wide, first_half * sin_wide + second_half * cos_wide], axis=-1)

def merge_branches(attention_result, branch_output, out_biases, merge_logits):
    weights = jax.nn.softmax(merge_logits)
    return weights[0] * (attention_result + out_biases[0]) + weights[1] * (branch_output + out_biases[1])

def depthwise(normed_gate, conv_weight, conv_bias):
    tap_count = conv_weight.shape[0]
    margin = (tap_count - 1) // 2
    length = normed_gate.shape[1]
    padded = jnp.pad(normed_gate, ((0, 0), (margin, margin), (0, 0)))
    running = jnp.zeros_like(normed_gate)
    for tap_index in range(tap_count):
        running = running + conv_weight[tap_index] * padded[:, tap_index:tap_index + length]
    return running + conv_bias

def attend(queries, key_heads, value_heads, frame_mask):
    utterances, length, head_count, head_width = queries.shape
    block_rows = min(512, length)
    block_count = length // block_rows
    score_scale = 1.0 / math.sqrt(head_width)
    stacked = queries.reshape(utterances, block_count, block_rows, head_count, head_width).transpose(1, 0, 2, 3, 4)

    def one_block(query_block):
        scores = jnp.einsum('sqhe,skhe->shqk', query_block, key_heads, precision=highest_precision) * score_scale
        scores = jnp.where(frame_mask[:, None, None, :], scores, -1000000000.0)
        scores = lower_backward(scores)
        probabilities = low(jax.nn.softmax(scores, axis=-1))
        return jnp.einsum('shqk,skhe->sqhe', probabilities, value_heads, precision=highest_precision)
    mixed_head_rows = lax.map(jax.checkpoint(one_block), stacked)
    return mixed_head_rows.transpose(1, 0, 2, 3, 4).reshape(utterances, length, head_count * head_width)

def branchformer_layer(hidden, frame_mask, cosine, sine_table, weights):
    norm_gains, norm_biases, query_key_value_weight, query_key_value_bias, output_weight, upward_weight, upward_bias, gate_gain, gate_biases, conv_weight, downward_weight, out_biases, merge_logits = weights
    utterances, length, model_width = hidden.shape
    head_width = model_width // HEADS
    heads_shape = (utterances, length, HEADS, head_width)
    attention_normalized = low(layer_norm(hidden, norm_gains[0], norm_biases[0]))
    projected_rows = jnp.einsum('kpu,hur->hkpr', attention_normalized, query_key_value_weight, precision=highest_precision) + query_key_value_bias[:, None, None, :]
    queries = low(rotate(lower_backward(projected_rows[0]).reshape(heads_shape), cosine, sine_table))
    key_heads = low(rotate(lower_backward(projected_rows[1]).reshape(heads_shape), cosine, sine_table))
    value_heads = lower_backward(low(projected_rows[2])).reshape(heads_shape)
    mixed_head_rows = lower_backward(low(attend(queries, key_heads, value_heads, frame_mask)))
    attention_result = lower_backward(jnp.einsum('rwc,cb->rwb', mixed_head_rows, output_weight, precision=highest_precision))
    perceptron_normalized = low(layer_norm(hidden, norm_gains[1], norm_biases[1]))
    upward_rows = lower_backward(jnp.einsum('kpu,hur->hkpr', perceptron_normalized, upward_weight, precision=highest_precision) + upward_bias[:, None, None, :])
    activated = jax.nn.gelu(upward_rows, approximate=False)
    frame_weight = frame_mask.astype(jnp.float32)[..., None]
    normed_gate = layer_norm(activated[1], gate_gain, gate_biases[0]) * frame_weight
    conv_out = depthwise(normed_gate, conv_weight, gate_biases[1])
    gated_result = lower_backward(low(activated[0] * conv_out))
    branch_output = lower_backward(jnp.einsum('rwc,cb->rwb', gated_result, downward_weight, precision=highest_precision))
    return layer_norm(hidden + merge_branches(attention_result, branch_output, out_biases, merge_logits), norm_gains[2], norm_biases[2])

def reference(frames, lengths, out_grad, norm_gains, norm_biases, query_key_value_weight, query_key_value_bias, output_weight, upward_weight, upward_bias, gate_gain, gate_biases, conv_weight, downward_weight, out_biases, merge_logits):
    params = tuple((weight_array.astype(jnp.float32) for weight_array in (norm_gains, norm_biases, query_key_value_weight, query_key_value_bias, output_weight, upward_weight, upward_bias, gate_gain, gate_biases, conv_weight, downward_weight, out_biases, merge_logits)))
    group_size = 4
    model_width = frames.shape[-1]
    group_count = MB * SEQS // group_size
    inputs = frames.astype(jnp.float32).reshape(group_count, group_size, LEN, model_width)
    cotangents = out_grad.astype(jnp.float32).reshape(group_count, group_size, LEN, model_width)
    masks = (jnp.arange(LEN, dtype=jnp.int32)[None, None, :] < lengths[:, :, None]).reshape(group_count, group_size, LEN)
    cosine, sine_table = rotary_tables(LEN, model_width // HEADS)

    def forward(weights, first_input, probe_in, frame_mask):
        first_out = branchformer_layer(first_input, frame_mask, cosine, sine_table, tuple((stacked[0] for stacked in weights)))
        sent_out = lower_backward(low(first_out))
        second_out = branchformer_layer(sent_out + probe_in, frame_mask, cosine, sine_table, tuple((stacked[1] for stacked in weights)))
        return (sent_out, second_out)

    def group_step(totals, pieces):
        group_input, group_cot, group_mask = pieces
        probe_zero = jnp.zeros_like(group_input)
        outputs, pull_back = jax.vjp(lambda weights, first_input, probe_in: forward(weights, first_input, probe_in, group_mask), params, group_input, probe_zero)
        grad_weights, grad_input, grad_probe = pull_back((jnp.zeros_like(outputs[0]), group_cot))
        totals = jax.tree.map(jnp.add, totals, grad_weights)
        return (totals, (outputs[0].astype(jnp.bfloat16), outputs[1].astype(jnp.bfloat16), grad_input.astype(jnp.bfloat16), grad_probe.astype(jnp.bfloat16)))
    zero_grads = jax.tree.map(jnp.zeros_like, params)
    totals, pieces = lax.scan(group_step, zero_grads, (inputs, cotangents, masks))
    full_shape = (MB, SEQS, LEN, model_width)
    layer_out = jnp.stack([pieces[0].reshape(full_shape), pieces[1].reshape(full_shape)])
    input_grad = jnp.stack([pieces[2].reshape(full_shape), pieces[3].reshape(full_shape)])
    return (layer_out, input_grad, totals[0], totals[1], totals[2], totals[3], totals[4], totals[5], totals[6], totals[7], totals[8], totals[9], totals[10], totals[11], totals[12])
```

```python
import functools
import math

import jax
import jax.numpy as jnp
import numpy as np
from jax import lax
from jax.experimental import pallas as pl
from jax.experimental.pallas import tpu as pltpu
from jax.sharding import PartitionSpec as P

BF = jnp.bfloat16
F32 = jnp.float32
HEAD = 64
LANES = 128
SEGS = 8
HALO = 16
EPS = 1e-05
NEG = -1000000000.0
NN = (((1,), (0,)), ((), ()))
NT = (((1,), (1,)), ((), ()))
TN = (((0,), (0,)), ((), ()))

TAPS = 31
BLOCK_ROWS = 40
ROW_UP0, ROW_UP1, ROW_GAIN, ROW_GB0, ROW_GB1 = 31, 32, 33, 34, 35
ROW_QKV = 120
ROW_NG, ROW_NB, ROW_OB, ROW_LOGIT = 128, 140, 152, 160
PACK_ROWS = 168

OUT_ROWS, DOWN_ROWS, UP_ROWS, QKV_ROWS = 512, 1536, 3072, 1536
D_ROWS = OUT_ROWS + DOWN_ROWS
M_ROWS = UP_ROWS + 128
A_ROWS = QKV_ROWS + 64

W_UP, W_ROWS = 512, 3584
SPLIT = 2048

VMEM = pl.BlockSpec(memory_space=pltpu.VMEM)
SMEM = pl.BlockSpec(memory_space=pltpu.SMEM)
ANY = pl.BlockSpec(memory_space=pltpu.HBM)


def dot(a, b, dims):
    return lax.dot_general(a, b, dims, preferred_element_type=F32)


def call(kernel, ins, in_specs, outs, scratch, flops, mib):
    moved = sum(math.prod(x.shape) * x.dtype.itemsize for x in list(ins) + list(outs))
    ins = [pltpu.with_memory_space_constraint(x, pltpu.HBM) if p is ANY else x for x, p in zip(ins, in_specs)]
    return pl.pallas_call(
        kernel,
        in_specs=in_specs,
        out_specs=[VMEM] * len(outs),
        out_shape=outs,
        scratch_shapes=scratch,
        compiler_params=pltpu.CompilerParams(vmem_limit_bytes=mib << 20),
        cost_estimate=pl.CostEstimate(flops=flops, bytes_accessed=moved, transcendentals=0),
    )(*ins)


def shape(dims, dtype):
    return jax.ShapeDtypeStruct(dims, dtype)


def fetch(flag, here, there, sems):
    @pl.when(flag)
    def _():
        for i, (a, d) in enumerate(here):
            pltpu.make_async_copy(a, d, sems.at[i]).start()

    @pl.when(jnp.logical_not(flag))
    def _():
        for i, (a, d) in enumerate(there):
            pltpu.make_async_copy(a, d, sems.at[i]).start()


def landed(pairs, sems):
    for i, (a, d) in enumerate(pairs):
        pltpu.make_async_copy(a, d, sems.at[i]).wait()


def slab_copies(sets, dst, lo, hi):
    here, there = [], []
    for j in range(4):
        for a, b in ((lo, min(hi, SPLIT)), (max(lo, SPLIT), hi)):
            if a >= b:
                continue
            d = dst.at[j, pl.ds(a - lo, b - a), :]
            here.append((sets[j].at[pl.ds(a, b - a), :], d))
            if j < 2:
                there.append((sets[4 + j].at[pl.ds(a, b - a), :], d))
            elif a < SPLIT:
                there.append((sets[4 + j].at[pl.ds(a, b - a), :], d))
            else:
                there.append((sets[6 + j].at[pl.ds(a - SPLIT, b - a), :], d))
    return here, there


def shard_copies(sets, dst):
    return [(sets[j], dst.at[j]) for j in range(4)], [(sets[4 + j], dst.at[j]) for j in range(4)]


def wide(sp, row, count=4):
    return jnp.concatenate([sp[0, 0, row + i : row + i + 1, :] for i in range(count)], axis=1)


def branch_weights(sp):
    l0 = sp[0, 0, ROW_LOGIT : ROW_LOGIT + 1, :]
    l1 = sp[0, 0, ROW_LOGIT + 1 : ROW_LOGIT + 2, :]
    top = jnp.maximum(l0, l1)
    e0, e1 = jnp.exp(l0 - top), jnp.exp(l1 - top)
    total = e0 + e1
    return jnp.concatenate([e0 / total] * 4, axis=1), jnp.concatenate([e1 / total] * 4, axis=1)


def normalized(x):
    center = jnp.mean(x, axis=-1, keepdims=True)
    d = x - center
    inverse = lax.rsqrt(jnp.mean(d * d, axis=-1, keepdims=True) + EPS)
    return d * inverse, inverse


def frame_of(row, half, rows):
    return half * rows + (row & (SEGS - 1)) * (rows // SEGS) + (row >> 3)


def order_matrix(rows, back):
    r = lax.broadcasted_iota(jnp.int32, (rows, rows), 1 if back else 0)
    t = lax.broadcasted_iota(jnp.int32, (rows, rows), 0 if back else 1)
    return jnp.where(frame_of(r, 0, rows) == t, 1.0, 0.0).astype(BF)


def halo_pick(rows, start_seg_even):
    start, seg = start_seg_even
    i = lax.broadcasted_iota(jnp.int32, (HALO, rows), 0)
    r = lax.broadcasted_iota(jnp.int32, (HALO, rows), 1)
    return jnp.where(r == (i + start) * SEGS + seg, 1.0, 0.0).astype(BF)


def swap_halves(x):
    lane = lax.broadcasted_iota(jnp.int32, x.shape, 1)
    return jnp.where(
        (lane & (HEAD - 1)) < HEAD // 2,
        pltpu.roll(x, LANES - HEAD // 2, 1),
        pltpu.roll(x, HEAD // 2, 1),
    )


def rotate(x, cosine, sine):
    return x * cosine + swap_halves(x) * sine


def rotate_back(x, cosine, sine):
    return x * cosine - swap_halves(x) * sine


def pieces(x):
    hi = x.astype(BF).astype(F32)
    rest = x - hi
    mid = rest.astype(BF).astype(F32)
    return hi, mid, rest - mid


def pack_kernel(cw, bup, ggain, gbias, bqkv, ngain, nbias, obias, logits, sp_o):
    sp_o[...] = jnp.zeros_like(sp_o)
    for b in range(3):
        lanes = slice(b * LANES, (b + 1) * LANES)
        at = b * BLOCK_ROWS
        sp_o[at : at + TAPS, :] = cw[:, lanes]
        sp_o[at + ROW_UP0 : at + ROW_UP0 + 2, :] = bup[:, lanes]
        sp_o[at + ROW_GAIN : at + ROW_GAIN + 1, :] = ggain[:, lanes]
        sp_o[at + ROW_GB0 : at + ROW_GB0 + 2, :] = gbias[:, lanes]
    sp_o[ROW_QKV : ROW_QKV + 3, :] = bqkv[...]
    for i in range(4):
        lanes = slice(i * LANES, (i + 1) * LANES)
        for n in range(3):
            sp_o[ROW_NG + 4 * n + i : ROW_NG + 4 * n + i + 1, :] = ngain[n : n + 1, lanes]
            sp_o[ROW_NB + 4 * n + i : ROW_NB + 4 * n + i + 1, :] = nbias[n : n + 1, lanes]
        for n in range(2):
            sp_o[ROW_OB + 4 * n + i : ROW_OB + 4 * n + i + 1, :] = obias[n : n + 1, lanes]
    for n in range(2):
        sp_o[ROW_LOGIT + n : ROW_LOGIT + n + 1, :] = jnp.full((1, LANES), logits[n], F32)


def prologue_kernel(scal, frames, cotangent, wout, wup, wdown, own_o, oth_o, g_o, u_o, v_o, buf, sems):
    rows = own_o.shape[0]
    u, half = scal[0], scal[1]
    mine = pl.ds(pl.multiple_of(half * rows, rows), rows)
    other = pl.ds(pl.multiple_of((1 - half) * rows, rows), rows)
    copies = [
        pltpu.make_async_copy(frames.at[u, 0, mine, :], buf.at[0], sems.at[0]),
        pltpu.make_async_copy(frames.at[u, 0, other, :], buf.at[1], sems.at[1]),
        pltpu.make_async_copy(cotangent.at[u, 0, mine, :], buf.at[2], sems.at[2]),
    ]
    for c in copies:
        c.start()
    model, shard = wup.shape[1], wup.shape[2]
    for lb in range(4):
        lanes = slice(lb * LANES, (lb + 1) * LANES)
        u_o[lb * LANES : (lb + 1) * LANES, :] = wout[:, lanes]
        v_o[lb * shard : (lb + 1) * shard, :] = wdown[:, lanes]
    for hh in range(2):
        for b in range(3):
            at = W_UP + (hh * 3 + b) * model
            u_o[at : at + model, :] = wup[hh, :, b * LANES : (b + 1) * LANES]
    order = order_matrix(rows, False)
    for c, i, out in zip(copies, range(3), (own_o, oth_o, g_o)):
        c.wait()
        out[...] = dot(order, buf[i], NN).astype(BF)


def attention_forward_kernel(layer, scal, sp, cos_t, sin_t, h_own, h_oth, *refs):
    sets, refs = refs[:8], refs[8:]
    q_o, k_o, v_o, mix_o, lse_o, w_s, cs, sn, norm, lse_s, wsem, tsem = refs
    sp = sp.at[pl.ds(layer, 1)]
    rows, model = h_own.shape
    half, length = scal[1], scal[2]
    here, there = shard_copies(sets, w_s)
    fetch(scal[3] == layer, here, there, wsem)
    tables = [
        pltpu.make_async_copy(cos_t.at[half], cs, tsem.at[0]),
        pltpu.make_async_copy(sin_t.at[half], sn, tsem.at[1]),
    ]
    for c in tables:
        c.start()
    gain, bias = wide(sp, ROW_NG), wide(sp, ROW_NB)
    step = 64
    for src, base in ((h_own, 0), (h_oth, rows)):
        for r in range(0, rows, step):
            hat, unused = normalized(src[r : r + step, :].astype(F32))
            norm[base + r : base + r + step, :] = (hat * gain + bias).astype(BF)
    lse_s[...] = jnp.zeros_like(lse_s)
    for c in tables:
        c.wait()
    landed(here, wsem)
    total = 2 * rows
    row = lax.broadcasted_iota(jnp.int32, (total, LANES), 0)
    part = jnp.where(row < rows, half, 1 - half)
    position = frame_of(row & (rows - 1), part, rows)
    mask = jnp.where(position < length, 0.0, NEG)
    lane_k = lax.broadcasted_iota(jnp.int32, (total, LANES), 1)
    lane_q = lax.broadcasted_iota(jnp.int32, (rows, LANES), 1)

    def shard(j, carry):
        mj = scal[4 + j]
        bq = sp[0, mj, ROW_QKV : ROW_QKV + 1, :]
        bk = sp[0, mj, ROW_QKV + 1 : ROW_QKV + 2, :]
        bv = sp[0, mj, ROW_QKV + 2 : ROW_QKV + 3, :]
        everything = norm[...]
        q = rotate(dot(norm[:rows, :], w_s[j, 0], NN) + bq, cs[:rows, :], sn[:rows, :])
        q = q.astype(BF).astype(F32) * (1.0 / math.sqrt(HEAD))
        k = rotate(dot(everything, w_s[j, 1], NN) + bk, cs[...], sn[...]).astype(BF)
        v = (dot(everything, w_s[j, 2], NN) + bv).astype(BF)
        q_o[j] = q.astype(BF)
        k_o[j] = k
        v_o[j] = v
        kf = k.astype(F32)
        vt = v.astype(F32).T.astype(BF)
        outs = []
        block = 256
        for hd in range(2):
            spare = (1 - hd) * HEAD
            qm = jnp.where((lane_q >> 6) == hd, q, jnp.where(lane_q == spare, 1.0, 0.0)).astype(BF)
            km = jnp.where((lane_k >> 6) == hd, kf, jnp.where(lane_k == spare, mask, 0.0)).astype(BF)
            parts = []
            for b in range(0, rows, block):
                s = dot(km, qm[b : b + block, :], NT)
                top = jnp.max(s, axis=0, keepdims=True)
                p = jnp.exp(s - top)
                den = jnp.sum(p, axis=0, keepdims=True)
                p = (p * (1.0 / den)).astype(BF)
                parts.append(dot(vt[hd * HEAD : (hd + 1) * HEAD, :], p, NN))
                lse_s[pl.ds(2 * j + hd, 1), b : b + block] = top + jnp.log(den)
            outs.append(jnp.concatenate(parts, axis=1))
        mix_o[j] = jnp.concatenate(outs, axis=0).T.astype(BF)
        return carry

    lax.fori_loop(0, 4, shard, 0)
    lse_o[...] = lse_s[...].T


def gelu_parts(u):
    a = jnp.abs(u)
    t = 1.0 / (1.0 + (0.3275911 / math.sqrt(2.0)) * a)
    e = jnp.exp(-0.5 * u * u)
    poly = ((((1.061405429 * t - 1.453152027) * t + 1.421413741) * t - 0.284496736) * t + 0.254829592) * t
    tail = 0.5 * poly * e
    phi = jnp.where(u >= 0, 1.0 - tail, tail)
    return u * phi, phi + u * e * (1.0 / math.sqrt(2.0 * math.pi))


def halo_pads(pad, block, halo_ref, half, right_is_even):
    count = block.shape[0]
    pad[15 : 15 + count] = block
    seg = lax.broadcasted_iota(jnp.int32, (SEGS, LANES), 0)
    from_left = half.astype(F32)
    from_right = 1.0 - from_left
    for i in range(15):
        tail = pltpu.roll(block[count - 15 + i], 1, 0)
        edge = jnp.broadcast_to(halo_ref[i + 1 : i + 2, :], (SEGS, LANES)) * from_left
        pad[i] = jnp.where(seg == 0, edge, tail)
        head = pltpu.roll(block[i], SEGS - 1, 0)
        edge = jnp.broadcast_to(halo_ref[i : i + 1, :], (SEGS, LANES)) * from_right
        pad[15 + count + i] = jnp.where(seg == SEGS - 1, edge, head)


def mlp_forward_kernel(layer, scal, sp, h_own, h_oth, *refs):
    sets, refs = refs[:10], refs[10:]
    (act0_o, dact0_o, dact1_o, ghat_o, conv_o, gated_o, ginv_o, norm_o,
     ws, act0, act1, sums, gmean, ginv, pad, halo, wsem) = refs
    sp = sp.at[pl.ds(layer, 1)]
    rows, model = h_own.shape
    every = rows + HALO
    hidden = act0.shape[1]
    shard = hidden // 4
    half, length = scal[1], scal[2]
    here, there = slab_copies(sets, ws, W_UP, W_ROWS)
    fetch(scal[3] == layer, here, there, wsem)
    gain, bias = wide(sp, ROW_NG + 4), wide(sp, ROW_NB + 4)
    step = 64
    for r in range(0, rows, step):
        hat, unused = normalized(h_own[r : r + step, :].astype(F32))
        norm_o[r : r + step, :] = (hat * gain + bias).astype(BF)
    i = lax.broadcasted_iota(jnp.int32, (HALO, rows), 0)
    r = lax.broadcasted_iota(jnp.int32, (HALO, rows), 1)
    wanted = jnp.where(half == 0, i * SEGS, (i + rows // SEGS - HALO) * SEGS + SEGS - 1)
    pick = jnp.where(r == wanted, 1.0, 0.0).astype(BF)
    hat, unused = normalized(dot(pick, h_oth[...], NN))
    norm_o[rows:every, :] = (hat * gain + bias).astype(BF)
    sums[...] = jnp.zeros_like(sums)
    landed(here, wsem)

    width = 256
    chunk = 48

    def up(i, carry):
        lanes = pl.ds(pl.multiple_of(i * width, width), width)
        rows_of = []
        for hh, base in ((0, ROW_UP0), (1, ROW_UP1)):
            got = []
            for t in range(2):
                c = 2 * i + t
                got.append(sp[0, scal[8 + c], pl.ds(lax.rem(c, 3) * BLOCK_ROWS + base, 1), :])
            rows_of.append(jnp.concatenate(got, axis=1))
        slabs = []
        for hh in range(2):
            pair = []
            for t in range(2):
                c = 2 * i + t
                at = (hh * 3 + lax.rem(c, 3)) * model
                pair.append(ws[lax.div(c, 3), pl.ds(pl.multiple_of(at, model), model), :])
            slabs.append(jnp.concatenate(pair, axis=1))
        u0 = dot(norm_o[...], slabs[0], NN)
        u1 = dot(norm_o[...], slabs[1], NN)
        for r in range(0, every, chunk):
            a, d = gelu_parts(u0[r : r + chunk] + rows_of[0])
            act0[r : r + chunk, lanes] = a
            act0_o[r : r + chunk, lanes] = a.astype(BF)
            dact0_o[r : r + chunk, lanes] = d.astype(BF)
        for r in range(0, every, chunk):
            a, d = gelu_parts(u1[r : r + chunk] + rows_of[1])
            act1[r : r + chunk, lanes] = a
            dact1_o[r : r + chunk, lanes] = d.astype(BF)
            sums[r : r + chunk, :] += a[:, :LANES] + a[:, LANES:]
        return carry

    lax.fori_loop(0, hidden // width, up, 0)
    for r in range(0, every, chunk):
        center = jnp.sum(sums[r : r + chunk, :], axis=1, keepdims=True) * (1.0 / hidden)
        d = act1[r : r + chunk, :] - center
        spread = jnp.sum(d * d, axis=1, keepdims=True) * (1.0 / hidden)
        gmean[r : r + chunk, :] = jnp.broadcast_to(center, (chunk, LANES))
        ginv[r : r + chunk, :] = jnp.broadcast_to(lax.rsqrt(spread + EPS), (chunk, LANES))
    ginv_o[...] = ginv[0:rows, :]

    row = lax.broadcasted_iota(jnp.int32, (rows, LANES), 0)
    valid = jnp.where(frame_of(row, half, rows) < length, 1.0, 0.0)
    hrow = lax.broadcasted_iota(jnp.int32, (HALO, LANES), 0)
    valid_halo = jnp.where(jnp.where(half == 0, rows, rows - HALO) + hrow < length, 1.0, 0.0)
    count = rows // SEGS

    def gate(c, carry):
        lanes = pl.ds(pl.multiple_of(c * LANES, LANES), LANES)
        mj = scal[8 + c]
        base = lax.rem(c, 3) * BLOCK_ROWS
        ggain = sp[0, mj, pl.ds(base + ROW_GAIN, 1), :]
        gb0 = sp[0, mj, pl.ds(base + ROW_GB0, 1), :]
        gb1 = sp[0, mj, pl.ds(base + ROW_GB1, 1), :]
        hat = (act1[rows:every, lanes] - gmean[rows:every, :]) * ginv[rows:every, :]
        ghat_o[rows:every, lanes] = hat.astype(BF)
        halo[...] = (hat * ggain + gb0) * valid_halo
        hat = (act1[0:rows, lanes] - gmean[0:rows, :]) * ginv[0:rows, :]
        ghat_o[0:rows, lanes] = hat.astype(BF)
        normed = (hat * ggain + gb0) * valid
        halo_pads(pad, normed.reshape(count, SEGS, LANES), halo, half, True)
        part = 32
        for t0 in range(0, count, part):
            accs = [jnp.zeros((SEGS, LANES), F32) for _ in range(part)]
            for k in range(TAPS):
                w = jnp.broadcast_to(sp[0, mj, pl.ds(base + k, 1), :], (SEGS, LANES))
                for t in range(part):
                    accs[t] = accs[t] + w * pad[t0 + t + k]
            for t in range(0, part, 2):
                at = (t0 + t) * SEGS
                cv = jnp.concatenate([accs[t] + gb1, accs[t + 1] + gb1], axis=0)
                conv_o[at : at + 16, lanes] = cv.astype(BF)
                gated_o[at : at + 16, lanes] = (act0[at : at + 16, lanes] * cv).astype(BF)
        return carry

    lax.fori_loop(0, hidden // LANES, gate, 0)


def merge_forward_kernel(layer, scal, sp, h_own, mix, gated, *refs):
    u_sets, v_sets, refs = refs[:10], refs[10:18], refs[18:]
    o_o, nat_o, rhat_o, rstd_o, diff_o, ws, wv, usem, vsem = refs
    sp = sp.at[pl.ds(layer, 1)]
    rows, model = h_own.shape
    shard = wv.shape[1] // 4
    here, there = slab_copies(u_sets, ws, 0, W_UP)
    fetch(scal[3] == layer, here, there, usem)
    here_v, there_v = shard_copies(v_sets, wv)
    fetch(scal[3] == layer, here_v, there_v, vsem)
    landed(here, usem)
    landed(here_v, vsem)
    step = 64
    w0, w1 = branch_weights(sp)
    gain, bias = wide(sp, ROW_NG + 8), wide(sp, ROW_NB + 8)
    b0, b1 = wide(sp, ROW_OB), wide(sp, ROW_OB + 4)
    block = 256
    for r in range(0, rows, block):
        mixed = jnp.concatenate([mix[j, r : r + block, :] for j in range(4)], axis=1)
        brs, atts = [], []
        for lb in range(0, 4, 2):
            w = [
                jnp.concatenate(
                    [wv[j, (lb + t) * shard : (lb + t + 1) * shard, :] for j in range(4)], axis=0
                )
                for t in range(2)
            ]
            brs.append(dot(gated[r : r + block, :], jnp.concatenate(w, axis=1), NN))
            w = [
                jnp.concatenate(
                    [ws[j, (lb + t) * LANES : (lb + t + 1) * LANES, :] for j in range(4)], axis=0
                )
                for t in range(2)
            ]
            atts.append(dot(mixed, jnp.concatenate(w, axis=1), NN))
        br = jnp.concatenate(brs, axis=1)
        att = jnp.concatenate(atts, axis=1)
        for q in range(0, block, step):
            at = att[q : q + step] + b0
            bt = br[q : q + step] + b1
            res = h_own[r + q : r + q + step, :].astype(F32) + w0 * at + w1 * bt
            hat, inverse = normalized(res)
            diff_o[r + q : r + q + step, :] = at - bt
            rhat_o[r + q : r + q + step, :] = hat
            rstd_o[r + q : r + q + step, :] = jnp.broadcast_to(inverse, (step, LANES))
            o_o[r + q : r + q + step, :] = (hat * gain + bias).astype(BF)
    nat_o[...] = dot(order_matrix(rows, True), o_o[...], NN).astype(BF)


def merge_backward_kernel(
    layer, scal, sp, g, rhat, rstd, diff, mix, gated, gres_o, gatt_o, gbr_o, halo_o, sums_o, keep_o, send_o
):
    sp = sp.at[pl.ds(layer, 1)]
    rows, model = g.shape
    half = scal[1]
    gain = wide(sp, ROW_NG + 8)
    w0, w1 = branch_weights(sp)
    step = 64
    dgain = dbias = slope = jnp.zeros((1, model), F32)
    db = jnp.zeros((1, model), F32)
    for r in range(0, rows, step):
        gg = g[r : r + step, :].astype(F32)
        hat = rhat[r : r + step, :]
        dgain = dgain + jnp.sum(gg * hat, axis=0, keepdims=True)
        dbias = dbias + jnp.sum(gg, axis=0, keepdims=True)
        gg = gg * gain
        gr = rstd[r : r + step, 0:1] * (
            gg - jnp.mean(gg, axis=1, keepdims=True) - hat * jnp.mean(gg * hat, axis=1, keepdims=True)
        )
        gres_o[r : r + step, :] = gr
        gatt_o[r : r + step, :] = (w0 * gr).astype(BF)
        gbr_o[r : r + step, :] = (w1 * gr).astype(BF)
        db = db + jnp.sum(gr, axis=0, keepdims=True)
        slope = slope + jnp.sum(gr * diff[r : r + step, :], axis=0, keepdims=True)
    i = lax.broadcasted_iota(jnp.int32, (HALO, rows), 0)
    r = lax.broadcasted_iota(jnp.int32, (HALO, rows), 1)
    wanted = jnp.where(half == 0, (i + rows // SEGS - HALO) * SEGS + SEGS - 1, i * SEGS)
    pick = jnp.where(r == wanted, 1.0, 0.0).astype(BF)
    halo_o[...] = dot(pick, gbr_o[...], NN).astype(BF)
    slope = jnp.sum(slope, axis=1, keepdims=True)
    sums_o[...] = jnp.concatenate(
        [dgain, dbias, w0 * db, w1 * db, jnp.broadcast_to(slope, (1, model)), jnp.zeros((3, model), F32)], axis=0
    )
    shards = (keep_o.at[0], send_o.at[0], keep_o.at[1], send_o.at[1])
    shard = gated.shape[1] // 4
    for j in range(4):
        w = dot(mix[j], gatt_o[...], TN).astype(BF)
        for i in range(4):
            shards[j][i * LANES : (i + 1) * LANES, :] = w[:, i * LANES : (i + 1) * LANES]
        w = dot(gated[:, j * shard : (j + 1) * shard], gbr_o[...], TN).astype(BF)
        for i in range(4):
            at = OUT_ROWS + i * shard
            shards[j][at : at + shard, :] = w[:, i * LANES : (i + 1) * LANES]


def attention_backward_kernel(layer, scal, gatt, q_r, k_r, v_r, mix, lse, *refs):
    sets, refs = refs[:10], refs[10:]
    cos_t, sin_t, dq_o, own_o, oth_o, w_s, cs, sn, pbuf, dsbuf, dom, qm2, wsem, tsem = refs
    rows = gatt.shape[0]
    total = 2 * rows
    half, length = scal[1], scal[2]
    here, there = slab_copies(sets, w_s, 0, W_UP)
    fetch(scal[3] == layer, here, there, wsem)
    tables = [
        pltpu.make_async_copy(cos_t.at[half, pl.ds(0, rows), :], cs, tsem.at[0]),
        pltpu.make_async_copy(sin_t.at[half, pl.ds(0, rows), :], sn, tsem.at[1]),
    ]
    for c in tables:
        c.start()
    row = lax.broadcasted_iota(jnp.int32, (total, LANES), 0)
    part = jnp.where(row < rows, half, 1 - half)
    position = frame_of(row & (rows - 1), part, rows)
    mask = jnp.where(position < length, 0.0, NEG)
    lane_k = lax.broadcasted_iota(jnp.int32, (total, LANES), 1)
    lane_q = lax.broadcasted_iota(jnp.int32, (rows, LANES), 1)
    for c in tables:
        c.wait()
    landed(here, wsem)
    block = 256

    def shard(j, carry):
        wo = jnp.concatenate([w_s[j, lb * LANES : (lb + 1) * LANES, :] for lb in range(4)], axis=1)
        dm = dot(gatt[...], wo, NT).astype(BF).astype(F32)
        prod = dm * mix[j].astype(F32)
        q = q_r[j].astype(F32)
        k = k_r[j].astype(F32)
        v = v_r[j].astype(F32)
        kt = k.T.astype(BF)
        dqs = []
        for hd in range(2):
            spare = (1 - hd) * HEAD
            in_q, in_k = (lane_q >> 6) == hd, (lane_k >> 6) == hd
            minus_lse = -jnp.sum(jnp.where(lane_q == 2 * j + hd, lse[...], 0.0), axis=1, keepdims=True)
            minus_delta = -jnp.sum(jnp.where(in_q, prod, 0.0), axis=1, keepdims=True)
            l0, l1, l2 = pieces(minus_lse)
            e0, e1, e2 = pieces(minus_delta)
            qx = jnp.where(lane_q == spare, 1.0, 0.0)
            dx = jnp.zeros_like(qx)
            for n, (lp, ep) in enumerate(((l0, e0), (l1, e1), (l2, e2))):
                here = lane_q == spare + 1 + n
                qx = jnp.where(here, lp, qx)
                dx = jnp.where(here, ep, dx)
            one = jnp.where((lane_k > spare) & (lane_k < spare + 4), 1.0, 0.0)
            qh = jnp.where(in_q, q, qx).astype(BF)
            dh = jnp.where(in_q, dm, dx).astype(BF)
            kh = jnp.where(in_k, k, jnp.where(lane_k == spare, mask, one)).astype(BF)
            vh = jnp.where(in_k, v, one).astype(BF)
            dom[hd * rows : (hd + 1) * rows, :] = jnp.where(in_q, dm, 0.0).astype(BF)
            qm2[hd * rows : (hd + 1) * rows, :] = jnp.where(in_q, q, 0.0).astype(BF)
            parts = []
            for b in range(0, rows, block):
                p = jnp.exp(dot(kh, qh[b : b + block, :], NT))
                dp = dot(vh, dh[b : b + block, :], NT)
                ds = (p * dp).astype(BF)
                at = hd * rows + b
                pbuf[:, at : at + block] = p.astype(BF)
                dsbuf[:, at : at + block] = ds
                parts.append(dot(kt[hd * HEAD : (hd + 1) * HEAD, :], ds, NN))
            dqs.append(jnp.concatenate(parts, axis=1))
        dq = jnp.concatenate(dqs, axis=0).T * (1.0 / math.sqrt(HEAD))
        dq_o[j] = rotate_back(dq, cs[...], sn[...]).astype(BF)
        dk = dot(dsbuf[...], qm2[...], NN)
        dv = dot(pbuf[...], dom[...], NN)
        own_o[j, :, 0:LANES] = dk[:rows]
        own_o[j, :, LANES:] = dv[:rows]
        oth_o[j, :, 0:LANES] = dk[rows:].astype(BF)
        oth_o[j, :, LANES:] = dv[rows:].astype(BF)
        return carry

    lax.fori_loop(0, 4, shard, 0)


def mlp_backward_kernel(layer, scal, sp, gbr, ghalo, act0, dact0, dact1, ghat, conv, ginv, norm, *refs):
    sets, v_sets, refs = refs[:10], refs[10:18], refs[18:]
    dn_o, keep_o, send_o, ws, wv, dup, gpad, xpad, halo, hgrad, gcv, gbuf, hs, xs, small, wsem, vsem = refs
    sp = sp.at[pl.ds(layer, 1)]
    rows, model = gbr.shape
    every = rows + HALO
    hidden = gcv.shape[1]
    shard = hidden // 4
    half, length = scal[1], scal[2]
    here, there = slab_copies(sets, ws, W_UP, W_ROWS)
    fetch(scal[3] == layer, here, there, wsem)
    here_v, there_v = shard_copies(v_sets, wv)
    fetch(scal[3] == layer, here_v, there_v, vsem)
    gbuf[0:rows, :] = gbr[...]
    gbuf[rows:every, :] = ghalo[...]
    hs[...] = jnp.zeros_like(hs)
    xs[...] = jnp.zeros_like(xs)
    small[...] = jnp.zeros_like(small)
    landed(here_v, vsem)
    count = rows // SEGS
    width = 256
    chunk = 48

    def down(i, carry):
        lanes = pl.ds(pl.multiple_of(i * width, width), width)
        pair = []
        for t in range(2):
            c = 2 * i + t
            base = lax.rem(c, 3) * LANES
            pair.append(
                jnp.concatenate(
                    [
                        wv[lax.div(c, 3), pl.ds(pl.multiple_of(base + lb * shard, LANES), LANES), :]
                        for lb in range(4)
                    ],
                    axis=1,
                )
            )
        g = dot(gbuf[...], jnp.concatenate(pair, axis=0), NT)
        for r in range(0, every, chunk):
            gr = g[r : r + chunk].astype(BF).astype(F32)
            gcv[r : r + chunk, lanes] = gr * act0[r : r + chunk, lanes].astype(F32)
        for r in range(0, rows, 64):
            gr = g[r : r + 64].astype(BF).astype(F32)
            keep = gr * conv[r : r + 64, lanes].astype(F32) * dact0[r : r + 64, lanes].astype(F32)
            dup[0, r : r + 64, lanes] = keep.astype(BF)
        return carry

    lax.fori_loop(0, hidden // width, down, 0)
    row = lax.broadcasted_iota(jnp.int32, (rows, LANES), 0)
    valid = jnp.where(frame_of(row, half, rows) < length, 1.0, 0.0)
    hrow = lax.broadcasted_iota(jnp.int32, (HALO, LANES), 0)
    valid_halo = jnp.where(jnp.where(half == 0, rows, rows - HALO) + hrow < length, 1.0, 0.0)

    def fold(x):
        return jnp.sum(x, axis=0, keepdims=True)

    def conv_back(c, carry):
        lanes = pl.ds(pl.multiple_of(c * LANES, LANES), LANES)
        mj = scal[8 + c]
        b = lax.rem(c, 3)
        j = lax.div(c, 3)
        base = b * BLOCK_ROWS
        ggain = sp[0, mj, pl.ds(base + ROW_GAIN, 1), :]
        gb0 = sp[0, mj, pl.ds(base + ROW_GB0, 1), :]
        halo[...] = (ghat[rows:every, lanes].astype(F32) * ggain + gb0) * valid_halo
        normed = (ghat[0:rows, lanes].astype(F32) * ggain + gb0) * valid
        halo_pads(xpad, normed.reshape(count, SEGS, LANES), halo, half, True)
        halo[...] = gcv[rows:every, lanes]
        gown = gcv[0:rows, lanes]
        halo_pads(gpad, gown.reshape(count, SEGS, LANES), halo, half, True)
        small[j, pl.ds(base + ROW_GB1, 1), :] = fold(gown)
        accs = [jnp.zeros((SEGS, LANES), F32) for _ in range(TAPS)]
        for t in range(count):
            gt = gpad[15 + t]
            for k in range(TAPS):
                accs[k] = accs[k] + gt * xpad[t + k]
        for k in range(TAPS):
            small[j, pl.ds(base + k, 1), :] = fold(accs[k])
        part = 32
        dgain = jnp.zeros((SEGS, LANES), F32)
        dbias = jnp.zeros((SEGS, LANES), F32)
        for t0 in range(0, count, part):
            accs = [jnp.zeros((SEGS, LANES), F32) for _ in range(part)]
            for k in range(TAPS):
                w = jnp.broadcast_to(sp[0, mj, pl.ds(base + k, 1), :], (SEGS, LANES))
                for t in range(part):
                    accs[t] = accs[t] + w * gpad[t0 + t + (TAPS - 1) - k]
            for t in range(0, part, 2):
                at = (t0 + t) * SEGS
                gn = jnp.concatenate([accs[t], accs[t + 1]], axis=0) * valid[at : at + 16]
                hat = ghat[at : at + 16, lanes].astype(F32)
                gh = gn * hat
                dgain = dgain + gh[0:8] + gh[8:16]
                dbias = dbias + gn[0:8] + gn[8:16]
                gn = gn * ggain
                hgrad[at : at + 16, lanes] = gn
                hs[at : at + 16, :] += gn
                xs[at : at + 16, :] += gn * hat
        small[j, pl.ds(base + ROW_GAIN, 1), :] = fold(dgain)
        small[j, pl.ds(base + ROW_GB0, 1), :] = fold(dbias)
        return carry

    lax.fori_loop(0, hidden // LANES, conv_back, 0)
    for r in range(0, rows, 64):
        a = jnp.sum(hs[r : r + 64, :], axis=1, keepdims=True) * (1.0 / hidden)
        x = jnp.sum(xs[r : r + 64, :], axis=1, keepdims=True) * (1.0 / hidden)
        hs[r : r + 64, :] = jnp.broadcast_to(a, (64, LANES))
        xs[r : r + 64, :] = jnp.broadcast_to(x, (64, LANES))

    def gate_back(c, carry):
        lanes = pl.ds(pl.multiple_of(c * LANES, LANES), LANES)
        b = lax.rem(c, 3)
        j = lax.div(c, 3)
        base = b * BLOCK_ROWS
        s0 = jnp.zeros((1, LANES), F32)
        s1 = jnp.zeros((1, LANES), F32)
        for r in range(0, rows, 64):
            hat = ghat[r : r + 64, lanes].astype(F32)
            gi = ginv[r : r + 64, :] * (hgrad[r : r + 64, lanes] - hs[r : r + 64, :] - hat * xs[r : r + 64, :])
            d1 = (gi * dact1[r : r + 64, lanes].astype(F32)).astype(BF)
            dup[1, r : r + 64, lanes] = d1
            s1 = s1 + fold(d1.astype(F32))
            s0 = s0 + fold(dup[0, r : r + 64, lanes].astype(F32))
        small[j, pl.ds(base + ROW_UP0, 1), :] = s0
        small[j, pl.ds(base + ROW_UP1, 1), :] = s1
        return carry

    lax.fori_loop(0, hidden // LANES, gate_back, 0)
    landed(here, wsem)
    for hh in range(2):
        w = jnp.concatenate(
            [ws[j, (hh * 3 + b) * model : (hh * 3 + b + 1) * model, :] for j in range(4) for b in range(3)], axis=1
        )
        if hh == 0:
            dn_o[...] = dot(dup[hh], w, NT)
        else:
            dn_o[...] += dot(dup[hh], w, NT)
    shards = (keep_o.at[0], send_o.at[0], keep_o.at[1], send_o.at[1])
    own_norm = norm[0:rows, :]
    for i in range(hidden // width):
        lo = i * width
        for hh in range(2):
            w = dot(own_norm, dup[hh, :, lo : lo + width], TN).astype(BF)
            for t in range(2):
                j, b = divmod(2 * i + t, 3)
                at = (hh * 3 + b) * model
                shards[j][at : at + model, :] = w[:, t * LANES : (t + 1) * LANES]
    for j in range(4):
        shards[j][UP_ROWS:M_ROWS, :] = small[j].astype(BF)


def input_backward_kernel(layer, scal, sp, h_own, gres, dn_mlp, dq, dkv_own, dkv_got, *refs):
    sets, refs = refs[:8], refs[8:]
    cos_t, sin_t, g_o, nat_o, keep_o, send_o, wq, cs, sn, dall, norm, xhat, xinv, small, wsem, tsem = refs
    sp = sp.at[pl.ds(layer, 1)]
    rows, model = h_own.shape
    half = scal[1]
    here, there = shard_copies(sets, wq)
    fetch(scal[3] == layer, here, there, wsem)
    shards = (keep_o.at[0], send_o.at[0], keep_o.at[1], send_o.at[1])
    tables = [
        pltpu.make_async_copy(cos_t.at[half, pl.ds(0, rows), :], cs, tsem.at[0]),
        pltpu.make_async_copy(sin_t.at[half, pl.ds(0, rows), :], sn, tsem.at[1]),
    ]
    for c in tables:
        c.start()
    gain, bias = wide(sp, ROW_NG), wide(sp, ROW_NB)
    gain_mlp = wide(sp, ROW_NG + 4)
    step = 64
    for r in range(0, rows, step):
        hat, inverse = normalized(h_own[r : r + step, :].astype(F32))
        xhat[r : r + step, :] = hat
        xinv[r : r + step, :] = jnp.broadcast_to(inverse, (step, LANES))
        norm[r : r + step, :] = (hat * gain + bias).astype(BF)
    for c in tables:
        c.wait()
    for j in range(4):
        at = j * 3 * LANES
        dall[:, at : at + LANES] = dq[j]
        dk = dkv_own[j, :, 0:LANES] + dkv_got[j ^ 1, :, 0:LANES].astype(F32)
        dall[:, at + LANES : at + 2 * LANES] = rotate_back(dk, cs[...], sn[...]).astype(BF)
        dv = dkv_own[j, :, LANES:] + dkv_got[j ^ 1, :, LANES:].astype(F32)
        dall[:, at + 2 * LANES : at + 3 * LANES] = dv.astype(BF)
    landed(here, wsem)
    small[...] = jnp.zeros_like(small)
    dn = dot(dall[...], jnp.concatenate([wq[j, i] for j in range(4) for i in range(3)], axis=1), NT)
    dg0 = db0 = dg1 = db1 = jnp.zeros((1, model), F32)
    for r in range(0, rows, step):
        hat = xhat[r : r + step, :]
        a = dn[r : r + step]
        m = dn_mlp[r : r + step, :]
        dg0 = dg0 + jnp.sum(a * hat, axis=0, keepdims=True)
        db0 = db0 + jnp.sum(a, axis=0, keepdims=True)
        dg1 = dg1 + jnp.sum(m * hat, axis=0, keepdims=True)
        db1 = db1 + jnp.sum(m, axis=0, keepdims=True)
        gg = a * gain + m * gain_mlp
        dx = xinv[r : r + step, 0:1] * (
            gg - jnp.mean(gg, axis=1, keepdims=True) - hat * jnp.mean(gg * hat, axis=1, keepdims=True)
        )
        g_o[r : r + step, :] = (gres[r : r + step, :] + dx).astype(BF)
    nat_o[...] = dot(order_matrix(rows, True), g_o[...], NN).astype(BF)
    for j in range(4):
        for n, v in enumerate((dg0, dg1, db0, db1)):
            for i in range(4):
                small[j, 8 + 4 * n + i : 9 + 4 * n + i, :] = v[:, i * LANES : (i + 1) * LANES]
    for j in range(4):
        at = j * 3 * LANES
        d = dall[:, at : at + 3 * LANES]
        w = dot(norm[...], d, TN).astype(BF)
        s = jnp.sum(d.astype(F32), axis=0, keepdims=True)
        for i in range(3):
            lo = i * model
            shards[j][lo : lo + model, :] = w[:, i * LANES : (i + 1) * LANES]
            small[j, i : i + 1, :] = s[:, i * LANES : (i + 1) * LANES]
        shards[j][QKV_ROWS:A_ROWS, :] = small[j].astype(BF)


def assemble_kernel(scal, *refs):
    parts, out = refs[:4], refs[4]
    rows = parts[0].shape[1]
    for n in range(8):
        place, half = scal[24 + n], scal[32 + n]
        part = parts[(n & 1) + (n & 2)]
        out[place, pl.ds(pl.multiple_of(half * rows, rows), rows), :] = part[n >> 2]


def finale_kernel(d_lo, d_hi, m_lo, m_hi, a_lo, a_hi, qkv_o, out_o, up_o, down_o, small_o):
    def rows_of(lo, hi, a, b):
        n = lo.shape[0]
        if b <= n:
            return lo[a:b, :].astype(F32)
        if a >= n:
            return hi[a - n : b - n, :].astype(F32)
        return jnp.concatenate([lo[a:n, :], hi[0 : b - n, :]], axis=0).astype(F32)

    model, shard = up_o.shape[1], up_o.shape[2]
    for i in range(3):
        qkv_o[i] = rows_of(a_lo, a_hi, i * model, (i + 1) * model)
    for lb in range(4):
        lanes = slice(lb * LANES, (lb + 1) * LANES)
        out_o[:, lanes] = rows_of(d_lo, d_hi, lb * LANES, (lb + 1) * LANES)
        down_o[:, lanes] = rows_of(d_lo, d_hi, OUT_ROWS + lb * shard, OUT_ROWS + (lb + 1) * shard)
    for hh in range(2):
        for b in range(3):
            at = (hh * 3 + b) * model
            up_o[hh, :, b * LANES : (b + 1) * LANES] = rows_of(m_lo, m_hi, at, at + model)
    small_o[0:128, :] = rows_of(m_lo, m_hi, UP_ROWS, UP_ROWS + 128)
    small_o[128:192, :] = rows_of(a_lo, a_hi, QKV_ROWS, A_ROWS)


def exchange(x, axis, bit):
    n = lax.axis_size(axis)
    return lax.ppermute(x, axis, [(i, i ^ bit) for i in range(n)])


def fence(*xs):
    return lax.optimization_barrier(xs)


def total(*xs):
    out = xs[0].astype(F32)
    for x in xs[1:]:
        out = out + x.astype(F32)
    return out


def sum_over_dp(x):
    n = lax.axis_size("dp")
    if n & (n - 1):
        return lax.psum(x.astype(F32), "dp").astype(BF)
    d = lax.axis_index("dp")
    bits = [1 << i for i in range(n.bit_length() - 1)]
    for bit in bits:
        rows = x.shape[0] // 2
        low = (d & bit) == 0
        send = jnp.where(low, x[rows:], x[:rows])
        keep = jnp.where(low, x[:rows], x[rows:])
        x = total(keep, exchange(send, "dp", bit)).astype(BF)
    for bit in reversed(bits):
        low = (d & bit) == 0
        got = exchange(x, "dp", bit)
        x = jnp.concatenate([jnp.where(low, x, got), jnp.where(low, got, x)], axis=0)
    return x


def halves(x, owner):
    rows = x.shape[0] // 2
    return jnp.where(owner, x[:rows], x[rows:]), jnp.where(owner, x[rows:], x[:rows])


def rotary_constants(length):
    half_width = HEAD // 2
    freq = np.exp(np.arange(half_width, dtype=np.float32) * np.float32(-math.log(10000.0) / half_width))
    rows = length // 2
    r = np.arange(rows)
    place = (r % SEGS) * (rows // SEGS) + r // SEGS
    cosines, sines = [], []
    for half in range(2):
        t = np.concatenate([half * rows + place, (1 - half) * rows + place]).astype(np.float32)
        angle = (t[:, None] * freq.astype(np.float32)[None, :]).astype(np.float32)
        c, s = np.cos(angle.astype(np.float64)), np.sin(angle.astype(np.float64))
        cosines.append(np.concatenate([c, c, c, c], axis=1))
        sines.append(np.concatenate([-s, s, -s, s], axis=1))
    return np.stack(cosines).astype(np.float32), np.stack(sines).astype(np.float32)


def per_device(frames, lengths, out_grad, *weights):
    (norm_gains, norm_biases, wqkv, bqkv, wout, wup, bup, ggain, gbias, cw, wdown, obias, logits) = [
        w[0] for w in weights
    ]
    micro, utterances, length, model = frames.shape
    n_sec, n_mp = lax.axis_size("section"), lax.axis_size("mp")
    assert utterances == 1 and n_sec == 2 and n_mp == 4 and micro == 4
    rows = length // 2
    shard = wdown.shape[0]
    hidden = shard * n_mp
    every = rows + HALO
    s, m = lax.axis_index("section"), lax.axis_index("mp")
    u = s * 2 + (m >> 1)
    half = m & 1
    own_length = lax.dynamic_index_in_dim(lengths[:, 0], u, 0, keepdims=False)
    ns = np.arange(40)
    xors = np.zeros(40, np.int32)
    xors[4:8] = np.arange(4)
    xors[8:20] = np.arange(12) // 3
    xors[24:32] = ns[:8] >> 1 & 1
    xors[32:40] = ns[:8] & 1
    sec_bits = np.zeros(40, np.int32)
    sec_bits[24:32] = ns[:8] >> 2
    idx = jnp.asarray(ns)
    by_shard = jnp.asarray(xors)
    by_place = (s ^ jnp.asarray(sec_bits)) * 2 + ((m >> 1) ^ jnp.asarray(xors))
    by_half = half ^ jnp.asarray(xors)
    scal = jnp.where(idx < 24, by_shard, jnp.where(idx < 32, by_place, by_half))
    for i, v in enumerate((u, half, own_length, s)):
        scal = jnp.where(idx == i, v, scal)
    scal = scal.astype(jnp.int32)

    x_of = lambda v: exchange(v, "section", 1)
    y_of = lambda v: exchange(v, "mp", 2)
    core_of = lambda v: exchange(v, "mp", 1)
    flat = shape((rows, model), BF)
    rows_f32 = shape((rows, model), F32)
    stat = shape((rows, LANES), F32)
    wide_bf = shape((rows, hidden), BF)
    halo_bf = shape((every, hidden), BF)

    def head_pack(n):
        return shape((4, n, LANES), BF)

    first = s == 0

    q_x, q_y, q_sib = x_of(wqkv), y_of(wqkv), core_of(wqkv)
    packed = call(
        pack_kernel,
        [cw, bup, ggain[None], gbias, bqkv, norm_gains, norm_biases, obias, logits],
        [VMEM] * 8 + [SMEM],
        [shape((PACK_ROWS, LANES), F32)],
        [],
        0, 8)[0]
    packed_x = x_of(packed)
    h_own, h_oth, g_last, u_own, v_own = call(
        prologue_kernel,
        [scal, frames, out_grad, wout, wup, wdown],
        [SMEM, ANY, ANY] + [VMEM] * 3,
        [flat, flat, flat, shape((W_ROWS, LANES), BF), shape((DOWN_ROWS, LANES), BF)],
        [pltpu.VMEM((3, rows, model), BF), pltpu.SemaphoreType.DMA((3,))],
        6 * rows * rows * model, 16)
    h_own, packed_x = fence(h_own, packed_x)
    sections = jnp.stack([jnp.where(first, packed, packed_x), jnp.where(first, packed_x, packed)])
    sections, q_x, q_y = fence(sections, q_x, q_y)
    u_x = x_of(u_own)
    sections_y = y_of(sections)
    q_d = y_of(q_x)
    q_xs, q_ys = core_of(q_x), core_of(q_y)
    sp_a = jnp.stack([sections, sections_y], axis=1)
    sp_b = core_of(sp_a)
    sp = jnp.stack([sp_a, sp_b], axis=2).reshape(2, n_mp, PACK_ROWS, LANES)
    sp, q_d, u_late = fence(sp, q_d, u_own)
    u_y = y_of(u_late)
    q_ds = core_of(q_d)
    w_qkv = [wqkv, q_sib, q_y, q_ys, q_x, q_xs, q_d, q_ds]

    cos_np, sin_np = rotary_constants(length)
    cos_t, sin_t = jnp.asarray(cos_np), jnp.asarray(sin_np)

    def attention_forward(layer, scal, h_own, h_oth):
        return call(
            functools.partial(attention_forward_kernel, layer),
            [scal, sp, cos_t, sin_t, h_own, h_oth, *w_qkv],
            [SMEM, VMEM, ANY, ANY, VMEM, VMEM] + [ANY] * 8,
            [head_pack(rows), head_pack(length), head_pack(length), head_pack(rows), stat],
            [
                pltpu.VMEM((4, 3, model, LANES), BF),
                pltpu.VMEM((length, LANES), F32),
                pltpu.VMEM((length, LANES), F32),
                pltpu.VMEM((length, model), BF),
                pltpu.VMEM((LANES, rows), F32),
                pltpu.SemaphoreType.DMA((4,)),
                pltpu.SemaphoreType.DMA((2,)),
            ],
            10 * rows * length * model, 20)

    def mlp_forward(layer, scal, h_own, h_oth):
        return call(
            functools.partial(mlp_forward_kernel, layer),
            [scal, sp, h_own, h_oth, *w_u],
            [SMEM, VMEM, VMEM, VMEM] + [ANY] * 10,
            [halo_bf, halo_bf, halo_bf, halo_bf, wide_bf, wide_bf, stat, shape((every, model), BF)],
            [
                pltpu.VMEM((4, W_ROWS - W_UP, LANES), BF),
                pltpu.VMEM((every, hidden), F32),
                pltpu.VMEM((every, hidden), F32),
                pltpu.VMEM((every, LANES), F32),
                pltpu.VMEM((every, LANES), F32),
                pltpu.VMEM((every, LANES), F32),
                pltpu.VMEM((rows // SEGS + 30, SEGS, LANES), F32),
                pltpu.VMEM((HALO, LANES), F32),
                pltpu.SemaphoreType.DMA((8,)),
            ],
            8 * rows * model * hidden, 32)

    def merge_forward(layer, scal, h_own, mix, gated):
        return call(
            functools.partial(merge_forward_kernel, layer),
            [scal, sp, h_own, mix, gated, *w_u, *w_v],
            [SMEM, VMEM, VMEM, VMEM, VMEM] + [ANY] * 18,
            [flat, flat, rows_f32, stat, rows_f32],
            [
                pltpu.VMEM((4, W_UP, LANES), BF),
                pltpu.VMEM((4, DOWN_ROWS, LANES), BF),
                pltpu.SemaphoreType.DMA((8,)),
                pltpu.SemaphoreType.DMA((4,)),
            ],
            2 * rows * model * hidden, 16)

    att = attention_forward(0, scal, h_own, h_oth)
    att, u_x, v_late = fence(att, u_x, v_own)
    u_xs = core_of(u_x)
    v_x = x_of(v_late)
    v_late, u_y = fence(v_late, u_y)
    d1, d2 = y_of(u_x[:SPLIT]), x_of(u_y[SPLIT:])
    u_sib, u_ys = core_of(u_own), core_of(u_y)
    v_y = y_of(v_late)
    d1s, d2s = core_of(d1), core_of(d2)
    w_u = [u_own, u_sib, u_y, u_ys, u_x, u_xs, d1, d1s, d2, d2s]
    mlp0 = mlp_forward(0, scal, h_own, h_oth)
    mlp0, v_x, v_y = fence(mlp0, v_x, v_y)
    v_d = x_of(v_y)
    v_sib, v_xs, v_ys = core_of(v_own), core_of(v_x), core_of(v_y)
    v_ds = core_of(v_d)
    w_v = [v_own, v_sib, v_y, v_ys, v_x, v_xs, v_d, v_ds]
    top0 = merge_forward(0, scal, h_own, att[3], mlp0[5])
    saved = [(h_own, att, mlp0, top0)]
    h_own, h_oth = top0[0], core_of(top0[0])
    att = attention_forward(1, scal, h_own, h_oth)
    mlp1 = mlp_forward(1, scal, h_own, h_oth)
    top1 = merge_forward(1, scal, h_own, att[3], mlp1[5])
    saved.append((h_own, att, mlp1, top1))

    def merge_backward(layer, scal, g):
        h, att, mlp, top = saved[layer]
        return call(
            functools.partial(merge_backward_kernel, layer),
            [scal, sp, g, top[2], top[3], top[4], att[3], mlp[5]],
            [SMEM, VMEM] + [VMEM] * 6,
            [rows_f32, flat, flat, shape((HALO, model), BF), shape((8, model), F32),
             shape((2, D_ROWS, LANES), BF), shape((2, D_ROWS, LANES), BF)],
            [],
            2 * rows * model * (hidden + model), 16)

    def mlp_backward(layer, scal, gbr, halo_in):
        mlp = saved[layer][2]
        return call(
            functools.partial(mlp_backward_kernel, layer),
            [scal, sp, gbr, halo_in, *mlp[0:5], *mlp[6:8], *w_u, *w_v],
            [SMEM, VMEM] + [VMEM] * 9 + [ANY] * 18,
            [rows_f32, shape((2, M_ROWS, LANES), BF), shape((2, M_ROWS, LANES), BF)],
            [
                pltpu.VMEM((4, W_ROWS - W_UP, LANES), BF),
                pltpu.VMEM((4, DOWN_ROWS, LANES), BF),
                pltpu.VMEM((2, rows, hidden), BF),
                pltpu.VMEM((rows // SEGS + 30, SEGS, LANES), F32),
                pltpu.VMEM((rows // SEGS + 30, SEGS, LANES), F32),
                pltpu.VMEM((HALO, LANES), F32),
                pltpu.VMEM((rows, hidden), F32),
                pltpu.VMEM((every, hidden), F32),
                pltpu.VMEM((every, model), BF),
                pltpu.VMEM((rows, LANES), F32),
                pltpu.VMEM((rows, LANES), F32),
                pltpu.VMEM((4, LANES, LANES), F32),
                pltpu.SemaphoreType.DMA((8,)),
                pltpu.SemaphoreType.DMA((4,)),
            ],
            16 * rows * model * hidden, 40)

    def attention_backward(layer, scal, gatt):
        att = saved[layer][1]
        return call(
            functools.partial(attention_backward_kernel, layer),
            [scal, gatt, *att, *w_u, cos_t, sin_t],
            [SMEM] + [VMEM] * 6 + [ANY] * 12,
            [head_pack(rows), shape((4, rows, 2 * LANES), F32), shape((4, rows, 2 * LANES), BF)],
            [
                pltpu.VMEM((4, W_UP, LANES), BF),
                pltpu.VMEM((rows, LANES), F32),
                pltpu.VMEM((rows, LANES), F32),
                pltpu.VMEM((length, 2 * rows), BF),
                pltpu.VMEM((length, 2 * rows), BF),
                pltpu.VMEM((2 * rows, LANES), BF),
                pltpu.VMEM((2 * rows, LANES), BF),
                pltpu.SemaphoreType.DMA((4,)),
                pltpu.SemaphoreType.DMA((2,)),
            ],
            12 * rows * length * model, 26)

    def input_backward(layer, scal, gres, dn_mlp, dq, dkv_own, dkv_got):
        h = saved[layer][0]
        return call(
            functools.partial(input_backward_kernel, layer),
            [scal, sp, h, gres, dn_mlp, dq, dkv_own, dkv_got, *w_qkv, cos_t, sin_t],
            [SMEM, VMEM] + [VMEM] * 6 + [ANY] * 10,
            [flat, flat, shape((2, A_ROWS, LANES), BF), shape((2, A_ROWS, LANES), BF)],
            [
                pltpu.VMEM((4, 3, model, LANES), BF),
                pltpu.VMEM((rows, LANES), F32),
                pltpu.VMEM((rows, LANES), F32),
                pltpu.VMEM((rows, 12 * LANES), BF),
                pltpu.VMEM((rows, model), BF),
                pltpu.VMEM((rows, model), F32),
                pltpu.VMEM((rows, LANES), F32),
                pltpu.VMEM((4, 64, LANES), F32),
                pltpu.SemaphoreType.DMA((4,)),
                pltpu.SemaphoreType.DMA((2,)),
            ],
            14 * rows * model * model, 24)

    natural0, natural1 = top0[1], top1[1]
    out_keep = jnp.where(first, natural0, natural1)
    out_send = jnp.where(first, natural1, natural0)
    sc, out_send, out_keep = fence(scal, out_send, out_keep)
    out_got = x_of(out_send)
    gres, gatt, gbr, halo_out, tops1, d_keep, d_send = merge_backward(1, sc, g_last)
    gbr, halo_out, d_send = fence(gbr, halo_out, d_send)
    halo_in = core_of(halo_out)
    d_got = core_of(d_send)
    dn_mlp, m_keep, m_send = mlp_backward(1, scal, gbr, halo_in)
    gatt, out_got, d_got, m_send = fence(gatt, out_got, d_got, m_send)
    out_pair = jnp.stack([out_keep, out_got])
    d_away = total(d_keep[1], d_got[1]).astype(BF)
    sc, d_away, out_pair = fence(scal, d_away, out_pair)
    m_got = core_of(m_send)
    d_y = y_of(d_away)
    dq, dkv_own, dkv_oth = attention_backward(1, sc, gatt)
    dq, dkv_oth, m_got, d_y = fence(dq, dkv_oth, m_got, d_y)
    dkv_got = core_of(dkv_oth)
    m_away = total(m_keep[1], m_got[1]).astype(BF)
    owner1 = jnp.logical_not(first)
    d_mine, d_give = halves(total(d_keep[0], d_got[0], d_y), owner1)
    sc, m_away, d_give = fence(scal, m_away, d_give.astype(BF))
    m_y = y_of(m_away)
    d_x = x_of(d_give)
    g, ingrad1, a_keep, a_send = input_backward(1, sc, gres, dn_mlp, dq, dkv_own, dkv_got)

    g, a_send, d_x = fence(g, a_send, d_x)
    a_got = core_of(a_send)
    d1_part = total(d_mine, d_x).astype(BF)
    gres, gatt, gbr, halo_out, tops0, d0_keep, d0_send = merge_backward(0, scal, g)
    gbr, halo_out, d0_send, m_y, a_got, d1_part = fence(gbr, halo_out, d0_send, m_y, a_got, d1_part)
    halo_in = core_of(halo_out)
    d0_got = core_of(d0_send)
    m_mine, m_give = halves(total(m_keep[0], m_got[0], m_y), owner1)
    a_away = total(a_keep[1], a_got[1]).astype(BF)
    sc, m_give, a_away = fence(scal, m_give.astype(BF), a_away)
    m_x = x_of(m_give)
    a_y = y_of(a_away)
    out_y = y_of(out_pair)
    dn_mlp, m0_keep, m0_send = mlp_backward(0, sc, gbr, halo_in)
    gatt, m_x, a_y, m0_send, d0_got = fence(gatt, m_x, a_y, m0_send, d0_got)
    m1_part = total(m_mine, m_x).astype(BF)
    dm1_half = lax.psum(jnp.concatenate([d1_part, m1_part], axis=0), "dp")
    a_mine, a_give = halves(total(a_keep[0], a_got[0], a_y), owner1)
    d_away = total(d0_keep[1], d0_got[1]).astype(BF)
    sc, a_give, d_away = fence(scal, a_give.astype(BF), d_away)
    a_x = x_of(a_give)
    d_y = y_of(d_away)
    m0_got = core_of(m0_send)
    dq, dkv_own, dkv_oth = attention_backward(0, sc, gatt)
    dq, dkv_oth, a_x, m0_got, d_y, out_y = fence(dq, dkv_oth, a_x, m0_got, d_y, out_y)
    dkv_got = core_of(dkv_oth)
    m_away = total(m0_keep[1], m0_got[1]).astype(BF)
    d_mine, d_give = halves(total(d0_keep[0], d0_got[0], d_y), first)
    a1_part = total(a_mine, a_x).astype(BF)
    sc, m_away, d_give, a1_part = fence(scal, m_away, d_give.astype(BF), a1_part)
    m_y = y_of(m_away)
    d_x = x_of(d_give)
    out_ps, out_ys = core_of(out_pair), core_of(out_y)
    g, ingrad0, a_keep, a_send = input_backward(0, sc, gres, dn_mlp, dq, dkv_own, dkv_got)
    ingrad0, a_send, m_y, d_x, out_ps, out_ys = fence(ingrad0, a_send, m_y, d_x, out_ps, out_ys)

    a_got = core_of(a_send)
    m_mine, m_give = halves(total(m0_keep[0], m0_got[0], m_y), first)
    m_x = x_of(m_give.astype(BF))
    a_y = y_of(total(a_keep[1], a_got[1]).astype(BF))
    in_keep = jnp.where(first, ingrad0, ingrad1)
    in_got = x_of(jnp.where(first, ingrad1, ingrad0))
    dm0_half = sum_over_dp(jnp.concatenate([total(d_mine, d_x), total(m_mine, m_x)], axis=0).astype(BF))
    a_mine, a_give = halves(total(a_keep[0], a_got[0], a_y), first)
    a0_part = total(a_mine, x_of(a_give.astype(BF))).astype(BF)
    a0_half = sum_over_dp(jnp.concatenate([a0_part, a1_part], axis=0))
    a1_half = a0_half[A_ROWS // 2 :]
    a0_half = a0_half[: A_ROWS // 2]
    in_pair = jnp.stack([in_keep, in_got])
    in_y = y_of(in_pair)
    in_ps, in_ys = core_of(in_pair), core_of(in_y)

    def assemble(parts):
        return call(
            assemble_kernel, [scal, *parts], [SMEM] + [VMEM] * 4, [shape((micro, length, model), BF)], [], 0, 10)[0]

    layer_out = assemble([out_pair, out_ps, out_y, out_ys])
    input_grad = assemble([in_pair, in_ps, in_y, in_ys])

    dm_lo, dm_hi = jnp.where(first, dm0_half, dm1_half), x_of(jnp.where(first, dm1_half, dm0_half))
    a_lo, a_hi = jnp.where(first, a0_half, a1_half), x_of(jnp.where(first, a1_half, a0_half))
    cut = D_ROWS // 2
    g_qkv, g_out, g_up, g_down, small = call(
        finale_kernel,
        [dm_lo[:cut], dm_hi[:cut], dm_lo[cut:], dm_hi[cut:], a_lo, a_hi],
        [VMEM] * 6,
        [shape((3, model, LANES), F32), shape((LANES, model), F32), shape((2, model, shard), F32),
         shape((shard, model), F32), shape((192, LANES), F32)],
        [],
        0, 16)
    tops = jnp.stack([tops0, tops1])
    for axis, bit in [("mp", 1), ("mp", 2), ("section", 1)]:
        tops = tops + exchange(tops, axis, bit)
    n_dp = lax.axis_size("dp")
    if n_dp & (n_dp - 1):
        tops = lax.psum(tops, "dp")
    else:
        for i in range(n_dp.bit_length() - 1):
            tops = tops + exchange(tops, "dp", 1 << i)
    tops = jnp.where(first, tops[0], tops[1])
    sm = small[: 3 * BLOCK_ROWS].reshape(3, BLOCK_ROWS, LANES)
    sm = sm.transpose(1, 0, 2).reshape(BLOCK_ROWS, shard)
    asm = small[128:]
    lower = asm[8:24].reshape(4, model)
    g_gains = jnp.stack([lower[0], lower[1], tops[0]])
    g_biases = jnp.stack([lower[2], lower[3], tops[1]])
    weights = jax.nn.softmax(logits)
    slope = weights[0] * weights[1] * tops[4, 0]
    g_logits = jnp.stack([slope, -slope])
    outs = (
        layer_out.reshape(micro, 1, length, model),
        input_grad.reshape(micro, 1, length, model),
        g_gains,
        g_biases,
        g_qkv,
        asm[0:3],
        g_out,
        g_up,
        sm[ROW_UP0 : ROW_UP1 + 1],
        sm[ROW_GAIN],
        sm[ROW_GB0 : ROW_GB1 + 1],
        sm[:TAPS],
        g_down,
        tops[2:4],
        g_logits,
    )
    return tuple(x[None] for x in outs)


def solution(mesh):
    placed = (
        P(None, "dp", None, None),
        P(None, "dp"),
        P(None, "dp", None, None),
        P("section", None, None),
        P("section", None, None),
        P("section", None, None, "mp"),
        P("section", None, "mp"),
        P("section", "mp", None),
        P("section", None, None, "mp"),
        P("section", None, "mp"),
        P("section", "mp"),
        P("section", None, "mp"),
        P("section", None, "mp"),
        P("section", "mp", None),
        P("section", None, None),
        P("section", None),
    )
    return jax.shard_map(
        per_device,
        mesh=mesh,
        in_specs=placed,
        out_specs=(
            P("section", None, "dp", None, None),
            P("section", None, "dp", None, None),
            P("section", None, None),
            P("section", None, None),
            P("section", None, None, "mp"),
            P("section", None, "mp"),
            P("section", "mp", None),
            P("section", None, None, "mp"),
            P("section", None, "mp"),
            P("section", "mp"),
            P("section", None, "mp"),
            P("section", None, "mp"),
            P("section", "mp", None),
            P("section", None, None),
            P("section", None),
        ),
        check_vma=False,
    )
```

```python
import functools
import math

import jax
import jax.numpy as jnp
import numpy as np
from jax import lax
from jax.experimental import pallas as pl
from jax.experimental.pallas import tpu as pltpu
from jax.sharding import PartitionSpec as P

BF = jnp.bfloat16
F32 = jnp.float32
HEAD = 64
LANES = 128
SEGS = 8
HALO = 16
EPS = 1e-05
NEG = -1000000000.0
NN = (((1,), (0,)), ((), ()))
NT = (((1,), (1,)), ((), ()))
TN = (((0,), (0,)), ((), ()))

TAPS = 31
BLOCK_ROWS = 40
ROW_UP0, ROW_UP1, ROW_GAIN, ROW_GB0, ROW_GB1 = 31, 32, 33, 34, 35
ROW_QKV = 120
ROW_NG, ROW_NB, ROW_OB, ROW_LOGIT = 128, 140, 152, 160
PACK_ROWS = 168

OUT_ROWS, DOWN_ROWS, UP_ROWS, QKV_ROWS = 512, 1536, 3072, 1536
D_ROWS = OUT_ROWS + DOWN_ROWS
M_ROWS = UP_ROWS + 128
A_ROWS = QKV_ROWS + 64

W_UP, W_ROWS = 512, 3584
SPLIT = 2048

VMEM = pl.BlockSpec(memory_space=pltpu.VMEM)
SMEM = pl.BlockSpec(memory_space=pltpu.SMEM)
ANY = pl.BlockSpec(memory_space=pltpu.HBM)


def dot(a, b, dims):
    return lax.dot_general(a, b, dims, preferred_element_type=F32)


def call(kernel, ins, in_specs, outs, scratch, flops, mib, far=(), home=()):
    ins = [pltpu.with_memory_space_constraint(x, pltpu.HBM) if p is ANY else x for x, p in zip(ins, in_specs)]
    return pl.pallas_call(
        kernel,
        in_specs=in_specs,
        out_specs=[ANY if i in far else VMEM for i in range(len(outs))],
        out_shape=[pltpu.HBM(x.shape, x.dtype) if i in far or i in home else x for i, x in enumerate(outs)],
        scratch_shapes=scratch,
        compiler_params=pltpu.CompilerParams(vmem_limit_bytes=mib << 20),
        cost_estimate=pl.CostEstimate(flops=1, bytes_accessed=1, transcendentals=0),
    )(*ins)


def shape(dims, dtype):
    return jax.ShapeDtypeStruct(dims, dtype)


def fetch(flag, here, there, sems):
    @pl.when(flag)
    def _():
        for i, (a, d) in enumerate(here):
            pltpu.make_async_copy(a, d, sems.at[i]).start()

    @pl.when(jnp.logical_not(flag))
    def _():
        for i, (a, d) in enumerate(there):
            pltpu.make_async_copy(a, d, sems.at[i]).start()


def landed(pairs, sems):
    for i, (a, d) in enumerate(pairs):
        pltpu.make_async_copy(a, d, sems.at[i]).wait()


def slab_copies(sets, dst, lo, hi):
    here, there = [], []
    for j in range(4):
        for a, b in ((lo, min(hi, SPLIT)), (max(lo, SPLIT), hi)):
            if a >= b:
                continue
            d = dst.at[j, pl.ds(a - lo, b - a), :]
            here.append((sets[j].at[pl.ds(a, b - a), :], d))
            if j < 2:
                there.append((sets[4 + j].at[pl.ds(a, b - a), :], d))
            elif a < SPLIT:
                there.append((sets[4 + j].at[pl.ds(a, b - a), :], d))
            else:
                there.append((sets[6 + j].at[pl.ds(a - SPLIT, b - a), :], d))
    return here, there


def shard_copies(sets, dst):
    return [(sets[j], dst.at[j]) for j in range(4)], [(sets[4 + j], dst.at[j]) for j in range(4)]


def wide(sp, row, count=4):
    return jnp.concatenate([sp[0, 0, row + i : row + i + 1, :] for i in range(count)], axis=1)


def branch_weights(sp):
    l0 = sp[0, 0, ROW_LOGIT : ROW_LOGIT + 1, :]
    l1 = sp[0, 0, ROW_LOGIT + 1 : ROW_LOGIT + 2, :]
    top = jnp.maximum(l0, l1)
    e0, e1 = jnp.exp(l0 - top), jnp.exp(l1 - top)
    total = e0 + e1
    return jnp.concatenate([e0 / total] * 4, axis=1), jnp.concatenate([e1 / total] * 4, axis=1)


def normalized(x):
    center = jnp.mean(x, axis=-1, keepdims=True)
    d = x - center
    inverse = lax.rsqrt(jnp.mean(d * d, axis=-1, keepdims=True) + EPS)
    return d * inverse, inverse


def frame_of(row, half, rows):
    return half * rows + (row & (SEGS - 1)) * (rows // SEGS) + (row >> 3)


def order_matrix(rows, back):
    r = lax.broadcasted_iota(jnp.int32, (rows, rows), 1 if back else 0)
    t = lax.broadcasted_iota(jnp.int32, (rows, rows), 0 if back else 1)
    return jnp.where(frame_of(r, 0, rows) == t, 1.0, 0.0).astype(BF)


def halo_pick(rows, start_seg_even):
    start, seg = start_seg_even
    i = lax.broadcasted_iota(jnp.int32, (HALO, rows), 0)
    r = lax.broadcasted_iota(jnp.int32, (HALO, rows), 1)
    return jnp.where(r == (i + start) * SEGS + seg, 1.0, 0.0).astype(BF)


def swap_halves(x):
    lane = lax.broadcasted_iota(jnp.int32, x.shape, 1)
    return jnp.where(
        (lane & (HEAD - 1)) < HEAD // 2,
        pltpu.roll(x, LANES - HEAD // 2, 1),
        pltpu.roll(x, HEAD // 2, 1),
    )


def rotate(x, cosine, sine):
    return x * cosine + swap_halves(x) * sine


def rotate_back(x, cosine, sine):
    return x * cosine - swap_halves(x) * sine


def pieces(x):
    hi = x.astype(BF).astype(F32)
    rest = x - hi
    mid = rest.astype(BF).astype(F32)
    return hi, mid, rest - mid


def pack_kernel(
    wout_h, wup_h, wdown_h, cw, bup, ggain, gbias, bqkv, ngain, nbias, obias, logits,
    sp_o, u_o, v_o, wout, wup, wdown, sems,
):
    loads = [
        pltpu.make_async_copy(a, b, sems.at[i])
        for i, (a, b) in enumerate(((wup_h, wup), (wdown_h, wdown), (wout_h, wout)))
    ]
    for c in loads:
        c.start()
    sp_o[...] = jnp.zeros_like(sp_o)
    for b in range(3):
        lanes = slice(b * LANES, (b + 1) * LANES)
        at = b * BLOCK_ROWS
        sp_o[at : at + TAPS, :] = cw[:, lanes]
        sp_o[at + ROW_UP0 : at + ROW_UP0 + 2, :] = bup[:, lanes]
        sp_o[at + ROW_GAIN : at + ROW_GAIN + 1, :] = ggain[:, lanes]
        sp_o[at + ROW_GB0 : at + ROW_GB0 + 2, :] = gbias[:, lanes]
    sp_o[ROW_QKV : ROW_QKV + 3, :] = bqkv[...]
    for i in range(4):
        lanes = slice(i * LANES, (i + 1) * LANES)
        for n in range(3):
            sp_o[ROW_NG + 4 * n + i : ROW_NG + 4 * n + i + 1, :] = ngain[n : n + 1, lanes]
            sp_o[ROW_NB + 4 * n + i : ROW_NB + 4 * n + i + 1, :] = nbias[n : n + 1, lanes]
        for n in range(2):
            sp_o[ROW_OB + 4 * n + i : ROW_OB + 4 * n + i + 1, :] = obias[n : n + 1, lanes]
    for n in range(2):
        sp_o[ROW_LOGIT + n : ROW_LOGIT + n + 1, :] = jnp.full((1, LANES), logits[n], F32)
    for c in loads:
        c.wait()
    model, shard = wup.shape[1], wup.shape[2]
    for lb in range(4):
        lanes = slice(lb * LANES, (lb + 1) * LANES)
        u_o[lb * LANES : (lb + 1) * LANES, :] = wout[:, lanes]
        v_o[lb * shard : (lb + 1) * shard, :] = wdown[:, lanes]
    for hh in range(2):
        for b in range(3):
            at = W_UP + (hh * 3 + b) * model
            u_o[at : at + model, :] = wup[hh, :, b * LANES : (b + 1) * LANES]


def prologue_kernel(scal, frames, cotangent, own_o, oth_o, g_o, buf, sems):
    rows = own_o.shape[0]
    u, half = scal[0], scal[1]
    mine = pl.ds(pl.multiple_of(half * rows, rows), rows)
    other = pl.ds(pl.multiple_of((1 - half) * rows, rows), rows)
    copies = [
        pltpu.make_async_copy(frames.at[u, 0, mine, :], buf.at[0], sems.at[0]),
        pltpu.make_async_copy(frames.at[u, 0, other, :], buf.at[1], sems.at[1]),
        pltpu.make_async_copy(cotangent.at[u, 0, mine, :], buf.at[2], sems.at[2]),
    ]
    for c in copies:
        c.start()
    order = order_matrix(rows, False)
    for c, i, out in zip(copies, range(3), (own_o, oth_o, g_o)):
        c.wait()
        out[...] = dot(order, buf[i], NN).astype(BF)


def attention_forward_kernel(layer, scal, sp, cos_t, sin_t, h_own, h_oth, *refs):
    sets, refs = refs[:8], refs[8:]
    q_h, k_h, v_h, mix_h, lse_h, mix_o, w_s, cs, sn, norm, lse_s, q_o, k_o, v_o, lse_o, wsem, tsem, osem = refs
    sp = sp.at[pl.ds(layer, 1)]
    rows, model = h_own.shape
    half, length = scal[1], scal[2]
    here, there = shard_copies(sets, w_s)
    fetch(scal[3] == layer, here, there, wsem)
    tables = [
        pltpu.make_async_copy(cos_t.at[half], cs, tsem.at[0]),
        pltpu.make_async_copy(sin_t.at[half], sn, tsem.at[1]),
    ]
    for c in tables:
        c.start()
    gain, bias = wide(sp, ROW_NG), wide(sp, ROW_NB)
    step = 64
    for src, base in ((h_own, 0), (h_oth, rows)):
        for r in range(0, rows, step):
            hat, unused = normalized(src[r : r + step, :].astype(F32))
            norm[base + r : base + r + step, :] = (hat * gain + bias).astype(BF)
    lse_s[...] = jnp.zeros_like(lse_s)
    for c in tables:
        c.wait()
    landed(here, wsem)
    total = 2 * rows
    row = lax.broadcasted_iota(jnp.int32, (total, LANES), 0)
    part = jnp.where(row < rows, half, 1 - half)
    position = frame_of(row & (rows - 1), part, rows)
    mask = jnp.where(position < length, 0.0, NEG)
    lane_k = lax.broadcasted_iota(jnp.int32, (total, LANES), 1)
    lane_q = lax.broadcasted_iota(jnp.int32, (rows, LANES), 1)

    def stores(j):
        pairs = ((q_o, q_h), (k_o, k_h), (v_o, v_h), (mix_o, mix_h))
        return [pltpu.make_async_copy(a.at[j], b.at[j], osem.at[j, i]) for i, (a, b) in enumerate(pairs)]

    def shard(j):
        mj = scal[4 + j]
        bq = sp[0, mj, ROW_QKV : ROW_QKV + 1, :]
        bk = sp[0, mj, ROW_QKV + 1 : ROW_QKV + 2, :]
        bv = sp[0, mj, ROW_QKV + 2 : ROW_QKV + 3, :]
        everything = norm[...]
        q = rotate(dot(norm[:rows, :], w_s[j, 0], NN) + bq, cs[:rows, :], sn[:rows, :])
        q = q.astype(BF).astype(F32) * (1.0 / math.sqrt(HEAD))
        k = rotate(dot(everything, w_s[j, 1], NN) + bk, cs[...], sn[...]).astype(BF)
        v = (dot(everything, w_s[j, 2], NN) + bv).astype(BF)
        q_o[j] = q.astype(BF)
        k_o[j] = k
        v_o[j] = v
        kf = k.astype(F32)
        vt = v.astype(F32).T.astype(BF)
        outs = []
        work = []
        for hd in range(2):
            spare = (1 - hd) * HEAD
            qm = jnp.where((lane_q >> 6) == hd, q, jnp.where(lane_q == spare, 1.0, 0.0)).astype(BF)
            km = jnp.where((lane_k >> 6) == hd, kf, jnp.where(lane_k == spare, mask, 0.0)).astype(BF)
            work.append((km, qm))
        score = dot(*work[0], NT)
        for hd in range(2):
            s = score
            if hd == 0:
                score = dot(*work[1], NT)
            top = jnp.max(s, axis=0, keepdims=True)
            p = jnp.exp(s - top)
            den = jnp.sum(p, axis=0, keepdims=True)
            p = (p * (1.0 / den)).astype(BF)
            outs.append(dot(vt[hd * HEAD : (hd + 1) * HEAD, :], p, NN))
            lse_s[2 * j + hd : 2 * j + hd + 1, :] = top + jnp.log(den)
        mix_o[j] = jnp.concatenate(outs, axis=0).T.astype(BF)
        for c in stores(j):
            c.start()

    for j in range(4):
        shard(j)
    lse_o[...] = lse_s[...].T
    last = pltpu.make_async_copy(lse_o, lse_h, osem.at[4, 0])
    last.start()
    for j in range(4):
        for c in stores(j):
            c.wait()
    last.wait()


def gelu_parts(u):
    d = 1.0 + (0.3275911 / math.sqrt(2.0)) * jnp.abs(u)
    t = pl.reciprocal(d, approx=True)
    t = t * (2.0 - d * t)
    e = jnp.exp2((-0.5 / math.log(2.0)) * (u * u))
    half = [0.5 * c for c in (1.061405429, -1.453152027, 1.421413741, -0.284496736, 0.254829592)]
    poly = ((((half[0] * t + half[1]) * t + half[2]) * t + half[3]) * t + half[4]) * t
    tail = poly * e
    phi = jnp.where(u >= 0, 1.0 - tail, tail)
    return u * phi, phi + (u * e) * (1.0 / math.sqrt(2.0 * math.pi))


PHASES = ((0,), (2,), (2, 4), (1,), (3,), (3, 5), (1, 2), (3, 4), (3, 4, 5, 6))
TAP_PHASES = ((0,), (2,), (0, 2), (1,), (3,), (1, 3), (0, 1), (2, 3), (0, 1, 2, 3))


def phase(ref, rows, n):
    out = ref[4 * n + rows[0]]
    for r in rows[1:]:
        out = out + ref[4 * n + r]
    return out


def correlate(taps, xs, count):
    accs = [None] * count
    for m, tap in enumerate(taps):
        for n in range(count):
            term = tap * xs[n + m]
            accs[n] = term if accs[n] is None else accs[n] + term
    return accs


def unfold(q0, q1, q2):
    out = []
    for n in range(len(q2)):
        out.append(q0[n] + q1[n])
        out.append(q2[n] - (q0[n + 1] + q1[n]))
    if len(q1) > len(q2):
        out.append(q0[len(q2)] + q1[len(q2)])
    return out


def fill_filters(filt, row):
    for m in range(8):
        w = [
            jnp.broadcast_to(row(4 * m + r), (SEGS, LANES)) if 4 * m + r < TAPS else jnp.zeros((SEGS, LANES), F32)
            for r in range(4)
        ]
        for i, rows in enumerate(TAP_PHASES):
            out = w[rows[0]]
            for r in rows[1:]:
                out = out + w[r]
            filt[i * 8 + m] = out


def fast_fir(pad, filt, out, keep):
    count = out.shape[0]
    half = count // 2
    for g in range(3):
        qs = []
        for i in range(3):
            n = half // 2 + 1 if i == 0 or (i == 1 and g == 0) else half // 2
            xs = [phase(pad, PHASES[3 * g + i], x) for x in range(n + 7)]
            qs.append(correlate([filt[(3 * g + i) * 8 + m] for m in range(8)], xs, n))
        p = unfold(*qs)
        for n in range(len(p)):
            if g == 0:
                keep[n] = p[n]
            elif g == 1:
                out[2 * n] = keep[n] + p[n]
                out[2 * n + 1] = keep[n + 1] + p[n]
            else:
                out[2 * n + 1] = p[n] - out[2 * n + 1]


def tap_sums(gpad, xpad, count):
    ps = []
    for g in range(3):
        qs = []
        for i in range(3):
            rows = [15 + r for r in TAP_PHASES[3 * g + i]]
            n = 9 if i == 0 else 8
            steps = count // 4
            xs = [phase(xpad, PHASES[3 * g + i], x) for x in range(n + steps - 1)]
            qs.append(correlate([phase(gpad, rows, x) for x in range(steps)], xs, n))
        ps.append(unfold(*qs))
    out = []
    for m in range(16):
        out.append(ps[0][m] + ps[1][m])
        if m < 15:
            out.append(ps[2][m] - (ps[0][m + 1] + ps[1][m]))
    return out


def halo_pads(pad, block, halo_ref, half, right_is_even):
    count = block.shape[0]
    pad[15 : 15 + count] = block
    pad[30 + count : 32 + count] = jnp.zeros((2, SEGS, LANES), F32)
    seg = lax.broadcasted_iota(jnp.int32, (SEGS, LANES), 0)
    from_left = half.astype(F32)
    from_right = 1.0 - from_left
    for i in range(15):
        tail = pltpu.roll(block[count - 15 + i], 1, 0)
        edge = jnp.broadcast_to(halo_ref[i + 1 : i + 2, :], (SEGS, LANES)) * from_left
        pad[i] = jnp.where(seg == 0, edge, tail)
        head = pltpu.roll(block[i], SEGS - 1, 0)
        edge = jnp.broadcast_to(halo_ref[i : i + 1, :], (SEGS, LANES)) * from_right
        pad[15 + count + i] = jnp.where(seg == SEGS - 1, edge, head)


def mlp_forward_kernel(layer, scal, sp, h_own, h_oth, *refs):
    sets, refs = refs[:10], refs[10:]
    (act0_h, dact0_h, dact1_h, ghat_h, conv_h, gated_h, ginv_h, norm_h, gated_o,
     ws, act0, act1, sums, gmean, ginv, pad, filt, fir, keep, halo, act0_o, dact0_o, dact1_o, ghat_o, conv_o, norm_o, wsem, osem) = refs
    sp = sp.at[pl.ds(layer, 1)]
    rows, model = h_own.shape
    every = rows + HALO
    hidden = act0.shape[1]
    shard = hidden // 4
    half, length = scal[1], scal[2]
    here, there = slab_copies(sets, ws, W_UP, W_ROWS)
    fetch(scal[3] == layer, here, there, wsem)
    gain, bias = wide(sp, ROW_NG + 4), wide(sp, ROW_NB + 4)
    step = 64
    for r in range(0, rows, step):
        hat, unused = normalized(h_own[r : r + step, :].astype(F32))
        norm_o[r : r + step, :] = (hat * gain + bias).astype(BF)
    i = lax.broadcasted_iota(jnp.int32, (HALO, rows), 0)
    r = lax.broadcasted_iota(jnp.int32, (HALO, rows), 1)
    wanted = jnp.where(half == 0, i * SEGS, (i + rows // SEGS - HALO) * SEGS + SEGS - 1)
    pick = jnp.where(r == wanted, 1.0, 0.0).astype(BF)
    hat, unused = normalized(dot(pick, h_oth[...], NN))
    norm_o[rows:every, :] = (hat * gain + bias).astype(BF)
    sums[...] = jnp.zeros_like(sums)
    landed(here, wsem)

    width = 256
    chunk = 48

    def up(i, carry):
        lanes = pl.ds(pl.multiple_of(i * width, width), width)
        rows_of = []
        for hh, base in ((0, ROW_UP0), (1, ROW_UP1)):
            got = []
            for t in range(2):
                c = 2 * i + t
                got.append(sp[0, scal[8 + c], pl.ds(lax.rem(c, 3) * BLOCK_ROWS + base, 1), :])
            rows_of.append(jnp.concatenate(got, axis=1))
        slabs = []
        for hh in range(2):
            pair = []
            for t in range(2):
                c = 2 * i + t
                at = (hh * 3 + lax.rem(c, 3)) * model
                pair.append(ws[lax.div(c, 3), pl.ds(pl.multiple_of(at, model), model), :])
            slabs.append(jnp.concatenate(pair, axis=1))
        u0 = dot(norm_o[...], slabs[0], NN)
        u1 = dot(norm_o[...], slabs[1], NN)
        for r in range(0, every, chunk):
            a, d = gelu_parts(u0[r : r + chunk] + rows_of[0])
            act0[r : r + chunk, lanes] = a
            act0_o[r : r + chunk, lanes] = a.astype(BF)
            dact0_o[r : r + chunk, lanes] = d.astype(BF)
        for r in range(0, every, chunk):
            a, d = gelu_parts(u1[r : r + chunk] + rows_of[1])
            act1[r : r + chunk, lanes] = a
            dact1_o[r : r + chunk, lanes] = d.astype(BF)
            sums[r : r + chunk, :] += a[:, :LANES] + a[:, LANES:]
        return carry

    lax.fori_loop(0, hidden // width, up, 0)
    for r in range(0, every, chunk):
        center = jnp.sum(sums[r : r + chunk, :], axis=1, keepdims=True) * (1.0 / hidden)
        d = act1[r : r + chunk, :] - center
        spread = jnp.sum(d * d, axis=1, keepdims=True) * (1.0 / hidden)
        gmean[r : r + chunk, :] = jnp.broadcast_to(center, (chunk, LANES))
        ginv[r : r + chunk, :] = jnp.broadcast_to(lax.rsqrt(spread + EPS), (chunk, LANES))
    stores = [
        pltpu.make_async_copy(a, b, osem.at[i])
        for i, (a, b) in enumerate(
            ((act0_o, act0_h), (dact0_o, dact0_h), (dact1_o, dact1_h), (norm_o, norm_h), (ginv.at[pl.ds(0, rows)], ginv_h))
        )
    ]
    for c in stores:
        c.start()

    def column_stores(c):
        lanes = pl.ds(pl.multiple_of(c * LANES, LANES), LANES)
        pairs = ((ghat_o, ghat_h), (conv_o, conv_h), (gated_o, gated_h))
        return [
            pltpu.make_async_copy(a.at[:, lanes], b.at[:, lanes], osem.at[5 + 3 * c + i]) for i, (a, b) in enumerate(pairs)
        ]


    row = lax.broadcasted_iota(jnp.int32, (rows, LANES), 0)
    valid = jnp.where(frame_of(row, half, rows) < length, 1.0, 0.0)
    hrow = lax.broadcasted_iota(jnp.int32, (HALO, LANES), 0)
    valid_halo = jnp.where(jnp.where(half == 0, rows, rows - HALO) + hrow < length, 1.0, 0.0)
    count = rows // SEGS

    def gate(c, carry):
        lanes = pl.ds(pl.multiple_of(c * LANES, LANES), LANES)
        mj = scal[8 + c]
        base = lax.rem(c, 3) * BLOCK_ROWS
        ggain = sp[0, mj, pl.ds(base + ROW_GAIN, 1), :]
        gb0 = sp[0, mj, pl.ds(base + ROW_GB0, 1), :]
        gb1 = sp[0, mj, pl.ds(base + ROW_GB1, 1), :]
        hat = (act1[rows:every, lanes] - gmean[rows:every, :]) * ginv[rows:every, :]
        ghat_o[rows:every, lanes] = hat.astype(BF)
        halo[...] = (hat * ggain + gb0) * valid_halo
        hat = (act1[0:rows, lanes] - gmean[0:rows, :]) * ginv[0:rows, :]
        ghat_o[0:rows, lanes] = hat.astype(BF)
        normed = (hat * ggain + gb0) * valid
        halo_pads(pad, normed.reshape(count, SEGS, LANES), halo, half, True)
        fill_filters(filt, lambda k: sp[0, mj, pl.ds(base + k, 1), :])
        fast_fir(pad, filt, fir, keep)
        for t in range(0, count, 8):
            at = t * SEGS
            cv = fir[t : t + 8].reshape(64, LANES) + gb1
            conv_o[at : at + 64, lanes] = cv.astype(BF)
            gated_o[at : at + 64, lanes] = (act0[at : at + 64, lanes] * cv).astype(BF)
        for store in column_stores(c):
            store.start()
        return carry

    lax.fori_loop(0, hidden // LANES, gate, 0)
    for c in range(hidden // LANES):
        stores.extend(column_stores(c))
    for c in stores:
        c.wait()


def merge_forward_kernel(layer, scal, sp, h_own, mix, gated, *refs):
    u_sets, v_sets, refs = refs[:10], refs[10:18], refs[18:]
    o_o, nat_o, rhat_h, rstd_h, diff_h, ws, wv, rhat_o, rstd_o, diff_o, usem, vsem, osem = refs
    sp = sp.at[pl.ds(layer, 1)]
    rows, model = h_own.shape
    shard = wv.shape[1] // 4
    here, there = slab_copies(u_sets, ws, 0, W_UP)
    fetch(scal[3] == layer, here, there, usem)
    here_v, there_v = shard_copies(v_sets, wv)
    fetch(scal[3] == layer, here_v, there_v, vsem)
    landed(here, usem)
    landed(here_v, vsem)
    step = 64

    def stores(r, n):
        part = pl.ds(r, n)
        pairs = ((rhat_o, rhat_h), (rstd_o, rstd_h), (diff_o, diff_h))
        return [
            pltpu.make_async_copy(a.at[part], b.at[part], osem.at[r // n, i]) for i, (a, b) in enumerate(pairs)
        ]

    w0, w1 = branch_weights(sp)
    gain, bias = wide(sp, ROW_NG + 8), wide(sp, ROW_NB + 8)
    b0, b1 = wide(sp, ROW_OB), wide(sp, ROW_OB + 4)
    block = 256
    for r in range(0, rows, block):
        mixed = jnp.concatenate([mix[j, r : r + block, :] for j in range(4)], axis=1)
        brs, atts = [], []
        for lb in range(0, 4, 2):
            w = [
                jnp.concatenate(
                    [wv[j, (lb + t) * shard : (lb + t + 1) * shard, :] for j in range(4)], axis=0
                )
                for t in range(2)
            ]
            brs.append(dot(gated[r : r + block, :], jnp.concatenate(w, axis=1), NN))
            w = [
                jnp.concatenate(
                    [ws[j, (lb + t) * LANES : (lb + t + 1) * LANES, :] for j in range(4)], axis=0
                )
                for t in range(2)
            ]
            atts.append(dot(mixed, jnp.concatenate(w, axis=1), NN))
        br = jnp.concatenate(brs, axis=1)
        att = jnp.concatenate(atts, axis=1)
        for q in range(0, block, step):
            at = att[q : q + step] + b0
            bt = br[q : q + step] + b1
            res = h_own[r + q : r + q + step, :].astype(F32) + w0 * at + w1 * bt
            hat, inverse = normalized(res)
            diff_o[r + q : r + q + step, :] = at - bt
            rhat_o[r + q : r + q + step, :] = hat
            rstd_o[r + q : r + q + step, :] = jnp.broadcast_to(inverse, (step, LANES))
            o_o[r + q : r + q + step, :] = (hat * gain + bias).astype(BF)
        for c in stores(r, block):
            c.start()
    nat_o[...] = dot(order_matrix(rows, True), o_o[...], NN).astype(BF)
    for r in range(0, rows, block):
        for c in stores(r, block):
            c.wait()


def merge_backward_kernel(
    layer, scal, sp, g, rhat_h, rstd_h, diff_h, mix_h, gated_h,
    gres_o, gatt_o, gbr_o, halo_o, sums_o, keep_o, send_o, rhat, rstd, diff, mix, gated, sems,
):
    sp = sp.at[pl.ds(layer, 1)]
    rows, model = g.shape
    half = scal[1]
    loads = [
        pltpu.make_async_copy(a, b, sems.at[i])
        for i, (a, b) in enumerate(
            ((rstd_h, rstd), (rhat_h, rhat), (diff_h, diff), (mix_h, mix), (gated_h, gated))
        )
    ]
    for c in loads:
        c.start()
    gain = wide(sp, ROW_NG + 8)
    w0, w1 = branch_weights(sp)
    for c in loads[:3]:
        c.wait()
    step = 64
    dgain = dbias = slope = jnp.zeros((1, model), F32)
    db = jnp.zeros((1, model), F32)
    for r in range(0, rows, step):
        gg = g[r : r + step, :].astype(F32)
        hat = rhat[r : r + step, :]
        dgain = dgain + jnp.sum(gg * hat, axis=0, keepdims=True)
        dbias = dbias + jnp.sum(gg, axis=0, keepdims=True)
        gg = gg * gain
        gr = rstd[r : r + step, 0:1] * (
            gg - jnp.mean(gg, axis=1, keepdims=True) - hat * jnp.mean(gg * hat, axis=1, keepdims=True)
        )
        gres_o[r : r + step, :] = gr
        gatt_o[r : r + step, :] = (w0 * gr).astype(BF)
        gbr_o[r : r + step, :] = (w1 * gr).astype(BF)
        db = db + jnp.sum(gr, axis=0, keepdims=True)
        slope = slope + jnp.sum(gr * diff[r : r + step, :], axis=0, keepdims=True)
    i = lax.broadcasted_iota(jnp.int32, (HALO, rows), 0)
    r = lax.broadcasted_iota(jnp.int32, (HALO, rows), 1)
    wanted = jnp.where(half == 0, (i + rows // SEGS - HALO) * SEGS + SEGS - 1, i * SEGS)
    pick = jnp.where(r == wanted, 1.0, 0.0).astype(BF)
    halo_o[...] = dot(pick, gbr_o[...], NN).astype(BF)
    slope = jnp.sum(slope, axis=1, keepdims=True)
    sums_o[...] = jnp.concatenate(
        [dgain, dbias, w0 * db, w1 * db, jnp.broadcast_to(slope, (1, model)), jnp.zeros((3, model), F32)], axis=0
    )
    shards = (keep_o.at[0], send_o.at[0], keep_o.at[1], send_o.at[1])
    shard = gated.shape[1] // 4
    for c in loads[3:]:
        c.wait()
    for j in range(4):
        w = dot(mix[j], gatt_o[...], TN).astype(BF)
        for i in range(4):
            shards[j][i * LANES : (i + 1) * LANES, :] = w[:, i * LANES : (i + 1) * LANES]
        w = dot(gated[:, j * shard : (j + 1) * shard], gbr_o[...], TN).astype(BF)
        for i in range(4):
            at = OUT_ROWS + i * shard
            shards[j][at : at + shard, :] = w[:, i * LANES : (i + 1) * LANES]


def attention_backward_kernel(layer, scal, gatt, q_h, k_h, v_h, mix_h, lse_h, *refs):
    sets, refs = refs[:10], refs[10:]
    cos_t, sin_t, dq_o, own_o, oth_o, w_s, cs, sn, pbuf, dsbuf, dom, qm2, q_r, k_r, v_r, mix, lse, wsem, tsem = refs
    rows = gatt.shape[0]
    total = 2 * rows
    half, length = scal[1], scal[2]
    here, there = slab_copies(sets, w_s, 0, W_UP)
    fetch(scal[3] == layer, here, there, wsem)
    tables = [
        pltpu.make_async_copy(cos_t.at[half, pl.ds(0, rows), :], cs, tsem.at[0]),
        pltpu.make_async_copy(sin_t.at[half, pl.ds(0, rows), :], sn, tsem.at[1]),
    ]
    for i, (a, b) in enumerate(((q_h, q_r), (k_h, k_r), (v_h, v_r), (mix_h, mix), (lse_h, lse))):
        tables.append(pltpu.make_async_copy(a, b, tsem.at[2 + i]))
    for c in tables:
        c.start()
    row = lax.broadcasted_iota(jnp.int32, (total, LANES), 0)
    part = jnp.where(row < rows, half, 1 - half)
    position = frame_of(row & (rows - 1), part, rows)
    mask = jnp.where(position < length, 0.0, NEG)
    lane_k = lax.broadcasted_iota(jnp.int32, (total, LANES), 1)
    lane_q = lax.broadcasted_iota(jnp.int32, (rows, LANES), 1)
    for c in tables:
        c.wait()
    landed(here, wsem)

    def shard(j):
        wo = jnp.concatenate([w_s[j, lb * LANES : (lb + 1) * LANES, :] for lb in range(4)], axis=1)
        dm = dot(gatt[...], wo, NT).astype(BF).astype(F32)
        prod = dm * mix[j].astype(F32)
        q = q_r[j].astype(F32)
        k = k_r[j].astype(F32)
        v = v_r[j].astype(F32)
        kt = k.T.astype(BF)
        dqs = []
        for hd in range(2):
            spare = (1 - hd) * HEAD
            in_q, in_k = (lane_q >> 6) == hd, (lane_k >> 6) == hd
            minus_lse = -jnp.sum(jnp.where(lane_q == 2 * j + hd, lse[...], 0.0), axis=1, keepdims=True)
            minus_delta = -jnp.sum(jnp.where(in_q, prod, 0.0), axis=1, keepdims=True)
            l0, l1, l2 = pieces(minus_lse)
            e0, e1, e2 = pieces(minus_delta)
            qx = jnp.where(lane_q == spare, 1.0, 0.0)
            dx = jnp.zeros_like(qx)
            for n, (lp, ep) in enumerate(((l0, e0), (l1, e1), (l2, e2))):
                here = lane_q == spare + 1 + n
                qx = jnp.where(here, lp, qx)
                dx = jnp.where(here, ep, dx)
            one = jnp.where((lane_k > spare) & (lane_k < spare + 4), 1.0, 0.0)
            qh = jnp.where(in_q, q, qx).astype(BF)
            dh = jnp.where(in_q, dm, dx).astype(BF)
            kh = jnp.where(in_k, k, jnp.where(lane_k == spare, mask, one)).astype(BF)
            vh = jnp.where(in_k, v, one).astype(BF)
            dom[hd * rows : (hd + 1) * rows, :] = jnp.where(in_q, dm, 0.0).astype(BF)
            qm2[hd * rows : (hd + 1) * rows, :] = jnp.where(in_q, q, 0.0).astype(BF)
            p = jnp.exp(dot(kh, qh, NT))
            dp = dot(vh, dh, NT)
            ds = (p * dp).astype(BF)
            pbuf[:, hd * rows : (hd + 1) * rows] = p.astype(BF)
            dsbuf[:, hd * rows : (hd + 1) * rows] = ds
            dqs.append(dot(kt[hd * HEAD : (hd + 1) * HEAD, :], ds, NN))
        dq = jnp.concatenate(dqs, axis=0).T * (1.0 / math.sqrt(HEAD))
        dq_o[j] = rotate_back(dq, cs[...], sn[...]).astype(BF)
        dk = dot(dsbuf[...], qm2[...], NN)
        dv = dot(pbuf[...], dom[...], NN)
        own_o[j, :, 0:LANES] = dk[:rows]
        own_o[j, :, LANES:] = dv[:rows]
        oth_o[j, :, 0:LANES] = dk[rows:].astype(BF)
        oth_o[j, :, LANES:] = dv[rows:].astype(BF)

    for j in range(4):
        shard(j)


def conv_backward_kernel(layer, scal, sp, gbr, ghalo, act0_h, dact0_h, ghat_h, conv_h, *refs):
    v_sets, refs = refs[:8], refs[8:]
    (dup_o, hgrad, hs, xs, small, wv, act0, dact0, ghat, conv, gpad, xpad, filt, fir, keep, halo, gcv, gbuf, vsem, asem) = refs
    sp = sp.at[pl.ds(layer, 1)]
    rows, model = gbr.shape
    every = rows + HALO
    hidden = gcv.shape[1]
    shard = hidden // 4
    half, length = scal[1], scal[2]
    here_v, there_v = shard_copies(v_sets, wv)
    fetch(scal[3] == layer, here_v, there_v, vsem)
    loads = [
        pltpu.make_async_copy(a, b, asem.at[i])
        for i, (a, b) in enumerate(((act0_h, act0), (conv_h, conv), (dact0_h, dact0), (ghat_h, ghat)))
    ]
    for c in loads:
        c.start()
    gbuf[0:rows, :] = gbr[...]
    gbuf[rows:every, :] = ghalo[...]
    hs[...] = jnp.zeros_like(hs)
    xs[...] = jnp.zeros_like(xs)
    small[...] = jnp.zeros_like(small)
    landed(here_v, vsem)
    for c in loads[:3]:
        c.wait()
    count = rows // SEGS
    width = 256
    chunk = 48

    def down(i, carry):
        lanes = pl.ds(pl.multiple_of(i * width, width), width)
        pair = []
        for t in range(2):
            c = 2 * i + t
            base = lax.rem(c, 3) * LANES
            pair.append(
                jnp.concatenate(
                    [
                        wv[lax.div(c, 3), pl.ds(pl.multiple_of(base + lb * shard, LANES), LANES), :]
                        for lb in range(4)
                    ],
                    axis=1,
                )
            )
        g = dot(gbuf[...], jnp.concatenate(pair, axis=0), NT)
        for r in range(0, every, chunk):
            gr = g[r : r + chunk].astype(BF).astype(F32)
            gcv[r : r + chunk, lanes] = gr * act0[r : r + chunk, lanes].astype(F32)
        for r in range(0, rows, 64):
            gr = g[r : r + 64].astype(BF).astype(F32)
            keep = gr * conv[r : r + 64, lanes].astype(F32) * dact0[r : r + 64, lanes].astype(F32)
            dup_o[r : r + 64, lanes] = keep.astype(BF)
        return carry

    lax.fori_loop(0, hidden // width, down, 0)
    loads[3].wait()
    row = lax.broadcasted_iota(jnp.int32, (rows, LANES), 0)
    valid = jnp.where(frame_of(row, half, rows) < length, 1.0, 0.0)
    hrow = lax.broadcasted_iota(jnp.int32, (HALO, LANES), 0)
    valid_halo = jnp.where(jnp.where(half == 0, rows, rows - HALO) + hrow < length, 1.0, 0.0)

    def fold(x):
        return jnp.sum(x, axis=0, keepdims=True)

    def conv_back(c, carry):
        lanes = pl.ds(pl.multiple_of(c * LANES, LANES), LANES)
        mj = scal[8 + c]
        b = lax.rem(c, 3)
        j = lax.div(c, 3)
        base = b * BLOCK_ROWS
        ggain = sp[0, mj, pl.ds(base + ROW_GAIN, 1), :]
        gb0 = sp[0, mj, pl.ds(base + ROW_GB0, 1), :]
        halo[...] = (ghat[rows:every, lanes].astype(F32) * ggain + gb0) * valid_halo
        normed = (ghat[0:rows, lanes].astype(F32) * ggain + gb0) * valid
        halo_pads(xpad, normed.reshape(count, SEGS, LANES), halo, half, True)
        halo[...] = gcv[rows:every, lanes]
        gown = gcv[0:rows, lanes]
        halo_pads(gpad, gown.reshape(count, SEGS, LANES), halo, half, True)
        small[j, pl.ds(base + ROW_GB1, 1), :] = fold(gown)
        for k, t in enumerate(tap_sums(gpad, xpad, count)):
            small[j, pl.ds(base + k, 1), :] = fold(t)
        fill_filters(filt, lambda k: sp[0, mj, pl.ds(base + TAPS - 1 - k, 1), :])
        fast_fir(gpad, filt, fir, keep)
        dgain = jnp.zeros((SEGS, LANES), F32)
        dbias = jnp.zeros((SEGS, LANES), F32)
        for t in range(0, count, 8):
            at = t * SEGS
            gn = fir[t : t + 8].reshape(64, LANES) * valid[at : at + 64]
            hat = ghat[at : at + 64, lanes].astype(F32)
            dgain = dgain + jnp.sum((gn * hat).reshape(8, SEGS, LANES), axis=0)
            dbias = dbias + jnp.sum(gn.reshape(8, SEGS, LANES), axis=0)
            gn = gn * ggain
            hgrad[at : at + 64, lanes] = gn
            hs[at : at + 64, :] += gn
            xs[at : at + 64, :] += gn * hat
        small[j, pl.ds(base + ROW_GAIN, 1), :] = fold(dgain)
        small[j, pl.ds(base + ROW_GB0, 1), :] = fold(dbias)
        return carry

    lax.fori_loop(0, hidden // LANES, conv_back, 0)
    for r in range(0, rows, 64):
        a = jnp.sum(hs[r : r + 64, :], axis=1, keepdims=True) * (1.0 / hidden)
        x = jnp.sum(xs[r : r + 64, :], axis=1, keepdims=True) * (1.0 / hidden)
        hs[r : r + 64, :] = jnp.broadcast_to(a, (64, LANES))
        xs[r : r + 64, :] = jnp.broadcast_to(x, (64, LANES))


def up_backward_kernel(layer, scal, dup0, hgrad, hs, xs, small_i, ghat_h, dact1_h, ginv_h, norm_h, *refs):
    sets, refs = refs[:10], refs[10:]
    dn_o, keep_o, send_o, ws, ghat, dact1, ginv, norm, dup1, small, wsem, asem = refs
    rows, hidden = hgrad.shape
    model = norm.shape[1]
    width = 256
    here, there = slab_copies(sets, ws, W_UP, W_ROWS)
    fetch(scal[3] == layer, here, there, wsem)
    own = pl.ds(0, rows)
    loads = [
        pltpu.make_async_copy(a, b, asem.at[i])
        for i, (a, b) in enumerate(
            ((ghat_h.at[own, :], ghat), (dact1_h.at[own, :], dact1), (ginv_h, ginv), (norm_h, norm))
        )
    ]
    for c in loads:
        c.start()
    small[...] = small_i[...]

    def fold(x):
        return jnp.sum(x, axis=0, keepdims=True)

    for c in loads[:3]:
        c.wait()

    def gate_back(c, carry):
        lanes = pl.ds(pl.multiple_of(c * LANES, LANES), LANES)
        b = lax.rem(c, 3)
        j = lax.div(c, 3)
        base = b * BLOCK_ROWS
        s0 = jnp.zeros((1, LANES), F32)
        s1 = jnp.zeros((1, LANES), F32)
        for r in range(0, rows, 64):
            hat = ghat[r : r + 64, lanes].astype(F32)
            gi = ginv[r : r + 64, :] * (hgrad[r : r + 64, lanes] - hs[r : r + 64, :] - hat * xs[r : r + 64, :])
            d1 = (gi * dact1[r : r + 64, lanes].astype(F32)).astype(BF)
            dup1[r : r + 64, lanes] = d1
            s1 = s1 + fold(d1.astype(F32))
            s0 = s0 + fold(dup0[r : r + 64, lanes].astype(F32))
        small[j, pl.ds(base + ROW_UP0, 1), :] = s0
        small[j, pl.ds(base + ROW_UP1, 1), :] = s1
        return carry

    lax.fori_loop(0, hidden // LANES, gate_back, 0)
    landed(here, wsem)
    loads[3].wait()
    dups = (dup0, dup1)
    for hh in range(2):
        w = jnp.concatenate(
            [ws[j, (hh * 3 + b) * model : (hh * 3 + b + 1) * model, :] for j in range(4) for b in range(3)], axis=1
        )
        if hh == 0:
            dn_o[...] = dot(dups[hh][...], w, NT)
        else:
            dn_o[...] += dot(dups[hh][...], w, NT)
    shards = (keep_o.at[0], send_o.at[0], keep_o.at[1], send_o.at[1])
    own_norm = norm[0:rows, :]
    for i in range(hidden // width):
        lo = i * width
        for hh in range(2):
            w = dot(own_norm, dups[hh][:, lo : lo + width], TN).astype(BF)
            for t in range(2):
                j, b = divmod(2 * i + t, 3)
                at = (hh * 3 + b) * model
                shards[j][at : at + model, :] = w[:, t * LANES : (t + 1) * LANES]
    for j in range(4):
        shards[j][UP_ROWS:M_ROWS, :] = small[j].astype(BF)


def input_backward_kernel(layer, scal, sp, h_h, gres_h, dn_mlp, dq, dkv_own, dkv_got, *refs):
    sets, refs = refs[:8], refs[8:]
    cos_t, sin_t, g_o, nat_o, keep_o, send_o, wq, cs, sn, dall, norm, xhat, xinv, small, h_own, gres, wsem, tsem = refs
    sp = sp.at[pl.ds(layer, 1)]
    rows, model = h_own.shape
    half = scal[1]
    here, there = shard_copies(sets, wq)
    fetch(scal[3] == layer, here, there, wsem)
    shards = (keep_o.at[0], send_o.at[0], keep_o.at[1], send_o.at[1])
    tables = [
        pltpu.make_async_copy(cos_t.at[half, pl.ds(0, rows), :], cs, tsem.at[0]),
        pltpu.make_async_copy(sin_t.at[half, pl.ds(0, rows), :], sn, tsem.at[1]),
    ]
    tables.append(pltpu.make_async_copy(gres_h, gres, tsem.at[2]))
    first = pltpu.make_async_copy(h_h, h_own, tsem.at[3])
    first.start()
    for c in tables:
        c.start()
    first.wait()
    gain, bias = wide(sp, ROW_NG), wide(sp, ROW_NB)
    gain_mlp = wide(sp, ROW_NG + 4)
    step = 64
    for r in range(0, rows, step):
        hat, inverse = normalized(h_own[r : r + step, :].astype(F32))
        xhat[r : r + step, :] = hat
        xinv[r : r + step, :] = jnp.broadcast_to(inverse, (step, LANES))
        norm[r : r + step, :] = (hat * gain + bias).astype(BF)
    for c in tables:
        c.wait()
    for j in range(4):
        at = j * 3 * LANES
        dall[:, at : at + LANES] = dq[j]
        dk = dkv_own[j, :, 0:LANES] + dkv_got[j ^ 1, :, 0:LANES].astype(F32)
        dall[:, at + LANES : at + 2 * LANES] = rotate_back(dk, cs[...], sn[...]).astype(BF)
        dv = dkv_own[j, :, LANES:] + dkv_got[j ^ 1, :, LANES:].astype(F32)
        dall[:, at + 2 * LANES : at + 3 * LANES] = dv.astype(BF)
    landed(here, wsem)
    small[...] = jnp.zeros_like(small)
    dn = dot(dall[...], jnp.concatenate([wq[j, i] for j in range(4) for i in range(3)], axis=1), NT)
    dg0 = db0 = dg1 = db1 = jnp.zeros((1, model), F32)
    for r in range(0, rows, step):
        hat = xhat[r : r + step, :]
        a = dn[r : r + step]
        m = dn_mlp[r : r + step, :]
        dg0 = dg0 + jnp.sum(a * hat, axis=0, keepdims=True)
        db0 = db0 + jnp.sum(a, axis=0, keepdims=True)
        dg1 = dg1 + jnp.sum(m * hat, axis=0, keepdims=True)
        db1 = db1 + jnp.sum(m, axis=0, keepdims=True)
        gg = a * gain + m * gain_mlp
        dx = xinv[r : r + step, 0:1] * (
            gg - jnp.mean(gg, axis=1, keepdims=True) - hat * jnp.mean(gg * hat, axis=1, keepdims=True)
        )
        g_o[r : r + step, :] = (gres[r : r + step, :] + dx).astype(BF)
    nat_o[...] = dot(order_matrix(rows, True), g_o[...], NN).astype(BF)
    for j in range(4):
        for n, v in enumerate((dg0, dg1, db0, db1)):
            for i in range(4):
                small[j, 8 + 4 * n + i : 9 + 4 * n + i, :] = v[:, i * LANES : (i + 1) * LANES]
    for j in range(4):
        at = j * 3 * LANES
        d = dall[:, at : at + 3 * LANES]
        w = dot(norm[...], d, TN).astype(BF)
        s = jnp.sum(d.astype(F32), axis=0, keepdims=True)
        for i in range(3):
            lo = i * model
            shards[j][lo : lo + model, :] = w[:, i * LANES : (i + 1) * LANES]
            small[j, i : i + 1, :] = s[:, i * LANES : (i + 1) * LANES]
        shards[j][QKV_ROWS:A_ROWS, :] = small[j].astype(BF)


def assemble_kernel(scal, here, there, out):
    rows = here.shape[1]
    for n in range(8):
        place, half = scal[24 + n], scal[32 + n]
        part = there if n & 1 else here
        out[place, pl.ds(pl.multiple_of(half * rows, rows), rows), :] = part[n >> 1]


def finale_kernel(
    dm_lo, dm_hi, a, tops, logits,
    qkv_o, out_o, up_o, down_o, bqkv_o, bup_o, gain_o, gbias_o, conv_o, ng_o, nb_o, ob_o, logit_o,
):
    cut = D_ROWS // 2

    def rows_of(lo, hi, at, n, a, b):
        if b <= n:
            return lo[at + a : at + b, :].astype(F32)
        if a >= n:
            return hi[at + a - n : at + b - n, :].astype(F32)
        return jnp.concatenate([lo[at + a : at + n, :], hi[at : at + b - n, :]], axis=0).astype(F32)

    d_of = functools.partial(rows_of, dm_lo, dm_hi, 0, cut)
    m_of = functools.partial(rows_of, dm_lo, dm_hi, cut, M_ROWS // 2)
    def a_of(lo, hi):
        return a[lo:hi, :].astype(F32)

    model, shard = up_o.shape[1], up_o.shape[2]
    for i in range(3):
        qkv_o[i] = a_of(i * model, (i + 1) * model)
    for lb in range(4):
        lanes = slice(lb * LANES, (lb + 1) * LANES)
        out_o[:, lanes] = d_of(lb * LANES, (lb + 1) * LANES)
        down_o[:, lanes] = d_of(OUT_ROWS + lb * shard, OUT_ROWS + (lb + 1) * shard)
    for hh in range(2):
        for b in range(3):
            at = (hh * 3 + b) * model
            up_o[hh, :, b * LANES : (b + 1) * LANES] = m_of(at, at + model)
    small = m_of(UP_ROWS, M_ROWS)
    for b in range(3):
        lanes = slice(b * LANES, (b + 1) * LANES)
        at = b * BLOCK_ROWS
        conv_o[:, lanes] = small[at : at + TAPS]
        bup_o[:, lanes] = small[at + ROW_UP0 : at + ROW_UP0 + 2]
        gain_o[:, lanes] = small[at + ROW_GAIN : at + ROW_GAIN + 1]
        gbias_o[:, lanes] = small[at + ROW_GB0 : at + ROW_GB0 + 2]
    small = a_of(QKV_ROWS, A_ROWS)
    bqkv_o[...] = small[0:3]
    for n in range(2):
        for i in range(4):
            lanes = slice(i * LANES, (i + 1) * LANES)
            ng_o[n : n + 1, lanes] = small[8 + 4 * n + i : 9 + 4 * n + i]
            nb_o[n : n + 1, lanes] = small[16 + 4 * n + i : 17 + 4 * n + i]
    ng_o[2:3, :] = tops[0:1, :]
    nb_o[2:3, :] = tops[1:2, :]
    ob_o[...] = tops[2:4, :]
    l0, l1 = jnp.full((1, LANES), logits[0], F32), jnp.full((1, LANES), logits[1], F32)
    top = jnp.maximum(l0, l1)
    e0, e1 = jnp.exp(l0 - top), jnp.exp(l1 - top)
    slope = e0 * e1 / ((e0 + e1) * (e0 + e1)) * tops[4:5, 0:LANES]
    logit_o[0:1, :] = slope
    logit_o[1:2, :] = -slope


def exchange(x, axis, bit):
    n = lax.axis_size(axis)
    return lax.ppermute(x, axis, [(i, i ^ bit) for i in range(n)])


def fence(*xs):
    return lax.optimization_barrier(xs)


def total(*xs):
    out = xs[0].astype(F32)
    for x in xs[1:]:
        out = out + x.astype(F32)
    return out


def scatter_over_dp(x):
    n = lax.axis_size("dp")
    if n != 4:
        return (lax.psum(x.astype(F32), "dp").astype(BF),)
    d = lax.axis_index("dp")
    x = x.reshape(n, x.shape[0] // n, LANES)
    own = lax.dynamic_index_in_dim(x, d, 0, keepdims=False)
    return (own, *[exchange(lax.dynamic_index_in_dim(x, d ^ k, 0, keepdims=False), "dp", k) for k in range(1, n)])


def gather_over_dp(x):
    n = lax.axis_size("dp")
    return (x, *[exchange(x, "dp", k) for k in range(1, n)]) if n == 4 else (x,)


def in_order(parts):
    if len(parts) == 1:
        return parts[0]
    d = lax.axis_index("dp")
    low, high = (d & 1) == 0, (d & 2) == 0
    pairs = [
        (jnp.where(low, parts[k], parts[k + 1]), jnp.where(low, parts[k + 1], parts[k])) for k in (0, 2)
    ]
    return jnp.concatenate([jnp.where(high, pairs[i][t], pairs[1 - i][t]) for i in range(2) for t in range(2)], axis=0)


def halves(x, owner):
    rows = x.shape[0] // 2
    return jnp.where(owner, x[:rows], x[rows:]), jnp.where(owner, x[rows:], x[:rows])


def rotary_constants(length):
    half_width = HEAD // 2
    freq = np.exp(np.arange(half_width, dtype=np.float32) * np.float32(-math.log(10000.0) / half_width))
    rows = length // 2
    r = np.arange(rows)
    place = (r % SEGS) * (rows // SEGS) + r // SEGS
    cosines, sines = [], []
    for half in range(2):
        t = np.concatenate([half * rows + place, (1 - half) * rows + place]).astype(np.float32)
        angle = (t[:, None] * freq.astype(np.float32)[None, :]).astype(np.float32)
        c, s = np.cos(angle.astype(np.float64)), np.sin(angle.astype(np.float64))
        cosines.append(np.concatenate([c, c, c, c], axis=1))
        sines.append(np.concatenate([-s, s, -s, s], axis=1))
    return np.stack(cosines).astype(np.float32), np.stack(sines).astype(np.float32)


def per_device(frames, lengths, out_grad, *weights):
    (norm_gains, norm_biases, wqkv, bqkv, wout, wup, bup, ggain, gbias, cw, wdown, obias, logits) = [
        w[0] for w in weights
    ]
    micro, utterances, length, model = frames.shape
    n_sec, n_mp = lax.axis_size("section"), lax.axis_size("mp")
    assert utterances == 1 and n_sec == 2 and n_mp == 4 and micro == 4
    rows = length // 2
    shard = wdown.shape[0]
    hidden = shard * n_mp
    every = rows + HALO
    s, m = lax.axis_index("section"), lax.axis_index("mp")
    u = s * 2 + (m >> 1)
    half = m & 1
    own_length = lax.dynamic_index_in_dim(lengths[:, 0], u, 0, keepdims=False)
    ns = np.arange(40)
    xors = np.zeros(40, np.int32)
    xors[4:8] = np.arange(4)
    xors[8:20] = np.arange(12) // 3
    xors[24:32] = ns[:8] >> 1 & 1
    xors[32:40] = ns[:8] & 1
    sec_bits = np.zeros(40, np.int32)
    sec_bits[24:32] = ns[:8] >> 2
    idx = jnp.asarray(ns)
    by_shard = jnp.asarray(xors)
    by_place = (s ^ jnp.asarray(sec_bits)) * 2 + ((m >> 1) ^ jnp.asarray(xors))
    by_half = half ^ jnp.asarray(xors)
    scal = jnp.where(idx < 24, by_shard, jnp.where(idx < 32, by_place, by_half))
    for i, v in enumerate((u, half, own_length, s)):
        scal = jnp.where(idx == i, v, scal)
    scal = scal.astype(jnp.int32)

    x_of = lambda v: exchange(v, "section", 1)
    y_of = lambda v: exchange(v, "mp", 2)
    core_of = lambda v: exchange(v, "mp", 1)
    flat = shape((rows, model), BF)
    rows_f32 = shape((rows, model), F32)
    stat = shape((rows, LANES), F32)
    wide_bf = shape((rows, hidden), BF)
    halo_bf = shape((every, hidden), BF)

    def head_pack(n):
        return shape((4, n, LANES), BF)

    first = s == 0

    q_x, q_y, q_sib = x_of(wqkv), y_of(wqkv), core_of(wqkv)
    packed, u_own, v_own = call(
        pack_kernel,
        [wout, wup, wdown, cw, bup, ggain[None], gbias, bqkv, norm_gains, norm_biases, obias, logits],
        [ANY] * 3 + [VMEM] * 8 + [SMEM],
        [shape((PACK_ROWS, LANES), F32), shape((W_ROWS, LANES), BF), shape((DOWN_ROWS, LANES), BF)],
        [
            pltpu.VMEM(wout.shape, BF),
            pltpu.VMEM(wup.shape, BF),
            pltpu.VMEM(wdown.shape, BF),
            pltpu.SemaphoreType.DMA((3,)),
        ],
        0,
        12,
    )
    packed, q_x, q_y, scal, u_own, v_own = fence(packed, q_x, q_y, scal, u_own, v_own)
    packed_x = x_of(packed)
    q_d = y_of(q_x)
    packed_x, packed, q_y, q_x, v_early = fence(packed_x, packed, q_y, q_x, v_own)
    v_x = x_of(v_early)
    sections = jnp.stack([jnp.where(first, packed, packed_x), jnp.where(first, packed_x, packed)])
    sc, sections = fence(scal, sections)
    sections_y = y_of(sections)
    h_own, h_oth, g_last = call(
        prologue_kernel,
        [sc, frames, out_grad],
        [SMEM] + [ANY] * 2,
        [flat, flat, flat],
        [pltpu.VMEM((3, rows, model), BF), pltpu.SemaphoreType.DMA((3,))],
        0,
        12,
    )
    h_own, q_d, sections_y, v_x, u_own = fence(h_own, q_d, sections_y, v_x, u_own)
    u_x = x_of(u_own)
    q_xs, q_ys = core_of(q_x), core_of(q_y)
    sp_a = jnp.stack([sections, sections_y], axis=1)
    sp_b = core_of(sp_a)
    sp = jnp.stack([sp_a, sp_b], axis=2).reshape(2, n_mp, PACK_ROWS, LANES)
    sp, q_d, u_late = fence(sp, q_d, u_own)
    q_ds = core_of(q_d)
    u_y = y_of(u_late)
    w_qkv = [wqkv, q_sib, q_y, q_ys, q_x, q_xs, q_d, q_ds]

    cos_np, sin_np = rotary_constants(length)
    cos_t, sin_t = jnp.asarray(cos_np), jnp.asarray(sin_np)

    def attention_forward(layer, scal, h_own, h_oth):
        return call(
            functools.partial(attention_forward_kernel, layer),
            [scal, sp, cos_t, sin_t, h_own, h_oth, *w_qkv],
            [SMEM, VMEM, ANY, ANY, VMEM, VMEM] + [ANY] * 8,
            [head_pack(rows), head_pack(length), head_pack(length), head_pack(rows), stat, head_pack(rows)],
            [
                pltpu.VMEM((4, 3, model, LANES), BF),
                pltpu.VMEM((length, LANES), F32),
                pltpu.VMEM((length, LANES), F32),
                pltpu.VMEM((length, model), BF),
                pltpu.VMEM((LANES, rows), F32),
                pltpu.VMEM((4, rows, LANES), BF),
                pltpu.VMEM((4, length, LANES), BF),
                pltpu.VMEM((4, length, LANES), BF),
                pltpu.VMEM((rows, LANES), F32),
                pltpu.SemaphoreType.DMA((4,)),
                pltpu.SemaphoreType.DMA((2,)),
                pltpu.SemaphoreType.DMA((5, 4)),
            ],
            10 * rows * length * model, 24, range(5))

    def mlp_forward(layer, scal, h_own, h_oth):
        return call(
            functools.partial(mlp_forward_kernel, layer),
            [scal, sp, h_own, h_oth, *w_u],
            [SMEM, VMEM, VMEM, VMEM] + [ANY] * 10,
            [halo_bf, halo_bf, halo_bf, halo_bf, wide_bf, wide_bf, stat, shape((every, model), BF), wide_bf],
            [
                pltpu.VMEM((4, W_ROWS - W_UP, LANES), BF),
                pltpu.VMEM((every, hidden), F32),
                pltpu.VMEM((every, hidden), F32),
                pltpu.VMEM((every, LANES), F32),
                pltpu.VMEM((every, LANES), F32),
                pltpu.VMEM((every, LANES), F32),
                pltpu.VMEM((rows // SEGS + 32, SEGS, LANES), F32),
                pltpu.VMEM((72, SEGS, LANES), F32),
                pltpu.VMEM((rows // SEGS, SEGS, LANES), F32),
                pltpu.VMEM((rows // SEGS // 2 + 1, SEGS, LANES), F32),
                pltpu.VMEM((HALO, LANES), F32),
                pltpu.VMEM((every, hidden), BF),
                pltpu.VMEM((every, hidden), BF),
                pltpu.VMEM((every, hidden), BF),
                pltpu.VMEM((every, hidden), BF),
                pltpu.VMEM((rows, hidden), BF),
                pltpu.VMEM((every, model), BF),
                pltpu.SemaphoreType.DMA((8,)),
                pltpu.SemaphoreType.DMA((5 + 3 * hidden // LANES,)),
            ],
            8 * rows * model * hidden, 34, range(8))

    def merge_forward(layer, scal, h_own, mix, gated):
        return call(
            functools.partial(merge_forward_kernel, layer),
            [scal, sp, h_own, mix, gated, *w_u, *w_v],
            [SMEM, VMEM, VMEM, VMEM, VMEM] + [ANY] * 18,
            [flat, flat, rows_f32, stat, rows_f32],
            [
                pltpu.VMEM((4, W_UP, LANES), BF),
                pltpu.VMEM((4, DOWN_ROWS, LANES), BF),
                pltpu.VMEM((rows, model), F32),
                pltpu.VMEM((rows, LANES), F32),
                pltpu.VMEM((rows, model), F32),
                pltpu.SemaphoreType.DMA((8,)),
                pltpu.SemaphoreType.DMA((4,)),
                pltpu.SemaphoreType.DMA((2, 3)),
            ],
            2 * rows * model * hidden, 18, (2, 3, 4))

    att = attention_forward(0, scal, h_own, h_oth)
    att, u_x, u_y, v_late = fence(att, u_x, u_y, v_own)
    d1, d2 = y_of(u_x[:SPLIT]), x_of(u_y[SPLIT:])
    u_sib, u_xs, u_ys = core_of(u_own), core_of(u_x), core_of(u_y)
    d1, d2, v_late, v_x = fence(d1, d2, v_late, v_x)
    d1s, d2s = core_of(d1), core_of(d2)
    v_y = y_of(v_late)
    v_d = y_of(v_x)
    v_sib, v_xs = core_of(v_late), core_of(v_x)
    w_u = [u_own, u_sib, u_y, u_ys, u_x, u_xs, d1, d1s, d2, d2s]
    mlp0 = mlp_forward(0, scal, h_own, h_oth)
    mlp0, v_y, v_d, v_sib, v_xs = fence(mlp0, v_y, v_d, v_sib, v_xs)
    v_ys, v_ds = core_of(v_y), core_of(v_d)
    w_v = [v_own, v_sib, v_y, v_ys, v_x, v_xs, v_d, v_ds]
    top0 = merge_forward(0, scal, h_own, att[5], mlp0[8])
    saved = [(h_own, att, mlp0, top0)]
    h_own, h_oth = top0[0], core_of(top0[0])
    att = attention_forward(1, scal, h_own, h_oth)
    mlp1 = mlp_forward(1, scal, h_own, h_oth)
    top1 = merge_forward(1, scal, h_own, att[5], mlp1[8])
    saved.append((h_own, att, mlp1, top1))

    def merge_backward(layer, scal, g):
        h, att, mlp, top = saved[layer]
        return call(
            functools.partial(merge_backward_kernel, layer),
            [scal, sp, g, top[2], top[3], top[4], att[3], mlp[5]],
            [SMEM, VMEM, VMEM] + [ANY] * 5,
            [rows_f32, flat, flat, shape((HALO, model), BF), shape((8, model), F32),
             shape((2, D_ROWS, LANES), BF), shape((2, D_ROWS, LANES), BF)],
            [
                pltpu.VMEM((rows, model), F32),
                pltpu.VMEM((rows, LANES), F32),
                pltpu.VMEM((rows, model), F32),
                pltpu.VMEM((4, rows, LANES), BF),
                pltpu.VMEM((rows, hidden), BF),
                pltpu.SemaphoreType.DMA((5,)),
            ],
            2 * rows * model * (hidden + model), 16, (), (0, 5, 6))

    def conv_backward(layer, scal, gbr, halo_in):
        mlp = saved[layer][2]
        return call(
            functools.partial(conv_backward_kernel, layer),
            [scal, sp, gbr, halo_in, mlp[0], mlp[1], mlp[3], mlp[4], *w_v],
            [SMEM, VMEM, VMEM, VMEM] + [ANY] * 12,
            [wide_bf, shape((rows, hidden), F32), stat, stat, shape((4, LANES, LANES), F32)],
            [
                pltpu.VMEM((4, DOWN_ROWS, LANES), BF),
                pltpu.VMEM((every, hidden), BF),
                pltpu.VMEM((every, hidden), BF),
                pltpu.VMEM((every, hidden), BF),
                pltpu.VMEM((rows, hidden), BF),
                pltpu.VMEM((rows // SEGS + 32, SEGS, LANES), F32),
                pltpu.VMEM((rows // SEGS + 32, SEGS, LANES), F32),
                pltpu.VMEM((72, SEGS, LANES), F32),
                pltpu.VMEM((rows // SEGS, SEGS, LANES), F32),
                pltpu.VMEM((rows // SEGS // 2 + 1, SEGS, LANES), F32),
                pltpu.VMEM((HALO, LANES), F32),
                pltpu.VMEM((every, hidden), F32),
                pltpu.VMEM((every, model), BF),
                pltpu.SemaphoreType.DMA((4,)),
                pltpu.SemaphoreType.DMA((4,)),
            ],
            0,
            30,
        )

    def up_backward(layer, scal, dup0, hgrad, hs, xs, small):
        mlp = saved[layer][2]
        return call(
            functools.partial(up_backward_kernel, layer),
            [scal, dup0, hgrad, hs, xs, small, mlp[3], mlp[2], mlp[6], mlp[7], *w_u],
            [SMEM] + [VMEM] * 5 + [ANY] * 14,
            [rows_f32, shape((2, M_ROWS, LANES), BF), shape((2, M_ROWS, LANES), BF)],
            [
                pltpu.VMEM((4, W_ROWS - W_UP, LANES), BF),
                pltpu.VMEM((rows, hidden), BF),
                pltpu.VMEM((rows, hidden), BF),
                pltpu.VMEM((rows, LANES), F32),
                pltpu.VMEM((every, model), BF),
                pltpu.VMEM((rows, hidden), BF),
                pltpu.VMEM((4, LANES, LANES), F32),
                pltpu.SemaphoreType.DMA((8,)),
                pltpu.SemaphoreType.DMA((4,)),
            ],
            0,
            30,
            (),
            (1, 2),
        )

    def attention_backward(layer, scal, gatt):
        att = saved[layer][1]
        return call(
            functools.partial(attention_backward_kernel, layer),
            [scal, gatt, *att[:5], *w_u, cos_t, sin_t],
            [SMEM, VMEM] + [ANY] * 17,
            [head_pack(rows), shape((4, rows, 2 * LANES), F32), shape((4, rows, 2 * LANES), BF)],
            [
                pltpu.VMEM((4, W_UP, LANES), BF),
                pltpu.VMEM((rows, LANES), F32),
                pltpu.VMEM((rows, LANES), F32),
                pltpu.VMEM((length, 2 * rows), BF),
                pltpu.VMEM((length, 2 * rows), BF),
                pltpu.VMEM((2 * rows, LANES), BF),
                pltpu.VMEM((2 * rows, LANES), BF),
                pltpu.VMEM((4, rows, LANES), BF),
                pltpu.VMEM((4, length, LANES), BF),
                pltpu.VMEM((4, length, LANES), BF),
                pltpu.VMEM((4, rows, LANES), BF),
                pltpu.VMEM((rows, LANES), F32),
                pltpu.SemaphoreType.DMA((4,)),
                pltpu.SemaphoreType.DMA((7,)),
            ],
            12 * rows * length * model, 26)

    def input_backward(layer, scal, gres, dn_mlp, dq, dkv_own, dkv_got):
        h = saved[layer][0]
        return call(
            functools.partial(input_backward_kernel, layer),
            [scal, sp, h, gres, dn_mlp, dq, dkv_own, dkv_got, *w_qkv, cos_t, sin_t],
            [SMEM, VMEM, ANY, ANY] + [VMEM] * 4 + [ANY] * 10,
            [flat, flat, shape((2, A_ROWS, LANES), BF), shape((2, A_ROWS, LANES), BF)],
            [
                pltpu.VMEM((4, 3, model, LANES), BF),
                pltpu.VMEM((rows, LANES), F32),
                pltpu.VMEM((rows, LANES), F32),
                pltpu.VMEM((rows, 12 * LANES), BF),
                pltpu.VMEM((rows, model), BF),
                pltpu.VMEM((rows, model), F32),
                pltpu.VMEM((rows, LANES), F32),
                pltpu.VMEM((4, 64, LANES), F32),
                pltpu.VMEM((rows, model), BF),
                pltpu.VMEM((rows, model), F32),
                pltpu.SemaphoreType.DMA((4,)),
                pltpu.SemaphoreType.DMA((4,)),
            ],
            14 * rows * model * model, 24, (), (2, 3))

    owner1 = jnp.logical_not(first)
    natural0, natural1 = top0[1], top1[1]
    out_keep = jnp.where(first, natural0, natural1)
    out_send = jnp.where(first, natural1, natural0)
    sc, out_send, out_keep = fence(scal, out_send, out_keep)
    out_got = x_of(out_send)
    gres, gatt, gbr, halo_out, tops1, d_keep, d_send = merge_backward(1, sc, g_last)
    gbr, halo_out, d_send = fence(gbr, halo_out, d_send)
    halo_in, d_got = core_of(halo_out), core_of(d_send)
    gbr, halo_in, d_got = fence(gbr, halo_in, d_got)
    d_away = total(d_keep[1], d_got[1]).astype(BF)
    sc, d_away = fence(scal, d_away)
    d_y = y_of(d_away)
    part = conv_backward(1, sc, gbr, halo_in)
    part, d_y, out_got = fence(part, d_y, out_got)
    d_mine, d_give = halves(total(d_keep[0], d_got[0], d_y), owner1)
    sc, d_give, out_keep = fence(scal, d_give.astype(BF), out_keep)
    d_x = x_of(d_give)
    out_y = y_of(out_keep)
    dn_mlp, m_keep, m_send = up_backward(1, sc, *part)
    gatt, d_x, m_send, out_y = fence(gatt, d_x, m_send, out_y)
    m_got = core_of(m_send)
    m_away = total(m_keep[1], m_got[1]).astype(BF)
    sc, m_away = fence(scal, m_away)
    m_y = y_of(m_away)
    dq, dkv_own, dkv_oth = attention_backward(1, sc, gatt)
    dq, dkv_oth, m_y = fence(dq, dkv_oth, m_y)
    dkv_got = core_of(dkv_oth)
    m_mine, m_give = halves(total(m_keep[0], m_got[0], m_y), owner1)
    sc, m_give, out_got = fence(scal, m_give.astype(BF), out_got)
    m_x = x_of(m_give)
    out_yg = y_of(out_got)
    g, ingrad1, a_keep, a_send = input_backward(1, sc, gres, dn_mlp, dq, dkv_own, dkv_got)

    g, a_send, m_x = fence(g, a_send, m_x)
    a_got = core_of(a_send)
    dm1_half = jnp.concatenate([total(d_mine, d_x), total(m_mine, m_x)], axis=0).astype(BF)
    sc, dm1_half = fence(scal, dm1_half)
    dm1_half = lax.psum(dm1_half, "dp")
    gres, gatt, gbr, halo_out, tops0, d0_keep, d0_send = merge_backward(0, sc, g)
    gbr, halo_out, d0_send, a_got, out_yg = fence(gbr, halo_out, d0_send, a_got, out_yg)
    halo_in, d0_got = core_of(halo_out), core_of(d0_send)
    tops = jnp.stack([tops0, tops1])
    tops_core = core_of(tops)
    a_away = total(a_keep[1], a_got[1]).astype(BF)
    gbr, halo_in, d0_got, a_away, tops_core = fence(gbr, halo_in, d0_got, a_away, tops_core)
    d_away = total(d0_keep[1], d0_got[1]).astype(BF)
    sc, a_away, d_away = fence(scal, a_away, d_away)
    ad_y = y_of(jnp.concatenate([a_away, d_away], axis=0))
    tops = tops + tops_core
    tops, sc = fence(tops, sc)
    tops_y = y_of(tops)
    part = conv_backward(0, sc, gbr, halo_in)
    part, ad_y, tops_y = fence(part, ad_y, tops_y)
    a_y, d_y = ad_y[:A_ROWS], ad_y[A_ROWS:]
    tops = tops + tops_y
    a_mine, a_give = halves(total(a_keep[0], a_got[0], a_y), owner1)
    d_mine, d_give = halves(total(d0_keep[0], d0_got[0], d_y), first)
    sc, give, tops = fence(scal, jnp.concatenate([a_give, d_give], axis=0).astype(BF), tops)
    got = x_of(give)
    tops_x = x_of(tops)
    dn_mlp, m0_keep, m0_send = up_backward(0, sc, *part)
    gatt, got, m0_send, dm1_half, tops_x = fence(gatt, got, m0_send, dm1_half, tops_x)
    tops = tops + tops_x
    m0_got = core_of(m0_send)
    ad_half = total(jnp.concatenate([a_mine, d_mine], axis=0), got).astype(BF)
    m_away = total(m0_keep[1], m0_got[1]).astype(BF)
    sc, m_away, ad_half, tops = fence(scal, m_away, ad_half, tops)
    m_y = y_of(m_away)
    ad_terms = scatter_over_dp(ad_half)
    n_dp = lax.axis_size("dp")
    tops = tops + exchange(tops, "dp", 1) if n_dp == 4 else lax.psum(tops, "dp")
    dq, dkv_own, dkv_oth = attention_backward(0, sc, gatt)
    dq, dkv_oth, m_y, tops, ad_terms = fence(dq, dkv_oth, m_y, tops, ad_terms)
    dkv_got = core_of(dkv_oth)
    m_mine, m_give = halves(total(m0_keep[0], m0_got[0], m_y), first)
    sc, m_give, tops, ad_half = fence(scal, m_give.astype(BF), tops, total(*ad_terms).astype(BF))
    m_x = x_of(m_give)
    ad_half = gather_over_dp(ad_half)
    if n_dp == 4:
        tops = tops + exchange(tops, "dp", 2)
    out_half = jnp.stack([out_keep, out_y, out_got, out_yg])
    out_other = core_of(out_half)
    g, ingrad0, a_keep, a_send = input_backward(0, sc, gres, dn_mlp, dq, dkv_own, dkv_got)

    ingrad0, a_send, m_x, ad_half, tops, out_other = fence(ingrad0, a_send, m_x, ad_half, tops, out_other)
    a_got = core_of(a_send)
    in_keep = jnp.where(first, ingrad0, ingrad1)
    in_got = x_of(jnp.where(first, ingrad1, ingrad0))
    m_terms = scatter_over_dp(total(m_mine, m_x).astype(BF))
    a_away = total(a_keep[1], a_got[1]).astype(BF)
    a_away, m_terms, in_keep = fence(a_away, m_terms, in_keep)
    a_y = y_of(a_away)
    in_y = y_of(in_keep)
    m_parts = gather_over_dp(total(*m_terms).astype(BF))
    a_y, m_parts, in_got, ad_half = fence(a_y, m_parts, in_got, ad_half)
    a_sum = total(a_keep[0], a_got[0], a_y).astype(BF)
    a_x = x_of(a_sum)
    in_yg = y_of(in_got)
    ad_half = in_order(ad_half)
    dm0_half = jnp.concatenate([ad_half[A_ROWS // 2 :], in_order(m_parts)], axis=0)
    a1_half = ad_half[: A_ROWS // 2]
    dm_lo = jnp.where(first, dm0_half, dm1_half)
    back = x_of(jnp.concatenate([jnp.where(first, dm1_half, dm0_half), a1_half], axis=0))
    a_x, in_y = fence(a_x, in_y)
    a_terms = scatter_over_dp(total(a_sum, a_x).astype(BF))
    a_terms, in_yg, in_y, in_got, back = fence(a_terms, in_yg, in_y, in_got, back)
    a_parts = gather_over_dp(total(*a_terms).astype(BF))
    in_half = jnp.stack([in_keep, in_y, in_got, in_yg])
    in_other = core_of(in_half)

    def assemble(here, there):
        return call(
            assemble_kernel, [scal, here, there], [SMEM, VMEM, VMEM], [shape((micro, length, model), BF)], [], 0, 10
        )[0]

    layer_out = assemble(out_half, out_other)
    input_grad = assemble(in_half, in_other)

    tops = jnp.where(first, tops[0], tops[1])
    a_parts, layer_out, input_grad, tops, back = fence(a_parts, layer_out, input_grad, tops, back)
    cut = dm_lo.shape[0]
    a_whole = jnp.where(first, in_order(a_parts), jnp.concatenate([a1_half, back[cut:]], axis=0))
    (g_qkv, g_out, g_up, g_down, g_bqkv, g_bup, g_gain, g_gbias, g_conv, g_ng, g_nb, g_ob, g_logit) = call(
        finale_kernel,
        [dm_lo, back, a_whole, tops, logits],
        [VMEM] * 4 + [SMEM],
        [shape((3, model, LANES), F32), shape((LANES, model), F32), shape((2, model, shard), F32),
         shape((shard, model), F32), shape((3, LANES), F32), shape((2, shard), F32), shape((1, shard), F32),
         shape((2, shard), F32), shape((TAPS, shard), F32), shape((3, model), F32), shape((3, model), F32),
         shape((2, model), F32), shape((2, LANES), F32)],
        [],
        0,
        16,
    )
    outs = (
        layer_out.reshape(micro, 1, length, model),
        input_grad.reshape(micro, 1, length, model),
        g_ng,
        g_nb,
        g_qkv,
        g_bqkv,
        g_out,
        g_up,
        g_bup,
        g_gain[0],
        g_gbias,
        g_conv,
        g_down,
        g_ob,
        g_logit[:, 0],
    )
    return tuple(x[None] for x in outs)


def solution(mesh):
    placed = (
        P(None, "dp", None, None),
        P(None, "dp"),
        P(None, "dp", None, None),
        P("section", None, None),
        P("section", None, None),
        P("section", None, None, "mp"),
        P("section", None, "mp"),
        P("section", "mp", None),
        P("section", None, None, "mp"),
        P("section", None, "mp"),
        P("section", "mp"),
        P("section", None, "mp"),
        P("section", None, "mp"),
        P("section", "mp", None),
        P("section", None, None),
        P("section", None),
    )
    return jax.shard_map(
        per_device,
        mesh=mesh,
        in_specs=placed,
        out_specs=(
            P("section", None, "dp", None, None),
            P("section", None, "dp", None, None),
            P("section", None, None),
            P("section", None, None),
            P("section", None, None, "mp"),
            P("section", None, "mp"),
            P("section", "mp", None),
            P("section", None, None, "mp"),
            P("section", None, "mp"),
            P("section", "mp"),
            P("section", None, "mp"),
            P("section", None, "mp"),
            P("section", "mp", None),
            P("section", None, None),
            P("section", None),
        ),
        check_vma=False,
    )
```

```python
import functools
import math

import jax
import jax.numpy as jnp
import numpy as np
from jax import lax
from jax.experimental import pallas as pl
from jax.experimental.pallas import tpu as pltpu
from jax.sharding import PartitionSpec as P

BF = jnp.bfloat16
F32 = jnp.float32
HEAD = 64
LANES = 128
SEGS = 8
HALO = 16
EPS = 1e-05
NEG = -1000000000.0
NN = (((1,), (0,)), ((), ()))
NT = (((1,), (1,)), ((), ()))
TN = (((0,), (0,)), ((), ()))

TAPS = 31
BLOCK_ROWS = 40
ROW_UP0, ROW_UP1, ROW_GAIN, ROW_GB0, ROW_GB1 = 31, 32, 33, 34, 35
ROW_QKV = 120
ROW_NG, ROW_NB, ROW_OB, ROW_LOGIT = 128, 140, 152, 160
PACK_ROWS = 168

OUT_ROWS, DOWN_ROWS, UP_ROWS, QKV_ROWS = 512, 1536, 3072, 1536
D_SMALL = OUT_ROWS + DOWN_ROWS
D_ROWS = D_SMALL + 64
M_ROWS = UP_ROWS + 128
A_ROWS = QKV_ROWS + 64

W_UP, W_ROWS = 512, 3584
SPLIT = 2560

VMEM = pl.BlockSpec(memory_space=pltpu.VMEM)
SMEM = pl.BlockSpec(memory_space=pltpu.SMEM)
ANY = pl.BlockSpec(memory_space=pltpu.HBM)


def dot(a, b, dims):
    return lax.dot_general(a, b, dims, preferred_element_type=F32)


def call(kernel, ins, in_specs, outs, scratch, flops, mib, far=(), home=()):
    ins = [pltpu.with_memory_space_constraint(x, pltpu.HBM) if p is ANY else x for x, p in zip(ins, in_specs)]
    return pl.pallas_call(
        kernel,
        in_specs=in_specs,
        out_specs=[ANY if i in far else VMEM for i in range(len(outs))],
        out_shape=[pltpu.HBM(x.shape, x.dtype) if i in far or i in home else x for i, x in enumerate(outs)],
        scratch_shapes=scratch,
        compiler_params=pltpu.CompilerParams(vmem_limit_bytes=mib << 20),
        cost_estimate=pl.CostEstimate(flops=1, bytes_accessed=1, transcendentals=0),
    )(*ins)


def shape(dims, dtype):
    return jax.ShapeDtypeStruct(dims, dtype)


def fetch(flag, here, there, sems):
    @pl.when(flag)
    def _():
        for i, (a, d) in enumerate(here):
            pltpu.make_async_copy(a, d, sems.at[i]).start()

    @pl.when(jnp.logical_not(flag))
    def _():
        for i, (a, d) in enumerate(there):
            pltpu.make_async_copy(a, d, sems.at[i]).start()


def landed(pairs, sems):
    for i, (a, d) in enumerate(pairs):
        pltpu.make_async_copy(a, d, sems.at[i]).wait()


def slab_copies(sets, dst, lo, hi):
    here, there = [], []
    for j in range(4):
        for a, b in ((lo, min(hi, SPLIT)), (max(lo, SPLIT), hi)):
            if a >= b:
                continue
            d = dst.at[j, pl.ds(a - lo, b - a), :]
            here.append((sets[j].at[pl.ds(a, b - a), :], d))
            if j < 2:
                there.append((sets[4 + j].at[pl.ds(a, b - a), :], d))
            elif a < SPLIT:
                there.append((sets[4 + j].at[pl.ds(a, b - a), :], d))
            else:
                there.append((sets[6 + j].at[pl.ds(a - SPLIT, b - a), :], d))
    return here, there


def shard_copies(sets, dst):
    return [(sets[j], dst.at[j]) for j in range(4)], [(sets[4 + j], dst.at[j]) for j in range(4)]


def wide(sp, row, count=4):
    return jnp.concatenate([sp[0, 0, row + i : row + i + 1, :] for i in range(count)], axis=1)


def branch_weights(sp):
    l0 = sp[0, 0, ROW_LOGIT : ROW_LOGIT + 1, :]
    l1 = sp[0, 0, ROW_LOGIT + 1 : ROW_LOGIT + 2, :]
    top = jnp.maximum(l0, l1)
    e0, e1 = jnp.exp(l0 - top), jnp.exp(l1 - top)
    total = e0 + e1
    return jnp.concatenate([e0 / total] * 4, axis=1), jnp.concatenate([e1 / total] * 4, axis=1)


def normalized(x):
    center = jnp.mean(x, axis=-1, keepdims=True)
    d = x - center
    inverse = lax.rsqrt(jnp.mean(d * d, axis=-1, keepdims=True) + EPS)
    return d * inverse, inverse


def frame_of(row, half, rows):
    return half * rows + (row & (SEGS - 1)) * (rows // SEGS) + (row >> 3)


def order_matrix(rows, back):
    r = lax.broadcasted_iota(jnp.int32, (rows, rows), 1 if back else 0)
    t = lax.broadcasted_iota(jnp.int32, (rows, rows), 0 if back else 1)
    return jnp.where(frame_of(r, 0, rows) == t, 1.0, 0.0).astype(BF)


def halo_pick(rows, start_seg_even):
    start, seg = start_seg_even
    i = lax.broadcasted_iota(jnp.int32, (HALO, rows), 0)
    r = lax.broadcasted_iota(jnp.int32, (HALO, rows), 1)
    return jnp.where(r == (i + start) * SEGS + seg, 1.0, 0.0).astype(BF)


def swap_halves(x):
    lane = lax.broadcasted_iota(jnp.int32, x.shape, 1)
    return jnp.where(
        (lane & (HEAD - 1)) < HEAD // 2,
        pltpu.roll(x, LANES - HEAD // 2, 1),
        pltpu.roll(x, HEAD // 2, 1),
    )


def rotate(x, cosine, sine):
    return x * cosine + swap_halves(x) * sine


def rotate_back(x, cosine, sine):
    return x * cosine - swap_halves(x) * sine


def pieces(x):
    hi = x.astype(BF).astype(F32)
    rest = x - hi
    mid = rest.astype(BF).astype(F32)
    return hi, mid, rest - mid


def pack_kernel(
    wout_h, wup_h, wdown_h, cw, bup, ggain, gbias, bqkv, ngain, nbias, obias, logits,
    sp_o, u_o, v_o, wout, wup, wdown, sems,
):
    loads = [
        pltpu.make_async_copy(a, b, sems.at[i])
        for i, (a, b) in enumerate(((wup_h, wup), (wdown_h, wdown), (wout_h, wout)))
    ]
    for c in loads:
        c.start()
    sp_o[...] = jnp.zeros_like(sp_o)
    for b in range(3):
        lanes = slice(b * LANES, (b + 1) * LANES)
        at = b * BLOCK_ROWS
        sp_o[at : at + TAPS, :] = cw[:, lanes]
        sp_o[at + ROW_UP0 : at + ROW_UP0 + 2, :] = bup[:, lanes]
        sp_o[at + ROW_GAIN : at + ROW_GAIN + 1, :] = ggain[:, lanes]
        sp_o[at + ROW_GB0 : at + ROW_GB0 + 2, :] = gbias[:, lanes]
    sp_o[ROW_QKV : ROW_QKV + 3, :] = bqkv[...]
    for i in range(4):
        lanes = slice(i * LANES, (i + 1) * LANES)
        for n in range(3):
            sp_o[ROW_NG + 4 * n + i : ROW_NG + 4 * n + i + 1, :] = ngain[n : n + 1, lanes]
            sp_o[ROW_NB + 4 * n + i : ROW_NB + 4 * n + i + 1, :] = nbias[n : n + 1, lanes]
        for n in range(2):
            sp_o[ROW_OB + 4 * n + i : ROW_OB + 4 * n + i + 1, :] = obias[n : n + 1, lanes]
    for n in range(2):
        sp_o[ROW_LOGIT + n : ROW_LOGIT + n + 1, :] = jnp.full((1, LANES), logits[n], F32)
    for c in loads:
        c.wait()
    model, shard = wup.shape[1], wup.shape[2]
    for lb in range(4):
        lanes = slice(lb * LANES, (lb + 1) * LANES)
        u_o[lb * LANES : (lb + 1) * LANES, :] = wout[:, lanes]
        v_o[lb * shard : (lb + 1) * shard, :] = wdown[:, lanes]
    for hh in range(2):
        for b in range(3):
            at = W_UP + (hh * 3 + b) * model
            u_o[at : at + model, :] = wup[hh, :, b * LANES : (b + 1) * LANES]


def prologue_kernel(scal, frames, cotangent, own_o, oth_o, g_o, buf, sems):
    rows = own_o.shape[0]
    u, half = scal[0], scal[1]
    mine = pl.ds(pl.multiple_of(half * rows, rows), rows)
    other = pl.ds(pl.multiple_of((1 - half) * rows, rows), rows)
    copies = [
        pltpu.make_async_copy(frames.at[u, 0, mine, :], buf.at[0], sems.at[0]),
        pltpu.make_async_copy(frames.at[u, 0, other, :], buf.at[1], sems.at[1]),
        pltpu.make_async_copy(cotangent.at[u, 0, mine, :], buf.at[2], sems.at[2]),
    ]
    for c in copies:
        c.start()
    order = order_matrix(rows, False)
    for c, i, out in zip(copies, range(3), (own_o, oth_o, g_o)):
        c.wait()
        out[...] = dot(order, buf[i], NN).astype(BF)


def attention_forward_kernel(layer, scal, sp, cos_t, sin_t, h_own, h_oth, *refs):
    sets, refs = refs[:8], refs[8:]
    q_h, k_h, v_h, mix_h, lse_h, mix_o, w_s, cs, sn, norm, lse_s, q_o, k_o, v_o, lse_o, wsem, tsem, osem = refs
    sp = sp.at[pl.ds(layer, 1)]
    rows, model = h_own.shape
    half, length = scal[1], scal[2]
    here, there = shard_copies(sets, w_s)
    fetch(scal[3] == layer, here, there, wsem)
    tables = [
        pltpu.make_async_copy(cos_t.at[half], cs, tsem.at[0]),
        pltpu.make_async_copy(sin_t.at[half], sn, tsem.at[1]),
    ]
    for c in tables:
        c.start()
    gain, bias = wide(sp, ROW_NG), wide(sp, ROW_NB)
    step = 64
    for src, base in ((h_own, 0), (h_oth, rows)):
        for r in range(0, rows, step):
            hat, unused = normalized(src[r : r + step, :].astype(F32))
            norm[base + r : base + r + step, :] = (hat * gain + bias).astype(BF)
    lse_s[...] = jnp.zeros_like(lse_s)
    for c in tables:
        c.wait()
    landed(here, wsem)
    total = 2 * rows
    row = lax.broadcasted_iota(jnp.int32, (total, LANES), 0)
    part = jnp.where(row < rows, half, 1 - half)
    position = frame_of(row & (rows - 1), part, rows)
    mask = jnp.where(position < length, 0.0, NEG)
    lane_k = lax.broadcasted_iota(jnp.int32, (total, LANES), 1)
    lane_q = lax.broadcasted_iota(jnp.int32, (rows, LANES), 1)

    def stores(j):
        pairs = ((q_o, q_h), (k_o, k_h), (v_o, v_h), (mix_o, mix_h))
        return [pltpu.make_async_copy(a.at[j], b.at[j], osem.at[j, i]) for i, (a, b) in enumerate(pairs)]

    def shard(j):
        mj = scal[4 + j]
        bq = sp[0, mj, ROW_QKV : ROW_QKV + 1, :]
        bk = sp[0, mj, ROW_QKV + 1 : ROW_QKV + 2, :]
        bv = sp[0, mj, ROW_QKV + 2 : ROW_QKV + 3, :]
        everything = norm[...]
        q = rotate(dot(norm[:rows, :], w_s[j, 0], NN) + bq, cs[:rows, :], sn[:rows, :])
        q = q.astype(BF).astype(F32) * (1.0 / math.sqrt(HEAD))
        k = rotate(dot(everything, w_s[j, 1], NN) + bk, cs[...], sn[...]).astype(BF)
        v = (dot(everything, w_s[j, 2], NN) + bv).astype(BF)
        q_o[j] = q.astype(BF)
        k_o[j] = k
        v_o[j] = v
        kf = k.astype(F32)
        vt = v.astype(F32).T.astype(BF)
        outs = []
        work = []
        for hd in range(2):
            spare = (1 - hd) * HEAD
            qm = jnp.where((lane_q >> 6) == hd, q, jnp.where(lane_q == spare, 1.0, 0.0)).astype(BF)
            km = jnp.where((lane_k >> 6) == hd, kf, jnp.where(lane_k == spare, mask, 0.0)).astype(BF)
            work.append((km, qm))
        score = dot(*work[0], NT)
        for hd in range(2):
            s = score
            if hd == 0:
                score = dot(*work[1], NT)
            top = jnp.max(s, axis=0, keepdims=True)
            p = jnp.exp(s - top)
            den = jnp.sum(p, axis=0, keepdims=True)
            p = (p * (1.0 / den)).astype(BF)
            outs.append(dot(vt[hd * HEAD : (hd + 1) * HEAD, :], p, NN))
            lse_s[2 * j + hd : 2 * j + hd + 1, :] = top + jnp.log(den)
        mix_o[j] = jnp.concatenate(outs, axis=0).T.astype(BF)
        for c in stores(j):
            c.start()

    for j in range(4):
        shard(j)
    lse_o[...] = lse_s[...].T
    last = pltpu.make_async_copy(lse_o, lse_h, osem.at[4, 0])
    last.start()
    for j in range(4):
        for c in stores(j):
            c.wait()
    last.wait()


def gelu_parts(u):
    d = 1.0 + (0.3275911 / math.sqrt(2.0)) * jnp.abs(u)
    t = pl.reciprocal(d, approx=True)
    t = t * (2.0 - d * t)
    e = jnp.exp2((-0.5 / math.log(2.0)) * (u * u))
    half = [0.5 * c for c in (1.061405429, -1.453152027, 1.421413741, -0.284496736, 0.254829592)]
    poly = ((((half[0] * t + half[1]) * t + half[2]) * t + half[3]) * t + half[4]) * t
    tail = poly * e
    phi = jnp.where(u >= 0, 1.0 - tail, tail)
    return u * phi, phi + (u * e) * (1.0 / math.sqrt(2.0 * math.pi))


PHASES = ((0,), (2,), (2, 4), (1,), (3,), (3, 5), (1, 2), (3, 4), (3, 4, 5, 6))
TAP_PHASES = ((0,), (2,), (0, 2), (1,), (3,), (1, 3), (0, 1), (2, 3), (0, 1, 2, 3))


def phase(ref, rows, n):
    out = ref[4 * n + rows[0]]
    for r in rows[1:]:
        out = out + ref[4 * n + r]
    return out


def correlate(taps, xs, count):
    accs = [None] * count
    for m, tap in enumerate(taps):
        for n in range(count):
            term = tap * xs[n + m]
            accs[n] = term if accs[n] is None else accs[n] + term
    return accs


def unfold(q0, q1, q2):
    out = []
    for n in range(len(q2)):
        out.append(q0[n] + q1[n])
        out.append(q2[n] - (q0[n + 1] + q1[n]))
    if len(q1) > len(q2):
        out.append(q0[len(q2)] + q1[len(q2)])
    return out


def fill_filters(filt, row):
    for m in range(8):
        w = [
            jnp.broadcast_to(row(4 * m + r), (SEGS, LANES)) if 4 * m + r < TAPS else jnp.zeros((SEGS, LANES), F32)
            for r in range(4)
        ]
        for i, rows in enumerate(TAP_PHASES):
            out = w[rows[0]]
            for r in rows[1:]:
                out = out + w[r]
            filt[i * 8 + m] = out


def fast_fir(pad, filt, out, keep):
    count = out.shape[0]
    half = count // 2
    for g in range(3):
        qs = []
        for i in range(3):
            n = half // 2 + 1 if i == 0 or (i == 1 and g == 0) else half // 2
            xs = [phase(pad, PHASES[3 * g + i], x) for x in range(n + 7)]
            qs.append(correlate([filt[(3 * g + i) * 8 + m] for m in range(8)], xs, n))
        p = unfold(*qs)
        for n in range(len(p)):
            if g == 0:
                keep[n] = p[n]
            elif g == 1:
                out[2 * n] = keep[n] + p[n]
                out[2 * n + 1] = keep[n + 1] + p[n]
            else:
                out[2 * n + 1] = p[n] - out[2 * n + 1]


def tap_sums(gpad, xpad, count):
    ps = []
    for g in range(3):
        qs = []
        for i in range(3):
            rows = [15 + r for r in TAP_PHASES[3 * g + i]]
            n = 9 if i == 0 else 8
            steps = count // 4
            xs = [phase(xpad, PHASES[3 * g + i], x) for x in range(n + steps - 1)]
            qs.append(correlate([phase(gpad, rows, x) for x in range(steps)], xs, n))
        ps.append(unfold(*qs))
    out = []
    for m in range(16):
        out.append(ps[0][m] + ps[1][m])
        if m < 15:
            out.append(ps[2][m] - (ps[0][m + 1] + ps[1][m]))
    return out


def halo_pads(pad, block, halo_ref, half, right_is_even):
    count = block.shape[0]
    pad[15 : 15 + count] = block
    pad[30 + count : 32 + count] = jnp.zeros((2, SEGS, LANES), F32)
    seg = lax.broadcasted_iota(jnp.int32, (SEGS, LANES), 0)
    from_left = half.astype(F32)
    from_right = 1.0 - from_left
    for i in range(15):
        tail = pltpu.roll(block[count - 15 + i], 1, 0)
        edge = jnp.broadcast_to(halo_ref[i + 1 : i + 2, :], (SEGS, LANES)) * from_left
        pad[i] = jnp.where(seg == 0, edge, tail)
        head = pltpu.roll(block[i], SEGS - 1, 0)
        edge = jnp.broadcast_to(halo_ref[i : i + 1, :], (SEGS, LANES)) * from_right
        pad[15 + count + i] = jnp.where(seg == SEGS - 1, edge, head)


def mlp_forward_kernel(layer, scal, sp, h_own, h_oth, *refs):
    sets, refs = refs[:10], refs[10:]
    (act0_h, dact0_h, dact1_h, ghat_h, conv_h, gated_h, ginv_h, norm_h, gated_o,
     ws, act0, act1, sums, gmean, ginv, pad, filt, fir, keep, halo, act0_o, dact0_o, dact1_o, ghat_o, conv_o, norm_o, wsem, osem) = refs
    sp = sp.at[pl.ds(layer, 1)]
    rows, model = h_own.shape
    every = rows + HALO
    hidden = act0.shape[1]
    shard = hidden // 4
    half, length = scal[1], scal[2]
    here, there = slab_copies(sets, ws, W_UP, W_ROWS)
    fetch(scal[3] == layer, here, there, wsem)
    gain, bias = wide(sp, ROW_NG + 4), wide(sp, ROW_NB + 4)
    step = 64
    for r in range(0, rows, step):
        hat, unused = normalized(h_own[r : r + step, :].astype(F32))
        norm_o[r : r + step, :] = (hat * gain + bias).astype(BF)
    i = lax.broadcasted_iota(jnp.int32, (HALO, rows), 0)
    r = lax.broadcasted_iota(jnp.int32, (HALO, rows), 1)
    wanted = jnp.where(half == 0, i * SEGS, (i + rows // SEGS - HALO) * SEGS + SEGS - 1)
    pick = jnp.where(r == wanted, 1.0, 0.0).astype(BF)
    hat, unused = normalized(dot(pick, h_oth[...], NN))
    norm_o[rows:every, :] = (hat * gain + bias).astype(BF)
    sums[...] = jnp.zeros_like(sums)
    landed(here, wsem)

    width = 256
    chunk = 48

    def up(i, carry):
        lanes = pl.ds(pl.multiple_of(i * width, width), width)
        rows_of = []
        for hh, base in ((0, ROW_UP0), (1, ROW_UP1)):
            got = []
            for t in range(2):
                c = 2 * i + t
                got.append(sp[0, scal[8 + c], pl.ds(lax.rem(c, 3) * BLOCK_ROWS + base, 1), :])
            rows_of.append(jnp.concatenate(got, axis=1))
        slabs = []
        for hh in range(2):
            pair = []
            for t in range(2):
                c = 2 * i + t
                at = (hh * 3 + lax.rem(c, 3)) * model
                pair.append(ws[lax.div(c, 3), pl.ds(pl.multiple_of(at, model), model), :])
            slabs.append(jnp.concatenate(pair, axis=1))
        u0 = dot(norm_o[...], slabs[0], NN)
        u1 = dot(norm_o[...], slabs[1], NN)
        for r in range(0, every, chunk):
            a, d = gelu_parts(u0[r : r + chunk] + rows_of[0])
            act0[r : r + chunk, lanes] = a
            act0_o[r : r + chunk, lanes] = a.astype(BF)
            dact0_o[r : r + chunk, lanes] = d.astype(BF)
        for r in range(0, every, chunk):
            a, d = gelu_parts(u1[r : r + chunk] + rows_of[1])
            act1[r : r + chunk, lanes] = a
            dact1_o[r : r + chunk, lanes] = d.astype(BF)
            sums[r : r + chunk, :] += a[:, :LANES] + a[:, LANES:]
        return carry

    lax.fori_loop(0, hidden // width, up, 0)
    for r in range(0, every, chunk):
        center = jnp.sum(sums[r : r + chunk, :], axis=1, keepdims=True) * (1.0 / hidden)
        d = act1[r : r + chunk, :] - center
        spread = jnp.sum(d * d, axis=1, keepdims=True) * (1.0 / hidden)
        gmean[r : r + chunk, :] = jnp.broadcast_to(center, (chunk, LANES))
        ginv[r : r + chunk, :] = jnp.broadcast_to(lax.rsqrt(spread + EPS), (chunk, LANES))
    stores = [
        pltpu.make_async_copy(a, b, osem.at[i])
        for i, (a, b) in enumerate(
            ((act0_o, act0_h), (dact0_o, dact0_h), (dact1_o, dact1_h), (norm_o, norm_h), (ginv.at[pl.ds(0, rows)], ginv_h))
        )
    ]
    for c in stores:
        c.start()

    def column_stores(c):
        lanes = pl.ds(pl.multiple_of(c * LANES, LANES), LANES)
        pairs = ((ghat_o, ghat_h), (conv_o, conv_h), (gated_o, gated_h))
        return [
            pltpu.make_async_copy(a.at[:, lanes], b.at[:, lanes], osem.at[5 + 3 * c + i]) for i, (a, b) in enumerate(pairs)
        ]


    row = lax.broadcasted_iota(jnp.int32, (rows, LANES), 0)
    valid = jnp.where(frame_of(row, half, rows) < length, 1.0, 0.0)
    hrow = lax.broadcasted_iota(jnp.int32, (HALO, LANES), 0)
    valid_halo = jnp.where(jnp.where(half == 0, rows, rows - HALO) + hrow < length, 1.0, 0.0)
    count = rows // SEGS

    def gate(c, carry):
        lanes = pl.ds(pl.multiple_of(c * LANES, LANES), LANES)
        mj = scal[8 + c]
        base = lax.rem(c, 3) * BLOCK_ROWS
        ggain = sp[0, mj, pl.ds(base + ROW_GAIN, 1), :]
        gb0 = sp[0, mj, pl.ds(base + ROW_GB0, 1), :]
        gb1 = sp[0, mj, pl.ds(base + ROW_GB1, 1), :]
        hat = (act1[rows:every, lanes] - gmean[rows:every, :]) * ginv[rows:every, :]
        ghat_o[rows:every, lanes] = hat.astype(BF)
        halo[...] = (hat * ggain + gb0) * valid_halo
        hat = (act1[0:rows, lanes] - gmean[0:rows, :]) * ginv[0:rows, :]
        ghat_o[0:rows, lanes] = hat.astype(BF)
        normed = (hat * ggain + gb0) * valid
        halo_pads(pad, normed.reshape(count, SEGS, LANES), halo, half, True)
        fill_filters(filt, lambda k: sp[0, mj, pl.ds(base + k, 1), :])
        fast_fir(pad, filt, fir, keep)
        for t in range(0, count, 8):
            at = t * SEGS
            cv = fir[t : t + 8].reshape(64, LANES) + gb1
            conv_o[at : at + 64, lanes] = cv.astype(BF)
            gated_o[at : at + 64, lanes] = (act0[at : at + 64, lanes] * cv).astype(BF)
        for store in column_stores(c):
            store.start()
        return carry

    lax.fori_loop(0, hidden // LANES, gate, 0)
    for c in range(hidden // LANES):
        stores.extend(column_stores(c))
    for c in stores:
        c.wait()


def merge_forward_kernel(layer, scal, sp, h_own, mix, gated, *refs):
    u_sets, v_sets, refs = refs[:10], refs[10:18], refs[18:]
    o_o, nat_o, rhat_h, rstd_h, diff_h, ws, wv, rhat_o, rstd_o, diff_o, usem, vsem, osem = refs
    sp = sp.at[pl.ds(layer, 1)]
    rows, model = h_own.shape
    shard = wv.shape[1] // 4
    here, there = slab_copies(u_sets, ws, 0, W_UP)
    fetch(scal[3] == layer, here, there, usem)
    here_v, there_v = shard_copies(v_sets, wv)
    fetch(scal[3] == layer, here_v, there_v, vsem)
    landed(here, usem)
    landed(here_v, vsem)
    step = 64

    def stores(r, n):
        part = pl.ds(r, n)
        pairs = ((rhat_o, rhat_h), (rstd_o, rstd_h), (diff_o, diff_h))
        return [
            pltpu.make_async_copy(a.at[part], b.at[part], osem.at[r // n, i]) for i, (a, b) in enumerate(pairs)
        ]

    w0, w1 = branch_weights(sp)
    gain, bias = wide(sp, ROW_NG + 8), wide(sp, ROW_NB + 8)
    b0, b1 = wide(sp, ROW_OB), wide(sp, ROW_OB + 4)
    block = 256
    for r in range(0, rows, block):
        mixed = jnp.concatenate([mix[j, r : r + block, :] for j in range(4)], axis=1)
        brs, atts = [], []
        for lb in range(0, 4, 2):
            w = [
                jnp.concatenate(
                    [wv[j, (lb + t) * shard : (lb + t + 1) * shard, :] for j in range(4)], axis=0
                )
                for t in range(2)
            ]
            brs.append(dot(gated[r : r + block, :], jnp.concatenate(w, axis=1), NN))
            w = [
                jnp.concatenate(
                    [ws[j, (lb + t) * LANES : (lb + t + 1) * LANES, :] for j in range(4)], axis=0
                )
                for t in range(2)
            ]
            atts.append(dot(mixed, jnp.concatenate(w, axis=1), NN))
        br = jnp.concatenate(brs, axis=1)
        att = jnp.concatenate(atts, axis=1)
        for q in range(0, block, step):
            at = att[q : q + step] + b0
            bt = br[q : q + step] + b1
            res = h_own[r + q : r + q + step, :].astype(F32) + w0 * at + w1 * bt
            hat, inverse = normalized(res)
            diff_o[r + q : r + q + step, :] = at - bt
            rhat_o[r + q : r + q + step, :] = hat
            rstd_o[r + q : r + q + step, :] = jnp.broadcast_to(inverse, (step, LANES))
            o_o[r + q : r + q + step, :] = (hat * gain + bias).astype(BF)
        for c in stores(r, block):
            c.start()
    nat_o[...] = dot(order_matrix(rows, True), o_o[...], NN).astype(BF)
    for r in range(0, rows, block):
        for c in stores(r, block):
            c.wait()


def binary_weights(down):
    lane = lax.broadcasted_iota(jnp.int32, (1, LANES), 1)
    out = jnp.full((1, LANES), 2.0 ** (63 if down else -63), F32)
    for b in range(7):
        out = jnp.where(((lane >> b) & 1) == 1, out * 2.0 ** (-(2**b) if down else 2**b), out)
    return out


def merge_backward_kernel(
    layer, scal, sp, g, rhat_h, rstd_h, diff_h, mix_h, gated_h,
    gres_o, gatt_o, gbr_o, halo_o, keep_o, send_o, rhat, rstd, diff, mix, gated, small, sems,
):
    sp = sp.at[pl.ds(layer, 1)]
    rows, model = g.shape
    half = scal[1]
    loads = [
        pltpu.make_async_copy(a, b, sems.at[i])
        for i, (a, b) in enumerate(
            ((rstd_h, rstd), (rhat_h, rhat), (diff_h, diff), (mix_h, mix), (gated_h, gated))
        )
    ]
    for c in loads:
        c.start()
    gain = wide(sp, ROW_NG + 8)
    w0, w1 = branch_weights(sp)
    for c in loads[:3]:
        c.wait()
    step = 64
    dgain = dbias = slope = jnp.zeros((1, model), F32)
    db = jnp.zeros((1, model), F32)
    for r in range(0, rows, step):
        gg = g[r : r + step, :].astype(F32)
        hat = rhat[r : r + step, :]
        dgain = dgain + jnp.sum(gg * hat, axis=0, keepdims=True)
        dbias = dbias + jnp.sum(gg, axis=0, keepdims=True)
        gg = gg * gain
        gr = rstd[r : r + step, 0:1] * (
            gg - jnp.mean(gg, axis=1, keepdims=True) - hat * jnp.mean(gg * hat, axis=1, keepdims=True)
        )
        gres_o[r : r + step, :] = gr
        gatt_o[r : r + step, :] = (w0 * gr).astype(BF)
        gbr_o[r : r + step, :] = (w1 * gr).astype(BF)
        db = db + jnp.sum(gr, axis=0, keepdims=True)
        slope = slope + jnp.sum(gr * diff[r : r + step, :], axis=0, keepdims=True)
    i = lax.broadcasted_iota(jnp.int32, (HALO, rows), 0)
    r = lax.broadcasted_iota(jnp.int32, (HALO, rows), 1)
    wanted = jnp.where(half == 0, (i + rows // SEGS - HALO) * SEGS + SEGS - 1, i * SEGS)
    pick = jnp.where(r == wanted, 1.0, 0.0).astype(BF)
    halo_o[...] = dot(pick, gbr_o[...], NN).astype(BF)
    slope = jnp.sum(slope, axis=1, keepdims=True)
    small[...] = jnp.zeros_like(small)
    for n, v in enumerate((dgain, dbias, w0 * db, w1 * db)):
        for i in range(4):
            small[4 * n + i : 4 * n + i + 1, :] = v[:, i * LANES : (i + 1) * LANES]
    scaled = jnp.abs(slope) * binary_weights(False)
    digits = jnp.floor(scaled) - 2.0 * jnp.floor(0.5 * scaled)
    small[16:17, :] = jnp.where(slope < 0, -digits, digits)
    shards = (keep_o.at[0], send_o.at[0], keep_o.at[1], send_o.at[1])
    shard = gated.shape[1] // 4
    for c in loads[3:]:
        c.wait()
    for j in range(4):
        shards[j][D_SMALL:D_ROWS, :] = small[...].astype(BF)
    for j in range(4):
        w = dot(mix[j], gatt_o[...], TN).astype(BF)
        for i in range(4):
            shards[j][i * LANES : (i + 1) * LANES, :] = w[:, i * LANES : (i + 1) * LANES]
        w = dot(gated[:, j * shard : (j + 1) * shard], gbr_o[...], TN).astype(BF)
        for i in range(4):
            at = OUT_ROWS + i * shard
            shards[j][at : at + shard, :] = w[:, i * LANES : (i + 1) * LANES]


def attention_backward_kernel(layer, scal, gatt, q_h, k_h, v_h, mix_h, lse_h, *refs):
    sets, refs = refs[:10], refs[10:]
    cos_t, sin_t, dq_o, own_o, oth_o, w_s, cs, sn, pbuf, dsbuf, dom, qm2, q_r, k_r, v_r, mix, lse, wsem, tsem = refs
    rows = gatt.shape[0]
    total = 2 * rows
    half, length = scal[1], scal[2]
    here, there = slab_copies(sets, w_s, 0, W_UP)
    fetch(scal[3] == layer, here, there, wsem)
    tables = [
        pltpu.make_async_copy(cos_t.at[half, pl.ds(0, rows), :], cs, tsem.at[0]),
        pltpu.make_async_copy(sin_t.at[half, pl.ds(0, rows), :], sn, tsem.at[1]),
    ]
    for i, (a, b) in enumerate(((q_h, q_r), (k_h, k_r), (v_h, v_r), (mix_h, mix), (lse_h, lse))):
        tables.append(pltpu.make_async_copy(a, b, tsem.at[2 + i]))
    for c in tables:
        c.start()
    row = lax.broadcasted_iota(jnp.int32, (total, LANES), 0)
    part = jnp.where(row < rows, half, 1 - half)
    position = frame_of(row & (rows - 1), part, rows)
    mask = jnp.where(position < length, 0.0, NEG)
    lane_k = lax.broadcasted_iota(jnp.int32, (total, LANES), 1)
    lane_q = lax.broadcasted_iota(jnp.int32, (rows, LANES), 1)
    for c in tables:
        c.wait()
    landed(here, wsem)

    def shard(j):
        wo = jnp.concatenate([w_s[j, lb * LANES : (lb + 1) * LANES, :] for lb in range(4)], axis=1)
        dm = dot(gatt[...], wo, NT).astype(BF).astype(F32)
        prod = dm * mix[j].astype(F32)
        q = q_r[j].astype(F32)
        k = k_r[j].astype(F32)
        v = v_r[j].astype(F32)
        kt = k.T.astype(BF)
        dqs = []
        for hd in range(2):
            spare = (1 - hd) * HEAD
            in_q, in_k = (lane_q >> 6) == hd, (lane_k >> 6) == hd
            minus_lse = -jnp.sum(jnp.where(lane_q == 2 * j + hd, lse[...], 0.0), axis=1, keepdims=True)
            minus_delta = -jnp.sum(jnp.where(in_q, prod, 0.0), axis=1, keepdims=True)
            l0, l1, l2 = pieces(minus_lse)
            e0, e1, e2 = pieces(minus_delta)
            qx = jnp.where(lane_q == spare, 1.0, 0.0)
            dx = jnp.zeros_like(qx)
            for n, (lp, ep) in enumerate(((l0, e0), (l1, e1), (l2, e2))):
                here = lane_q == spare + 1 + n
                qx = jnp.where(here, lp, qx)
                dx = jnp.where(here, ep, dx)
            one = jnp.where((lane_k > spare) & (lane_k < spare + 4), 1.0, 0.0)
            qh = jnp.where(in_q, q, qx).astype(BF)
            dh = jnp.where(in_q, dm, dx).astype(BF)
            kh = jnp.where(in_k, k, jnp.where(lane_k == spare, mask, one)).astype(BF)
            vh = jnp.where(in_k, v, one).astype(BF)
            dom[hd * rows : (hd + 1) * rows, :] = jnp.where(in_q, dm, 0.0).astype(BF)
            qm2[hd * rows : (hd + 1) * rows, :] = jnp.where(in_q, q, 0.0).astype(BF)
            p = jnp.exp(dot(kh, qh, NT))
            dp = dot(vh, dh, NT)
            ds = (p * dp).astype(BF)
            pbuf[:, hd * rows : (hd + 1) * rows] = p.astype(BF)
            dsbuf[:, hd * rows : (hd + 1) * rows] = ds
            dqs.append(dot(kt[hd * HEAD : (hd + 1) * HEAD, :], ds, NN))
        dq = jnp.concatenate(dqs, axis=0).T * (1.0 / math.sqrt(HEAD))
        dq_o[j] = rotate_back(dq, cs[...], sn[...]).astype(BF)
        dk = dot(dsbuf[...], qm2[...], NN)
        dv = dot(pbuf[...], dom[...], NN)
        own_o[j, :, 0:LANES] = dk[:rows]
        own_o[j, :, LANES:] = dv[:rows]
        oth_o[j, :, 0:LANES] = dk[rows:].astype(BF)
        oth_o[j, :, LANES:] = dv[rows:].astype(BF)

    for j in range(4):
        shard(j)


def conv_backward_kernel(layer, scal, sp, gbr, ghalo, act0_h, dact0_h, ghat_h, conv_h, *refs):
    v_sets, refs = refs[:8], refs[8:]
    (dup_o, hgrad, hs, xs, small, wv, act0, dact0, ghat, conv, gpad, xpad, filt, fir, keep, halo, gcv, gbuf, vsem, asem) = refs
    sp = sp.at[pl.ds(layer, 1)]
    rows, model = gbr.shape
    every = rows + HALO
    hidden = gcv.shape[1]
    shard = hidden // 4
    half, length = scal[1], scal[2]
    here_v, there_v = shard_copies(v_sets, wv)
    fetch(scal[3] == layer, here_v, there_v, vsem)
    loads = [
        pltpu.make_async_copy(a, b, asem.at[i])
        for i, (a, b) in enumerate(((act0_h, act0), (conv_h, conv), (dact0_h, dact0), (ghat_h, ghat)))
    ]
    for c in loads:
        c.start()
    gbuf[0:rows, :] = gbr[...]
    gbuf[rows:every, :] = ghalo[...]
    hs[...] = jnp.zeros_like(hs)
    xs[...] = jnp.zeros_like(xs)
    small[...] = jnp.zeros_like(small)
    landed(here_v, vsem)
    for c in loads[:3]:
        c.wait()
    count = rows // SEGS
    width = 256
    chunk = 48

    def down(i, carry):
        lanes = pl.ds(pl.multiple_of(i * width, width), width)
        pair = []
        for t in range(2):
            c = 2 * i + t
            base = lax.rem(c, 3) * LANES
            pair.append(
                jnp.concatenate(
                    [
                        wv[lax.div(c, 3), pl.ds(pl.multiple_of(base + lb * shard, LANES), LANES), :]
                        for lb in range(4)
                    ],
                    axis=1,
                )
            )
        g = dot(gbuf[...], jnp.concatenate(pair, axis=0), NT)
        for r in range(0, every, chunk):
            gr = g[r : r + chunk].astype(BF).astype(F32)
            gcv[r : r + chunk, lanes] = gr * act0[r : r + chunk, lanes].astype(F32)
        for r in range(0, rows, 64):
            gr = g[r : r + 64].astype(BF).astype(F32)
            keep = gr * conv[r : r + 64, lanes].astype(F32) * dact0[r : r + 64, lanes].astype(F32)
            dup_o[r : r + 64, lanes] = keep.astype(BF)
        return carry

    lax.fori_loop(0, hidden // width, down, 0)
    loads[3].wait()
    row = lax.broadcasted_iota(jnp.int32, (rows, LANES), 0)
    valid = jnp.where(frame_of(row, half, rows) < length, 1.0, 0.0)
    hrow = lax.broadcasted_iota(jnp.int32, (HALO, LANES), 0)
    valid_halo = jnp.where(jnp.where(half == 0, rows, rows - HALO) + hrow < length, 1.0, 0.0)

    def fold(x):
        return jnp.sum(x, axis=0, keepdims=True)

    def conv_back(c, carry):
        lanes = pl.ds(pl.multiple_of(c * LANES, LANES), LANES)
        mj = scal[8 + c]
        b = lax.rem(c, 3)
        j = lax.div(c, 3)
        base = b * BLOCK_ROWS
        ggain = sp[0, mj, pl.ds(base + ROW_GAIN, 1), :]
        gb0 = sp[0, mj, pl.ds(base + ROW_GB0, 1), :]
        halo[...] = (ghat[rows:every, lanes].astype(F32) * ggain + gb0) * valid_halo
        normed = (ghat[0:rows, lanes].astype(F32) * ggain + gb0) * valid
        halo_pads(xpad, normed.reshape(count, SEGS, LANES), halo, half, True)
        halo[...] = gcv[rows:every, lanes]
        gown = gcv[0:rows, lanes]
        halo_pads(gpad, gown.reshape(count, SEGS, LANES), halo, half, True)
        small[j, pl.ds(base + ROW_GB1, 1), :] = fold(gown)
        for k, t in enumerate(tap_sums(gpad, xpad, count)):
            small[j, pl.ds(base + k, 1), :] = fold(t)
        fill_filters(filt, lambda k: sp[0, mj, pl.ds(base + TAPS - 1 - k, 1), :])
        fast_fir(gpad, filt, fir, keep)
        dgain = jnp.zeros((SEGS, LANES), F32)
        dbias = jnp.zeros((SEGS, LANES), F32)
        for t in range(0, count, 8):
            at = t * SEGS
            gn = fir[t : t + 8].reshape(64, LANES) * valid[at : at + 64]
            hat = ghat[at : at + 64, lanes].astype(F32)
            dgain = dgain + jnp.sum((gn * hat).reshape(8, SEGS, LANES), axis=0)
            dbias = dbias + jnp.sum(gn.reshape(8, SEGS, LANES), axis=0)
            gn = gn * ggain
            hgrad[at : at + 64, lanes] = gn
            hs[at : at + 64, :] += gn
            xs[at : at + 64, :] += gn * hat
        small[j, pl.ds(base + ROW_GAIN, 1), :] = fold(dgain)
        small[j, pl.ds(base + ROW_GB0, 1), :] = fold(dbias)
        return carry

    lax.fori_loop(0, hidden // LANES, conv_back, 0)
    for r in range(0, rows, 64):
        a = jnp.sum(hs[r : r + 64, :], axis=1, keepdims=True) * (1.0 / hidden)
        x = jnp.sum(xs[r : r + 64, :], axis=1, keepdims=True) * (1.0 / hidden)
        hs[r : r + 64, :] = jnp.broadcast_to(a, (64, LANES))
        xs[r : r + 64, :] = jnp.broadcast_to(x, (64, LANES))


def up_backward_kernel(layer, scal, dup0, hgrad, hs, xs, small_i, ghat_h, dact1_h, ginv_h, norm_h, *refs):
    sets, refs = refs[:10], refs[10:]
    dn_o, keep_o, send_o, ws, ghat, dact1, ginv, norm, dup1, small, wsem, asem = refs
    rows, hidden = hgrad.shape
    model = norm.shape[1]
    width = 256
    here, there = slab_copies(sets, ws, W_UP, W_ROWS)
    fetch(scal[3] == layer, here, there, wsem)
    own = pl.ds(0, rows)
    loads = [
        pltpu.make_async_copy(a, b, asem.at[i])
        for i, (a, b) in enumerate(
            ((ghat_h.at[own, :], ghat), (dact1_h.at[own, :], dact1), (ginv_h, ginv), (norm_h, norm))
        )
    ]
    for c in loads:
        c.start()
    small[...] = small_i[...]

    def fold(x):
        return jnp.sum(x, axis=0, keepdims=True)

    for c in loads[:3]:
        c.wait()

    def gate_back(c, carry):
        lanes = pl.ds(pl.multiple_of(c * LANES, LANES), LANES)
        b = lax.rem(c, 3)
        j = lax.div(c, 3)
        base = b * BLOCK_ROWS
        s0 = jnp.zeros((1, LANES), F32)
        s1 = jnp.zeros((1, LANES), F32)
        for r in range(0, rows, 64):
            hat = ghat[r : r + 64, lanes].astype(F32)
            gi = ginv[r : r + 64, :] * (hgrad[r : r + 64, lanes] - hs[r : r + 64, :] - hat * xs[r : r + 64, :])
            d1 = (gi * dact1[r : r + 64, lanes].astype(F32)).astype(BF)
            dup1[r : r + 64, lanes] = d1
            s1 = s1 + fold(d1.astype(F32))
            s0 = s0 + fold(dup0[r : r + 64, lanes].astype(F32))
        small[j, pl.ds(base + ROW_UP0, 1), :] = s0
        small[j, pl.ds(base + ROW_UP1, 1), :] = s1
        return carry

    lax.fori_loop(0, hidden // LANES, gate_back, 0)
    landed(here, wsem)
    loads[3].wait()
    dups = (dup0, dup1)
    for hh in range(2):
        w = jnp.concatenate(
            [ws[j, (hh * 3 + b) * model : (hh * 3 + b + 1) * model, :] for j in range(4) for b in range(3)], axis=1
        )
        if hh == 0:
            dn_o[...] = dot(dups[hh][...], w, NT)
        else:
            dn_o[...] += dot(dups[hh][...], w, NT)
    shards = (keep_o.at[0], send_o.at[0], keep_o.at[1], send_o.at[1])
    own_norm = norm[0:rows, :]
    for i in range(hidden // width):
        lo = i * width
        for hh in range(2):
            w = dot(own_norm, dups[hh][:, lo : lo + width], TN).astype(BF)
            for t in range(2):
                j, b = divmod(2 * i + t, 3)
                at = (hh * 3 + b) * model
                shards[j][at : at + model, :] = w[:, t * LANES : (t + 1) * LANES]
    for j in range(4):
        shards[j][UP_ROWS:M_ROWS, :] = small[j].astype(BF)


def input_backward_kernel(layer, scal, sp, h_h, gres_h, dn_mlp, dq, dkv_own, dkv_got, *refs):
    sets, refs = refs[:8], refs[8:]
    cos_t, sin_t, g_o, nat_o, keep_o, send_o, wq, cs, sn, dall, norm, xhat, xinv, small, h_own, gres, wsem, tsem = refs
    sp = sp.at[pl.ds(layer, 1)]
    rows, model = h_own.shape
    half = scal[1]
    here, there = shard_copies(sets, wq)
    fetch(scal[3] == layer, here, there, wsem)
    shards = (keep_o.at[0], send_o.at[0], keep_o.at[1], send_o.at[1])
    tables = [
        pltpu.make_async_copy(cos_t.at[half, pl.ds(0, rows), :], cs, tsem.at[0]),
        pltpu.make_async_copy(sin_t.at[half, pl.ds(0, rows), :], sn, tsem.at[1]),
    ]
    tables.append(pltpu.make_async_copy(gres_h, gres, tsem.at[2]))
    first = pltpu.make_async_copy(h_h, h_own, tsem.at[3])
    first.start()
    for c in tables:
        c.start()
    first.wait()
    gain, bias = wide(sp, ROW_NG), wide(sp, ROW_NB)
    gain_mlp = wide(sp, ROW_NG + 4)
    step = 64
    for r in range(0, rows, step):
        hat, inverse = normalized(h_own[r : r + step, :].astype(F32))
        xhat[r : r + step, :] = hat
        xinv[r : r + step, :] = jnp.broadcast_to(inverse, (step, LANES))
        norm[r : r + step, :] = (hat * gain + bias).astype(BF)
    for c in tables:
        c.wait()
    for j in range(4):
        at = j * 3 * LANES
        dall[:, at : at + LANES] = dq[j]
        dk = dkv_own[j, :, 0:LANES] + dkv_got[j ^ 1, :, 0:LANES].astype(F32)
        dall[:, at + LANES : at + 2 * LANES] = rotate_back(dk, cs[...], sn[...]).astype(BF)
        dv = dkv_own[j, :, LANES:] + dkv_got[j ^ 1, :, LANES:].astype(F32)
        dall[:, at + 2 * LANES : at + 3 * LANES] = dv.astype(BF)
    landed(here, wsem)
    small[...] = jnp.zeros_like(small)
    dn = dot(dall[...], jnp.concatenate([wq[j, i] for j in range(4) for i in range(3)], axis=1), NT)
    dg0 = db0 = dg1 = db1 = jnp.zeros((1, model), F32)
    for r in range(0, rows, step):
        hat = xhat[r : r + step, :]
        a = dn[r : r + step]
        m = dn_mlp[r : r + step, :]
        dg0 = dg0 + jnp.sum(a * hat, axis=0, keepdims=True)
        db0 = db0 + jnp.sum(a, axis=0, keepdims=True)
        dg1 = dg1 + jnp.sum(m * hat, axis=0, keepdims=True)
        db1 = db1 + jnp.sum(m, axis=0, keepdims=True)
        gg = a * gain + m * gain_mlp
        dx = xinv[r : r + step, 0:1] * (
            gg - jnp.mean(gg, axis=1, keepdims=True) - hat * jnp.mean(gg * hat, axis=1, keepdims=True)
        )
        g_o[r : r + step, :] = (gres[r : r + step, :] + dx).astype(BF)
    nat_o[...] = dot(order_matrix(rows, True), g_o[...], NN).astype(BF)
    for j in range(4):
        for n, v in enumerate((dg0, dg1, db0, db1)):
            for i in range(4):
                small[j, 8 + 4 * n + i : 9 + 4 * n + i, :] = v[:, i * LANES : (i + 1) * LANES]
    for j in range(4):
        at = j * 3 * LANES
        d = dall[:, at : at + 3 * LANES]
        w = dot(norm[...], d, TN).astype(BF)
        s = jnp.sum(d.astype(F32), axis=0, keepdims=True)
        for i in range(3):
            lo = i * model
            shards[j][lo : lo + model, :] = w[:, i * LANES : (i + 1) * LANES]
            small[j, i : i + 1, :] = s[:, i * LANES : (i + 1) * LANES]
        shards[j][QKV_ROWS:A_ROWS, :] = small[j].astype(BF)


def assemble_kernel(scal, here, there, out):
    rows = here.shape[1]
    for n in range(8):
        place, half = scal[24 + n], scal[32 + n]
        part = there if n & 1 else here
        out[place, pl.ds(pl.multiple_of(half * rows, rows), rows), :] = part[n >> 1]


def finale_kernel(
    dm_lo, d_hi, m_hi, a, logits,
    qkv_o, out_o, up_o, down_o, bqkv_o, bup_o, gain_o, gbias_o, conv_o, ng_o, nb_o, ob_o, logit_o,
):
    cut = D_ROWS // 2

    def rows_of(lo, hi, at, n, a, b):
        if b <= n:
            return lo[at + a : at + b, :].astype(F32)
        if a >= n:
            return hi[a - n : b - n, :].astype(F32)
        return jnp.concatenate([lo[at + a : at + n, :], hi[0 : b - n, :]], axis=0).astype(F32)

    d_of = functools.partial(rows_of, dm_lo, d_hi, 0, cut)
    m_of = functools.partial(rows_of, dm_lo, m_hi, cut, M_ROWS // 2)
    def a_of(lo, hi):
        return a[lo:hi, :].astype(F32)

    model, shard = up_o.shape[1], up_o.shape[2]
    for i in range(3):
        qkv_o[i] = a_of(i * model, (i + 1) * model)
    for lb in range(4):
        lanes = slice(lb * LANES, (lb + 1) * LANES)
        out_o[:, lanes] = d_of(lb * LANES, (lb + 1) * LANES)
        down_o[:, lanes] = d_of(OUT_ROWS + lb * shard, OUT_ROWS + (lb + 1) * shard)
    for hh in range(2):
        for b in range(3):
            at = (hh * 3 + b) * model
            up_o[hh, :, b * LANES : (b + 1) * LANES] = m_of(at, at + model)
    small = m_of(UP_ROWS, M_ROWS)
    for b in range(3):
        lanes = slice(b * LANES, (b + 1) * LANES)
        at = b * BLOCK_ROWS
        for k in range(TAPS):
            conv_o[k, :, lanes] = small[at + k : at + k + 1]
        bup_o[:, lanes] = small[at + ROW_UP0 : at + ROW_UP0 + 2]
        gain_o[:, lanes] = small[at + ROW_GAIN : at + ROW_GAIN + 1]
        gbias_o[:, lanes] = small[at + ROW_GB0 : at + ROW_GB0 + 2]
    small = a_of(QKV_ROWS, A_ROWS)
    for n in range(3):
        bqkv_o[n] = small[n : n + 1]
    for n in range(2):
        for i in range(4):
            lanes = slice(i * LANES, (i + 1) * LANES)
            ng_o[n, :, lanes] = small[8 + 4 * n + i : 9 + 4 * n + i]
            nb_o[n, :, lanes] = small[16 + 4 * n + i : 17 + 4 * n + i]
    small = d_of(D_SMALL, D_ROWS)
    for i in range(4):
        lanes = slice(i * LANES, (i + 1) * LANES)
        ng_o[2, :, lanes] = small[i : i + 1]
        nb_o[2, :, lanes] = small[4 + i : 5 + i]
        ob_o[0:1, lanes] = small[8 + i : 9 + i]
        ob_o[1:2, lanes] = small[12 + i : 13 + i]
    total_slope = jnp.sum(small[16:17] * binary_weights(True), axis=1, keepdims=True)
    l0, l1 = jnp.full((1, LANES), logits[0], F32), jnp.full((1, LANES), logits[1], F32)
    top = jnp.maximum(l0, l1)
    e0, e1 = jnp.exp(l0 - top), jnp.exp(l1 - top)
    slope = e0 * e1 / ((e0 + e1) * (e0 + e1)) * total_slope
    logit_o[0:1, :] = slope
    logit_o[1:2, :] = -slope


def exchange(x, axis, bit):
    n = lax.axis_size(axis)
    return lax.ppermute(x, axis, [(i, i ^ bit) for i in range(n)])


def fence(*xs):
    return lax.optimization_barrier(xs)


def total(*xs):
    out = xs[0].astype(F32)
    for x in xs[1:]:
        out = out + x.astype(F32)
    return out


def scatter_over_dp(x):
    n = lax.axis_size("dp")
    if n != 4:
        return (lax.psum(x.astype(F32), "dp").astype(BF),)
    d = lax.axis_index("dp")
    x = x.reshape(n, x.shape[0] // n, LANES)
    own = lax.dynamic_index_in_dim(x, d, 0, keepdims=False)
    return (own, *[exchange(lax.dynamic_index_in_dim(x, d ^ k, 0, keepdims=False), "dp", k) for k in range(1, n)])


def gather_over_dp(x):
    n = lax.axis_size("dp")
    return (x, *[exchange(x, "dp", k) for k in range(1, n)]) if n == 4 else (x,)


def in_order(parts):
    if len(parts) == 1:
        return parts[0]
    d = lax.axis_index("dp")
    low, high = (d & 1) == 0, (d & 2) == 0
    pairs = [
        (jnp.where(low, parts[k], parts[k + 1]), jnp.where(low, parts[k + 1], parts[k])) for k in (0, 2)
    ]
    return jnp.concatenate([jnp.where(high, pairs[i][t], pairs[1 - i][t]) for i in range(2) for t in range(2)], axis=0)


def halves(x, owner):
    rows = x.shape[0] // 2
    return jnp.where(owner, x[:rows], x[rows:]), jnp.where(owner, x[rows:], x[:rows])


def rotary_constants(length):
    half_width = HEAD // 2
    freq = np.exp(np.arange(half_width, dtype=np.float32) * np.float32(-math.log(10000.0) / half_width))
    rows = length // 2
    r = np.arange(rows)
    place = (r % SEGS) * (rows // SEGS) + r // SEGS
    cosines, sines = [], []
    for half in range(2):
        t = np.concatenate([half * rows + place, (1 - half) * rows + place]).astype(np.float32)
        angle = (t[:, None] * freq.astype(np.float32)[None, :]).astype(np.float32)
        c, s = np.cos(angle.astype(np.float64)), np.sin(angle.astype(np.float64))
        cosines.append(np.concatenate([c, c, c, c], axis=1))
        sines.append(np.concatenate([-s, s, -s, s], axis=1))
    return np.stack(cosines).astype(np.float32), np.stack(sines).astype(np.float32)


def per_device(frames, lengths, out_grad, *weights):
    (norm_gains, norm_biases, wqkv, bqkv, wout, wup, bup, ggain, gbias, cw, wdown, obias, logits) = [
        w[0] for w in weights
    ]
    micro, utterances, length, model = frames.shape
    n_sec, n_mp = lax.axis_size("section"), lax.axis_size("mp")
    assert utterances == 1 and n_sec == 2 and n_mp == 4 and micro == 4
    rows = length // 2
    shard = wdown.shape[0]
    hidden = shard * n_mp
    every = rows + HALO
    s, m = lax.axis_index("section"), lax.axis_index("mp")
    u = s * 2 + (m >> 1)
    half = m & 1
    own_length = lax.dynamic_index_in_dim(lengths[:, 0], u, 0, keepdims=False)
    ns = np.arange(40)
    xors = np.zeros(40, np.int32)
    xors[4:8] = np.arange(4)
    xors[8:20] = np.arange(12) // 3
    xors[24:32] = ns[:8] >> 1 & 1
    xors[32:40] = ns[:8] & 1
    sec_bits = np.zeros(40, np.int32)
    sec_bits[24:32] = ns[:8] >> 2
    idx = jnp.asarray(ns)
    by_shard = jnp.asarray(xors)
    by_place = (s ^ jnp.asarray(sec_bits)) * 2 + ((m >> 1) ^ jnp.asarray(xors))
    by_half = half ^ jnp.asarray(xors)
    scal = jnp.where(idx < 24, by_shard, jnp.where(idx < 32, by_place, by_half))
    for i, v in enumerate((u, half, own_length, s)):
        scal = jnp.where(idx == i, v, scal)
    scal = scal.astype(jnp.int32)

    x_of = lambda v: exchange(v, "section", 1)
    y_of = lambda v: exchange(v, "mp", 2)
    core_of = lambda v: exchange(v, "mp", 1)
    flat = shape((rows, model), BF)
    rows_f32 = shape((rows, model), F32)
    stat = shape((rows, LANES), F32)
    wide_bf = shape((rows, hidden), BF)
    halo_bf = shape((every, hidden), BF)

    def head_pack(n):
        return shape((4, n, LANES), BF)

    first = s == 0

    q_x, q_y, q_sib = x_of(wqkv), y_of(wqkv), core_of(wqkv)
    packed, u_own, v_own = call(
        pack_kernel,
        [wout, wup, wdown, cw, bup, ggain[None], gbias, bqkv, norm_gains, norm_biases, obias, logits],
        [ANY] * 3 + [VMEM] * 8 + [SMEM],
        [shape((PACK_ROWS, LANES), F32), shape((W_ROWS, LANES), BF), shape((DOWN_ROWS, LANES), BF)],
        [
            pltpu.VMEM(wout.shape, BF),
            pltpu.VMEM(wup.shape, BF),
            pltpu.VMEM(wdown.shape, BF),
            pltpu.SemaphoreType.DMA((3,)),
        ],
        0,
        12,
    )
    packed, q_x, q_y, scal, u_own, v_own = fence(packed, q_x, q_y, scal, u_own, v_own)
    packed_x = x_of(packed)
    q_d = x_of(q_y)
    packed_x, packed = fence(packed_x, packed)
    sections = jnp.stack([jnp.where(first, packed, packed_x), jnp.where(first, packed_x, packed)])
    sc, sections = fence(scal, sections)
    sections_y = y_of(sections)
    h_own, h_oth, g_last = call(
        prologue_kernel,
        [sc, frames, out_grad],
        [SMEM] + [ANY] * 2,
        [flat, flat, flat],
        [pltpu.VMEM((3, rows, model), BF), pltpu.SemaphoreType.DMA((3,))],
        0,
        12,
    )
    h_own, q_d, sections_y, u_own = fence(h_own, q_d, sections_y, u_own)
    u_x, u_y = x_of(u_own), y_of(u_own)
    q_xs, q_ys = core_of(q_x), core_of(q_y)
    sp_a = jnp.stack([sections, sections_y], axis=1)
    sp_b = core_of(sp_a)
    sp = jnp.stack([sp_a, sp_b], axis=2).reshape(2, n_mp, PACK_ROWS, LANES)
    q_ds = core_of(q_d)
    w_qkv = [wqkv, q_sib, q_y, q_ys, q_x, q_xs, q_d, q_ds]

    cos_np, sin_np = rotary_constants(length)
    cos_t, sin_t = jnp.asarray(cos_np), jnp.asarray(sin_np)

    def attention_forward(layer, scal, h_own, h_oth):
        return call(
            functools.partial(attention_forward_kernel, layer),
            [scal, sp, cos_t, sin_t, h_own, h_oth, *w_qkv],
            [SMEM, VMEM, ANY, ANY, VMEM, VMEM] + [ANY] * 8,
            [head_pack(rows), head_pack(length), head_pack(length), head_pack(rows), stat, head_pack(rows)],
            [
                pltpu.VMEM((4, 3, model, LANES), BF),
                pltpu.VMEM((length, LANES), F32),
                pltpu.VMEM((length, LANES), F32),
                pltpu.VMEM((length, model), BF),
                pltpu.VMEM((LANES, rows), F32),
                pltpu.VMEM((4, rows, LANES), BF),
                pltpu.VMEM((4, length, LANES), BF),
                pltpu.VMEM((4, length, LANES), BF),
                pltpu.VMEM((rows, LANES), F32),
                pltpu.SemaphoreType.DMA((4,)),
                pltpu.SemaphoreType.DMA((2,)),
                pltpu.SemaphoreType.DMA((5, 4)),
            ],
            10 * rows * length * model, 24, range(5))

    def mlp_forward(layer, scal, h_own, h_oth):
        return call(
            functools.partial(mlp_forward_kernel, layer),
            [scal, sp, h_own, h_oth, *w_u],
            [SMEM, VMEM, VMEM, VMEM] + [ANY] * 10,
            [halo_bf, halo_bf, halo_bf, halo_bf, wide_bf, wide_bf, stat, shape((every, model), BF), wide_bf],
            [
                pltpu.VMEM((4, W_ROWS - W_UP, LANES), BF),
                pltpu.VMEM((every, hidden), F32),
                pltpu.VMEM((every, hidden), F32),
                pltpu.VMEM((every, LANES), F32),
                pltpu.VMEM((every, LANES), F32),
                pltpu.VMEM((every, LANES), F32),
                pltpu.VMEM((rows // SEGS + 32, SEGS, LANES), F32),
                pltpu.VMEM((72, SEGS, LANES), F32),
                pltpu.VMEM((rows // SEGS, SEGS, LANES), F32),
                pltpu.VMEM((rows // SEGS // 2 + 1, SEGS, LANES), F32),
                pltpu.VMEM((HALO, LANES), F32),
                pltpu.VMEM((every, hidden), BF),
                pltpu.VMEM((every, hidden), BF),
                pltpu.VMEM((every, hidden), BF),
                pltpu.VMEM((every, hidden), BF),
                pltpu.VMEM((rows, hidden), BF),
                pltpu.VMEM((every, model), BF),
                pltpu.SemaphoreType.DMA((8,)),
                pltpu.SemaphoreType.DMA((5 + 3 * hidden // LANES,)),
            ],
            8 * rows * model * hidden, 34, range(8))

    def merge_forward(layer, scal, h_own, mix, gated):
        return call(
            functools.partial(merge_forward_kernel, layer),
            [scal, sp, h_own, mix, gated, *w_u, *w_v],
            [SMEM, VMEM, VMEM, VMEM, VMEM] + [ANY] * 18,
            [flat, flat, rows_f32, stat, rows_f32],
            [
                pltpu.VMEM((4, W_UP, LANES), BF),
                pltpu.VMEM((4, DOWN_ROWS, LANES), BF),
                pltpu.VMEM((rows, model), F32),
                pltpu.VMEM((rows, LANES), F32),
                pltpu.VMEM((rows, model), F32),
                pltpu.SemaphoreType.DMA((8,)),
                pltpu.SemaphoreType.DMA((4,)),
                pltpu.SemaphoreType.DMA((2, 3)),
            ],
            2 * rows * model * hidden, 18, (2, 3, 4))

    att = attention_forward(0, scal, h_own, h_oth)
    att, u_x, u_y, v_late = fence(att, u_x, u_y, v_own)
    cut = W_ROWS - SPLIT
    d1, both = y_of(u_x[:SPLIT]), x_of(jnp.concatenate([u_y[SPLIT:], v_late], axis=0))
    u_sib, u_xs, u_ys = core_of(u_own), core_of(u_x), core_of(u_y)
    d1, both, v_late = fence(d1, both, v_late)
    d1s, both_s = core_of(d1), core_of(both)
    d2, v_x, d2s, v_xs = both[:cut], both[cut:], both_s[:cut], both_s[cut:]
    v_y = y_of(v_late)
    v_d = y_of(v_x)
    v_sib = core_of(v_late)
    w_u = [u_own, u_sib, u_y, u_ys, u_x, u_xs, d1, d1s, d2, d2s]
    mlp0 = mlp_forward(0, scal, h_own, h_oth)
    mlp0, v_y, v_d, v_sib = fence(mlp0, v_y, v_d, v_sib)
    v_ys, v_ds = core_of(v_y), core_of(v_d)
    w_v = [v_own, v_sib, v_y, v_ys, v_x, v_xs, v_d, v_ds]
    top0 = merge_forward(0, scal, h_own, att[5], mlp0[8])
    saved = [(h_own, att, mlp0, top0)]
    h_own, h_oth = top0[0], core_of(top0[0])
    att = attention_forward(1, scal, h_own, h_oth)
    mlp1 = mlp_forward(1, scal, h_own, h_oth)
    top1 = merge_forward(1, scal, h_own, att[5], mlp1[8])
    saved.append((h_own, att, mlp1, top1))

    def merge_backward(layer, scal, g):
        h, att, mlp, top = saved[layer]
        return call(
            functools.partial(merge_backward_kernel, layer),
            [scal, sp, g, top[2], top[3], top[4], att[3], mlp[5]],
            [SMEM, VMEM, VMEM] + [ANY] * 5,
            [rows_f32, flat, flat, shape((HALO, model), BF),
             shape((2, D_ROWS, LANES), BF), shape((2, D_ROWS, LANES), BF)],
            [
                pltpu.VMEM((rows, model), F32),
                pltpu.VMEM((rows, LANES), F32),
                pltpu.VMEM((rows, model), F32),
                pltpu.VMEM((4, rows, LANES), BF),
                pltpu.VMEM((rows, hidden), BF),
                pltpu.VMEM((64, LANES), F32),
                pltpu.SemaphoreType.DMA((5,)),
            ],
            2 * rows * model * (hidden + model), 16, (), (0, 4, 5))

    def conv_backward(layer, scal, gbr, halo_in):
        mlp = saved[layer][2]
        return call(
            functools.partial(conv_backward_kernel, layer),
            [scal, sp, gbr, halo_in, mlp[0], mlp[1], mlp[3], mlp[4], *w_v],
            [SMEM, VMEM, VMEM, VMEM] + [ANY] * 12,
            [wide_bf, shape((rows, hidden), F32), stat, stat, shape((4, LANES, LANES), F32)],
            [
                pltpu.VMEM((4, DOWN_ROWS, LANES), BF),
                pltpu.VMEM((every, hidden), BF),
                pltpu.VMEM((every, hidden), BF),
                pltpu.VMEM((every, hidden), BF),
                pltpu.VMEM((rows, hidden), BF),
                pltpu.VMEM((rows // SEGS + 32, SEGS, LANES), F32),
                pltpu.VMEM((rows // SEGS + 32, SEGS, LANES), F32),
                pltpu.VMEM((72, SEGS, LANES), F32),
                pltpu.VMEM((rows // SEGS, SEGS, LANES), F32),
                pltpu.VMEM((rows // SEGS // 2 + 1, SEGS, LANES), F32),
                pltpu.VMEM((HALO, LANES), F32),
                pltpu.VMEM((every, hidden), F32),
                pltpu.VMEM((every, model), BF),
                pltpu.SemaphoreType.DMA((4,)),
                pltpu.SemaphoreType.DMA((4,)),
            ],
            0,
            30,
        )

    def up_backward(layer, scal, dup0, hgrad, hs, xs, small):
        mlp = saved[layer][2]
        return call(
            functools.partial(up_backward_kernel, layer),
            [scal, dup0, hgrad, hs, xs, small, mlp[3], mlp[2], mlp[6], mlp[7], *w_u],
            [SMEM] + [VMEM] * 5 + [ANY] * 14,
            [rows_f32, shape((2, M_ROWS, LANES), BF), shape((2, M_ROWS, LANES), BF)],
            [
                pltpu.VMEM((4, W_ROWS - W_UP, LANES), BF),
                pltpu.VMEM((rows, hidden), BF),
                pltpu.VMEM((rows, hidden), BF),
                pltpu.VMEM((rows, LANES), F32),
                pltpu.VMEM((every, model), BF),
                pltpu.VMEM((rows, hidden), BF),
                pltpu.VMEM((4, LANES, LANES), F32),
                pltpu.SemaphoreType.DMA((8,)),
                pltpu.SemaphoreType.DMA((4,)),
            ],
            0,
            30,
            (),
            (1, 2),
        )

    def attention_backward(layer, scal, gatt):
        att = saved[layer][1]
        return call(
            functools.partial(attention_backward_kernel, layer),
            [scal, gatt, *att[:5], *w_u, cos_t, sin_t],
            [SMEM, VMEM] + [ANY] * 17,
            [head_pack(rows), shape((4, rows, 2 * LANES), F32), shape((4, rows, 2 * LANES), BF)],
            [
                pltpu.VMEM((4, W_UP, LANES), BF),
                pltpu.VMEM((rows, LANES), F32),
                pltpu.VMEM((rows, LANES), F32),
                pltpu.VMEM((length, 2 * rows), BF),
                pltpu.VMEM((length, 2 * rows), BF),
                pltpu.VMEM((2 * rows, LANES), BF),
                pltpu.VMEM((2 * rows, LANES), BF),
                pltpu.VMEM((4, rows, LANES), BF),
                pltpu.VMEM((4, length, LANES), BF),
                pltpu.VMEM((4, length, LANES), BF),
                pltpu.VMEM((4, rows, LANES), BF),
                pltpu.VMEM((rows, LANES), F32),
                pltpu.SemaphoreType.DMA((4,)),
                pltpu.SemaphoreType.DMA((7,)),
            ],
            12 * rows * length * model, 26)

    def input_backward(layer, scal, gres, dn_mlp, dq, dkv_own, dkv_got):
        h = saved[layer][0]
        return call(
            functools.partial(input_backward_kernel, layer),
            [scal, sp, h, gres, dn_mlp, dq, dkv_own, dkv_got, *w_qkv, cos_t, sin_t],
            [SMEM, VMEM, ANY, ANY] + [VMEM] * 4 + [ANY] * 10,
            [flat, flat, shape((2, A_ROWS, LANES), BF), shape((2, A_ROWS, LANES), BF)],
            [
                pltpu.VMEM((4, 3, model, LANES), BF),
                pltpu.VMEM((rows, LANES), F32),
                pltpu.VMEM((rows, LANES), F32),
                pltpu.VMEM((rows, 12 * LANES), BF),
                pltpu.VMEM((rows, model), BF),
                pltpu.VMEM((rows, model), F32),
                pltpu.VMEM((rows, LANES), F32),
                pltpu.VMEM((4, 64, LANES), F32),
                pltpu.VMEM((rows, model), BF),
                pltpu.VMEM((rows, model), F32),
                pltpu.SemaphoreType.DMA((4,)),
                pltpu.SemaphoreType.DMA((4,)),
            ],
            14 * rows * model * model, 24, (), (2, 3))

    owner1 = jnp.logical_not(first)
    natural0, natural1 = top0[1], top1[1]
    out_keep = jnp.where(first, natural0, natural1)
    out_send = jnp.where(first, natural1, natural0)
    gres, gatt, gbr, halo_out, d_keep, d_send = merge_backward(1, scal, g_last)
    gbr, halo_out, d_send, out_send, out_keep = fence(gbr, halo_out, d_send, out_send, out_keep)
    halo_in = core_of(halo_out)
    sc, gbr, halo_in, out_send, out_keep, d_send = fence(scal, gbr, halo_in, out_send, out_keep, d_send)
    d_got, out_got, out_y = core_of(d_send), x_of(out_send), y_of(out_keep)
    part = conv_backward(1, sc, gbr, halo_in)
    part, d_got, out_got, out_y = fence(part, d_got, out_got, out_y)
    d_away = total(d_keep[1], d_got[1]).astype(BF)
    sc, d_away = fence(scal, d_away)
    d_y = y_of(d_away)
    dn_mlp, m_keep, m_send = up_backward(1, sc, *part)
    gatt, d_y, m_send = fence(gatt, d_y, m_send)
    m_got = core_of(m_send)
    d1_mine, d_give = halves(total(d_keep[0], d_got[0], d_y), owner1)
    m_away = total(m_keep[1], m_got[1]).astype(BF)
    sc, d_give, m_away = fence(scal, d_give.astype(BF), m_away)
    m_y = y_of(m_away)
    d_x = x_of(d_give)
    dq, dkv_own, dkv_oth = attention_backward(1, sc, gatt)
    dq, dkv_oth, m_y, d_x = fence(dq, dkv_oth, m_y, d_x)
    dkv_got = core_of(dkv_oth)
    m1_mine, m_give = halves(total(m_keep[0], m_got[0], m_y), owner1)
    sc, m_give, out_got = fence(scal, m_give.astype(BF), out_got)
    m_x = x_of(m_give)
    out_yg = y_of(out_got)
    g, ingrad1, a_keep, a_send = input_backward(1, sc, gres, dn_mlp, dq, dkv_own, dkv_got)

    g, a_send, m_x = fence(g, a_send, m_x)
    a_got = core_of(a_send)
    dm1_half = jnp.concatenate([total(d1_mine, d_x), total(m1_mine, m_x)], axis=0).astype(BF)
    sc, dm1_half = fence(scal, dm1_half)
    dm1_half = lax.psum(dm1_half, "dp")
    gres, gatt, gbr, halo_out, d0_keep, d0_send = merge_backward(0, sc, g)
    gbr, halo_out, d0_send, a_got, out_yg = fence(gbr, halo_out, d0_send, a_got, out_yg)
    halo_in, d0_got = core_of(halo_out), core_of(d0_send)
    a_away = total(a_keep[1], a_got[1]).astype(BF)
    gbr, halo_in, d0_got, a_away = fence(gbr, halo_in, d0_got, a_away)
    d_away = total(d0_keep[1], d0_got[1]).astype(BF)
    sc, a_away, d_away = fence(scal, a_away, d_away)
    ad_y = y_of(jnp.concatenate([a_away, d_away], axis=0))
    part = conv_backward(0, sc, gbr, halo_in)
    part, ad_y = fence(part, ad_y)
    a_y, d_y = ad_y[:A_ROWS], ad_y[A_ROWS:]
    a_mine, a_give = halves(total(a_keep[0], a_got[0], a_y), owner1)
    d_mine, d_give = halves(total(d0_keep[0], d0_got[0], d_y), first)
    sc, give = fence(scal, jnp.concatenate([a_give, d_give], axis=0).astype(BF))
    got = x_of(give)
    dn_mlp, m0_keep, m0_send = up_backward(0, sc, *part)
    gatt, got, m0_send, dm1_half = fence(gatt, got, m0_send, dm1_half)
    m0_got = core_of(m0_send)
    ad_half = total(jnp.concatenate([a_mine, d_mine], axis=0), got).astype(BF)
    m_away = total(m0_keep[1], m0_got[1]).astype(BF)
    sc, m_away, ad_half = fence(scal, m_away, ad_half)
    m_y = y_of(m_away)
    ad_terms = scatter_over_dp(ad_half)
    dq, dkv_own, dkv_oth = attention_backward(0, sc, gatt)
    dq, dkv_oth, m_y, ad_terms = fence(dq, dkv_oth, m_y, ad_terms)
    dkv_got = core_of(dkv_oth)
    m_mine, m_give = halves(total(m0_keep[0], m0_got[0], m_y), first)
    sc, m_give, ad_half = fence(scal, m_give.astype(BF), total(*ad_terms).astype(BF))
    m_x = x_of(m_give)
    ad_half = gather_over_dp(ad_half)
    g, ingrad0, a_keep, a_send = input_backward(0, sc, gres, dn_mlp, dq, dkv_own, dkv_got)

    ingrad0, a_send, m_x, ad_half, out_yg = fence(ingrad0, a_send, m_x, ad_half, out_yg)
    a_got = core_of(a_send)
    in_keep = jnp.where(first, ingrad0, ingrad1)
    in_got = x_of(jnp.where(first, ingrad1, ingrad0))
    m_terms = scatter_over_dp(total(m_mine, m_x).astype(BF))
    a_away = total(a_keep[1], a_got[1]).astype(BF)
    a_away, m_terms, in_keep = fence(a_away, m_terms, in_keep)
    a_y = y_of(a_away)
    in_y = y_of(in_keep)
    out_half = jnp.stack([out_keep, out_y, out_got, out_yg])
    out_other = core_of(out_half)
    m_parts = gather_over_dp(total(*m_terms).astype(BF))
    a_y, m_parts, in_got, ad_half, out_other = fence(a_y, m_parts, in_got, ad_half, out_other)
    a_sum = total(a_keep[0], a_got[0], a_y).astype(BF)
    a_x = x_of(a_sum)
    in_yg = y_of(in_got)
    ad_half = in_order(ad_half)
    a1_half = ad_half[: A_ROWS // 2]
    dm0_half = jnp.concatenate([ad_half[A_ROWS // 2 :], in_order(m_parts)], axis=0)
    dm_lo = jnp.where(first, dm0_half, dm1_half)
    cut = D_ROWS // 2
    away = jnp.where(first, dm1_half, dm0_half)
    m_back = x_of(away[cut:])
    d_away = jnp.concatenate([away[:cut], a1_half], axis=0)
    a_x, in_y = fence(a_x, in_y)
    a_terms = scatter_over_dp(total(a_sum, a_x).astype(BF))
    a_terms, in_yg, in_y, in_got, m_back, d_away = fence(a_terms, in_yg, in_y, in_got, m_back, d_away)
    d_back = x_of(d_away)
    a_parts = gather_over_dp(total(*a_terms).astype(BF))
    in_half = jnp.stack([in_keep, in_y, in_got, in_yg])
    in_other = core_of(in_half)

    def assemble(here, there):
        return call(
            assemble_kernel, [scal, here, there], [SMEM, VMEM, VMEM], [shape((micro, length, model), BF)], [], 0, 10
        )[0]

    layer_out = assemble(out_half, out_other)
    input_grad = assemble(in_half, in_other)

    a_parts, layer_out, input_grad, d_back = fence(a_parts, layer_out, input_grad, d_back)
    a_whole = jnp.where(first, in_order(a_parts), jnp.concatenate([a1_half, d_back[cut:]], axis=0))
    (g_qkv, g_out, g_up, g_down, g_bqkv, g_bup, g_gain, g_gbias, g_conv, g_ng, g_nb, g_ob, g_logit) = call(
        finale_kernel,
        [dm_lo, d_back, m_back, a_whole, logits],
        [VMEM] * 4 + [SMEM],
        [shape((3, model, LANES), F32), shape((LANES, model), F32), shape((2, model, shard), F32),
         shape((shard, model), F32), shape((3, 1, LANES), F32), shape((2, shard), F32), shape((1, shard), F32),
         shape((2, shard), F32), shape((TAPS, 1, shard), F32), shape((3, 1, model), F32), shape((3, 1, model), F32),
         shape((2, model), F32), shape((2, LANES), F32)],
        [],
        0,
        16,
    )
    outs = (
        layer_out.reshape(micro, 1, length, model),
        input_grad.reshape(micro, 1, length, model),
        g_ng[:, 0],
        g_nb[:, 0],
        g_qkv,
        g_bqkv[:, 0],
        g_out,
        g_up,
        g_bup,
        g_gain[0],
        g_gbias,
        g_conv[:, 0],
        g_down,
        g_ob,
        g_logit[:, 0],
    )
    return tuple(x[None] for x in outs)


def solution(mesh):
    placed = (
        P(None, "dp", None, None),
        P(None, "dp"),
        P(None, "dp", None, None),
        P("section", None, None),
        P("section", None, None),
        P("section", None, None, "mp"),
        P("section", None, "mp"),
        P("section", "mp", None),
        P("section", None, None, "mp"),
        P("section", None, "mp"),
        P("section", "mp"),
        P("section", None, "mp"),
        P("section", None, "mp"),
        P("section", "mp", None),
        P("section", None, None),
        P("section", None),
    )
    return jax.shard_map(
        per_device,
        mesh=mesh,
        in_specs=placed,
        out_specs=(
            P("section", None, "dp", None, None),
            P("section", None, "dp", None, None),
            P("section", None, None),
            P("section", None, None),
            P("section", None, None, "mp"),
            P("section", None, "mp"),
            P("section", "mp", None),
            P("section", None, None, "mp"),
            P("section", None, "mp"),
            P("section", "mp"),
            P("section", None, "mp"),
            P("section", None, "mp"),
            P("section", "mp", None),
            P("section", None, None),
            P("section", None),
        ),
        check_vma=False,
    )
```

```python
import functools
import math

import jax
import jax.numpy as jnp
import numpy as np
from jax import lax
from jax.experimental import pallas as pl
from jax.experimental.pallas import tpu as pltpu
from jax.sharding import PartitionSpec as P

BF = jnp.bfloat16
F32 = jnp.float32
HEAD = 64
LANES = 128
SEGS = 8
HALO = 16
EPS = 1e-05
NEG = -1000000000.0
NN = (((1,), (0,)), ((), ()))
NT = (((1,), (1,)), ((), ()))
TN = (((0,), (0,)), ((), ()))

TAPS = 31
BLOCK_ROWS = 40
ROW_UP0, ROW_UP1, ROW_GAIN, ROW_GB0, ROW_GB1 = 31, 32, 33, 34, 35
ROW_QKV = 120
ROW_NG, ROW_NB, ROW_OB, ROW_LOGIT = 128, 140, 152, 160
PACK_ROWS = 168

OUT_ROWS, DOWN_ROWS, UP_ROWS, QKV_ROWS = 512, 1536, 3072, 1536
D_SMALL = OUT_ROWS + DOWN_ROWS
D_ROWS = D_SMALL + 64
M_ROWS = UP_ROWS + 128
A_ROWS = QKV_ROWS + 64

W_UP, W_ROWS = 512, 3584
SPLIT = 2560

VMEM = pl.BlockSpec(memory_space=pltpu.VMEM)
SMEM = pl.BlockSpec(memory_space=pltpu.SMEM)
ANY = pl.BlockSpec(memory_space=pltpu.HBM)


def dot(a, b, dims):
    return lax.dot_general(a, b, dims, preferred_element_type=F32)


def call(kernel, ins, in_specs, outs, scratch, flops, mib, far=(), home=()):
    ins = [pltpu.with_memory_space_constraint(x, pltpu.HBM) if p is ANY else x for x, p in zip(ins, in_specs)]
    return pl.pallas_call(
        kernel,
        in_specs=in_specs,
        out_specs=[ANY if i in far else VMEM for i in range(len(outs))],
        out_shape=[pltpu.HBM(x.shape, x.dtype) if i in far or i in home else x for i, x in enumerate(outs)],
        scratch_shapes=scratch,
        compiler_params=pltpu.CompilerParams(vmem_limit_bytes=mib << 20),
        cost_estimate=pl.CostEstimate(flops=1, bytes_accessed=1, transcendentals=0),
    )(*ins)


def shape(dims, dtype):
    return jax.ShapeDtypeStruct(dims, dtype)


def fetch(flag, here, there, sems):
    @pl.when(flag)
    def _():
        for i, (a, d) in enumerate(here):
            pltpu.make_async_copy(a, d, sems.at[i]).start()

    @pl.when(jnp.logical_not(flag))
    def _():
        for i, (a, d) in enumerate(there):
            pltpu.make_async_copy(a, d, sems.at[i]).start()


def landed(pairs, sems):
    for i, (a, d) in enumerate(pairs):
        pltpu.make_async_copy(a, d, sems.at[i]).wait()


def slab_copies(sets, dst, lo, hi):
    here, there = [], []
    for j in range(4):
        for a, b in ((lo, min(hi, SPLIT)), (max(lo, SPLIT), hi)):
            if a >= b:
                continue
            d = dst.at[j, pl.ds(a - lo, b - a), :]
            here.append((sets[j].at[pl.ds(a, b - a), :], d))
            if j < 2:
                there.append((sets[4 + j].at[pl.ds(a, b - a), :], d))
            elif a < SPLIT:
                there.append((sets[4 + j].at[pl.ds(a, b - a), :], d))
            else:
                there.append((sets[6 + j].at[pl.ds(a - SPLIT, b - a), :], d))
    return here, there


def down_copies(sets, dst):
    here, there = shard_copies(sets, dst)
    rows = dst.shape[1]
    for j in range(2):
        there[j] = (sets[4 + j].at[pl.ds(W_ROWS - SPLIT, rows), :], dst.at[j])
    return here, there


def shard_copies(sets, dst):
    return [(sets[j], dst.at[j]) for j in range(4)], [(sets[4 + j], dst.at[j]) for j in range(4)]


def wide(sp, row, count=4):
    return jnp.concatenate([sp[0, 0, row + i : row + i + 1, :] for i in range(count)], axis=1)


def branch_weights(sp):
    l0 = sp[0, 0, ROW_LOGIT : ROW_LOGIT + 1, :]
    l1 = sp[0, 0, ROW_LOGIT + 1 : ROW_LOGIT + 2, :]
    top = jnp.maximum(l0, l1)
    e0, e1 = jnp.exp(l0 - top), jnp.exp(l1 - top)
    total = e0 + e1
    return jnp.concatenate([e0 / total] * 4, axis=1), jnp.concatenate([e1 / total] * 4, axis=1)


def normalized(x):
    center = jnp.mean(x, axis=-1, keepdims=True)
    d = x - center
    inverse = lax.rsqrt(jnp.mean(d * d, axis=-1, keepdims=True) + EPS)
    return d * inverse, inverse


def frame_of(row, half, rows):
    return half * rows + (row & (SEGS - 1)) * (rows // SEGS) + (row >> 3)


def order_matrix(rows, back):
    r = lax.broadcasted_iota(jnp.int32, (rows, rows), 1 if back else 0)
    t = lax.broadcasted_iota(jnp.int32, (rows, rows), 0 if back else 1)
    return jnp.where(frame_of(r, 0, rows) == t, 1.0, 0.0).astype(BF)


def halo_pick(rows, start_seg_even):
    start, seg = start_seg_even
    i = lax.broadcasted_iota(jnp.int32, (HALO, rows), 0)
    r = lax.broadcasted_iota(jnp.int32, (HALO, rows), 1)
    return jnp.where(r == (i + start) * SEGS + seg, 1.0, 0.0).astype(BF)


def swap_halves(x):
    lane = lax.broadcasted_iota(jnp.int32, x.shape, 1)
    return jnp.where(
        (lane & (HEAD - 1)) < HEAD // 2,
        pltpu.roll(x, LANES - HEAD // 2, 1),
        pltpu.roll(x, HEAD // 2, 1),
    )


def rotate(x, cosine, sine):
    return x * cosine + swap_halves(x) * sine


def rotate_back(x, cosine, sine):
    return x * cosine - swap_halves(x) * sine


def pieces(x):
    hi = x.astype(BF).astype(F32)
    rest = x - hi
    mid = rest.astype(BF).astype(F32)
    return hi, mid, rest - mid


def pack_kernel(
    wout_h, wup_h, wdown_h, cw, bup, ggain, gbias, bqkv, ngain, nbias, obias, logits,
    sp_o, u_o, v_o, wout, wup, wdown, sems,
):
    loads = [
        pltpu.make_async_copy(a, b, sems.at[i])
        for i, (a, b) in enumerate(((wup_h, wup), (wdown_h, wdown), (wout_h, wout)))
    ]
    for c in loads:
        c.start()
    sp_o[...] = jnp.zeros_like(sp_o)
    for b in range(3):
        lanes = slice(b * LANES, (b + 1) * LANES)
        at = b * BLOCK_ROWS
        sp_o[at : at + TAPS, :] = cw[:, lanes]
        sp_o[at + ROW_UP0 : at + ROW_UP0 + 2, :] = bup[:, lanes]
        sp_o[at + ROW_GAIN : at + ROW_GAIN + 1, :] = ggain[:, lanes]
        sp_o[at + ROW_GB0 : at + ROW_GB0 + 2, :] = gbias[:, lanes]
    sp_o[ROW_QKV : ROW_QKV + 3, :] = bqkv[...]
    for i in range(4):
        lanes = slice(i * LANES, (i + 1) * LANES)
        for n in range(3):
            sp_o[ROW_NG + 4 * n + i : ROW_NG + 4 * n + i + 1, :] = ngain[n : n + 1, lanes]
            sp_o[ROW_NB + 4 * n + i : ROW_NB + 4 * n + i + 1, :] = nbias[n : n + 1, lanes]
        for n in range(2):
            sp_o[ROW_OB + 4 * n + i : ROW_OB + 4 * n + i + 1, :] = obias[n : n + 1, lanes]
    for n in range(2):
        sp_o[ROW_LOGIT + n : ROW_LOGIT + n + 1, :] = jnp.full((1, LANES), logits[n], F32)
    for c in loads:
        c.wait()
    model, shard = wup.shape[1], wup.shape[2]
    for lb in range(4):
        lanes = slice(lb * LANES, (lb + 1) * LANES)
        u_o[lb * LANES : (lb + 1) * LANES, :] = wout[:, lanes]
        v_o[lb * shard : (lb + 1) * shard, :] = wdown[:, lanes]
    for hh in range(2):
        for b in range(3):
            at = W_UP + (hh * 3 + b) * model
            u_o[at : at + model, :] = wup[hh, :, b * LANES : (b + 1) * LANES]


def prologue_kernel(scal, frames, cotangent, own_o, oth_o, g_o, buf, sems):
    rows = own_o.shape[0]
    u, half = scal[0], scal[1]
    mine = pl.ds(pl.multiple_of(half * rows, rows), rows)
    other = pl.ds(pl.multiple_of((1 - half) * rows, rows), rows)
    copies = [
        pltpu.make_async_copy(frames.at[u, 0, mine, :], buf.at[0], sems.at[0]),
        pltpu.make_async_copy(frames.at[u, 0, other, :], buf.at[1], sems.at[1]),
        pltpu.make_async_copy(cotangent.at[u, 0, mine, :], buf.at[2], sems.at[2]),
    ]
    for c in copies:
        c.start()
    order = order_matrix(rows, False)
    for c, i, out in zip(copies, range(3), (own_o, oth_o, g_o)):
        c.wait()
        out[...] = dot(order, buf[i], NN).astype(BF)


def attention_forward_kernel(layer, scal, sp, cos_t, sin_t, h_own, h_oth, *refs):
    sets, refs = refs[:8], refs[8:]
    q_h, k_h, v_h, mix_h, lse_h, mix_o, w_s, cs, sn, norm, lse_s, q_o, k_o, v_o, lse_o, wsem, tsem, osem = refs
    sp = sp.at[pl.ds(layer, 1)]
    rows, model = h_own.shape
    half, length = scal[1], scal[2]
    here, there = shard_copies(sets, w_s)
    fetch(scal[3] == layer, here, there, wsem)
    tables = [
        pltpu.make_async_copy(cos_t.at[half], cs, tsem.at[0]),
        pltpu.make_async_copy(sin_t.at[half], sn, tsem.at[1]),
    ]
    for c in tables:
        c.start()
    gain, bias = wide(sp, ROW_NG), wide(sp, ROW_NB)
    step = 64
    for src, base in ((h_own, 0), (h_oth, rows)):
        for r in range(0, rows, step):
            hat, unused = normalized(src[r : r + step, :].astype(F32))
            norm[base + r : base + r + step, :] = (hat * gain + bias).astype(BF)
    lse_s[...] = jnp.zeros_like(lse_s)
    for c in tables:
        c.wait()
    landed(here, wsem)
    total = 2 * rows
    row = lax.broadcasted_iota(jnp.int32, (total, LANES), 0)
    part = jnp.where(row < rows, half, 1 - half)
    position = frame_of(row & (rows - 1), part, rows)
    mask = jnp.where(position < length, 0.0, NEG)
    lane_k = lax.broadcasted_iota(jnp.int32, (total, LANES), 1)
    lane_q = lax.broadcasted_iota(jnp.int32, (rows, LANES), 1)

    def stores(j):
        pairs = ((q_o, q_h), (k_o, k_h), (v_o, v_h), (mix_o, mix_h))
        return [pltpu.make_async_copy(a.at[j], b.at[j], osem.at[j, i]) for i, (a, b) in enumerate(pairs)]

    def shard(j):
        mj = scal[4 + j]
        bq = sp[0, mj, ROW_QKV : ROW_QKV + 1, :]
        bk = sp[0, mj, ROW_QKV + 1 : ROW_QKV + 2, :]
        bv = sp[0, mj, ROW_QKV + 2 : ROW_QKV + 3, :]
        everything = norm[...]
        q = rotate(dot(norm[:rows, :], w_s[j, 0], NN) + bq, cs[:rows, :], sn[:rows, :])
        q = q.astype(BF).astype(F32) * (1.0 / math.sqrt(HEAD))
        k = rotate(dot(everything, w_s[j, 1], NN) + bk, cs[...], sn[...]).astype(BF)
        v = (dot(everything, w_s[j, 2], NN) + bv).astype(BF)
        q_o[j] = q.astype(BF)
        k_o[j] = k
        v_o[j] = v
        kf = k.astype(F32)
        vt = v.astype(F32).T.astype(BF)
        outs = []
        work = []
        for hd in range(2):
            spare = (1 - hd) * HEAD
            qm = jnp.where((lane_q >> 6) == hd, q, jnp.where(lane_q == spare, 1.0, 0.0)).astype(BF)
            km = jnp.where((lane_k >> 6) == hd, kf, jnp.where(lane_k == spare, mask, 0.0)).astype(BF)
            work.append((km, qm))
        score = dot(*work[0], NT)
        for hd in range(2):
            s = score
            if hd == 0:
                score = dot(*work[1], NT)
            top = jnp.max(s, axis=0, keepdims=True)
            p = jnp.exp(s - top)
            den = jnp.sum(p, axis=0, keepdims=True)
            p = (p * (1.0 / den)).astype(BF)
            outs.append(dot(vt[hd * HEAD : (hd + 1) * HEAD, :], p, NN))
            lse_s[2 * j + hd : 2 * j + hd + 1, :] = top + jnp.log(den)
        mix_o[j] = jnp.concatenate(outs, axis=0).T.astype(BF)
        for c in stores(j):
            c.start()

    for j in range(4):
        shard(j)
    lse_o[...] = lse_s[...].T
    last = pltpu.make_async_copy(lse_o, lse_h, osem.at[4, 0])
    last.start()
    for j in range(4):
        for c in stores(j):
            c.wait()
    last.wait()


def gelu_parts(u):
    d = 1.0 + (0.3275911 / math.sqrt(2.0)) * jnp.abs(u)
    t = pl.reciprocal(d, approx=True)
    t = t * (2.0 - d * t)
    e = jnp.exp2((-0.5 / math.log(2.0)) * (u * u))
    half = [0.5 * c for c in (1.061405429, -1.453152027, 1.421413741, -0.284496736, 0.254829592)]
    poly = ((((half[0] * t + half[1]) * t + half[2]) * t + half[3]) * t + half[4]) * t
    tail = poly * e
    phi = jnp.where(u >= 0, 1.0 - tail, tail)
    return u * phi, phi + (u * e) * (1.0 / math.sqrt(2.0 * math.pi))


PHASES = ((0,), (2,), (2, 4), (1,), (3,), (3, 5), (1, 2), (3, 4), (3, 4, 5, 6))
TAP_PHASES = ((0,), (2,), (0, 2), (1,), (3,), (1, 3), (0, 1), (2, 3), (0, 1, 2, 3))


def phase(ref, rows, n):
    out = ref[4 * n + rows[0]]
    for r in rows[1:]:
        out = out + ref[4 * n + r]
    return out


def correlate(taps, xs, count):
    accs = [None] * count
    for m, tap in enumerate(taps):
        for n in range(count):
            term = tap * xs[n + m]
            accs[n] = term if accs[n] is None else accs[n] + term
    return accs


def unfold(q0, q1, q2):
    out = []
    for n in range(len(q2)):
        out.append(q0[n] + q1[n])
        out.append(q2[n] - (q0[n + 1] + q1[n]))
    if len(q1) > len(q2):
        out.append(q0[len(q2)] + q1[len(q2)])
    return out


def fill_filters(filt, row):
    for m in range(8):
        w = [
            jnp.broadcast_to(row(4 * m + r), (SEGS, LANES)) if 4 * m + r < TAPS else jnp.zeros((SEGS, LANES), F32)
            for r in range(4)
        ]
        for i, rows in enumerate(TAP_PHASES):
            out = w[rows[0]]
            for r in rows[1:]:
                out = out + w[r]
            filt[i * 8 + m] = out


def fast_fir(pad, filt, out, keep):
    count = out.shape[0]
    half = count // 2
    for g in range(3):
        qs = []
        for i in range(3):
            n = half // 2 + 1 if i == 0 or (i == 1 and g == 0) else half // 2
            xs = [phase(pad, PHASES[3 * g + i], x) for x in range(n + 7)]
            qs.append(correlate([filt[(3 * g + i) * 8 + m] for m in range(8)], xs, n))
        p = unfold(*qs)
        for n in range(len(p)):
            if g == 0:
                keep[n] = p[n]
            elif g == 1:
                out[2 * n] = keep[n] + p[n]
                out[2 * n + 1] = keep[n + 1] + p[n]
            else:
                out[2 * n + 1] = p[n] - out[2 * n + 1]


def tap_sums(gpad, xpad, count):
    ps = []
    for g in range(3):
        qs = []
        for i in range(3):
            rows = [15 + r for r in TAP_PHASES[3 * g + i]]
            n = 9 if i == 0 else 8
            steps = count // 4
            xs = [phase(xpad, PHASES[3 * g + i], x) for x in range(n + steps - 1)]
            qs.append(correlate([phase(gpad, rows, x) for x in range(steps)], xs, n))
        ps.append(unfold(*qs))
    out = []
    for m in range(16):
        out.append(ps[0][m] + ps[1][m])
        if m < 15:
            out.append(ps[2][m] - (ps[0][m + 1] + ps[1][m]))
    return out


def halo_pads(pad, block, halo_ref, half, right_is_even):
    count = block.shape[0]
    pad[15 : 15 + count] = block
    pad[30 + count : 32 + count] = jnp.zeros((2, SEGS, LANES), F32)
    seg = lax.broadcasted_iota(jnp.int32, (SEGS, LANES), 0)
    from_left = half.astype(F32)
    from_right = 1.0 - from_left
    for i in range(15):
        tail = pltpu.roll(block[count - 15 + i], 1, 0)
        edge = jnp.broadcast_to(halo_ref[i + 1 : i + 2, :], (SEGS, LANES)) * from_left
        pad[i] = jnp.where(seg == 0, edge, tail)
        head = pltpu.roll(block[i], SEGS - 1, 0)
        edge = jnp.broadcast_to(halo_ref[i : i + 1, :], (SEGS, LANES)) * from_right
        pad[15 + count + i] = jnp.where(seg == SEGS - 1, edge, head)


def mlp_forward_kernel(layer, scal, sp, h_own, h_oth, *refs):
    sets, refs = refs[:10], refs[10:]
    (act0_h, dact0_h, dact1_h, ghat_h, conv_h, gated_h, ginv_h, norm_h, gated_o,
     ws, act0, act1, sums, gmean, ginv, pad, filt, fir, keep, halo, act0_o, dact0_o, dact1_o, ghat_o, conv_o, norm_o, wsem, osem) = refs
    sp = sp.at[pl.ds(layer, 1)]
    rows, model = h_own.shape
    every = rows + HALO
    hidden = act0.shape[1]
    shard = hidden // 4
    half, length = scal[1], scal[2]
    here, there = slab_copies(sets, ws, W_UP, W_ROWS)
    fetch(scal[3] == layer, here, there, wsem)
    gain, bias = wide(sp, ROW_NG + 4), wide(sp, ROW_NB + 4)
    step = 64
    for r in range(0, rows, step):
        hat, unused = normalized(h_own[r : r + step, :].astype(F32))
        norm_o[r : r + step, :] = (hat * gain + bias).astype(BF)
    i = lax.broadcasted_iota(jnp.int32, (HALO, rows), 0)
    r = lax.broadcasted_iota(jnp.int32, (HALO, rows), 1)
    wanted = jnp.where(half == 0, i * SEGS, (i + rows // SEGS - HALO) * SEGS + SEGS - 1)
    pick = jnp.where(r == wanted, 1.0, 0.0).astype(BF)
    hat, unused = normalized(dot(pick, h_oth[...], NN))
    norm_o[rows:every, :] = (hat * gain + bias).astype(BF)
    sums[...] = jnp.zeros_like(sums)
    landed(here, wsem)

    width = 256
    chunk = 48

    def up(i, carry):
        lanes = pl.ds(pl.multiple_of(i * width, width), width)
        rows_of = []
        for hh, base in ((0, ROW_UP0), (1, ROW_UP1)):
            got = []
            for t in range(2):
                c = 2 * i + t
                got.append(sp[0, scal[8 + c], pl.ds(lax.rem(c, 3) * BLOCK_ROWS + base, 1), :])
            rows_of.append(jnp.concatenate(got, axis=1))
        slabs = []
        for hh in range(2):
            pair = []
            for t in range(2):
                c = 2 * i + t
                at = (hh * 3 + lax.rem(c, 3)) * model
                pair.append(ws[lax.div(c, 3), pl.ds(pl.multiple_of(at, model), model), :])
            slabs.append(jnp.concatenate(pair, axis=1))
        u0 = dot(norm_o[...], slabs[0], NN)
        u1 = dot(norm_o[...], slabs[1], NN)
        for r in range(0, every, chunk):
            a, d = gelu_parts(u0[r : r + chunk] + rows_of[0])
            act0[r : r + chunk, lanes] = a
            act0_o[r : r + chunk, lanes] = a.astype(BF)
            dact0_o[r : r + chunk, lanes] = d.astype(BF)
        for r in range(0, every, chunk):
            a, d = gelu_parts(u1[r : r + chunk] + rows_of[1])
            act1[r : r + chunk, lanes] = a
            dact1_o[r : r + chunk, lanes] = d.astype(BF)
            sums[r : r + chunk, :] += a[:, :LANES] + a[:, LANES:]
        return carry

    lax.fori_loop(0, hidden // width, up, 0)
    for r in range(0, every, chunk):
        center = jnp.sum(sums[r : r + chunk, :], axis=1, keepdims=True) * (1.0 / hidden)
        d = act1[r : r + chunk, :] - center
        spread = jnp.sum(d * d, axis=1, keepdims=True) * (1.0 / hidden)
        gmean[r : r + chunk, :] = jnp.broadcast_to(center, (chunk, LANES))
        ginv[r : r + chunk, :] = jnp.broadcast_to(lax.rsqrt(spread + EPS), (chunk, LANES))
    stores = [
        pltpu.make_async_copy(a, b, osem.at[i])
        for i, (a, b) in enumerate(
            ((act0_o, act0_h), (dact0_o, dact0_h), (dact1_o, dact1_h), (norm_o, norm_h), (ginv.at[pl.ds(0, rows)], ginv_h))
        )
    ]
    for c in stores:
        c.start()

    def column_stores(c):
        lanes = pl.ds(pl.multiple_of(c * LANES, LANES), LANES)
        pairs = ((ghat_o, ghat_h), (conv_o, conv_h), (gated_o, gated_h))
        return [
            pltpu.make_async_copy(a.at[:, lanes], b.at[:, lanes], osem.at[5 + 3 * c + i]) for i, (a, b) in enumerate(pairs)
        ]


    row = lax.broadcasted_iota(jnp.int32, (rows, LANES), 0)
    valid = jnp.where(frame_of(row, half, rows) < length, 1.0, 0.0)
    hrow = lax.broadcasted_iota(jnp.int32, (HALO, LANES), 0)
    valid_halo = jnp.where(jnp.where(half == 0, rows, rows - HALO) + hrow < length, 1.0, 0.0)
    count = rows // SEGS

    def gate(c, carry):
        lanes = pl.ds(pl.multiple_of(c * LANES, LANES), LANES)
        mj = scal[8 + c]
        base = lax.rem(c, 3) * BLOCK_ROWS
        ggain = sp[0, mj, pl.ds(base + ROW_GAIN, 1), :]
        gb0 = sp[0, mj, pl.ds(base + ROW_GB0, 1), :]
        gb1 = sp[0, mj, pl.ds(base + ROW_GB1, 1), :]
        hat = (act1[rows:every, lanes] - gmean[rows:every, :]) * ginv[rows:every, :]
        ghat_o[rows:every, lanes] = hat.astype(BF)
        halo[...] = (hat * ggain + gb0) * valid_halo
        hat = (act1[0:rows, lanes] - gmean[0:rows, :]) * ginv[0:rows, :]
        ghat_o[0:rows, lanes] = hat.astype(BF)
        normed = (hat * ggain + gb0) * valid
        halo_pads(pad, normed.reshape(count, SEGS, LANES), halo, half, True)
        fill_filters(filt, lambda k: sp[0, mj, pl.ds(base + k, 1), :])
        fast_fir(pad, filt, fir, keep)
        for t in range(0, count, 8):
            at = t * SEGS
            cv = fir[t : t + 8].reshape(64, LANES) + gb1
            conv_o[at : at + 64, lanes] = cv.astype(BF)
            gated_o[at : at + 64, lanes] = (act0[at : at + 64, lanes] * cv).astype(BF)
        for store in column_stores(c):
            store.start()
        return carry

    lax.fori_loop(0, hidden // LANES, gate, 0)
    for c in range(hidden // LANES):
        stores.extend(column_stores(c))
    for c in stores:
        c.wait()


def branch_rows(mix, gated, ws, wv, r, block):
    shard = wv.shape[1] // 4
    mixed = jnp.concatenate([mix[j, r : r + block, :] for j in range(4)], axis=1)
    brs, atts = [], []
    for lb in range(0, 4, 2):
        w = [
            jnp.concatenate(
                [wv[j, (lb + t) * shard : (lb + t + 1) * shard, :] for j in range(4)], axis=0
            )
            for t in range(2)
        ]
        brs.append(dot(gated[r : r + block, :], jnp.concatenate(w, axis=1), NN))
        w = [
            jnp.concatenate(
                [ws[j, (lb + t) * LANES : (lb + t + 1) * LANES, :] for j in range(4)], axis=0
            )
            for t in range(2)
        ]
        atts.append(dot(mixed, jnp.concatenate(w, axis=1), NN))
    return jnp.concatenate(atts, axis=1), jnp.concatenate(brs, axis=1)


def merge_forward_kernel(layer, scal, sp, h_own, mix, gated, *refs):
    u_sets, v_sets, refs = refs[:10], refs[10:18], refs[18:]
    o_o, nat_o, rhat_h, rstd_h, diff_h, ws, wv, rhat_o, rstd_o, diff_o, usem, vsem, osem = refs
    sp = sp.at[pl.ds(layer, 1)]
    rows, model = h_own.shape
    shard = wv.shape[1] // 4
    here, there = slab_copies(u_sets, ws, 0, W_UP)
    fetch(scal[3] == layer, here, there, usem)
    here_v, there_v = down_copies(v_sets, wv)
    fetch(scal[3] == layer, here_v, there_v, vsem)
    landed(here, usem)
    landed(here_v, vsem)
    step = 64

    def stores(r, n):
        part = pl.ds(r, n)
        pairs = ((rhat_o, rhat_h), (rstd_o, rstd_h), (diff_o, diff_h))
        return [
            pltpu.make_async_copy(a.at[part], b.at[part], osem.at[r // n, i]) for i, (a, b) in enumerate(pairs)
        ]

    w0, w1 = branch_weights(sp)
    gain, bias = wide(sp, ROW_NG + 8), wide(sp, ROW_NB + 8)
    b0, b1 = wide(sp, ROW_OB), wide(sp, ROW_OB + 4)
    block = 256
    for r in range(0, rows, block):
        att, br = branch_rows(mix, gated, ws, wv, r, block)
        for q in range(0, block, step):
            at = att[q : q + step] + b0
            bt = br[q : q + step] + b1
            res = h_own[r + q : r + q + step, :].astype(F32) + w0 * at + w1 * bt
            hat, inverse = normalized(res)
            diff_o[r + q : r + q + step, :] = at - bt
            rhat_o[r + q : r + q + step, :] = hat
            rstd_o[r + q : r + q + step, :] = jnp.broadcast_to(inverse, (step, LANES))
            o_o[r + q : r + q + step, :] = (hat * gain + bias).astype(BF)
        for c in stores(r, block):
            c.start()
    nat_o[...] = dot(order_matrix(rows, True), o_o[...], NN).astype(BF)
    for r in range(0, rows, block):
        for c in stores(r, block):
            c.wait()


def binary_weights(down):
    lane = lax.broadcasted_iota(jnp.int32, (1, LANES), 1)
    out = jnp.full((1, LANES), 2.0 ** (63 if down else -63), F32)
    for b in range(7):
        out = jnp.where(((lane >> b) & 1) == 1, out * 2.0 ** (-(2**b) if down else 2**b), out)
    return out


def merge_finish(half, sums, slope, mix, gated, gatt_o, gbr_o, halo_o, keep_o, send_o, small, late):
    rows = gbr_o.shape[0]
    i = lax.broadcasted_iota(jnp.int32, (HALO, rows), 0)
    r = lax.broadcasted_iota(jnp.int32, (HALO, rows), 1)
    wanted = jnp.where(half == 0, (i + rows // SEGS - HALO) * SEGS + SEGS - 1, i * SEGS)
    pick = jnp.where(r == wanted, 1.0, 0.0).astype(BF)
    halo_o[...] = dot(pick, gbr_o[...], NN).astype(BF)
    slope = jnp.sum(slope, axis=1, keepdims=True)
    small[...] = jnp.zeros_like(small)
    for n, v in enumerate(sums):
        for i in range(4):
            small[4 * n + i : 4 * n + i + 1, :] = v[:, i * LANES : (i + 1) * LANES]
    scaled = jnp.abs(slope) * binary_weights(False)
    digits = jnp.floor(scaled) - 2.0 * jnp.floor(0.5 * scaled)
    small[16:17, :] = jnp.where(slope < 0, -digits, digits)
    shards = (keep_o.at[0], send_o.at[0], keep_o.at[1], send_o.at[1])
    shard = gated.shape[1] // 4
    late()
    for j in range(4):
        shards[j][D_SMALL:D_ROWS, :] = small[...].astype(BF)
    for j in range(4):
        w = dot(mix[j], gatt_o[...], TN).astype(BF)
        for i in range(4):
            shards[j][i * LANES : (i + 1) * LANES, :] = w[:, i * LANES : (i + 1) * LANES]
        w = dot(gated[:, j * shard : (j + 1) * shard], gbr_o[...], TN).astype(BF)
        for i in range(4):
            at = OUT_ROWS + i * shard
            shards[j][at : at + shard, :] = w[:, i * LANES : (i + 1) * LANES]


def merge_backward_kernel(
    layer, scal, sp, g, rhat_h, rstd_h, diff_h, mix_h, gated_h,
    gres_o, gatt_o, gbr_o, halo_o, keep_o, send_o, rhat, rstd, diff, mix, gated, small, sems,
):
    sp = sp.at[pl.ds(layer, 1)]
    rows, model = g.shape
    half = scal[1]
    step = 64
    parts = [pl.ds(r, 2 * step) for r in range(0, rows, 2 * step)]
    loads = [
        [
            pltpu.make_async_copy(a.at[part], b.at[part], sems.at[i, n])
            for i, (a, b) in enumerate(((rstd_h, rstd), (rhat_h, rhat), (diff_h, diff)))
        ]
        for n, part in enumerate(parts)
    ]
    late = [
        pltpu.make_async_copy(a, b, sems.at[3, i]) for i, (a, b) in enumerate(((mix_h, mix), (gated_h, gated)))
    ]
    for c in sum(loads, []) + late:
        c.start()
    gain = wide(sp, ROW_NG + 8)
    w0, w1 = branch_weights(sp)
    dgain = dbias = slope = jnp.zeros((1, model), F32)
    db = jnp.zeros((1, model), F32)
    for r in range(0, rows, step):
        if r % (2 * step) == 0:
            for c in loads[r // (2 * step)]:
                c.wait()
        gg = g[r : r + step, :].astype(F32)
        hat = rhat[r : r + step, :]
        dgain = dgain + jnp.sum(gg * hat, axis=0, keepdims=True)
        dbias = dbias + jnp.sum(gg, axis=0, keepdims=True)
        gg = gg * gain
        gr = rstd[r : r + step, 0:1] * (
            gg - jnp.mean(gg, axis=1, keepdims=True) - hat * jnp.mean(gg * hat, axis=1, keepdims=True)
        )
        gres_o[r : r + step, :] = gr
        gatt_o[r : r + step, :] = (w0 * gr).astype(BF)
        gbr_o[r : r + step, :] = (w1 * gr).astype(BF)
        db = db + jnp.sum(gr, axis=0, keepdims=True)
        slope = slope + jnp.sum(gr * diff[r : r + step, :], axis=0, keepdims=True)
    merge_finish(
        half, (dgain, dbias, w0 * db, w1 * db), slope, mix, gated, gatt_o, gbr_o, halo_o, keep_o, send_o, small,
        lambda: [c.wait() for c in late],
    )


def merge_turn_kernel(layer, scal, sp, h_own, mix, gated, g, *refs):
    u_sets, v_sets, refs = refs[:10], refs[10:18], refs[18:]
    nat_o, gres_o, gatt_o, gbr_o, halo_o, keep_o, send_o, ws, wv, o_s, small, usem, vsem = refs
    sp = sp.at[pl.ds(layer, 1)]
    rows, model = h_own.shape
    here, there = slab_copies(u_sets, ws, 0, W_UP)
    fetch(scal[3] == layer, here, there, usem)
    here_v, there_v = down_copies(v_sets, wv)
    fetch(scal[3] == layer, here_v, there_v, vsem)
    landed(here, usem)
    landed(here_v, vsem)
    w0, w1 = branch_weights(sp)
    gain, bias = wide(sp, ROW_NG + 8), wide(sp, ROW_NB + 8)
    b0, b1 = wide(sp, ROW_OB), wide(sp, ROW_OB + 4)
    dgain = dbias = slope = db = jnp.zeros((1, model), F32)
    step, block = 64, 256
    for r in range(0, rows, block):
        att, br = branch_rows(mix, gated, ws, wv, r, block)
        for q in range(0, block, step):
            at = att[q : q + step] + b0
            bt = br[q : q + step] + b1
            lo, hi = r + q, r + q + step
            hat, inverse = normalized(h_own[lo:hi, :].astype(F32) + w0 * at + w1 * bt)
            o_s[lo:hi, :] = (hat * gain + bias).astype(BF)
            gg = g[lo:hi, :].astype(F32)
            dgain = dgain + jnp.sum(gg * hat, axis=0, keepdims=True)
            dbias = dbias + jnp.sum(gg, axis=0, keepdims=True)
            gg = gg * gain
            gr = inverse * (
                gg - jnp.mean(gg, axis=1, keepdims=True) - hat * jnp.mean(gg * hat, axis=1, keepdims=True)
            )
            gres_o[lo:hi, :] = gr
            gatt_o[lo:hi, :] = (w0 * gr).astype(BF)
            gbr_o[lo:hi, :] = (w1 * gr).astype(BF)
            db = db + jnp.sum(gr, axis=0, keepdims=True)
            slope = slope + jnp.sum(gr * (at - bt), axis=0, keepdims=True)
    nat_o[...] = dot(order_matrix(rows, True), o_s[...], NN).astype(BF)
    merge_finish(
        scal[1], (dgain, dbias, w0 * db, w1 * db), slope, mix, gated, gatt_o, gbr_o, halo_o, keep_o, send_o, small,
        lambda: None,
    )


def attention_backward_kernel(layer, scal, gatt_h, q_h, k_h, v_h, mix_h, lse_h, *refs):
    sets, refs = refs[:10], refs[10:]
    cos_t, sin_t, dq_o, own_o, oth_o, w_s, cs, sn, pbuf, dsbuf, dom, qm2, q_r, k_r, v_r, mix, lse, gatt, wsem, tsem = refs
    rows = gatt.shape[0]
    total = 2 * rows
    half, length = scal[1], scal[2]
    here, there = slab_copies(sets, w_s, 0, W_UP)
    fetch(scal[3] == layer, here, there, wsem)
    tables = [
        pltpu.make_async_copy(cos_t.at[half, pl.ds(0, rows), :], cs, tsem.at[0]),
        pltpu.make_async_copy(sin_t.at[half, pl.ds(0, rows), :], sn, tsem.at[1]),
    ]
    for i, (a, b) in enumerate(((q_h, q_r), (k_h, k_r), (v_h, v_r), (mix_h, mix), (lse_h, lse), (gatt_h, gatt))):
        tables.append(pltpu.make_async_copy(a, b, tsem.at[2 + i]))
    for c in tables:
        c.start()
    row = lax.broadcasted_iota(jnp.int32, (total, LANES), 0)
    part = jnp.where(row < rows, half, 1 - half)
    position = frame_of(row & (rows - 1), part, rows)
    mask = jnp.where(position < length, 0.0, NEG)
    lane_k = lax.broadcasted_iota(jnp.int32, (total, LANES), 1)
    lane_q = lax.broadcasted_iota(jnp.int32, (rows, LANES), 1)
    for c in tables:
        c.wait()
    landed(here, wsem)

    def shard(j):
        wo = jnp.concatenate([w_s[j, lb * LANES : (lb + 1) * LANES, :] for lb in range(4)], axis=1)
        dm = dot(gatt[...], wo, NT).astype(BF).astype(F32)
        prod = dm * mix[j].astype(F32)
        q = q_r[j].astype(F32)
        k = k_r[j].astype(F32)
        v = v_r[j].astype(F32)
        kt = k.T.astype(BF)
        dqs = []
        for hd in range(2):
            spare = (1 - hd) * HEAD
            in_q, in_k = (lane_q >> 6) == hd, (lane_k >> 6) == hd
            minus_lse = -jnp.sum(jnp.where(lane_q == 2 * j + hd, lse[...], 0.0), axis=1, keepdims=True)
            minus_delta = -jnp.sum(jnp.where(in_q, prod, 0.0), axis=1, keepdims=True)
            l0, l1, l2 = pieces(minus_lse)
            e0, e1, e2 = pieces(minus_delta)
            qx = jnp.where(lane_q == spare, 1.0, 0.0)
            dx = jnp.zeros_like(qx)
            for n, (lp, ep) in enumerate(((l0, e0), (l1, e1), (l2, e2))):
                here = lane_q == spare + 1 + n
                qx = jnp.where(here, lp, qx)
                dx = jnp.where(here, ep, dx)
            one = jnp.where((lane_k > spare) & (lane_k < spare + 4), 1.0, 0.0)
            qh = jnp.where(in_q, q, qx).astype(BF)
            dh = jnp.where(in_q, dm, dx).astype(BF)
            kh = jnp.where(in_k, k, jnp.where(lane_k == spare, mask, one)).astype(BF)
            vh = jnp.where(in_k, v, one).astype(BF)
            dom[hd * rows : (hd + 1) * rows, :] = jnp.where(in_q, dm, 0.0).astype(BF)
            qm2[hd * rows : (hd + 1) * rows, :] = jnp.where(in_q, q, 0.0).astype(BF)
            p = jnp.exp(dot(kh, qh, NT))
            dp = dot(vh, dh, NT)
            ds = (p * dp).astype(BF)
            pbuf[:, hd * rows : (hd + 1) * rows] = p.astype(BF)
            dsbuf[:, hd * rows : (hd + 1) * rows] = ds
            dqs.append(dot(kt[hd * HEAD : (hd + 1) * HEAD, :], ds, NN))
        dq = jnp.concatenate(dqs, axis=0).T * (1.0 / math.sqrt(HEAD))
        dq_o[j] = rotate_back(dq, cs[...], sn[...]).astype(BF)
        dk = dot(dsbuf[...], qm2[...], NN)
        dv = dot(pbuf[...], dom[...], NN)
        own_o[j, :, 0:LANES] = dk[:rows]
        own_o[j, :, LANES:] = dv[:rows]
        oth_o[j, :, 0:LANES] = dk[rows:].astype(BF)
        oth_o[j, :, LANES:] = dv[rows:].astype(BF)

    for j in range(4):
        shard(j)


def conv_backward_kernel(layer, scal, sp, gbr, ghalo, act0_h, dact0_h, ghat_h, conv_h, *refs):
    v_sets, refs = refs[:8], refs[8:]
    (dup_o, hgrad, hs, xs, small, wv, act0, dact0, ghat, conv, gpad, xpad, filt, fir, keep, halo, gcv, gbuf, vsem, asem) = refs
    sp = sp.at[pl.ds(layer, 1)]
    rows, model = gbr.shape
    every = rows + HALO
    hidden = gcv.shape[1]
    shard = hidden // 4
    half, length = scal[1], scal[2]
    here_v, there_v = down_copies(v_sets, wv)
    fetch(scal[3] == layer, here_v, there_v, vsem)
    width = 256

    def loads(i):
        lanes = pl.ds(pl.multiple_of(i * width, width), width)
        pairs = ((act0_h, act0), (conv_h, conv), (dact0_h, dact0))
        return [
            pltpu.make_async_copy(a.at[:, lanes], b.at[:, lanes], asem.at[n, i]) for n, (a, b) in enumerate(pairs)
        ]

    for i in range(hidden // width):
        for c in loads(i):
            c.start()
    last = pltpu.make_async_copy(ghat_h, ghat, asem.at[3, 0])
    last.start()
    gbuf[0:rows, :] = gbr[...]
    gbuf[rows:every, :] = ghalo[...]
    hs[...] = jnp.zeros_like(hs)
    xs[...] = jnp.zeros_like(xs)
    small[...] = jnp.zeros_like(small)
    landed(here_v, vsem)
    count = rows // SEGS
    chunk = 48

    def down(i, carry):
        for c in loads(i):
            c.wait()
        lanes = pl.ds(pl.multiple_of(i * width, width), width)
        pair = []
        for t in range(2):
            c = 2 * i + t
            base = lax.rem(c, 3) * LANES
            pair.append(
                jnp.concatenate(
                    [
                        wv[lax.div(c, 3), pl.ds(pl.multiple_of(base + lb * shard, LANES), LANES), :]
                        for lb in range(4)
                    ],
                    axis=1,
                )
            )
        g = dot(gbuf[...], jnp.concatenate(pair, axis=0), NT)
        for r in range(0, every, chunk):
            gr = g[r : r + chunk].astype(BF).astype(F32)
            gcv[r : r + chunk, lanes] = gr * act0[r : r + chunk, lanes].astype(F32)
        for r in range(0, rows, 64):
            gr = g[r : r + 64].astype(BF).astype(F32)
            keep = gr * conv[r : r + 64, lanes].astype(F32) * dact0[r : r + 64, lanes].astype(F32)
            dup_o[r : r + 64, lanes] = keep.astype(BF)
        return carry

    lax.fori_loop(0, hidden // width, down, 0)
    last.wait()
    row = lax.broadcasted_iota(jnp.int32, (rows, LANES), 0)
    valid = jnp.where(frame_of(row, half, rows) < length, 1.0, 0.0)
    hrow = lax.broadcasted_iota(jnp.int32, (HALO, LANES), 0)
    valid_halo = jnp.where(jnp.where(half == 0, rows, rows - HALO) + hrow < length, 1.0, 0.0)

    def fold(x):
        return jnp.sum(x, axis=0, keepdims=True)

    def conv_back(c, carry):
        lanes = pl.ds(pl.multiple_of(c * LANES, LANES), LANES)
        mj = scal[8 + c]
        b = lax.rem(c, 3)
        j = lax.div(c, 3)
        base = b * BLOCK_ROWS
        ggain = sp[0, mj, pl.ds(base + ROW_GAIN, 1), :]
        gb0 = sp[0, mj, pl.ds(base + ROW_GB0, 1), :]
        halo[...] = (ghat[rows:every, lanes].astype(F32) * ggain + gb0) * valid_halo
        normed = (ghat[0:rows, lanes].astype(F32) * ggain + gb0) * valid
        halo_pads(xpad, normed.reshape(count, SEGS, LANES), halo, half, True)
        halo[...] = gcv[rows:every, lanes]
        gown = gcv[0:rows, lanes]
        halo_pads(gpad, gown.reshape(count, SEGS, LANES), halo, half, True)
        small[j, pl.ds(base + ROW_GB1, 1), :] = fold(gown)
        for k, t in enumerate(tap_sums(gpad, xpad, count)):
            small[j, pl.ds(base + k, 1), :] = fold(t)
        fill_filters(filt, lambda k: sp[0, mj, pl.ds(base + TAPS - 1 - k, 1), :])
        fast_fir(gpad, filt, fir, keep)
        dgain = jnp.zeros((SEGS, LANES), F32)
        dbias = jnp.zeros((SEGS, LANES), F32)
        for t in range(0, count, 8):
            at = t * SEGS
            gn = fir[t : t + 8].reshape(64, LANES) * valid[at : at + 64]
            hat = ghat[at : at + 64, lanes].astype(F32)
            dgain = dgain + jnp.sum((gn * hat).reshape(8, SEGS, LANES), axis=0)
            dbias = dbias + jnp.sum(gn.reshape(8, SEGS, LANES), axis=0)
            gn = gn * ggain
            hgrad[at : at + 64, lanes] = gn
            hs[at : at + 64, :] += gn
            xs[at : at + 64, :] += gn * hat
        small[j, pl.ds(base + ROW_GAIN, 1), :] = fold(dgain)
        small[j, pl.ds(base + ROW_GB0, 1), :] = fold(dbias)
        return carry

    lax.fori_loop(0, hidden // LANES, conv_back, 0)
    for r in range(0, rows, 64):
        a = jnp.sum(hs[r : r + 64, :], axis=1, keepdims=True) * (1.0 / hidden)
        x = jnp.sum(xs[r : r + 64, :], axis=1, keepdims=True) * (1.0 / hidden)
        hs[r : r + 64, :] = jnp.broadcast_to(a, (64, LANES))
        xs[r : r + 64, :] = jnp.broadcast_to(x, (64, LANES))


def up_backward_kernel(layer, scal, dup0, hgrad, hs, xs, small_i, ghat_h, dact1_h, ginv_h, norm_h, *refs):
    sets, refs = refs[:10], refs[10:]
    dn_o, keep_o, send_o, ws, ghat, dact1, ginv, norm, dup1, small, wsem, asem = refs
    rows, hidden = hgrad.shape
    model = norm.shape[1]
    width = 256
    here, there = slab_copies(sets, ws, W_UP, W_ROWS)
    fetch(scal[3] == layer, here, there, wsem)
    own = pl.ds(0, rows)
    blocks = hidden // LANES

    def columns(c):
        lanes = pl.ds(pl.multiple_of(c * LANES, LANES), LANES)
        return [
            pltpu.make_async_copy(ghat_h.at[own, lanes], ghat.at[:, lanes], asem.at[0, c]),
            pltpu.make_async_copy(dact1_h.at[own, lanes], dact1.at[:, lanes], asem.at[1, c]),
        ]

    first = pltpu.make_async_copy(ginv_h, ginv, asem.at[2, 0])
    first.start()
    for c in range(blocks):
        for load in columns(c):
            load.start()
    last = pltpu.make_async_copy(norm_h, norm, asem.at[2, 1])
    last.start()
    small[...] = small_i[...]

    def fold(x):
        return jnp.sum(x, axis=0, keepdims=True)

    first.wait()

    def gate_back(c, carry):
        for load in columns(c):
            load.wait()
        lanes = pl.ds(pl.multiple_of(c * LANES, LANES), LANES)
        b = lax.rem(c, 3)
        j = lax.div(c, 3)
        base = b * BLOCK_ROWS
        s0 = jnp.zeros((1, LANES), F32)
        s1 = jnp.zeros((1, LANES), F32)
        for r in range(0, rows, 64):
            hat = ghat[r : r + 64, lanes].astype(F32)
            gi = ginv[r : r + 64, :] * (hgrad[r : r + 64, lanes] - hs[r : r + 64, :] - hat * xs[r : r + 64, :])
            d1 = (gi * dact1[r : r + 64, lanes].astype(F32)).astype(BF)
            dup1[r : r + 64, lanes] = d1
            s1 = s1 + fold(d1.astype(F32))
            s0 = s0 + fold(dup0[r : r + 64, lanes].astype(F32))
        small[j, pl.ds(base + ROW_UP0, 1), :] = s0
        small[j, pl.ds(base + ROW_UP1, 1), :] = s1
        return carry

    lax.fori_loop(0, hidden // LANES, gate_back, 0)
    landed(here, wsem)
    last.wait()
    dups = (dup0, dup1)
    for hh in range(2):
        w = jnp.concatenate(
            [ws[j, (hh * 3 + b) * model : (hh * 3 + b + 1) * model, :] for j in range(4) for b in range(3)], axis=1
        )
        if hh == 0:
            dn_o[...] = dot(dups[hh][...], w, NT)
        else:
            dn_o[...] += dot(dups[hh][...], w, NT)
    shards = (keep_o.at[0], send_o.at[0], keep_o.at[1], send_o.at[1])
    own_norm = norm[0:rows, :]
    for i in range(hidden // width):
        lo = i * width
        for hh in range(2):
            w = dot(own_norm, dups[hh][:, lo : lo + width], TN).astype(BF)
            for t in range(2):
                j, b = divmod(2 * i + t, 3)
                at = (hh * 3 + b) * model
                shards[j][at : at + model, :] = w[:, t * LANES : (t + 1) * LANES]
    for j in range(4):
        shards[j][UP_ROWS:M_ROWS, :] = small[j].astype(BF)


def input_backward_kernel(layer, scal, sp, h_h, gres_h, dn_h, dq, dkv_own, dkv_got, *refs):
    sets, refs = refs[:8], refs[8:]
    cos_t, sin_t, g_o, nat_o, keep_o, send_o, wq, cs, sn, dall, norm, xhat, xinv, small, h_own, gres, dn_mlp, wsem, tsem = refs
    sp = sp.at[pl.ds(layer, 1)]
    rows, model = h_own.shape
    half = scal[1]
    here, there = shard_copies(sets, wq)
    fetch(scal[3] == layer, here, there, wsem)
    shards = (keep_o.at[0], send_o.at[0], keep_o.at[1], send_o.at[1])
    tables = [
        pltpu.make_async_copy(cos_t.at[half, pl.ds(0, rows), :], cs, tsem.at[0]),
        pltpu.make_async_copy(sin_t.at[half, pl.ds(0, rows), :], sn, tsem.at[1]),
    ]
    tables.append(pltpu.make_async_copy(gres_h, gres, tsem.at[2]))
    tables.append(pltpu.make_async_copy(dn_h, dn_mlp, tsem.at[4]))
    first = pltpu.make_async_copy(h_h, h_own, tsem.at[3])
    first.start()
    for c in tables:
        c.start()
    first.wait()
    gain, bias = wide(sp, ROW_NG), wide(sp, ROW_NB)
    gain_mlp = wide(sp, ROW_NG + 4)
    step = 64
    for r in range(0, rows, step):
        hat, inverse = normalized(h_own[r : r + step, :].astype(F32))
        xhat[r : r + step, :] = hat
        xinv[r : r + step, :] = jnp.broadcast_to(inverse, (step, LANES))
        norm[r : r + step, :] = (hat * gain + bias).astype(BF)
    for c in tables:
        c.wait()
    for j in range(4):
        at = j * 3 * LANES
        dall[:, at : at + LANES] = dq[j]
        dk = dkv_own[j, :, 0:LANES] + dkv_got[j ^ 1, :, 0:LANES].astype(F32)
        dall[:, at + LANES : at + 2 * LANES] = rotate_back(dk, cs[...], sn[...]).astype(BF)
        dv = dkv_own[j, :, LANES:] + dkv_got[j ^ 1, :, LANES:].astype(F32)
        dall[:, at + 2 * LANES : at + 3 * LANES] = dv.astype(BF)
    landed(here, wsem)
    small[...] = jnp.zeros_like(small)
    dn = dot(dall[...], jnp.concatenate([wq[j, i] for j in range(4) for i in range(3)], axis=1), NT)
    dg0 = db0 = dg1 = db1 = jnp.zeros((1, model), F32)
    for r in range(0, rows, step):
        hat = xhat[r : r + step, :]
        a = dn[r : r + step]
        m = dn_mlp[r : r + step, :]
        dg0 = dg0 + jnp.sum(a * hat, axis=0, keepdims=True)
        db0 = db0 + jnp.sum(a, axis=0, keepdims=True)
        dg1 = dg1 + jnp.sum(m * hat, axis=0, keepdims=True)
        db1 = db1 + jnp.sum(m, axis=0, keepdims=True)
        gg = a * gain + m * gain_mlp
        dx = xinv[r : r + step, 0:1] * (
            gg - jnp.mean(gg, axis=1, keepdims=True) - hat * jnp.mean(gg * hat, axis=1, keepdims=True)
        )
        g_o[r : r + step, :] = (gres[r : r + step, :] + dx).astype(BF)
    nat_o[...] = dot(order_matrix(rows, True), g_o[...], NN).astype(BF)
    for j in range(4):
        for n, v in enumerate((dg0, dg1, db0, db1)):
            for i in range(4):
                small[j, 8 + 4 * n + i : 9 + 4 * n + i, :] = v[:, i * LANES : (i + 1) * LANES]
    for j in range(4):
        at = j * 3 * LANES
        d = dall[:, at : at + 3 * LANES]
        w = dot(norm[...], d, TN).astype(BF)
        s = jnp.sum(d.astype(F32), axis=0, keepdims=True)
        for i in range(3):
            lo = i * model
            shards[j][lo : lo + model, :] = w[:, i * LANES : (i + 1) * LANES]
            small[j, i : i + 1, :] = s[:, i * LANES : (i + 1) * LANES]
        shards[j][QKV_ROWS:A_ROWS, :] = small[j].astype(BF)


def assemble_kernel(scal, here, there, out):
    rows = here.shape[1]
    for n in range(8):
        place, half = scal[24 + n], scal[32 + n]
        part = there if n & 1 else here
        out[place, pl.ds(pl.multiple_of(half * rows, rows), rows), :] = part[n >> 1]


def finale_kernel(
    dm_lo, d_hi, m_hi, a, logits,
    qkv_o, out_o, up_o, down_o, bqkv_o, bup_o, gain_o, gbias_o, conv_o, ng_o, nb_o, ob_o, logit_o,
):
    cut = D_ROWS // 2

    def rows_of(lo, hi, at, n, a, b):
        if b <= n:
            return lo[at + a : at + b, :].astype(F32)
        if a >= n:
            return hi[a - n : b - n, :].astype(F32)
        return jnp.concatenate([lo[at + a : at + n, :], hi[0 : b - n, :]], axis=0).astype(F32)

    d_of = functools.partial(rows_of, dm_lo, d_hi, 0, cut)
    m_of = functools.partial(rows_of, dm_lo, m_hi, cut, M_ROWS // 2)
    def a_of(lo, hi):
        return a[lo:hi, :].astype(F32)

    model, shard = up_o.shape[1], up_o.shape[2]
    for i in range(3):
        qkv_o[i] = a_of(i * model, (i + 1) * model)
    for lb in range(4):
        lanes = slice(lb * LANES, (lb + 1) * LANES)
        out_o[:, lanes] = d_of(lb * LANES, (lb + 1) * LANES)
        down_o[:, lanes] = d_of(OUT_ROWS + lb * shard, OUT_ROWS + (lb + 1) * shard)
    for hh in range(2):
        for b in range(3):
            at = (hh * 3 + b) * model
            up_o[hh, :, b * LANES : (b + 1) * LANES] = m_of(at, at + model)
    small = m_of(UP_ROWS, M_ROWS)
    for b in range(3):
        lanes = slice(b * LANES, (b + 1) * LANES)
        at = b * BLOCK_ROWS
        for k in range(TAPS):
            conv_o[k, :, lanes] = small[at + k : at + k + 1]
        bup_o[:, lanes] = small[at + ROW_UP0 : at + ROW_UP0 + 2]
        gain_o[:, lanes] = small[at + ROW_GAIN : at + ROW_GAIN + 1]
        gbias_o[:, lanes] = small[at + ROW_GB0 : at + ROW_GB0 + 2]
    small = a_of(QKV_ROWS, A_ROWS)
    for n in range(3):
        bqkv_o[n] = small[n : n + 1]
    for n in range(2):
        for i in range(4):
            lanes = slice(i * LANES, (i + 1) * LANES)
            ng_o[n, :, lanes] = small[8 + 4 * n + i : 9 + 4 * n + i]
            nb_o[n, :, lanes] = small[16 + 4 * n + i : 17 + 4 * n + i]
    small = d_of(D_SMALL, D_ROWS)
    for i in range(4):
        lanes = slice(i * LANES, (i + 1) * LANES)
        ng_o[2, :, lanes] = small[i : i + 1]
        nb_o[2, :, lanes] = small[4 + i : 5 + i]
        ob_o[0:1, lanes] = small[8 + i : 9 + i]
        ob_o[1:2, lanes] = small[12 + i : 13 + i]
    total_slope = jnp.sum(small[16:17] * binary_weights(True), axis=1, keepdims=True)
    l0, l1 = jnp.full((1, LANES), logits[0], F32), jnp.full((1, LANES), logits[1], F32)
    top = jnp.maximum(l0, l1)
    e0, e1 = jnp.exp(l0 - top), jnp.exp(l1 - top)
    slope = e0 * e1 / ((e0 + e1) * (e0 + e1)) * total_slope
    logit_o[0:1, :] = slope
    logit_o[1:2, :] = -slope


def exchange(x, axis, bit):
    n = lax.axis_size(axis)
    return lax.ppermute(x, axis, [(i, i ^ bit) for i in range(n)])


def fence(*xs):
    return lax.optimization_barrier(xs)


def total(*xs):
    out = xs[0].astype(F32)
    for x in xs[1:]:
        out = out + x.astype(F32)
    return out


def scatter_over_dp(x):
    n = lax.axis_size("dp")
    if n != 4:
        return (lax.psum(x.astype(F32), "dp").astype(BF),)
    d = lax.axis_index("dp")
    x = x.reshape(n, x.shape[0] // n, LANES)
    own = lax.dynamic_index_in_dim(x, d, 0, keepdims=False)
    return (own, *[exchange(lax.dynamic_index_in_dim(x, d ^ k, 0, keepdims=False), "dp", k) for k in range(1, n)])


def gather_over_dp(x):
    n = lax.axis_size("dp")
    return (x, *[exchange(x, "dp", k) for k in range(1, n)]) if n == 4 else (x,)


def in_order(parts):
    if len(parts) == 1:
        return parts[0]
    d = lax.axis_index("dp")
    low, high = (d & 1) == 0, (d & 2) == 0
    pairs = [
        (jnp.where(low, parts[k], parts[k + 1]), jnp.where(low, parts[k + 1], parts[k])) for k in (0, 2)
    ]
    return jnp.concatenate([jnp.where(high, pairs[i][t], pairs[1 - i][t]) for i in range(2) for t in range(2)], axis=0)


def halves(x, owner):
    rows = x.shape[0] // 2
    return jnp.where(owner, x[:rows], x[rows:]), jnp.where(owner, x[rows:], x[:rows])


def rotary_constants(length):
    half_width = HEAD // 2
    freq = np.exp(np.arange(half_width, dtype=np.float32) * np.float32(-math.log(10000.0) / half_width))
    rows = length // 2
    r = np.arange(rows)
    place = (r % SEGS) * (rows // SEGS) + r // SEGS
    cosines, sines = [], []
    for half in range(2):
        t = np.concatenate([half * rows + place, (1 - half) * rows + place]).astype(np.float32)
        angle = (t[:, None] * freq.astype(np.float32)[None, :]).astype(np.float32)
        c, s = np.cos(angle.astype(np.float64)), np.sin(angle.astype(np.float64))
        cosines.append(np.concatenate([c, c, c, c], axis=1))
        sines.append(np.concatenate([-s, s, -s, s], axis=1))
    return np.stack(cosines).astype(np.float32), np.stack(sines).astype(np.float32)


def per_device(frames, lengths, out_grad, *weights):
    (norm_gains, norm_biases, wqkv, bqkv, wout, wup, bup, ggain, gbias, cw, wdown, obias, logits) = [
        w[0] for w in weights
    ]
    micro, utterances, length, model = frames.shape
    n_sec, n_mp = lax.axis_size("section"), lax.axis_size("mp")
    assert utterances == 1 and n_sec == 2 and n_mp == 4 and micro == 4
    rows = length // 2
    shard = wdown.shape[0]
    hidden = shard * n_mp
    every = rows + HALO
    s, m = lax.axis_index("section"), lax.axis_index("mp")
    u = s * 2 + (m >> 1)
    half = m & 1
    own_length = lax.dynamic_index_in_dim(lengths[:, 0], u, 0, keepdims=False)
    ns = np.arange(40)
    xors = np.zeros(40, np.int32)
    xors[4:8] = np.arange(4)
    xors[8:20] = np.arange(12) // 3
    xors[24:32] = ns[:8] >> 1 & 1
    xors[32:40] = ns[:8] & 1
    sec_bits = np.zeros(40, np.int32)
    sec_bits[24:32] = ns[:8] >> 2
    idx = jnp.asarray(ns)
    by_shard = jnp.asarray(xors)
    by_place = (s ^ jnp.asarray(sec_bits)) * 2 + ((m >> 1) ^ jnp.asarray(xors))
    by_half = half ^ jnp.asarray(xors)
    scal = jnp.where(idx < 24, by_shard, jnp.where(idx < 32, by_place, by_half))
    for i, v in enumerate((u, half, own_length, s)):
        scal = jnp.where(idx == i, v, scal)
    scal = scal.astype(jnp.int32)

    x_of = lambda v: exchange(v, "section", 1)
    y_of = lambda v: exchange(v, "mp", 2)
    core_of = lambda v: exchange(v, "mp", 1)
    flat = shape((rows, model), BF)
    rows_f32 = shape((rows, model), F32)
    stat = shape((rows, LANES), F32)
    wide_bf = shape((rows, hidden), BF)
    halo_bf = shape((every, hidden), BF)

    def head_pack(n):
        return shape((4, n, LANES), BF)

    first = s == 0

    q_x, q_y, q_sib = x_of(wqkv), y_of(wqkv), core_of(wqkv)
    packed, u_own, v_own = call(
        pack_kernel,
        [wout, wup, wdown, cw, bup, ggain[None], gbias, bqkv, norm_gains, norm_biases, obias, logits],
        [ANY] * 3 + [VMEM] * 8 + [SMEM],
        [shape((PACK_ROWS, LANES), F32), shape((W_ROWS, LANES), BF), shape((DOWN_ROWS, LANES), BF)],
        [
            pltpu.VMEM(wout.shape, BF),
            pltpu.VMEM(wup.shape, BF),
            pltpu.VMEM(wdown.shape, BF),
            pltpu.SemaphoreType.DMA((3,)),
        ],
        0,
        12,
    )
    packed, q_x, q_y, scal, u_own, v_own = fence(packed, q_x, q_y, scal, u_own, v_own)
    packed_x = x_of(packed)
    q_d = x_of(q_y)
    packed_x, packed = fence(packed_x, packed)
    sections = jnp.stack([jnp.where(first, packed, packed_x), jnp.where(first, packed_x, packed)])
    sc, sections = fence(scal, sections)
    sections_y = y_of(sections)
    h_own, h_oth, g_last = call(
        prologue_kernel,
        [sc, frames, out_grad],
        [SMEM] + [ANY] * 2,
        [flat, flat, flat],
        [pltpu.VMEM((3, rows, model), BF), pltpu.SemaphoreType.DMA((3,))],
        0,
        12,
    )
    h_own, q_d, sections_y, u_own = fence(h_own, q_d, sections_y, u_own)
    u_x, u_y = x_of(u_own), y_of(u_own)
    q_xs, q_ys = core_of(q_x), core_of(q_y)
    sp_a = jnp.stack([sections, sections_y], axis=1)
    sp_b = core_of(sp_a)
    sp = jnp.stack([sp_a, sp_b], axis=2).reshape(2, n_mp, PACK_ROWS, LANES)
    q_ds = core_of(q_d)
    w_qkv = [wqkv, q_sib, q_y, q_ys, q_x, q_xs, q_d, q_ds]

    cos_np, sin_np = rotary_constants(length)
    cos_t, sin_t = jnp.asarray(cos_np), jnp.asarray(sin_np)

    def attention_forward(layer, scal, h_own, h_oth):
        return call(
            functools.partial(attention_forward_kernel, layer),
            [scal, sp, cos_t, sin_t, h_own, h_oth, *w_qkv],
            [SMEM, VMEM, ANY, ANY, VMEM, VMEM] + [ANY] * 8,
            [head_pack(rows), head_pack(length), head_pack(length), head_pack(rows), stat, head_pack(rows)],
            [
                pltpu.VMEM((4, 3, model, LANES), BF),
                pltpu.VMEM((length, LANES), F32),
                pltpu.VMEM((length, LANES), F32),
                pltpu.VMEM((length, model), BF),
                pltpu.VMEM((LANES, rows), F32),
                pltpu.VMEM((4, rows, LANES), BF),
                pltpu.VMEM((4, length, LANES), BF),
                pltpu.VMEM((4, length, LANES), BF),
                pltpu.VMEM((rows, LANES), F32),
                pltpu.SemaphoreType.DMA((4,)),
                pltpu.SemaphoreType.DMA((2,)),
                pltpu.SemaphoreType.DMA((5, 4)),
            ],
            10 * rows * length * model, 24, range(5))

    def mlp_forward(layer, scal, h_own, h_oth):
        return call(
            functools.partial(mlp_forward_kernel, layer),
            [scal, sp, h_own, h_oth, *w_u],
            [SMEM, VMEM, VMEM, VMEM] + [ANY] * 10,
            [halo_bf, halo_bf, halo_bf, halo_bf, wide_bf, wide_bf, stat, shape((every, model), BF), wide_bf],
            [
                pltpu.VMEM((4, W_ROWS - W_UP, LANES), BF),
                pltpu.VMEM((every, hidden), F32),
                pltpu.VMEM((every, hidden), F32),
                pltpu.VMEM((every, LANES), F32),
                pltpu.VMEM((every, LANES), F32),
                pltpu.VMEM((every, LANES), F32),
                pltpu.VMEM((rows // SEGS + 32, SEGS, LANES), F32),
                pltpu.VMEM((72, SEGS, LANES), F32),
                pltpu.VMEM((rows // SEGS, SEGS, LANES), F32),
                pltpu.VMEM((rows // SEGS // 2 + 1, SEGS, LANES), F32),
                pltpu.VMEM((HALO, LANES), F32),
                pltpu.VMEM((every, hidden), BF),
                pltpu.VMEM((every, hidden), BF),
                pltpu.VMEM((every, hidden), BF),
                pltpu.VMEM((every, hidden), BF),
                pltpu.VMEM((rows, hidden), BF),
                pltpu.VMEM((every, model), BF),
                pltpu.SemaphoreType.DMA((8,)),
                pltpu.SemaphoreType.DMA((5 + 3 * hidden // LANES,)),
            ],
            8 * rows * model * hidden, 34, range(8))

    def merge_forward(layer, scal, h_own, mix, gated):
        return call(
            functools.partial(merge_forward_kernel, layer),
            [scal, sp, h_own, mix, gated, *w_u, *w_v],
            [SMEM, VMEM, VMEM, VMEM, VMEM] + [ANY] * 18,
            [flat, flat, rows_f32, stat, rows_f32],
            [
                pltpu.VMEM((4, W_UP, LANES), BF),
                pltpu.VMEM((4, DOWN_ROWS, LANES), BF),
                pltpu.VMEM((rows, model), F32),
                pltpu.VMEM((rows, LANES), F32),
                pltpu.VMEM((rows, model), F32),
                pltpu.SemaphoreType.DMA((8,)),
                pltpu.SemaphoreType.DMA((4,)),
                pltpu.SemaphoreType.DMA((2, 3)),
            ],
            2 * rows * model * hidden, 18, (2, 3, 4))

    att = attention_forward(0, scal, h_own, h_oth)
    att, u_x, u_y, v_late = fence(att, u_x, u_y, v_own)
    cut = W_ROWS - SPLIT
    d1, both = y_of(u_x[:SPLIT]), x_of(jnp.concatenate([u_y[SPLIT:], v_late], axis=0))
    u_sib, u_xs, u_ys = core_of(u_own), core_of(u_x), core_of(u_y)
    d1, both, v_late = fence(d1, both, v_late)
    d1s, both_s = core_of(d1), core_of(both)
    v_x = both[cut:]
    v_y = y_of(v_late)
    v_d = y_of(v_x)
    v_sib = core_of(v_late)
    w_u = [u_own, u_sib, u_y, u_ys, u_x, u_xs, d1, d1s, both, both_s]
    mlp0 = mlp_forward(0, scal, h_own, h_oth)
    mlp0, v_y, v_d, v_sib = fence(mlp0, v_y, v_d, v_sib)
    v_ys, v_ds = core_of(v_y), core_of(v_d)
    w_v = [v_own, v_sib, v_y, v_ys, both, both_s, v_d, v_ds]
    top0 = merge_forward(0, scal, h_own, att[5], mlp0[8])
    saved = [(h_own, att, mlp0, top0)]
    h_own, h_oth = top0[0], core_of(top0[0])
    att = attention_forward(1, scal, h_own, h_oth)
    mlp1 = mlp_forward(1, scal, h_own, h_oth)
    top1 = call(
        functools.partial(merge_turn_kernel, 1),
        [scal, sp, h_own, att[5], mlp1[8], g_last, *w_u, *w_v],
        [SMEM] + [VMEM] * 5 + [ANY] * 18,
        [flat, rows_f32, flat, flat, shape((HALO, model), BF), shape((2, D_ROWS, LANES), BF), shape((2, D_ROWS, LANES), BF)],
        [
            pltpu.VMEM((4, W_UP, LANES), BF),
            pltpu.VMEM((4, DOWN_ROWS, LANES), BF),
            pltpu.VMEM((rows, model), BF),
            pltpu.VMEM((64, LANES), F32),
            pltpu.SemaphoreType.DMA((8,)),
            pltpu.SemaphoreType.DMA((4,)),
        ],
        0,
        22,
        (),
        (1, 2, 5, 6),
    )
    saved.append((h_own, att, mlp1, top1))

    def merge_backward(layer, scal, g):
        h, att, mlp, top = saved[layer]
        return call(
            functools.partial(merge_backward_kernel, layer),
            [scal, sp, g, top[2], top[3], top[4], att[3], mlp[5]],
            [SMEM, VMEM, VMEM] + [ANY] * 5,
            [rows_f32, flat, flat, shape((HALO, model), BF),
             shape((2, D_ROWS, LANES), BF), shape((2, D_ROWS, LANES), BF)],
            [
                pltpu.VMEM((rows, model), F32),
                pltpu.VMEM((rows, LANES), F32),
                pltpu.VMEM((rows, model), F32),
                pltpu.VMEM((4, rows, LANES), BF),
                pltpu.VMEM((rows, hidden), BF),
                pltpu.VMEM((64, LANES), F32),
                pltpu.SemaphoreType.DMA((4, 4)),
            ],
            2 * rows * model * (hidden + model), 16, (), (0, 1, 4, 5))

    def conv_backward(layer, scal, gbr, halo_in):
        mlp = saved[layer][2]
        return call(
            functools.partial(conv_backward_kernel, layer),
            [scal, sp, gbr, halo_in, mlp[0], mlp[1], mlp[3], mlp[4], *w_v],
            [SMEM, VMEM, VMEM, VMEM] + [ANY] * 12,
            [wide_bf, shape((rows, hidden), F32), stat, stat, shape((4, LANES, LANES), F32)],
            [
                pltpu.VMEM((4, DOWN_ROWS, LANES), BF),
                pltpu.VMEM((every, hidden), BF),
                pltpu.VMEM((every, hidden), BF),
                pltpu.VMEM((every, hidden), BF),
                pltpu.VMEM((rows, hidden), BF),
                pltpu.VMEM((rows // SEGS + 32, SEGS, LANES), F32),
                pltpu.VMEM((rows // SEGS + 32, SEGS, LANES), F32),
                pltpu.VMEM((72, SEGS, LANES), F32),
                pltpu.VMEM((rows // SEGS, SEGS, LANES), F32),
                pltpu.VMEM((rows // SEGS // 2 + 1, SEGS, LANES), F32),
                pltpu.VMEM((HALO, LANES), F32),
                pltpu.VMEM((every, hidden), F32),
                pltpu.VMEM((every, model), BF),
                pltpu.SemaphoreType.DMA((4,)),
                pltpu.SemaphoreType.DMA((4, hidden // 256)),
            ],
            0,
            30,
        )

    def up_backward(layer, scal, dup0, hgrad, hs, xs, small):
        mlp = saved[layer][2]
        return call(
            functools.partial(up_backward_kernel, layer),
            [scal, dup0, hgrad, hs, xs, small, mlp[3], mlp[2], mlp[6], mlp[7], *w_u],
            [SMEM] + [VMEM] * 5 + [ANY] * 14,
            [rows_f32, shape((2, M_ROWS, LANES), BF), shape((2, M_ROWS, LANES), BF)],
            [
                pltpu.VMEM((4, W_ROWS - W_UP, LANES), BF),
                pltpu.VMEM((rows, hidden), BF),
                pltpu.VMEM((rows, hidden), BF),
                pltpu.VMEM((rows, LANES), F32),
                pltpu.VMEM((every, model), BF),
                pltpu.VMEM((rows, hidden), BF),
                pltpu.VMEM((4, LANES, LANES), F32),
                pltpu.SemaphoreType.DMA((8,)),
                pltpu.SemaphoreType.DMA((3, hidden // LANES)),
            ],
            0,
            30,
            (),
            (0, 1, 2),
        )

    def attention_backward(layer, scal, gatt):
        att = saved[layer][1]
        return call(
            functools.partial(attention_backward_kernel, layer),
            [scal, gatt, *att[:5], *w_u, cos_t, sin_t],
            [SMEM] + [ANY] * 18,
            [head_pack(rows), shape((4, rows, 2 * LANES), F32), shape((4, rows, 2 * LANES), BF)],
            [
                pltpu.VMEM((4, W_UP, LANES), BF),
                pltpu.VMEM((rows, LANES), F32),
                pltpu.VMEM((rows, LANES), F32),
                pltpu.VMEM((length, 2 * rows), BF),
                pltpu.VMEM((length, 2 * rows), BF),
                pltpu.VMEM((2 * rows, LANES), BF),
                pltpu.VMEM((2 * rows, LANES), BF),
                pltpu.VMEM((4, rows, LANES), BF),
                pltpu.VMEM((4, length, LANES), BF),
                pltpu.VMEM((4, length, LANES), BF),
                pltpu.VMEM((4, rows, LANES), BF),
                pltpu.VMEM((rows, LANES), F32),
                pltpu.VMEM((rows, model), BF),
                pltpu.SemaphoreType.DMA((4,)),
                pltpu.SemaphoreType.DMA((8,)),
            ],
            12 * rows * length * model, 26)

    def input_backward(layer, scal, gres, dn_mlp, dq, dkv_own, dkv_got):
        h = saved[layer][0]
        return call(
            functools.partial(input_backward_kernel, layer),
            [scal, sp, h, gres, dn_mlp, dq, dkv_own, dkv_got, *w_qkv, cos_t, sin_t],
            [SMEM, VMEM, ANY, ANY, ANY] + [VMEM] * 3 + [ANY] * 10,
            [flat, flat, shape((2, A_ROWS, LANES), BF), shape((2, A_ROWS, LANES), BF)],
            [
                pltpu.VMEM((4, 3, model, LANES), BF),
                pltpu.VMEM((rows, LANES), F32),
                pltpu.VMEM((rows, LANES), F32),
                pltpu.VMEM((rows, 12 * LANES), BF),
                pltpu.VMEM((rows, model), BF),
                pltpu.VMEM((rows, model), F32),
                pltpu.VMEM((rows, LANES), F32),
                pltpu.VMEM((4, 64, LANES), F32),
                pltpu.VMEM((rows, model), BF),
                pltpu.VMEM((rows, model), F32),
                pltpu.VMEM((rows, model), F32),
                pltpu.SemaphoreType.DMA((4,)),
                pltpu.SemaphoreType.DMA((5,)),
            ],
            14 * rows * model * model, 24, (), (2, 3))

    owner1 = jnp.logical_not(first)
    natural0, natural1 = top0[1], top1[0]
    out_keep = jnp.where(first, natural0, natural1)
    out_send = jnp.where(first, natural1, natural0)
    gres, gatt, gbr, halo_out, d_keep, d_send = top1[1:]
    gbr, halo_out, d_send, out_send, out_keep = fence(gbr, halo_out, d_send, out_send, out_keep)
    halo_in = core_of(halo_out)
    sc, gbr, halo_in, out_send, out_keep, d_send = fence(scal, gbr, halo_in, out_send, out_keep, d_send)
    d_got, out_got, out_y = core_of(d_send), x_of(out_send), y_of(out_keep)
    part = conv_backward(1, sc, gbr, halo_in)
    part, d_got, out_got, out_y = fence(part, d_got, out_got, out_y)
    d_away = total(d_keep[1], d_got[1]).astype(BF)
    sc, d_away = fence(scal, d_away)
    d_y = y_of(d_away)
    dn_mlp, m_keep, m_send = up_backward(1, sc, *part)
    gatt, d_y, m_send = fence(gatt, d_y, m_send)
    m_got = core_of(m_send)
    d1_mine, d_give = halves(total(d_keep[0], d_got[0], d_y), owner1)
    m_away = total(m_keep[1], m_got[1]).astype(BF)
    sc, d_give, m_away = fence(scal, d_give.astype(BF), m_away)
    m_y = y_of(m_away)
    d_x = x_of(d_give)
    dq, dkv_own, dkv_oth = attention_backward(1, sc, gatt)
    dq, dkv_oth, m_y, d_x = fence(dq, dkv_oth, m_y, d_x)
    dkv_got = core_of(dkv_oth)
    m1_mine, m_give = halves(total(m_keep[0], m_got[0], m_y), owner1)
    sc, m_give, out_got = fence(scal, m_give.astype(BF), out_got)
    m_x = x_of(m_give)
    out_yg = y_of(out_got)
    g, ingrad1, a_keep, a_send = input_backward(1, sc, gres, dn_mlp, dq, dkv_own, dkv_got)

    g, a_send, m_x = fence(g, a_send, m_x)
    a_got = core_of(a_send)
    dm1_half = jnp.concatenate([total(d1_mine, d_x), total(m1_mine, m_x)], axis=0).astype(BF)
    sc, dm1_half = fence(scal, dm1_half)
    dm1_half = lax.psum(dm1_half, "dp")
    gres, gatt, gbr, halo_out, d0_keep, d0_send = merge_backward(0, sc, g)
    gbr, halo_out, d0_send, a_got, out_yg = fence(gbr, halo_out, d0_send, a_got, out_yg)
    halo_in, d0_got = core_of(halo_out), core_of(d0_send)
    a_away = total(a_keep[1], a_got[1]).astype(BF)
    gbr, halo_in, d0_got, a_away = fence(gbr, halo_in, d0_got, a_away)
    d_away = total(d0_keep[1], d0_got[1]).astype(BF)
    sc, a_away, d_away = fence(scal, a_away, d_away)
    a_y, d_y = y_of(a_away), y_of(d_away)
    part = conv_backward(0, sc, gbr, halo_in)
    part, a_y, d_y = fence(part, a_y, d_y)
    a_mine, a_give = halves(total(a_keep[0], a_got[0], a_y), owner1)
    d_mine, d_give = halves(total(d0_keep[0], d0_got[0], d_y), first)
    sc, give = fence(scal, jnp.concatenate([a_give, d_give], axis=0).astype(BF))
    got = x_of(give)
    dn_mlp, m0_keep, m0_send = up_backward(0, sc, *part)
    gatt, got, m0_send, dm1_half = fence(gatt, got, m0_send, dm1_half)
    m0_got = core_of(m0_send)
    ad_half = total(jnp.concatenate([a_mine, d_mine], axis=0), got).astype(BF)
    m_away = total(m0_keep[1], m0_got[1]).astype(BF)
    sc, m_away, ad_half = fence(scal, m_away, ad_half)
    m_y = y_of(m_away)
    ad_terms = scatter_over_dp(ad_half)
    dq, dkv_own, dkv_oth = attention_backward(0, sc, gatt)
    dq, dkv_oth, m_y, ad_terms = fence(dq, dkv_oth, m_y, ad_terms)
    dkv_got = core_of(dkv_oth)
    m_mine, m_give = halves(total(m0_keep[0], m0_got[0], m_y), first)
    sc, m_give, ad_half = fence(scal, m_give.astype(BF), total(*ad_terms).astype(BF))
    m_x = x_of(m_give)
    ad_half = gather_over_dp(ad_half)
    g, ingrad0, a_keep, a_send = input_backward(0, sc, gres, dn_mlp, dq, dkv_own, dkv_got)

    ingrad0, a_send, m_x, ad_half, out_yg = fence(ingrad0, a_send, m_x, ad_half, out_yg)
    a_got = core_of(a_send)
    in_keep = jnp.where(first, ingrad0, ingrad1)
    in_got = x_of(jnp.where(first, ingrad1, ingrad0))
    m_terms = scatter_over_dp(total(m_mine, m_x).astype(BF))
    a_away = total(a_keep[1], a_got[1]).astype(BF)
    a_away, m_terms, in_keep = fence(a_away, m_terms, in_keep)
    a_y = y_of(a_away)
    in_y = y_of(in_keep)
    out_half = jnp.stack([out_keep, out_y, out_got, out_yg])
    out_other = core_of(out_half)
    m_parts = gather_over_dp(total(*m_terms).astype(BF))
    a_y, m_parts, in_got, ad_half, out_other = fence(a_y, m_parts, in_got, ad_half, out_other)
    a_sum = total(a_keep[0], a_got[0], a_y).astype(BF)
    a_x = x_of(a_sum)
    in_yg = y_of(in_got)
    ad_half = in_order(ad_half)
    a1_half = ad_half[: A_ROWS // 2]
    dm0_half = jnp.concatenate([ad_half[A_ROWS // 2 :], in_order(m_parts)], axis=0)
    dm_lo = jnp.where(first, dm0_half, dm1_half)
    cut = D_ROWS // 2
    away = jnp.where(first, dm1_half, dm0_half)
    m_back = x_of(away[cut:])
    d_away = jnp.concatenate([away[:cut], a1_half], axis=0)
    a_x, in_y = fence(a_x, in_y)
    a_terms = scatter_over_dp(total(a_sum, a_x).astype(BF))
    a_terms, in_yg, in_y, in_got, m_back, d_away = fence(a_terms, in_yg, in_y, in_got, m_back, d_away)
    d_back = x_of(d_away)
    a_parts = gather_over_dp(total(*a_terms).astype(BF))
    in_half = jnp.stack([in_keep, in_y, in_got, in_yg])
    in_other = core_of(in_half)

    def assemble(here, there):
        return call(
            assemble_kernel, [scal, here, there], [SMEM, VMEM, VMEM], [shape((micro, length, model), BF)], [], 0, 10
        )[0]

    layer_out = assemble(out_half, out_other)
    input_grad = assemble(in_half, in_other)

    a_parts, layer_out, input_grad, d_back = fence(a_parts, layer_out, input_grad, d_back)
    a_whole = jnp.where(first, in_order(a_parts), jnp.concatenate([a1_half, d_back[cut:]], axis=0))
    (g_qkv, g_out, g_up, g_down, g_bqkv, g_bup, g_gain, g_gbias, g_conv, g_ng, g_nb, g_ob, g_logit) = call(
        finale_kernel,
        [dm_lo, d_back, m_back, a_whole, logits],
        [VMEM] * 4 + [SMEM],
        [shape((3, model, LANES), F32), shape((LANES, model), F32), shape((2, model, shard), F32),
         shape((shard, model), F32), shape((3, 1, LANES), F32), shape((2, shard), F32), shape((1, shard), F32),
         shape((2, shard), F32), shape((TAPS, 1, shard), F32), shape((3, 1, model), F32), shape((3, 1, model), F32),
         shape((2, model), F32), shape((2, LANES), F32)],
        [],
        0,
        16,
    )
    outs = (
        layer_out.reshape(micro, 1, length, model),
        input_grad.reshape(micro, 1, length, model),
        g_ng[:, 0],
        g_nb[:, 0],
        g_qkv,
        g_bqkv[:, 0],
        g_out,
        g_up,
        g_bup,
        g_gain[0],
        g_gbias,
        g_conv[:, 0],
        g_down,
        g_ob,
        g_logit[:, 0],
    )
    return tuple(x[None] for x in outs)


def solution(mesh):
    placed = (
        P(None, "dp", None, None),
        P(None, "dp"),
        P(None, "dp", None, None),
        P("section", None, None),
        P("section", None, None),
        P("section", None, None, "mp"),
        P("section", None, "mp"),
        P("section", "mp", None),
        P("section", None, None, "mp"),
        P("section", None, "mp"),
        P("section", "mp"),
        P("section", None, "mp"),
        P("section", None, "mp"),
        P("section", "mp", None),
        P("section", None, None),
        P("section", None),
    )
    return jax.shard_map(
        per_device,
        mesh=mesh,
        in_specs=placed,
        out_specs=(
            P("section", None, "dp", None, None),
            P("section", None, "dp", None, None),
            P("section", None, None),
            P("section", None, None),
            P("section", None, None, "mp"),
            P("section", None, "mp"),
            P("section", "mp", None),
            P("section", None, None, "mp"),
            P("section", None, "mp"),
            P("section", "mp"),
            P("section", None, "mp"),
            P("section", None, "mp"),
            P("section", "mp", None),
            P("section", None, None),
            P("section", None),
        ),
        check_vma=False,
    )
```

```python
import functools
import math

import jax
import jax.numpy as jnp
import numpy as np
from jax import lax
from jax.experimental import pallas as pl
from jax.experimental.pallas import tpu as pltpu
from jax.sharding import PartitionSpec as P

BF = jnp.bfloat16
F32 = jnp.float32
HEAD = 64
LANES = 128
SEGS = 8
HALO = 16
EPS = 1e-05
NEG = -1000000000.0
NN = (((1,), (0,)), ((), ()))
NT = (((1,), (1,)), ((), ()))
TN = (((0,), (0,)), ((), ()))

TAPS = 31
BLOCK_ROWS = 40
ROW_UP0, ROW_UP1, ROW_GAIN, ROW_GB0, ROW_GB1 = 31, 32, 33, 34, 35
ROW_QKV = 120
ROW_NG, ROW_NB, ROW_OB, ROW_LOGIT = 128, 140, 152, 160
PACK_ROWS = 168

OUT_ROWS, DOWN_ROWS, UP_ROWS, QKV_ROWS = 512, 1536, 3072, 1536
D_SMALL = OUT_ROWS + DOWN_ROWS
D_ROWS = D_SMALL + 64
M_ROWS = UP_ROWS + 128
A_ROWS = QKV_ROWS + 64

W_UP, W_ROWS = 512, 3584
SPLIT = 2560

VMEM = pl.BlockSpec(memory_space=pltpu.VMEM)
SMEM = pl.BlockSpec(memory_space=pltpu.SMEM)
ANY = pl.BlockSpec(memory_space=pltpu.HBM)


def dot(a, b, dims):
    return lax.dot_general(a, b, dims, preferred_element_type=F32)


def call(kernel, ins, in_specs, outs, scratch, flops, mib, far=(), home=()):
    ins = [pltpu.with_memory_space_constraint(x, pltpu.HBM) if p is ANY else x for x, p in zip(ins, in_specs)]
    return pl.pallas_call(
        kernel,
        in_specs=in_specs,
        out_specs=[ANY if i in far else VMEM for i in range(len(outs))],
        out_shape=[pltpu.HBM(x.shape, x.dtype) if i in far or i in home else x for i, x in enumerate(outs)],
        scratch_shapes=scratch,
        compiler_params=pltpu.CompilerParams(vmem_limit_bytes=mib << 20),
        cost_estimate=pl.CostEstimate(flops=1, bytes_accessed=1, transcendentals=0),
    )(*ins)


def shape(dims, dtype):
    return jax.ShapeDtypeStruct(dims, dtype)


def fetch(flag, here, there, sems):
    @pl.when(flag)
    def _():
        for i, (a, d) in enumerate(here):
            pltpu.make_async_copy(a, d, sems.at[i]).start()

    @pl.when(jnp.logical_not(flag))
    def _():
        for i, (a, d) in enumerate(there):
            pltpu.make_async_copy(a, d, sems.at[i]).start()


def landed(pairs, sems):
    for i, (a, d) in enumerate(pairs):
        pltpu.make_async_copy(a, d, sems.at[i]).wait()


def slab_copies(sets, dst, lo, hi):
    here, there = [], []
    for j in range(4):
        for a, b in ((lo, min(hi, SPLIT)), (max(lo, SPLIT), hi)):
            if a >= b:
                continue
            d = dst.at[j, pl.ds(a - lo, b - a), :]
            here.append((sets[j].at[pl.ds(a, b - a), :], d))
            if j < 2:
                there.append((sets[4 + j].at[pl.ds(a, b - a), :], d))
            elif a < SPLIT:
                there.append((sets[4 + j].at[pl.ds(a, b - a), :], d))
            else:
                there.append((sets[6 + j].at[pl.ds(a - SPLIT, b - a), :], d))
    return here, there


def down_copies(sets, dst):
    here, there = shard_copies(sets, dst)
    rows = dst.shape[1]
    for j in range(2):
        there[j] = (sets[4 + j].at[pl.ds(W_ROWS - SPLIT, rows), :], dst.at[j])
    return here, there


def shard_copies(sets, dst):
    return [(sets[j], dst.at[j]) for j in range(4)], [(sets[4 + j], dst.at[j]) for j in range(4)]


def wide(sp, row, count=4):
    return jnp.concatenate([sp[0, 0, row + i : row + i + 1, :] for i in range(count)], axis=1)


def branch_weights(sp):
    l0 = sp[0, 0, ROW_LOGIT : ROW_LOGIT + 1, :]
    l1 = sp[0, 0, ROW_LOGIT + 1 : ROW_LOGIT + 2, :]
    top = jnp.maximum(l0, l1)
    e0, e1 = jnp.exp(l0 - top), jnp.exp(l1 - top)
    total = e0 + e1
    return jnp.concatenate([e0 / total] * 4, axis=1), jnp.concatenate([e1 / total] * 4, axis=1)


def normalized(x):
    center = jnp.mean(x, axis=-1, keepdims=True)
    d = x - center
    inverse = lax.rsqrt(jnp.mean(d * d, axis=-1, keepdims=True) + EPS)
    return d * inverse, inverse


def frame_of(row, half, rows):
    return half * rows + (row & (SEGS - 1)) * (rows // SEGS) + (row >> 3)


def order_matrix(rows, back):
    r = lax.broadcasted_iota(jnp.int32, (rows, rows), 1 if back else 0)
    t = lax.broadcasted_iota(jnp.int32, (rows, rows), 0 if back else 1)
    return jnp.where(frame_of(r, 0, rows) == t, 1.0, 0.0).astype(BF)


def halo_pick(rows, start_seg_even):
    start, seg = start_seg_even
    i = lax.broadcasted_iota(jnp.int32, (HALO, rows), 0)
    r = lax.broadcasted_iota(jnp.int32, (HALO, rows), 1)
    return jnp.where(r == (i + start) * SEGS + seg, 1.0, 0.0).astype(BF)


def swap_halves(x):
    lane = lax.broadcasted_iota(jnp.int32, x.shape, 1)
    return jnp.where(
        (lane & (HEAD - 1)) < HEAD // 2,
        pltpu.roll(x, LANES - HEAD // 2, 1),
        pltpu.roll(x, HEAD // 2, 1),
    )


def rotate(x, cosine, sine):
    return x * cosine + swap_halves(x) * sine


def rotate_back(x, cosine, sine):
    return x * cosine - swap_halves(x) * sine


def pieces(x):
    hi = x.astype(BF).astype(F32)
    rest = x - hi
    mid = rest.astype(BF).astype(F32)
    return hi, mid, rest - mid


def pack_kernel(
    wout_h, wup_h, wdown_h, cw, bup, ggain, gbias, bqkv, ngain, nbias, obias, logits,
    sp_o, u_o, v_o, wout, wup, wdown, sems,
):
    loads = [
        pltpu.make_async_copy(a, b, sems.at[i])
        for i, (a, b) in enumerate(((wup_h, wup), (wdown_h, wdown), (wout_h, wout)))
    ]
    for c in loads:
        c.start()
    sp_o[...] = jnp.zeros_like(sp_o)
    for b in range(3):
        lanes = slice(b * LANES, (b + 1) * LANES)
        at = b * BLOCK_ROWS
        sp_o[at : at + TAPS, :] = cw[:, lanes]
        sp_o[at + ROW_UP0 : at + ROW_UP0 + 2, :] = bup[:, lanes]
        sp_o[at + ROW_GAIN : at + ROW_GAIN + 1, :] = ggain[:, lanes]
        sp_o[at + ROW_GB0 : at + ROW_GB0 + 2, :] = gbias[:, lanes]
    sp_o[ROW_QKV : ROW_QKV + 3, :] = bqkv[...]
    for i in range(4):
        lanes = slice(i * LANES, (i + 1) * LANES)
        for n in range(3):
            sp_o[ROW_NG + 4 * n + i : ROW_NG + 4 * n + i + 1, :] = ngain[n : n + 1, lanes]
            sp_o[ROW_NB + 4 * n + i : ROW_NB + 4 * n + i + 1, :] = nbias[n : n + 1, lanes]
        for n in range(2):
            sp_o[ROW_OB + 4 * n + i : ROW_OB + 4 * n + i + 1, :] = obias[n : n + 1, lanes]
    for n in range(2):
        sp_o[ROW_LOGIT + n : ROW_LOGIT + n + 1, :] = jnp.full((1, LANES), logits[n], F32)
    for c in loads:
        c.wait()
    model, shard = wup.shape[1], wup.shape[2]
    for lb in range(4):
        lanes = slice(lb * LANES, (lb + 1) * LANES)
        u_o[lb * LANES : (lb + 1) * LANES, :] = wout[:, lanes]
        v_o[lb * shard : (lb + 1) * shard, :] = wdown[:, lanes]
    for hh in range(2):
        for b in range(3):
            at = W_UP + (hh * 3 + b) * model
            u_o[at : at + model, :] = wup[hh, :, b * LANES : (b + 1) * LANES]


def prologue_kernel(scal, frames, cotangent, own_o, oth_o, g_o, buf, sems):
    rows = own_o.shape[0]
    u, half = scal[0], scal[1]
    mine = pl.ds(pl.multiple_of(half * rows, rows), rows)
    other = pl.ds(pl.multiple_of((1 - half) * rows, rows), rows)
    copies = [
        pltpu.make_async_copy(frames.at[u, 0, mine, :], buf.at[0], sems.at[0]),
        pltpu.make_async_copy(frames.at[u, 0, other, :], buf.at[1], sems.at[1]),
        pltpu.make_async_copy(cotangent.at[u, 0, mine, :], buf.at[2], sems.at[2]),
    ]
    for c in copies:
        c.start()
    order = order_matrix(rows, False)
    for c, i, out in zip(copies, range(3), (own_o, oth_o, g_o)):
        c.wait()
        out[...] = dot(order, buf[i], NN).astype(BF)


def attention_forward_kernel(layer, scal, sp, cos_t, sin_t, h_own, h_oth, *refs):
    sets, refs = refs[:8], refs[8:]
    q_h, k_h, v_h, mix_h, lse_h, mix_o, w_s, cs, sn, norm, lse_s, q_o, k_o, v_o, lse_o, wsem, tsem, osem = refs
    sp = sp.at[pl.ds(layer, 1)]
    rows, model = h_own.shape
    half, length = scal[1], scal[2]
    here, there = shard_copies(sets, w_s)
    fetch(scal[3] == layer, here, there, wsem)
    tables = [
        pltpu.make_async_copy(cos_t.at[half], cs, tsem.at[0]),
        pltpu.make_async_copy(sin_t.at[half], sn, tsem.at[1]),
    ]
    for c in tables:
        c.start()
    gain, bias = wide(sp, ROW_NG), wide(sp, ROW_NB)
    step = 64
    for src, base in ((h_own, 0), (h_oth, rows)):
        for r in range(0, rows, step):
            hat, unused = normalized(src[r : r + step, :].astype(F32))
            norm[base + r : base + r + step, :] = (hat * gain + bias).astype(BF)
    lse_s[...] = jnp.zeros_like(lse_s)
    for c in tables:
        c.wait()
    landed(here, wsem)
    total = 2 * rows
    row = lax.broadcasted_iota(jnp.int32, (total, LANES), 0)
    part = jnp.where(row < rows, half, 1 - half)
    position = frame_of(row & (rows - 1), part, rows)
    mask = jnp.where(position < length, 0.0, NEG)
    lane_k = lax.broadcasted_iota(jnp.int32, (total, LANES), 1)
    lane_q = lax.broadcasted_iota(jnp.int32, (rows, LANES), 1)

    def stores(j):
        pairs = ((q_o, q_h), (k_o, k_h), (v_o, v_h), (mix_o, mix_h))
        return [pltpu.make_async_copy(a.at[j], b.at[j], osem.at[j, i]) for i, (a, b) in enumerate(pairs)]

    def shard(j):
        mj = scal[4 + j]
        bq = sp[0, mj, ROW_QKV : ROW_QKV + 1, :]
        bk = sp[0, mj, ROW_QKV + 1 : ROW_QKV + 2, :]
        bv = sp[0, mj, ROW_QKV + 2 : ROW_QKV + 3, :]
        everything = norm[...]
        q = rotate(dot(norm[:rows, :], w_s[j, 0], NN) + bq, cs[:rows, :], sn[:rows, :])
        q = q.astype(BF).astype(F32) * (1.0 / math.sqrt(HEAD))
        k = rotate(dot(everything, w_s[j, 1], NN) + bk, cs[...], sn[...]).astype(BF)
        v = (dot(everything, w_s[j, 2], NN) + bv).astype(BF)
        q_o[j] = q.astype(BF)
        k_o[j] = k
        v_o[j] = v
        kf = k.astype(F32)
        vt = v.astype(F32).T.astype(BF)
        outs = []
        work = []
        for hd in range(2):
            spare = (1 - hd) * HEAD
            qm = jnp.where((lane_q >> 6) == hd, q, jnp.where(lane_q == spare, 1.0, 0.0)).astype(BF)
            km = jnp.where((lane_k >> 6) == hd, kf, jnp.where(lane_k == spare, mask, 0.0)).astype(BF)
            work.append((km, qm))
        score = dot(*work[0], NT)
        for hd in range(2):
            s = score
            if hd == 0:
                score = dot(*work[1], NT)
            top = jnp.max(s, axis=0, keepdims=True)
            p = jnp.exp(s - top)
            den = jnp.sum(p, axis=0, keepdims=True)
            p = (p * (1.0 / den)).astype(BF)
            outs.append(dot(vt[hd * HEAD : (hd + 1) * HEAD, :], p, NN))
            lse_s[2 * j + hd : 2 * j + hd + 1, :] = top + jnp.log(den)
        mix_o[j] = jnp.concatenate(outs, axis=0).T.astype(BF)
        for c in stores(j):
            c.start()

    for j in range(4):
        shard(j)
    lse_o[...] = lse_s[...].T
    last = pltpu.make_async_copy(lse_o, lse_h, osem.at[4, 0])
    last.start()
    for j in range(4):
        for c in stores(j):
            c.wait()
    last.wait()


def gelu_parts(u):
    d = 1.0 + (0.3275911 / math.sqrt(2.0)) * jnp.abs(u)
    t = pl.reciprocal(d, approx=True)
    t = t * (2.0 - d * t)
    e = jnp.exp2((-0.5 / math.log(2.0)) * (u * u))
    half = [0.5 * c for c in (1.061405429, -1.453152027, 1.421413741, -0.284496736, 0.254829592)]
    poly = ((((half[0] * t + half[1]) * t + half[2]) * t + half[3]) * t + half[4]) * t
    tail = poly * e
    phi = jnp.where(u >= 0, 1.0 - tail, tail)
    return u * phi, phi + (u * e) * (1.0 / math.sqrt(2.0 * math.pi))


PHASES = ((0,), (2,), (2, 4), (1,), (3,), (3, 5), (1, 2), (3, 4), (3, 4, 5, 6))
TAP_PHASES = ((0,), (2,), (0, 2), (1,), (3,), (1, 3), (0, 1), (2, 3), (0, 1, 2, 3))


def phase(ref, rows, n):
    out = ref[4 * n + rows[0]]
    for r in rows[1:]:
        out = out + ref[4 * n + r]
    return out


def correlate(taps, xs, count):
    accs = [None] * count
    for m, tap in enumerate(taps):
        for n in range(count):
            term = tap * xs[n + m]
            accs[n] = term if accs[n] is None else accs[n] + term
    return accs


def unfold(q0, q1, q2):
    out = []
    for n in range(len(q2)):
        out.append(q0[n] + q1[n])
        out.append(q2[n] - (q0[n + 1] + q1[n]))
    if len(q1) > len(q2):
        out.append(q0[len(q2)] + q1[len(q2)])
    return out


def fill_filters(filt, row):
    for m in range(8):
        w = [
            jnp.broadcast_to(row(4 * m + r), (SEGS, LANES)) if 4 * m + r < TAPS else jnp.zeros((SEGS, LANES), F32)
            for r in range(4)
        ]
        for i, rows in enumerate(TAP_PHASES):
            out = w[rows[0]]
            for r in rows[1:]:
                out = out + w[r]
            filt[i * 8 + m] = out


def fast_fir(pad, filt, out, keep):
    count = out.shape[0]
    half = count // 2
    for g in range(3):
        qs = []
        for i in range(3):
            n = half // 2 + 1 if i == 0 or (i == 1 and g == 0) else half // 2
            xs = [phase(pad, PHASES[3 * g + i], x) for x in range(n + 7)]
            qs.append(correlate([filt[(3 * g + i) * 8 + m] for m in range(8)], xs, n))
        p = unfold(*qs)
        for n in range(len(p)):
            if g == 0:
                keep[n] = p[n]
            elif g == 1:
                out[2 * n] = keep[n] + p[n]
                out[2 * n + 1] = keep[n + 1] + p[n]
            else:
                out[2 * n + 1] = p[n] - out[2 * n + 1]


def tap_sums(gpad, xpad, count):
    ps = []
    for g in range(3):
        qs = []
        for i in range(3):
            rows = [15 + r for r in TAP_PHASES[3 * g + i]]
            n = 9 if i == 0 else 8
            steps = count // 4
            xs = [phase(xpad, PHASES[3 * g + i], x) for x in range(n + steps - 1)]
            qs.append(correlate([phase(gpad, rows, x) for x in range(steps)], xs, n))
        ps.append(unfold(*qs))
    out = []
    for m in range(16):
        out.append(ps[0][m] + ps[1][m])
        if m < 15:
            out.append(ps[2][m] - (ps[0][m + 1] + ps[1][m]))
    return out


def halo_pads(pad, block, halo_ref, half, right_is_even):
    count = block.shape[0]
    pad[15 : 15 + count] = block
    pad[30 + count : 32 + count] = jnp.zeros((2, SEGS, LANES), F32)
    seg = lax.broadcasted_iota(jnp.int32, (SEGS, LANES), 0)
    from_left = half.astype(F32)
    from_right = 1.0 - from_left
    for i in range(15):
        tail = pltpu.roll(block[count - 15 + i], 1, 0)
        edge = jnp.broadcast_to(halo_ref[i + 1 : i + 2, :], (SEGS, LANES)) * from_left
        pad[i] = jnp.where(seg == 0, edge, tail)
        head = pltpu.roll(block[i], SEGS - 1, 0)
        edge = jnp.broadcast_to(halo_ref[i : i + 1, :], (SEGS, LANES)) * from_right
        pad[15 + count + i] = jnp.where(seg == SEGS - 1, edge, head)


def mlp_forward_kernel(layer, scal, sp, h_own, h_oth, *refs):
    sets, refs = refs[:10], refs[10:]
    (act0_h, dact0_h, dact1_h, ghat_h, conv_h, gated_h, ginv_h, norm_h, gated_o,
     ws, act0, act1, sums, gmean, ginv, pad, filt, fir, keep, halo, act0_o, dact0_o, dact1_o, ghat_o, conv_o, norm_o, wsem, osem) = refs
    sp = sp.at[pl.ds(layer, 1)]
    rows, model = h_own.shape
    every = rows + HALO
    hidden = act0.shape[1]
    shard = hidden // 4
    half, length = scal[1], scal[2]
    here, there = slab_copies(sets, ws, W_UP, W_ROWS)
    fetch(scal[3] == layer, here, there, wsem)
    gain, bias = wide(sp, ROW_NG + 4), wide(sp, ROW_NB + 4)
    step = 64
    for r in range(0, rows, step):
        hat, unused = normalized(h_own[r : r + step, :].astype(F32))
        norm_o[r : r + step, :] = (hat * gain + bias).astype(BF)
    i = lax.broadcasted_iota(jnp.int32, (HALO, rows), 0)
    r = lax.broadcasted_iota(jnp.int32, (HALO, rows), 1)
    wanted = jnp.where(half == 0, i * SEGS, (i + rows // SEGS - HALO) * SEGS + SEGS - 1)
    pick = jnp.where(r == wanted, 1.0, 0.0).astype(BF)
    hat, unused = normalized(dot(pick, h_oth[...], NN))
    norm_o[rows:every, :] = (hat * gain + bias).astype(BF)
    sums[...] = jnp.zeros_like(sums)

    width = 256
    chunk = 48

    def up(i, carry):
        lanes = pl.ds(pl.multiple_of(i * width, width), width)
        rows_of = []
        for hh, base in ((0, ROW_UP0), (1, ROW_UP1)):
            got = []
            for t in range(2):
                c = 2 * i + t
                got.append(sp[0, scal[8 + c], pl.ds(lax.rem(c, 3) * BLOCK_ROWS + base, 1), :])
            rows_of.append(jnp.concatenate(got, axis=1))
        slabs = []
        for hh in range(2):
            pair = []
            for t in range(2):
                c = 2 * i + t
                at = (hh * 3 + lax.rem(c, 3)) * model
                pair.append(ws[lax.div(c, 3), pl.ds(pl.multiple_of(at, model), model), :])
            slabs.append(jnp.concatenate(pair, axis=1))
        u0 = dot(norm_o[...], slabs[0], NN)
        u1 = dot(norm_o[...], slabs[1], NN)
        for r in range(0, every, chunk):
            a, d = gelu_parts(u0[r : r + chunk] + rows_of[0])
            act0[r : r + chunk, lanes] = a
            act0_o[r : r + chunk, lanes] = a.astype(BF)
            dact0_o[r : r + chunk, lanes] = d.astype(BF)
        for r in range(0, every, chunk):
            a, d = gelu_parts(u1[r : r + chunk] + rows_of[1])
            act1[r : r + chunk, lanes] = a
            dact1_o[r : r + chunk, lanes] = d.astype(BF)
            sums[r : r + chunk, :] += a[:, :LANES] + a[:, LANES:]
        return carry

    middle = hidden // width // 2
    for n in range(2):
        for i in range(4 * n, 4 * n + 4):
            pltpu.make_async_copy(*here[i], wsem.at[i]).wait()
        lax.fori_loop(n * middle, (n + 1) * middle, up, 0)
    for r in range(0, every, chunk):
        center = jnp.sum(sums[r : r + chunk, :], axis=1, keepdims=True) * (1.0 / hidden)
        d = act1[r : r + chunk, :] - center
        spread = jnp.sum(d * d, axis=1, keepdims=True) * (1.0 / hidden)
        gmean[r : r + chunk, :] = jnp.broadcast_to(center, (chunk, LANES))
        ginv[r : r + chunk, :] = jnp.broadcast_to(lax.rsqrt(spread + EPS), (chunk, LANES))
    stores = [
        pltpu.make_async_copy(a, b, osem.at[i])
        for i, (a, b) in enumerate(
            ((act0_o, act0_h), (dact0_o, dact0_h), (dact1_o, dact1_h), (norm_o, norm_h), (ginv.at[pl.ds(0, rows)], ginv_h))
        )
    ]
    for c in stores:
        c.start()

    def column_stores(c):
        lanes = pl.ds(pl.multiple_of(c * LANES, LANES), LANES)
        pairs = ((ghat_o, ghat_h), (conv_o, conv_h), (gated_o, gated_h))
        return [
            pltpu.make_async_copy(a.at[:, lanes], b.at[:, lanes], osem.at[5 + 3 * c + i]) for i, (a, b) in enumerate(pairs)
        ]


    row = lax.broadcasted_iota(jnp.int32, (rows, LANES), 0)
    valid = jnp.where(frame_of(row, half, rows) < length, 1.0, 0.0)
    hrow = lax.broadcasted_iota(jnp.int32, (HALO, LANES), 0)
    valid_halo = jnp.where(jnp.where(half == 0, rows, rows - HALO) + hrow < length, 1.0, 0.0)
    count = rows // SEGS

    def gate(c, carry):
        lanes = pl.ds(pl.multiple_of(c * LANES, LANES), LANES)
        mj = scal[8 + c]
        base = lax.rem(c, 3) * BLOCK_ROWS
        ggain = sp[0, mj, pl.ds(base + ROW_GAIN, 1), :]
        gb0 = sp[0, mj, pl.ds(base + ROW_GB0, 1), :]
        gb1 = sp[0, mj, pl.ds(base + ROW_GB1, 1), :]
        hat = (act1[rows:every, lanes] - gmean[rows:every, :]) * ginv[rows:every, :]
        ghat_o[rows:every, lanes] = hat.astype(BF)
        halo[...] = (hat * ggain + gb0) * valid_halo
        hat = (act1[0:rows, lanes] - gmean[0:rows, :]) * ginv[0:rows, :]
        ghat_o[0:rows, lanes] = hat.astype(BF)
        normed = (hat * ggain + gb0) * valid
        halo_pads(pad, normed.reshape(count, SEGS, LANES), halo, half, True)
        fill_filters(filt, lambda k: sp[0, mj, pl.ds(base + k, 1), :])
        fast_fir(pad, filt, fir, keep)
        for t in range(0, count, 8):
            at = t * SEGS
            cv = fir[t : t + 8].reshape(64, LANES) + gb1
            conv_o[at : at + 64, lanes] = cv.astype(BF)
            gated_o[at : at + 64, lanes] = (act0[at : at + 64, lanes] * cv).astype(BF)
        for store in column_stores(c):
            store.start()
        return carry

    lax.fori_loop(0, hidden // LANES, gate, 0)
    for c in range(hidden // LANES):
        stores.extend(column_stores(c))
    for c in stores:
        c.wait()


def branch_rows(mix, gated, ws, wv, r, block):
    shard = wv.shape[1] // 4
    mixed = jnp.concatenate([mix[j, r : r + block, :] for j in range(4)], axis=1)
    brs, atts = [], []
    for lb in range(0, 4, 2):
        w = [
            jnp.concatenate(
                [wv[j, (lb + t) * shard : (lb + t + 1) * shard, :] for j in range(4)], axis=0
            )
            for t in range(2)
        ]
        brs.append(dot(gated[r : r + block, :], jnp.concatenate(w, axis=1), NN))
        w = [
            jnp.concatenate(
                [ws[j, (lb + t) * LANES : (lb + t + 1) * LANES, :] for j in range(4)], axis=0
            )
            for t in range(2)
        ]
        atts.append(dot(mixed, jnp.concatenate(w, axis=1), NN))
    return jnp.concatenate(atts, axis=1), jnp.concatenate(brs, axis=1)


def merge_forward_kernel(layer, scal, sp, h_own, mix, gated, *refs):
    u_sets, v_sets, refs = refs[:10], refs[10:18], refs[18:]
    o_o, nat_o, rhat_h, rstd_h, diff_h, ws, wv, rhat_o, rstd_o, diff_o, usem, vsem, osem = refs
    sp = sp.at[pl.ds(layer, 1)]
    rows, model = h_own.shape
    shard = wv.shape[1] // 4
    here, there = slab_copies(u_sets, ws, 0, W_UP)
    fetch(scal[3] == layer, here, there, usem)
    here_v, there_v = down_copies(v_sets, wv)
    fetch(scal[3] == layer, here_v, there_v, vsem)
    landed(here, usem)
    landed(here_v, vsem)
    step = 64

    def stores(r, n):
        part = pl.ds(r, n)
        pairs = ((rhat_o, rhat_h), (rstd_o, rstd_h), (diff_o, diff_h))
        return [
            pltpu.make_async_copy(a.at[part], b.at[part], osem.at[r // n, i]) for i, (a, b) in enumerate(pairs)
        ]

    w0, w1 = branch_weights(sp)
    gain, bias = wide(sp, ROW_NG + 8), wide(sp, ROW_NB + 8)
    b0, b1 = wide(sp, ROW_OB), wide(sp, ROW_OB + 4)
    block = 256
    for r in range(0, rows, block):
        att, br = branch_rows(mix, gated, ws, wv, r, block)
        for q in range(0, block, step):
            at = att[q : q + step] + b0
            bt = br[q : q + step] + b1
            res = h_own[r + q : r + q + step, :].astype(F32) + w0 * at + w1 * bt
            hat, inverse = normalized(res)
            diff_o[r + q : r + q + step, :] = at - bt
            rhat_o[r + q : r + q + step, :] = hat
            rstd_o[r + q : r + q + step, :] = jnp.broadcast_to(inverse, (step, LANES))
            o_o[r + q : r + q + step, :] = (hat * gain + bias).astype(BF)
        for c in stores(r, block):
            c.start()
    nat_o[...] = dot(order_matrix(rows, True), o_o[...], NN).astype(BF)
    for r in range(0, rows, block):
        for c in stores(r, block):
            c.wait()


def binary_weights(down):
    lane = lax.broadcasted_iota(jnp.int32, (1, LANES), 1)
    out = jnp.full((1, LANES), 2.0 ** (63 if down else -63), F32)
    for b in range(7):
        out = jnp.where(((lane >> b) & 1) == 1, out * 2.0 ** (-(2**b) if down else 2**b), out)
    return out


def merge_finish(half, sums, slope, mix, gated, gatt_o, gbr_o, halo_o, keep_o, send_o, small, late):
    rows = gbr_o.shape[0]
    i = lax.broadcasted_iota(jnp.int32, (HALO, rows), 0)
    r = lax.broadcasted_iota(jnp.int32, (HALO, rows), 1)
    wanted = jnp.where(half == 0, (i + rows // SEGS - HALO) * SEGS + SEGS - 1, i * SEGS)
    pick = jnp.where(r == wanted, 1.0, 0.0).astype(BF)
    halo_o[...] = dot(pick, gbr_o[...], NN).astype(BF)
    slope = jnp.sum(slope, axis=1, keepdims=True)
    small[...] = jnp.zeros_like(small)
    for n, v in enumerate(sums):
        for i in range(4):
            small[4 * n + i : 4 * n + i + 1, :] = v[:, i * LANES : (i + 1) * LANES]
    scaled = jnp.abs(slope) * binary_weights(False)
    digits = jnp.floor(scaled) - 2.0 * jnp.floor(0.5 * scaled)
    small[16:17, :] = jnp.where(slope < 0, -digits, digits)
    shards = (keep_o.at[0], send_o.at[0], keep_o.at[1], send_o.at[1])
    shard = gated.shape[1] // 4
    late()
    for j in range(4):
        shards[j][D_SMALL:D_ROWS, :] = small[...].astype(BF)
    for j in range(4):
        w = dot(mix[j], gatt_o[...], TN).astype(BF)
        for i in range(4):
            shards[j][i * LANES : (i + 1) * LANES, :] = w[:, i * LANES : (i + 1) * LANES]
        w = dot(gated[:, j * shard : (j + 1) * shard], gbr_o[...], TN).astype(BF)
        for i in range(4):
            at = OUT_ROWS + i * shard
            shards[j][at : at + shard, :] = w[:, i * LANES : (i + 1) * LANES]


def merge_backward_kernel(
    layer, scal, sp, g, rhat_h, rstd_h, diff_h, mix_h, gated_h,
    gres_o, gatt_o, gbr_o, halo_o, keep_o, send_o, rhat, rstd, diff, mix, gated, small, sems,
):
    sp = sp.at[pl.ds(layer, 1)]
    rows, model = g.shape
    half = scal[1]
    step = 64
    parts = [pl.ds(r, 2 * step) for r in range(0, rows, 2 * step)]
    loads = [
        [
            pltpu.make_async_copy(a.at[part], b.at[part], sems.at[i, n])
            for i, (a, b) in enumerate(((rstd_h, rstd), (rhat_h, rhat), (diff_h, diff)))
        ]
        for n, part in enumerate(parts)
    ]
    late = [
        pltpu.make_async_copy(a, b, sems.at[3, i]) for i, (a, b) in enumerate(((mix_h, mix), (gated_h, gated)))
    ]
    for c in sum(loads, []) + late:
        c.start()
    gain = wide(sp, ROW_NG + 8)
    w0, w1 = branch_weights(sp)
    dgain = dbias = slope = jnp.zeros((1, model), F32)
    db = jnp.zeros((1, model), F32)
    for r in range(0, rows, step):
        if r % (2 * step) == 0:
            for c in loads[r // (2 * step)]:
                c.wait()
        gg = g[r : r + step, :].astype(F32)
        hat = rhat[r : r + step, :]
        dgain = dgain + jnp.sum(gg * hat, axis=0, keepdims=True)
        dbias = dbias + jnp.sum(gg, axis=0, keepdims=True)
        gg = gg * gain
        gr = rstd[r : r + step, 0:1] * (
            gg - jnp.mean(gg, axis=1, keepdims=True) - hat * jnp.mean(gg * hat, axis=1, keepdims=True)
        )
        gres_o[r : r + step, :] = gr
        gatt_o[r : r + step, :] = (w0 * gr).astype(BF)
        gbr_o[r : r + step, :] = (w1 * gr).astype(BF)
        db = db + jnp.sum(gr, axis=0, keepdims=True)
        slope = slope + jnp.sum(gr * diff[r : r + step, :], axis=0, keepdims=True)
    merge_finish(
        half, (dgain, dbias, w0 * db, w1 * db), slope, mix, gated, gatt_o, gbr_o, halo_o, keep_o, send_o, small,
        lambda: [c.wait() for c in late],
    )


def merge_turn_kernel(layer, scal, sp, h_own, mix, gated, g, *refs):
    u_sets, v_sets, refs = refs[:10], refs[10:18], refs[18:]
    nat_o, gres_o, gatt_o, gbr_o, halo_o, keep_o, send_o, ws, wv, o_s, small, usem, vsem = refs
    sp = sp.at[pl.ds(layer, 1)]
    rows, model = h_own.shape
    here, there = slab_copies(u_sets, ws, 0, W_UP)
    fetch(scal[3] == layer, here, there, usem)
    here_v, there_v = down_copies(v_sets, wv)
    fetch(scal[3] == layer, here_v, there_v, vsem)
    landed(here, usem)
    landed(here_v, vsem)
    w0, w1 = branch_weights(sp)
    gain, bias = wide(sp, ROW_NG + 8), wide(sp, ROW_NB + 8)
    b0, b1 = wide(sp, ROW_OB), wide(sp, ROW_OB + 4)
    dgain = dbias = slope = db = jnp.zeros((1, model), F32)
    step, block = 64, 256
    for r in range(0, rows, block):
        att, br = branch_rows(mix, gated, ws, wv, r, block)
        for q in range(0, block, step):
            at = att[q : q + step] + b0
            bt = br[q : q + step] + b1
            lo, hi = r + q, r + q + step
            hat, inverse = normalized(h_own[lo:hi, :].astype(F32) + w0 * at + w1 * bt)
            o_s[lo:hi, :] = (hat * gain + bias).astype(BF)
            gg = g[lo:hi, :].astype(F32)
            dgain = dgain + jnp.sum(gg * hat, axis=0, keepdims=True)
            dbias = dbias + jnp.sum(gg, axis=0, keepdims=True)
            gg = gg * gain
            gr = inverse * (
                gg - jnp.mean(gg, axis=1, keepdims=True) - hat * jnp.mean(gg * hat, axis=1, keepdims=True)
            )
            gres_o[lo:hi, :] = gr
            gatt_o[lo:hi, :] = (w0 * gr).astype(BF)
            gbr_o[lo:hi, :] = (w1 * gr).astype(BF)
            db = db + jnp.sum(gr, axis=0, keepdims=True)
            slope = slope + jnp.sum(gr * (at - bt), axis=0, keepdims=True)
    nat_o[...] = dot(order_matrix(rows, True), o_s[...], NN).astype(BF)
    merge_finish(
        scal[1], (dgain, dbias, w0 * db, w1 * db), slope, mix, gated, gatt_o, gbr_o, halo_o, keep_o, send_o, small,
        lambda: None,
    )


def attention_backward_kernel(layer, scal, gatt_h, q_h, k_h, v_h, mix_h, lse_h, *refs):
    sets, refs = refs[:10], refs[10:]
    cos_t, sin_t, dq_o, own_o, oth_o, w_s, cs, sn, pbuf, dsbuf, dom, qm2, q_r, k_r, v_r, mix, lse, gatt, wsem, tsem = refs
    rows = gatt.shape[0]
    total = 2 * rows
    half, length = scal[1], scal[2]
    here, there = slab_copies(sets, w_s, 0, W_UP)
    fetch(scal[3] == layer, here, there, wsem)
    tables = [
        pltpu.make_async_copy(cos_t.at[half, pl.ds(0, rows), :], cs, tsem.at[0]),
        pltpu.make_async_copy(sin_t.at[half, pl.ds(0, rows), :], sn, tsem.at[1]),
    ]
    for i, (a, b) in enumerate(((q_h, q_r), (k_h, k_r), (v_h, v_r), (mix_h, mix), (lse_h, lse), (gatt_h, gatt))):
        tables.append(pltpu.make_async_copy(a, b, tsem.at[2 + i]))
    for c in tables:
        c.start()
    row = lax.broadcasted_iota(jnp.int32, (total, LANES), 0)
    part = jnp.where(row < rows, half, 1 - half)
    position = frame_of(row & (rows - 1), part, rows)
    mask = jnp.where(position < length, 0.0, NEG)
    lane_k = lax.broadcasted_iota(jnp.int32, (total, LANES), 1)
    lane_q = lax.broadcasted_iota(jnp.int32, (rows, LANES), 1)
    for c in tables:
        c.wait()
    landed(here, wsem)

    def shard(j):
        wo = jnp.concatenate([w_s[j, lb * LANES : (lb + 1) * LANES, :] for lb in range(4)], axis=1)
        dm = dot(gatt[...], wo, NT).astype(BF).astype(F32)
        prod = dm * mix[j].astype(F32)
        q = q_r[j].astype(F32)
        k = k_r[j].astype(F32)
        v = v_r[j].astype(F32)
        kt = k.T.astype(BF)
        dqs = []
        for hd in range(2):
            spare = (1 - hd) * HEAD
            in_q, in_k = (lane_q >> 6) == hd, (lane_k >> 6) == hd
            minus_lse = -jnp.sum(jnp.where(lane_q == 2 * j + hd, lse[...], 0.0), axis=1, keepdims=True)
            minus_delta = -jnp.sum(jnp.where(in_q, prod, 0.0), axis=1, keepdims=True)
            l0, l1, l2 = pieces(minus_lse)
            e0, e1, e2 = pieces(minus_delta)
            qx = jnp.where(lane_q == spare, 1.0, 0.0)
            dx = jnp.zeros_like(qx)
            for n, (lp, ep) in enumerate(((l0, e0), (l1, e1), (l2, e2))):
                here = lane_q == spare + 1 + n
                qx = jnp.where(here, lp, qx)
                dx = jnp.where(here, ep, dx)
            one = jnp.where((lane_k > spare) & (lane_k < spare + 4), 1.0, 0.0)
            qh = jnp.where(in_q, q, qx).astype(BF)
            dh = jnp.where(in_q, dm, dx).astype(BF)
            kh = jnp.where(in_k, k, jnp.where(lane_k == spare, mask, one)).astype(BF)
            vh = jnp.where(in_k, v, one).astype(BF)
            dom[hd * rows : (hd + 1) * rows, :] = jnp.where(in_q, dm, 0.0).astype(BF)
            qm2[hd * rows : (hd + 1) * rows, :] = jnp.where(in_q, q, 0.0).astype(BF)
            p = jnp.exp(dot(kh, qh, NT))
            dp = dot(vh, dh, NT)
            ds = (p * dp).astype(BF)
            pbuf[:, hd * rows : (hd + 1) * rows] = p.astype(BF)
            dsbuf[:, hd * rows : (hd + 1) * rows] = ds
            dqs.append(dot(kt[hd * HEAD : (hd + 1) * HEAD, :], ds, NN))
        dq = jnp.concatenate(dqs, axis=0).T * (1.0 / math.sqrt(HEAD))
        dq_o[j] = rotate_back(dq, cs[...], sn[...]).astype(BF)
        dk = dot(dsbuf[...], qm2[...], NN)
        dv = dot(pbuf[...], dom[...], NN)
        own_o[j, :, 0:LANES] = dk[:rows]
        own_o[j, :, LANES:] = dv[:rows]
        oth_o[j, :, 0:LANES] = dk[rows:].astype(BF)
        oth_o[j, :, LANES:] = dv[rows:].astype(BF)

    for j in range(4):
        shard(j)


def conv_backward_kernel(layer, scal, sp, gbr, ghalo, act0_h, dact0_h, ghat_h, conv_h, *refs):
    v_sets, refs = refs[:8], refs[8:]
    (dup_o, hgrad, hs, xs, small, wv, act0, dact0, ghat, conv, gpad, xpad, filt, fir, keep, halo, gcv, gbuf, vsem, asem) = refs
    sp = sp.at[pl.ds(layer, 1)]
    rows, model = gbr.shape
    every = rows + HALO
    hidden = gcv.shape[1]
    shard = hidden // 4
    half, length = scal[1], scal[2]
    here_v, there_v = down_copies(v_sets, wv)
    fetch(scal[3] == layer, here_v, there_v, vsem)
    width = 256

    def loads(i):
        lanes = pl.ds(pl.multiple_of(i * width, width), width)
        pairs = ((act0_h, act0), (conv_h, conv), (dact0_h, dact0))
        return [
            pltpu.make_async_copy(a.at[:, lanes], b.at[:, lanes], asem.at[n, i]) for n, (a, b) in enumerate(pairs)
        ]

    for i in range(hidden // width):
        for c in loads(i):
            c.start()
    last = pltpu.make_async_copy(ghat_h, ghat, asem.at[3, 0])
    last.start()
    gbuf[0:rows, :] = gbr[...]
    gbuf[rows:every, :] = ghalo[...]
    hs[...] = jnp.zeros_like(hs)
    xs[...] = jnp.zeros_like(xs)
    small[...] = jnp.zeros_like(small)
    landed(here_v, vsem)
    count = rows // SEGS
    chunk = 48

    def down(i, carry):
        for c in loads(i):
            c.wait()
        lanes = pl.ds(pl.multiple_of(i * width, width), width)
        pair = []
        for t in range(2):
            c = 2 * i + t
            base = lax.rem(c, 3) * LANES
            pair.append(
                jnp.concatenate(
                    [
                        wv[lax.div(c, 3), pl.ds(pl.multiple_of(base + lb * shard, LANES), LANES), :]
                        for lb in range(4)
                    ],
                    axis=1,
                )
            )
        g = dot(gbuf[...], jnp.concatenate(pair, axis=0), NT)
        for r in range(0, every, chunk):
            gr = g[r : r + chunk].astype(BF).astype(F32)
            gcv[r : r + chunk, lanes] = gr * act0[r : r + chunk, lanes].astype(F32)
        for r in range(0, rows, 64):
            gr = g[r : r + 64].astype(BF).astype(F32)
            keep = gr * conv[r : r + 64, lanes].astype(F32) * dact0[r : r + 64, lanes].astype(F32)
            dup_o[r : r + 64, lanes] = keep.astype(BF)
        return carry

    lax.fori_loop(0, hidden // width, down, 0)
    last.wait()
    row = lax.broadcasted_iota(jnp.int32, (rows, LANES), 0)
    valid = jnp.where(frame_of(row, half, rows) < length, 1.0, 0.0)
    hrow = lax.broadcasted_iota(jnp.int32, (HALO, LANES), 0)
    valid_halo = jnp.where(jnp.where(half == 0, rows, rows - HALO) + hrow < length, 1.0, 0.0)

    def fold(x):
        return jnp.sum(x, axis=0, keepdims=True)

    def conv_back(c, carry):
        lanes = pl.ds(pl.multiple_of(c * LANES, LANES), LANES)
        mj = scal[8 + c]
        b = lax.rem(c, 3)
        j = lax.div(c, 3)
        base = b * BLOCK_ROWS
        ggain = sp[0, mj, pl.ds(base + ROW_GAIN, 1), :]
        gb0 = sp[0, mj, pl.ds(base + ROW_GB0, 1), :]
        halo[...] = (ghat[rows:every, lanes].astype(F32) * ggain + gb0) * valid_halo
        normed = (ghat[0:rows, lanes].astype(F32) * ggain + gb0) * valid
        halo_pads(xpad, normed.reshape(count, SEGS, LANES), halo, half, True)
        halo[...] = gcv[rows:every, lanes]
        gown = gcv[0:rows, lanes]
        halo_pads(gpad, gown.reshape(count, SEGS, LANES), halo, half, True)
        small[j, pl.ds(base + ROW_GB1, 1), :] = fold(gown)
        for k, t in enumerate(tap_sums(gpad, xpad, count)):
            small[j, pl.ds(base + k, 1), :] = fold(t)
        fill_filters(filt, lambda k: sp[0, mj, pl.ds(base + TAPS - 1 - k, 1), :])
        fast_fir(gpad, filt, fir, keep)
        dgain = jnp.zeros((SEGS, LANES), F32)
        dbias = jnp.zeros((SEGS, LANES), F32)
        for t in range(0, count, 8):
            at = t * SEGS
            gn = fir[t : t + 8].reshape(64, LANES) * valid[at : at + 64]
            hat = ghat[at : at + 64, lanes].astype(F32)
            dgain = dgain + jnp.sum((gn * hat).reshape(8, SEGS, LANES), axis=0)
            dbias = dbias + jnp.sum(gn.reshape(8, SEGS, LANES), axis=0)
            gn = gn * ggain
            hgrad[at : at + 64, lanes] = gn
            hs[at : at + 64, :] += gn
            xs[at : at + 64, :] += gn * hat
        small[j, pl.ds(base + ROW_GAIN, 1), :] = fold(dgain)
        small[j, pl.ds(base + ROW_GB0, 1), :] = fold(dbias)
        return carry

    lax.fori_loop(0, hidden // LANES, conv_back, 0)
    for r in range(0, rows, 64):
        a = jnp.sum(hs[r : r + 64, :], axis=1, keepdims=True) * (1.0 / hidden)
        x = jnp.sum(xs[r : r + 64, :], axis=1, keepdims=True) * (1.0 / hidden)
        hs[r : r + 64, :] = jnp.broadcast_to(a, (64, LANES))
        xs[r : r + 64, :] = jnp.broadcast_to(x, (64, LANES))


def up_backward_kernel(layer, scal, dup0, hgrad, hs, xs, small_i, ghat_h, dact1_h, ginv_h, norm_h, *refs):
    sets, refs = refs[:10], refs[10:]
    dn_o, keep_o, send_o, ws, ghat, dact1, ginv, norm, dup1, small, wsem, asem = refs
    rows, hidden = hgrad.shape
    model = norm.shape[1]
    width = 256
    here, there = slab_copies(sets, ws, W_UP, W_ROWS)
    fetch(scal[3] == layer, here, there, wsem)
    own = pl.ds(0, rows)
    blocks = hidden // LANES

    def columns(c):
        lanes = pl.ds(pl.multiple_of(c * LANES, LANES), LANES)
        return [
            pltpu.make_async_copy(ghat_h.at[own, lanes], ghat.at[:, lanes], asem.at[0, c]),
            pltpu.make_async_copy(dact1_h.at[own, lanes], dact1.at[:, lanes], asem.at[1, c]),
        ]

    first = pltpu.make_async_copy(ginv_h, ginv, asem.at[2, 0])
    first.start()
    for c in range(blocks):
        for load in columns(c):
            load.start()
    last = pltpu.make_async_copy(norm_h, norm, asem.at[2, 1])
    last.start()
    small[...] = small_i[...]

    def fold(x):
        return jnp.sum(x, axis=0, keepdims=True)

    first.wait()

    def gate_back(c, carry):
        for load in columns(c):
            load.wait()
        lanes = pl.ds(pl.multiple_of(c * LANES, LANES), LANES)
        b = lax.rem(c, 3)
        j = lax.div(c, 3)
        base = b * BLOCK_ROWS
        s0 = jnp.zeros((1, LANES), F32)
        s1 = jnp.zeros((1, LANES), F32)
        for r in range(0, rows, 64):
            hat = ghat[r : r + 64, lanes].astype(F32)
            gi = ginv[r : r + 64, :] * (hgrad[r : r + 64, lanes] - hs[r : r + 64, :] - hat * xs[r : r + 64, :])
            d1 = (gi * dact1[r : r + 64, lanes].astype(F32)).astype(BF)
            dup1[r : r + 64, lanes] = d1
            s1 = s1 + fold(d1.astype(F32))
            s0 = s0 + fold(dup0[r : r + 64, lanes].astype(F32))
        small[j, pl.ds(base + ROW_UP0, 1), :] = s0
        small[j, pl.ds(base + ROW_UP1, 1), :] = s1
        return carry

    lax.fori_loop(0, hidden // LANES, gate_back, 0)
    landed(here, wsem)
    last.wait()
    dups = (dup0, dup1)
    for hh in range(2):
        w = jnp.concatenate(
            [ws[j, (hh * 3 + b) * model : (hh * 3 + b + 1) * model, :] for j in range(4) for b in range(3)], axis=1
        )
        if hh == 0:
            dn_o[...] = dot(dups[hh][...], w, NT)
        else:
            dn_o[...] += dot(dups[hh][...], w, NT)
    shards = (keep_o.at[0], send_o.at[0], keep_o.at[1], send_o.at[1])
    own_norm = norm[0:rows, :]
    for i in range(hidden // width):
        lo = i * width
        for hh in range(2):
            w = dot(own_norm, dups[hh][:, lo : lo + width], TN).astype(BF)
            for t in range(2):
                j, b = divmod(2 * i + t, 3)
                at = (hh * 3 + b) * model
                shards[j][at : at + model, :] = w[:, t * LANES : (t + 1) * LANES]
    for j in range(4):
        shards[j][UP_ROWS:M_ROWS, :] = small[j].astype(BF)


def input_backward_kernel(layer, scal, sp, h_h, gres_h, dn_h, dq, dkv_own, dkv_got, *refs):
    sets, refs = refs[:8], refs[8:]
    cos_t, sin_t, g_o, nat_o, keep_o, send_o, wq, cs, sn, dall, norm, xhat, xinv, small, h_own, gres, dn_mlp, wsem, tsem = refs
    sp = sp.at[pl.ds(layer, 1)]
    rows, model = h_own.shape
    half = scal[1]
    here, there = shard_copies(sets, wq)
    fetch(scal[3] == layer, here, there, wsem)
    shards = (keep_o.at[0], send_o.at[0], keep_o.at[1], send_o.at[1])
    tables = [
        pltpu.make_async_copy(cos_t.at[half, pl.ds(0, rows), :], cs, tsem.at[0]),
        pltpu.make_async_copy(sin_t.at[half, pl.ds(0, rows), :], sn, tsem.at[1]),
    ]
    tables.append(pltpu.make_async_copy(gres_h, gres, tsem.at[2]))
    tables.append(pltpu.make_async_copy(dn_h, dn_mlp, tsem.at[4]))
    first = pltpu.make_async_copy(h_h, h_own, tsem.at[3])
    first.start()
    for c in tables:
        c.start()
    first.wait()
    gain, bias = wide(sp, ROW_NG), wide(sp, ROW_NB)
    gain_mlp = wide(sp, ROW_NG + 4)
    step = 64
    for r in range(0, rows, step):
        hat, inverse = normalized(h_own[r : r + step, :].astype(F32))
        xhat[r : r + step, :] = hat
        xinv[r : r + step, :] = jnp.broadcast_to(inverse, (step, LANES))
        norm[r : r + step, :] = (hat * gain + bias).astype(BF)
    for c in tables:
        c.wait()
    for j in range(4):
        at = j * 3 * LANES
        dall[:, at : at + LANES] = dq[j]
        dk = dkv_own[j, :, 0:LANES] + dkv_got[j ^ 1, :, 0:LANES].astype(F32)
        dall[:, at + LANES : at + 2 * LANES] = rotate_back(dk, cs[...], sn[...]).astype(BF)
        dv = dkv_own[j, :, LANES:] + dkv_got[j ^ 1, :, LANES:].astype(F32)
        dall[:, at + 2 * LANES : at + 3 * LANES] = dv.astype(BF)
    landed(here, wsem)
    small[...] = jnp.zeros_like(small)
    dn = dot(dall[...], jnp.concatenate([wq[j, i] for j in range(4) for i in range(3)], axis=1), NT)
    dg0 = db0 = dg1 = db1 = jnp.zeros((1, model), F32)
    for r in range(0, rows, step):
        hat = xhat[r : r + step, :]
        a = dn[r : r + step]
        m = dn_mlp[r : r + step, :]
        dg0 = dg0 + jnp.sum(a * hat, axis=0, keepdims=True)
        db0 = db0 + jnp.sum(a, axis=0, keepdims=True)
        dg1 = dg1 + jnp.sum(m * hat, axis=0, keepdims=True)
        db1 = db1 + jnp.sum(m, axis=0, keepdims=True)
        gg = a * gain + m * gain_mlp
        dx = xinv[r : r + step, 0:1] * (
            gg - jnp.mean(gg, axis=1, keepdims=True) - hat * jnp.mean(gg * hat, axis=1, keepdims=True)
        )
        g_o[r : r + step, :] = (gres[r : r + step, :] + dx).astype(BF)
    nat_o[...] = dot(order_matrix(rows, True), g_o[...], NN).astype(BF)
    for j in range(4):
        for n, v in enumerate((dg0, dg1, db0, db1)):
            for i in range(4):
                small[j, 8 + 4 * n + i : 9 + 4 * n + i, :] = v[:, i * LANES : (i + 1) * LANES]
    for j in range(4):
        at = j * 3 * LANES
        d = dall[:, at : at + 3 * LANES]
        w = dot(norm[...], d, TN).astype(BF)
        s = jnp.sum(d.astype(F32), axis=0, keepdims=True)
        for i in range(3):
            lo = i * model
            shards[j][lo : lo + model, :] = w[:, i * LANES : (i + 1) * LANES]
            small[j, i : i + 1, :] = s[:, i * LANES : (i + 1) * LANES]
        shards[j][QKV_ROWS:A_ROWS, :] = small[j].astype(BF)


def assemble_kernel(scal, here, there, out):
    rows = here.shape[1]
    for n in range(8):
        place, half = scal[24 + n], scal[32 + n]
        part = there if n & 1 else here
        out[place, pl.ds(pl.multiple_of(half * rows, rows), rows), :] = part[n >> 1]


def finale_kernel(
    dm_lo, d_hi, m_hi, a, logits,
    qkv_o, out_o, up_o, down_o, bqkv_o, bup_o, gain_o, gbias_o, conv_o, ng_o, nb_o, ob_o, logit_o,
):
    cut = D_ROWS // 2

    def rows_of(lo, hi, at, n, a, b):
        if b <= n:
            return lo[at + a : at + b, :].astype(F32)
        if a >= n:
            return hi[a - n : b - n, :].astype(F32)
        return jnp.concatenate([lo[at + a : at + n, :], hi[0 : b - n, :]], axis=0).astype(F32)

    d_of = functools.partial(rows_of, dm_lo, d_hi, 0, cut)
    m_of = functools.partial(rows_of, dm_lo, m_hi, cut, M_ROWS // 2)
    def a_of(lo, hi):
        return a[lo:hi, :].astype(F32)

    model, shard = up_o.shape[1], up_o.shape[2]
    for i in range(3):
        qkv_o[i] = a_of(i * model, (i + 1) * model)
    for lb in range(4):
        lanes = slice(lb * LANES, (lb + 1) * LANES)
        out_o[:, lanes] = d_of(lb * LANES, (lb + 1) * LANES)
        down_o[:, lanes] = d_of(OUT_ROWS + lb * shard, OUT_ROWS + (lb + 1) * shard)
    for hh in range(2):
        for b in range(3):
            at = (hh * 3 + b) * model
            up_o[hh, :, b * LANES : (b + 1) * LANES] = m_of(at, at + model)
    small = m_of(UP_ROWS, M_ROWS)
    for b in range(3):
        lanes = slice(b * LANES, (b + 1) * LANES)
        at = b * BLOCK_ROWS
        for k in range(TAPS):
            conv_o[k, :, lanes] = small[at + k : at + k + 1]
        bup_o[:, lanes] = small[at + ROW_UP0 : at + ROW_UP0 + 2]
        gain_o[:, lanes] = small[at + ROW_GAIN : at + ROW_GAIN + 1]
        gbias_o[:, lanes] = small[at + ROW_GB0 : at + ROW_GB0 + 2]
    small = a_of(QKV_ROWS, A_ROWS)
    for n in range(3):
        bqkv_o[n] = small[n : n + 1]
    for n in range(2):
        for i in range(4):
            lanes = slice(i * LANES, (i + 1) * LANES)
            ng_o[n, :, lanes] = small[8 + 4 * n + i : 9 + 4 * n + i]
            nb_o[n, :, lanes] = small[16 + 4 * n + i : 17 + 4 * n + i]
    small = d_of(D_SMALL, D_ROWS)
    for i in range(4):
        lanes = slice(i * LANES, (i + 1) * LANES)
        ng_o[2, :, lanes] = small[i : i + 1]
        nb_o[2, :, lanes] = small[4 + i : 5 + i]
        ob_o[0:1, lanes] = small[8 + i : 9 + i]
        ob_o[1:2, lanes] = small[12 + i : 13 + i]
    total_slope = jnp.sum(small[16:17] * binary_weights(True), axis=1, keepdims=True)
    l0, l1 = jnp.full((1, LANES), logits[0], F32), jnp.full((1, LANES), logits[1], F32)
    top = jnp.maximum(l0, l1)
    e0, e1 = jnp.exp(l0 - top), jnp.exp(l1 - top)
    slope = e0 * e1 / ((e0 + e1) * (e0 + e1)) * total_slope
    logit_o[0:1, :] = slope
    logit_o[1:2, :] = -slope


def exchange(x, axis, bit):
    n = lax.axis_size(axis)
    return lax.ppermute(x, axis, [(i, i ^ bit) for i in range(n)])


def fence(*xs):
    return lax.optimization_barrier(xs)


def total(*xs):
    out = xs[0].astype(F32)
    for x in xs[1:]:
        out = out + x.astype(F32)
    return out


def scatter_over_dp(x):
    n = lax.axis_size("dp")
    if n != 4:
        return (lax.psum(x.astype(F32), "dp").astype(BF),)
    d = lax.axis_index("dp")
    x = x.reshape(n, x.shape[0] // n, LANES)
    own = lax.dynamic_index_in_dim(x, d, 0, keepdims=False)
    return (own, *[exchange(lax.dynamic_index_in_dim(x, d ^ k, 0, keepdims=False), "dp", k) for k in range(1, n)])


def gather_over_dp(x):
    n = lax.axis_size("dp")
    return (x, *[exchange(x, "dp", k) for k in range(1, n)]) if n == 4 else (x,)


def in_order(parts):
    if len(parts) == 1:
        return parts[0]
    d = lax.axis_index("dp")
    low, high = (d & 1) == 0, (d & 2) == 0
    pairs = [
        (jnp.where(low, parts[k], parts[k + 1]), jnp.where(low, parts[k + 1], parts[k])) for k in (0, 2)
    ]
    return jnp.concatenate([jnp.where(high, pairs[i][t], pairs[1 - i][t]) for i in range(2) for t in range(2)], axis=0)


def halves(x, owner):
    rows = x.shape[0] // 2
    return jnp.where(owner, x[:rows], x[rows:]), jnp.where(owner, x[rows:], x[:rows])


def rotary_constants(length):
    half_width = HEAD // 2
    freq = np.exp(np.arange(half_width, dtype=np.float32) * np.float32(-math.log(10000.0) / half_width))
    rows = length // 2
    r = np.arange(rows)
    place = (r % SEGS) * (rows // SEGS) + r // SEGS
    cosines, sines = [], []
    for half in range(2):
        t = np.concatenate([half * rows + place, (1 - half) * rows + place]).astype(np.float32)
        angle = (t[:, None] * freq.astype(np.float32)[None, :]).astype(np.float32)
        c, s = np.cos(angle.astype(np.float64)), np.sin(angle.astype(np.float64))
        cosines.append(np.concatenate([c, c, c, c], axis=1))
        sines.append(np.concatenate([-s, s, -s, s], axis=1))
    return np.stack(cosines).astype(np.float32), np.stack(sines).astype(np.float32)


def per_device(frames, lengths, out_grad, *weights):
    (norm_gains, norm_biases, wqkv, bqkv, wout, wup, bup, ggain, gbias, cw, wdown, obias, logits) = [
        w[0] for w in weights
    ]
    micro, utterances, length, model = frames.shape
    n_sec, n_mp = lax.axis_size("section"), lax.axis_size("mp")
    assert utterances == 1 and n_sec == 2 and n_mp == 4 and micro == 4
    rows = length // 2
    shard = wdown.shape[0]
    hidden = shard * n_mp
    every = rows + HALO
    s, m = lax.axis_index("section"), lax.axis_index("mp")
    u = s * 2 + (m >> 1)
    half = m & 1
    own_length = lax.dynamic_index_in_dim(lengths[:, 0], u, 0, keepdims=False)
    ns = np.arange(40)
    xors = np.zeros(40, np.int32)
    xors[4:8] = np.arange(4)
    xors[8:20] = np.arange(12) // 3
    xors[24:32] = ns[:8] >> 1 & 1
    xors[32:40] = ns[:8] & 1
    sec_bits = np.zeros(40, np.int32)
    sec_bits[24:32] = ns[:8] >> 2
    idx = jnp.asarray(ns)
    by_shard = jnp.asarray(xors)
    by_place = (s ^ jnp.asarray(sec_bits)) * 2 + ((m >> 1) ^ jnp.asarray(xors))
    by_half = half ^ jnp.asarray(xors)
    scal = jnp.where(idx < 24, by_shard, jnp.where(idx < 32, by_place, by_half))
    for i, v in enumerate((u, half, own_length, s)):
        scal = jnp.where(idx == i, v, scal)
    scal = scal.astype(jnp.int32)

    x_of = lambda v: exchange(v, "section", 1)
    y_of = lambda v: exchange(v, "mp", 2)
    core_of = lambda v: exchange(v, "mp", 1)
    flat = shape((rows, model), BF)
    rows_f32 = shape((rows, model), F32)
    stat = shape((rows, LANES), F32)
    wide_bf = shape((rows, hidden), BF)
    halo_bf = shape((every, hidden), BF)

    def head_pack(n):
        return shape((4, n, LANES), BF)

    first = s == 0

    q_x, q_y, q_sib = x_of(wqkv), y_of(wqkv), core_of(wqkv)
    packed, u_own, v_own = call(
        pack_kernel,
        [wout, wup, wdown, cw, bup, ggain[None], gbias, bqkv, norm_gains, norm_biases, obias, logits],
        [ANY] * 3 + [VMEM] * 8 + [SMEM],
        [shape((PACK_ROWS, LANES), F32), shape((W_ROWS, LANES), BF), shape((DOWN_ROWS, LANES), BF)],
        [
            pltpu.VMEM(wout.shape, BF),
            pltpu.VMEM(wup.shape, BF),
            pltpu.VMEM(wdown.shape, BF),
            pltpu.SemaphoreType.DMA((3,)),
        ],
        0,
        12,
    )
    packed, q_x, q_y, scal, u_own, v_own = fence(packed, q_x, q_y, scal, u_own, v_own)
    packed_x = x_of(packed)
    q_d = x_of(q_y)
    packed_x, packed = fence(packed_x, packed)
    sections = jnp.stack([jnp.where(first, packed, packed_x), jnp.where(first, packed_x, packed)])
    sc, sections = fence(scal, sections)
    sections_y = y_of(sections)
    h_own, h_oth, g_last = call(
        prologue_kernel,
        [sc, frames, out_grad],
        [SMEM] + [ANY] * 2,
        [flat, flat, flat],
        [pltpu.VMEM((3, rows, model), BF), pltpu.SemaphoreType.DMA((3,))],
        0,
        12,
    )
    h_own, q_d, sections_y, u_own = fence(h_own, q_d, sections_y, u_own)
    u_x, u_y = x_of(u_own), y_of(u_own)
    q_xs, q_ys = core_of(q_x), core_of(q_y)
    sp_a = jnp.stack([sections, sections_y], axis=1)
    sp_b = core_of(sp_a)
    sp = jnp.stack([sp_a, sp_b], axis=2).reshape(2, n_mp, PACK_ROWS, LANES)
    q_ds = core_of(q_d)
    w_qkv = [wqkv, q_sib, q_y, q_ys, q_x, q_xs, q_d, q_ds]

    cos_np, sin_np = rotary_constants(length)
    cos_t, sin_t = jnp.asarray(cos_np), jnp.asarray(sin_np)

    def attention_forward(layer, scal, h_own, h_oth):
        return call(
            functools.partial(attention_forward_kernel, layer),
            [scal, sp, cos_t, sin_t, h_own, h_oth, *w_qkv],
            [SMEM, VMEM, ANY, ANY, VMEM, VMEM] + [ANY] * 8,
            [head_pack(rows), head_pack(length), head_pack(length), head_pack(rows), stat, head_pack(rows)],
            [
                pltpu.VMEM((4, 3, model, LANES), BF),
                pltpu.VMEM((length, LANES), F32),
                pltpu.VMEM((length, LANES), F32),
                pltpu.VMEM((length, model), BF),
                pltpu.VMEM((LANES, rows), F32),
                pltpu.VMEM((4, rows, LANES), BF),
                pltpu.VMEM((4, length, LANES), BF),
                pltpu.VMEM((4, length, LANES), BF),
                pltpu.VMEM((rows, LANES), F32),
                pltpu.SemaphoreType.DMA((4,)),
                pltpu.SemaphoreType.DMA((2,)),
                pltpu.SemaphoreType.DMA((5, 4)),
            ],
            10 * rows * length * model, 24, range(5))

    def mlp_forward(layer, scal, h_own, h_oth):
        return call(
            functools.partial(mlp_forward_kernel, layer),
            [scal, sp, h_own, h_oth, *w_u],
            [SMEM, VMEM, VMEM, VMEM] + [ANY] * 10,
            [halo_bf, halo_bf, halo_bf, halo_bf, wide_bf, wide_bf, stat, shape((every, model), BF), wide_bf],
            [
                pltpu.VMEM((4, W_ROWS - W_UP, LANES), BF),
                pltpu.VMEM((every, hidden), F32),
                pltpu.VMEM((every, hidden), F32),
                pltpu.VMEM((every, LANES), F32),
                pltpu.VMEM((every, LANES), F32),
                pltpu.VMEM((every, LANES), F32),
                pltpu.VMEM((rows // SEGS + 32, SEGS, LANES), F32),
                pltpu.VMEM((72, SEGS, LANES), F32),
                pltpu.VMEM((rows // SEGS, SEGS, LANES), F32),
                pltpu.VMEM((rows // SEGS // 2 + 1, SEGS, LANES), F32),
                pltpu.VMEM((HALO, LANES), F32),
                pltpu.VMEM((every, hidden), BF),
                pltpu.VMEM((every, hidden), BF),
                pltpu.VMEM((every, hidden), BF),
                pltpu.VMEM((every, hidden), BF),
                pltpu.VMEM((rows, hidden), BF),
                pltpu.VMEM((every, model), BF),
                pltpu.SemaphoreType.DMA((8,)),
                pltpu.SemaphoreType.DMA((5 + 3 * hidden // LANES,)),
            ],
            8 * rows * model * hidden, 34, range(8))

    def merge_forward(layer, scal, h_own, mix, gated):
        return call(
            functools.partial(merge_forward_kernel, layer),
            [scal, sp, h_own, mix, gated, *w_u, *w_v],
            [SMEM, VMEM, VMEM, VMEM, VMEM] + [ANY] * 18,
            [flat, flat, rows_f32, stat, rows_f32],
            [
                pltpu.VMEM((4, W_UP, LANES), BF),
                pltpu.VMEM((4, DOWN_ROWS, LANES), BF),
                pltpu.VMEM((rows, model), F32),
                pltpu.VMEM((rows, LANES), F32),
                pltpu.VMEM((rows, model), F32),
                pltpu.SemaphoreType.DMA((8,)),
                pltpu.SemaphoreType.DMA((4,)),
                pltpu.SemaphoreType.DMA((2, 3)),
            ],
            2 * rows * model * hidden, 18, (2, 3, 4))

    att = attention_forward(0, scal, h_own, h_oth)
    att, u_x, u_y, v_late = fence(att, u_x, u_y, v_own)
    cut = W_ROWS - SPLIT
    d1, both = y_of(u_x[:SPLIT]), x_of(jnp.concatenate([u_y[SPLIT:], v_late], axis=0))
    u_sib, u_xs, u_ys = core_of(u_own), core_of(u_x), core_of(u_y)
    d1, both, v_late = fence(d1, both, v_late)
    d1s, both_s = core_of(d1), core_of(both)
    v_x = both[cut:]
    v_y = y_of(v_late)
    v_d = y_of(v_x)
    v_sib = core_of(v_late)
    w_u = [u_own, u_sib, u_y, u_ys, u_x, u_xs, d1, d1s, both, both_s]
    mlp0 = mlp_forward(0, scal, h_own, h_oth)
    mlp0, v_y, v_d, v_sib = fence(mlp0, v_y, v_d, v_sib)
    v_ys, v_ds = core_of(v_y), core_of(v_d)
    w_v = [v_own, v_sib, v_y, v_ys, both, both_s, v_d, v_ds]
    top0 = merge_forward(0, scal, h_own, att[5], mlp0[8])
    saved = [(h_own, att, mlp0, top0)]
    h_own, h_oth = top0[0], core_of(top0[0])
    att = attention_forward(1, scal, h_own, h_oth)
    mlp1 = mlp_forward(1, scal, h_own, h_oth)
    top1 = call(
        functools.partial(merge_turn_kernel, 1),
        [scal, sp, h_own, att[5], mlp1[8], g_last, *w_u, *w_v],
        [SMEM] + [VMEM] * 5 + [ANY] * 18,
        [flat, rows_f32, flat, flat, shape((HALO, model), BF), shape((2, D_ROWS, LANES), BF), shape((2, D_ROWS, LANES), BF)],
        [
            pltpu.VMEM((4, W_UP, LANES), BF),
            pltpu.VMEM((4, DOWN_ROWS, LANES), BF),
            pltpu.VMEM((rows, model), BF),
            pltpu.VMEM((64, LANES), F32),
            pltpu.SemaphoreType.DMA((8,)),
            pltpu.SemaphoreType.DMA((4,)),
        ],
        0,
        22,
        (),
        (1, 2, 5, 6),
    )
    saved.append((h_own, att, mlp1, top1))

    def merge_backward(layer, scal, g):
        h, att, mlp, top = saved[layer]
        return call(
            functools.partial(merge_backward_kernel, layer),
            [scal, sp, g, top[2], top[3], top[4], att[3], mlp[5]],
            [SMEM, VMEM, VMEM] + [ANY] * 5,
            [rows_f32, flat, flat, shape((HALO, model), BF),
             shape((2, D_ROWS, LANES), BF), shape((2, D_ROWS, LANES), BF)],
            [
                pltpu.VMEM((rows, model), F32),
                pltpu.VMEM((rows, LANES), F32),
                pltpu.VMEM((rows, model), F32),
                pltpu.VMEM((4, rows, LANES), BF),
                pltpu.VMEM((rows, hidden), BF),
                pltpu.VMEM((64, LANES), F32),
                pltpu.SemaphoreType.DMA((4, 4)),
            ],
            2 * rows * model * (hidden + model), 16, (), (0, 1, 4, 5))

    def conv_backward(layer, scal, gbr, halo_in):
        mlp = saved[layer][2]
        return call(
            functools.partial(conv_backward_kernel, layer),
            [scal, sp, gbr, halo_in, mlp[0], mlp[1], mlp[3], mlp[4], *w_v],
            [SMEM, VMEM, VMEM, VMEM] + [ANY] * 12,
            [wide_bf, shape((rows, hidden), F32), stat, stat, shape((4, LANES, LANES), F32)],
            [
                pltpu.VMEM((4, DOWN_ROWS, LANES), BF),
                pltpu.VMEM((every, hidden), BF),
                pltpu.VMEM((every, hidden), BF),
                pltpu.VMEM((every, hidden), BF),
                pltpu.VMEM((rows, hidden), BF),
                pltpu.VMEM((rows // SEGS + 32, SEGS, LANES), F32),
                pltpu.VMEM((rows // SEGS + 32, SEGS, LANES), F32),
                pltpu.VMEM((72, SEGS, LANES), F32),
                pltpu.VMEM((rows // SEGS, SEGS, LANES), F32),
                pltpu.VMEM((rows // SEGS // 2 + 1, SEGS, LANES), F32),
                pltpu.VMEM((HALO, LANES), F32),
                pltpu.VMEM((every, hidden), F32),
                pltpu.VMEM((every, model), BF),
                pltpu.SemaphoreType.DMA((4,)),
                pltpu.SemaphoreType.DMA((4, hidden // 256)),
            ],
            0,
            30,
        )

    def up_backward(layer, scal, dup0, hgrad, hs, xs, small):
        mlp = saved[layer][2]
        return call(
            functools.partial(up_backward_kernel, layer),
            [scal, dup0, hgrad, hs, xs, small, mlp[3], mlp[2], mlp[6], mlp[7], *w_u],
            [SMEM] + [VMEM] * 5 + [ANY] * 14,
            [rows_f32, shape((2, M_ROWS, LANES), BF), shape((2, M_ROWS, LANES), BF)],
            [
                pltpu.VMEM((4, W_ROWS - W_UP, LANES), BF),
                pltpu.VMEM((rows, hidden), BF),
                pltpu.VMEM((rows, hidden), BF),
                pltpu.VMEM((rows, LANES), F32),
                pltpu.VMEM((every, model), BF),
                pltpu.VMEM((rows, hidden), BF),
                pltpu.VMEM((4, LANES, LANES), F32),
                pltpu.SemaphoreType.DMA((8,)),
                pltpu.SemaphoreType.DMA((3, hidden // LANES)),
            ],
            0,
            30,
            (),
            (0, 1, 2),
        )

    def attention_backward(layer, scal, gatt):
        att = saved[layer][1]
        return call(
            functools.partial(attention_backward_kernel, layer),
            [scal, gatt, *att[:5], *w_u, cos_t, sin_t],
            [SMEM] + [ANY] * 18,
            [head_pack(rows), shape((4, rows, 2 * LANES), F32), shape((4, rows, 2 * LANES), BF)],
            [
                pltpu.VMEM((4, W_UP, LANES), BF),
                pltpu.VMEM((rows, LANES), F32),
                pltpu.VMEM((rows, LANES), F32),
                pltpu.VMEM((length, 2 * rows), BF),
                pltpu.VMEM((length, 2 * rows), BF),
                pltpu.VMEM((2 * rows, LANES), BF),
                pltpu.VMEM((2 * rows, LANES), BF),
                pltpu.VMEM((4, rows, LANES), BF),
                pltpu.VMEM((4, length, LANES), BF),
                pltpu.VMEM((4, length, LANES), BF),
                pltpu.VMEM((4, rows, LANES), BF),
                pltpu.VMEM((rows, LANES), F32),
                pltpu.VMEM((rows, model), BF),
                pltpu.SemaphoreType.DMA((4,)),
                pltpu.SemaphoreType.DMA((8,)),
            ],
            12 * rows * length * model, 26)

    def input_backward(layer, scal, gres, dn_mlp, dq, dkv_own, dkv_got):
        h = saved[layer][0]
        return call(
            functools.partial(input_backward_kernel, layer),
            [scal, sp, h, gres, dn_mlp, dq, dkv_own, dkv_got, *w_qkv, cos_t, sin_t],
            [SMEM, VMEM, ANY, ANY, ANY] + [VMEM] * 3 + [ANY] * 10,
            [flat, flat, shape((2, A_ROWS, LANES), BF), shape((2, A_ROWS, LANES), BF)],
            [
                pltpu.VMEM((4, 3, model, LANES), BF),
                pltpu.VMEM((rows, LANES), F32),
                pltpu.VMEM((rows, LANES), F32),
                pltpu.VMEM((rows, 12 * LANES), BF),
                pltpu.VMEM((rows, model), BF),
                pltpu.VMEM((rows, model), F32),
                pltpu.VMEM((rows, LANES), F32),
                pltpu.VMEM((4, 64, LANES), F32),
                pltpu.VMEM((rows, model), BF),
                pltpu.VMEM((rows, model), F32),
                pltpu.VMEM((rows, model), F32),
                pltpu.SemaphoreType.DMA((4,)),
                pltpu.SemaphoreType.DMA((5,)),
            ],
            14 * rows * model * model, 24, (), (2, 3))

    owner1 = jnp.logical_not(first)
    natural0, natural1 = top0[1], top1[0]
    out_keep = jnp.where(first, natural0, natural1)
    out_send = jnp.where(first, natural1, natural0)
    gres, gatt, gbr, halo_out, d_keep, d_send = top1[1:]
    gbr, halo_out, d_send, out_send, out_keep = fence(gbr, halo_out, d_send, out_send, out_keep)
    halo_in = core_of(halo_out)
    sc, gbr, halo_in, out_send, out_keep, d_send = fence(scal, gbr, halo_in, out_send, out_keep, d_send)
    d_got, out_got, out_y = core_of(d_send), x_of(out_send), y_of(out_keep)
    part = conv_backward(1, sc, gbr, halo_in)
    part, d_got, out_got, out_y = fence(part, d_got, out_got, out_y)
    d_away = total(d_keep[1], d_got[1]).astype(BF)
    sc, d_away = fence(scal, d_away)
    d_y = y_of(d_away)
    dn_mlp, m_keep, m_send = up_backward(1, sc, *part)
    gatt, d_y, m_send = fence(gatt, d_y, m_send)
    m_got = core_of(m_send)
    d1_mine, d_give = halves(total(d_keep[0], d_got[0], d_y), owner1)
    m_away = total(m_keep[1], m_got[1]).astype(BF)
    sc, d_give, m_away = fence(scal, d_give.astype(BF), m_away)
    m_y = y_of(m_away)
    d_x = x_of(d_give)
    dq, dkv_own, dkv_oth = attention_backward(1, sc, gatt)
    dq, dkv_oth, m_y, d_x = fence(dq, dkv_oth, m_y, d_x)
    dkv_got = core_of(dkv_oth)
    m1_mine, m_give = halves(total(m_keep[0], m_got[0], m_y), owner1)
    sc, m_give, out_got = fence(scal, m_give.astype(BF), out_got)
    m_x = x_of(m_give)
    out_yg = y_of(out_got)
    g, ingrad1, a_keep, a_send = input_backward(1, sc, gres, dn_mlp, dq, dkv_own, dkv_got)

    g, a_send, m_x = fence(g, a_send, m_x)
    a_got = core_of(a_send)
    dm1_half = jnp.concatenate([total(d1_mine, d_x), total(m1_mine, m_x)], axis=0).astype(BF)
    sc, dm1_half = fence(scal, dm1_half)
    dm1_half = lax.psum(dm1_half, "dp")
    gres, gatt, gbr, halo_out, d0_keep, d0_send = merge_backward(0, sc, g)
    gbr, halo_out, d0_send, a_got, out_yg = fence(gbr, halo_out, d0_send, a_got, out_yg)
    halo_in, d0_got = core_of(halo_out), core_of(d0_send)
    a_away = total(a_keep[1], a_got[1]).astype(BF)
    gbr, halo_in, d0_got, a_away = fence(gbr, halo_in, d0_got, a_away)
    d_away = total(d0_keep[1], d0_got[1]).astype(BF)
    sc, a_away, d_away = fence(scal, a_away, d_away)
    a_y, d_y = y_of(a_away), y_of(d_away)
    part = conv_backward(0, sc, gbr, halo_in)
    part, a_y, d_y = fence(part, a_y, d_y)
    a_mine, a_give = halves(total(a_keep[0], a_got[0], a_y), owner1)
    d_mine, d_give = halves(total(d0_keep[0], d0_got[0], d_y), first)
    sc, give = fence(scal, jnp.concatenate([a_give, d_give], axis=0).astype(BF))
    got = x_of(give)
    dn_mlp, m0_keep, m0_send = up_backward(0, sc, *part)
    gatt, got, m0_send, dm1_half = fence(gatt, got, m0_send, dm1_half)
    m0_got = core_of(m0_send)
    ad_half = total(jnp.concatenate([a_mine, d_mine], axis=0), got).astype(BF)
    m_away = total(m0_keep[1], m0_got[1]).astype(BF)
    sc, m_away, ad_half = fence(scal, m_away, ad_half)
    m_y = y_of(m_away)
    ad_terms = scatter_over_dp(ad_half)
    dq, dkv_own, dkv_oth = attention_backward(0, sc, gatt)
    dq, dkv_oth, m_y, ad_terms = fence(dq, dkv_oth, m_y, ad_terms)
    dkv_got = core_of(dkv_oth)
    m_mine, m_give = halves(total(m0_keep[0], m0_got[0], m_y), first)
    sc, m_give, ad_half = fence(scal, m_give.astype(BF), total(*ad_terms).astype(BF))
    m_x = x_of(m_give)
    ad_half = gather_over_dp(ad_half)
    g, ingrad0, a_keep, a_send = input_backward(0, sc, gres, dn_mlp, dq, dkv_own, dkv_got)

    ingrad0, a_send, m_x, ad_half, out_yg = fence(ingrad0, a_send, m_x, ad_half, out_yg)
    a_got = core_of(a_send)
    in_keep = jnp.where(first, ingrad0, ingrad1)
    in_got = x_of(jnp.where(first, ingrad1, ingrad0))
    m_terms = scatter_over_dp(total(m_mine, m_x).astype(BF))
    a_away = total(a_keep[1], a_got[1]).astype(BF)
    a_y = y_of(a_away)
    a_y, m_terms, in_keep, in_got = fence(a_y, m_terms, in_keep, in_got)
    a_sum = total(a_keep[0], a_got[0], a_y).astype(BF)
    a_x = x_of(a_sum)
    in_y = y_of(in_keep)
    m_parts = gather_over_dp(total(*m_terms).astype(BF))
    out_half = jnp.stack([out_keep, out_y, out_got, out_yg])
    out_other = core_of(out_half)
    a_x, m_parts, ad_half, in_y, in_got, out_other = fence(a_x, m_parts, ad_half, in_y, in_got, out_other)
    a_terms = scatter_over_dp(total(a_sum, a_x).astype(BF))
    in_yg = y_of(in_got)
    ad_half = in_order(ad_half)
    a1_half = ad_half[: A_ROWS // 2]
    dm0_half = jnp.concatenate([ad_half[A_ROWS // 2 :], in_order(m_parts)], axis=0)
    dm_lo = jnp.where(first, dm0_half, dm1_half)
    cut = D_ROWS // 2
    away = jnp.where(first, dm1_half, dm0_half)
    m_back = x_of(away[cut:])
    d_away = jnp.concatenate([away[:cut], a1_half], axis=0)
    a_terms, in_yg, m_back, d_away = fence(a_terms, in_yg, m_back, d_away)
    d_back = x_of(d_away)
    a_parts = gather_over_dp(total(*a_terms).astype(BF))
    in_half = jnp.stack([in_keep, in_y, in_got, in_yg])
    in_other = core_of(in_half)

    def assemble(here, there):
        return call(
            assemble_kernel, [scal, here, there], [SMEM, VMEM, VMEM], [shape((micro, length, model), BF)], [], 0, 10
        )[0]

    layer_out = assemble(out_half, out_other)
    input_grad = assemble(in_half, in_other)

    a_parts, layer_out, input_grad, d_back = fence(a_parts, layer_out, input_grad, d_back)
    a_whole = jnp.where(first, in_order(a_parts), jnp.concatenate([a1_half, d_back[cut:]], axis=0))
    (g_qkv, g_out, g_up, g_down, g_bqkv, g_bup, g_gain, g_gbias, g_conv, g_ng, g_nb, g_ob, g_logit) = call(
        finale_kernel,
        [dm_lo, d_back, m_back, a_whole, logits],
        [VMEM] * 4 + [SMEM],
        [shape((3, model, LANES), F32), shape((LANES, model), F32), shape((2, model, shard), F32),
         shape((shard, model), F32), shape((3, 1, LANES), F32), shape((2, shard), F32), shape((1, shard), F32),
         shape((2, shard), F32), shape((TAPS, 1, shard), F32), shape((3, 1, model), F32), shape((3, 1, model), F32),
         shape((2, model), F32), shape((2, LANES), F32)],
        [],
        0,
        16,
    )
    outs = (
        layer_out.reshape(micro, 1, length, model),
        input_grad.reshape(micro, 1, length, model),
        g_ng[:, 0],
        g_nb[:, 0],
        g_qkv,
        g_bqkv[:, 0],
        g_out,
        g_up,
        g_bup,
        g_gain[0],
        g_gbias,
        g_conv[:, 0],
        g_down,
        g_ob,
        g_logit[:, 0],
    )
    return tuple(x[None] for x in outs)


def solution(mesh):
    placed = (
        P(None, "dp", None, None),
        P(None, "dp"),
        P(None, "dp", None, None),
        P("section", None, None),
        P("section", None, None),
        P("section", None, None, "mp"),
        P("section", None, "mp"),
        P("section", "mp", None),
        P("section", None, None, "mp"),
        P("section", None, "mp"),
        P("section", "mp"),
        P("section", None, "mp"),
        P("section", None, "mp"),
        P("section", "mp", None),
        P("section", None, None),
        P("section", None),
    )
    return jax.shard_map(
        per_device,
        mesh=mesh,
        in_specs=placed,
        out_specs=(
            P("section", None, "dp", None, None),
            P("section", None, "dp", None, None),
            P("section", None, None),
            P("section", None, None),
            P("section", None, None, "mp"),
            P("section", None, "mp"),
            P("section", "mp", None),
            P("section", None, None, "mp"),
            P("section", None, "mp"),
            P("section", "mp"),
            P("section", None, "mp"),
            P("section", None, "mp"),
            P("section", "mp", None),
            P("section", None, None),
            P("section", None),
        ),
        check_vma=False,
    )
```

```python
import functools
import math

import jax
import jax.numpy as jnp
import numpy as np
from jax import lax
from jax.experimental import pallas as pl
from jax.experimental.pallas import tpu as pltpu
from jax.sharding import PartitionSpec as P

BF = jnp.bfloat16
F32 = jnp.float32
HEAD = 64
LANES = 128
SEGS = 8
HALO = 16
EPS = 1e-05
NEG = -1000000000.0
NN = (((1,), (0,)), ((), ()))
NT = (((1,), (1,)), ((), ()))
TN = (((0,), (0,)), ((), ()))

TAPS = 31
BLOCK_ROWS = 40
ROW_UP0, ROW_UP1, ROW_GAIN, ROW_GB0, ROW_GB1 = 31, 32, 33, 34, 35
ROW_QKV = 120
ROW_NG, ROW_NB, ROW_OB, ROW_LOGIT = 128, 140, 152, 160
PACK_ROWS = 168

OUT_ROWS, DOWN_ROWS, UP_ROWS, QKV_ROWS = 512, 1536, 3072, 1536
D_SMALL = OUT_ROWS + DOWN_ROWS
D_ROWS = D_SMALL + 64
M_ROWS = UP_ROWS + 128
A_ROWS = QKV_ROWS + 64

W_UP, W_ROWS = 512, 3584
SPLIT = 2560

VMEM = pl.BlockSpec(memory_space=pltpu.VMEM)
SMEM = pl.BlockSpec(memory_space=pltpu.SMEM)
ANY = pl.BlockSpec(memory_space=pltpu.HBM)


def dot(a, b, dims):
    return lax.dot_general(a, b, dims, preferred_element_type=F32)


def call(kernel, ins, in_specs, outs, scratch, flops, mib, far=(), home=()):
    ins = [pltpu.with_memory_space_constraint(x, pltpu.HBM) if p is ANY else x for x, p in zip(ins, in_specs)]
    return pl.pallas_call(
        kernel,
        in_specs=in_specs,
        out_specs=[ANY if i in far else VMEM for i in range(len(outs))],
        out_shape=[pltpu.HBM(x.shape, x.dtype) if i in far or i in home else x for i, x in enumerate(outs)],
        scratch_shapes=scratch,
        compiler_params=pltpu.CompilerParams(vmem_limit_bytes=mib << 20),
        cost_estimate=pl.CostEstimate(flops=1, bytes_accessed=1, transcendentals=0),
    )(*ins)


def shape(dims, dtype):
    return jax.ShapeDtypeStruct(dims, dtype)


def fetch(flag, here, there, sems):
    @pl.when(flag)
    def _():
        for i, (a, d) in enumerate(here):
            pltpu.make_async_copy(a, d, sems.at[i]).start()

    @pl.when(jnp.logical_not(flag))
    def _():
        for i, (a, d) in enumerate(there):
            pltpu.make_async_copy(a, d, sems.at[i]).start()


def landed(pairs, sems):
    for i, (a, d) in enumerate(pairs):
        pltpu.make_async_copy(a, d, sems.at[i]).wait()


def slab_copies(sets, dst, lo, hi):
    here, there = [], []
    for j in range(4):
        for a, b in ((lo, min(hi, SPLIT)), (max(lo, SPLIT), hi)):
            if a >= b:
                continue
            d = dst.at[j, pl.ds(a - lo, b - a), :]
            here.append((sets[j].at[pl.ds(a, b - a), :], d))
            if j < 2:
                there.append((sets[4 + j].at[pl.ds(a, b - a), :], d))
            elif a < SPLIT:
                there.append((sets[4 + j].at[pl.ds(a, b - a), :], d))
            else:
                there.append((sets[6 + j].at[pl.ds(a - SPLIT, b - a), :], d))
    return here, there


def down_copies(sets, dst):
    here, there = shard_copies(sets, dst)
    rows = dst.shape[1]
    for j in range(2):
        there[j] = (sets[4 + j].at[pl.ds(W_ROWS - SPLIT, rows), :], dst.at[j])
    return here, there


def shard_copies(sets, dst):
    return [(sets[j], dst.at[j]) for j in range(4)], [(sets[4 + j], dst.at[j]) for j in range(4)]


def wide(sp, row, count=4):
    return jnp.concatenate([sp[0, 0, row + i : row + i + 1, :] for i in range(count)], axis=1)


def branch_weights(sp):
    l0 = sp[0, 0, ROW_LOGIT : ROW_LOGIT + 1, :]
    l1 = sp[0, 0, ROW_LOGIT + 1 : ROW_LOGIT + 2, :]
    top = jnp.maximum(l0, l1)
    e0, e1 = jnp.exp(l0 - top), jnp.exp(l1 - top)
    total = e0 + e1
    return jnp.concatenate([e0 / total] * 4, axis=1), jnp.concatenate([e1 / total] * 4, axis=1)


def normalized(x):
    center = jnp.mean(x, axis=-1, keepdims=True)
    d = x - center
    inverse = lax.rsqrt(jnp.mean(d * d, axis=-1, keepdims=True) + EPS)
    return d * inverse, inverse


def frame_of(row, half, rows):
    return half * rows + (row & (SEGS - 1)) * (rows // SEGS) + (row >> 3)


def order_matrix(rows, back):
    r = lax.broadcasted_iota(jnp.int32, (rows, rows), 1 if back else 0)
    t = lax.broadcasted_iota(jnp.int32, (rows, rows), 0 if back else 1)
    return jnp.where(frame_of(r, 0, rows) == t, 1.0, 0.0).astype(BF)


def halo_pick(rows, start_seg_even):
    start, seg = start_seg_even
    i = lax.broadcasted_iota(jnp.int32, (HALO, rows), 0)
    r = lax.broadcasted_iota(jnp.int32, (HALO, rows), 1)
    return jnp.where(r == (i + start) * SEGS + seg, 1.0, 0.0).astype(BF)


def swap_halves(x):
    lane = lax.broadcasted_iota(jnp.int32, x.shape, 1)
    return jnp.where(
        (lane & (HEAD - 1)) < HEAD // 2,
        pltpu.roll(x, LANES - HEAD // 2, 1),
        pltpu.roll(x, HEAD // 2, 1),
    )


def rotate(x, cosine, sine):
    return x * cosine + swap_halves(x) * sine


def rotate_back(x, cosine, sine):
    return x * cosine - swap_halves(x) * sine


def pieces(x):
    hi = x.astype(BF).astype(F32)
    rest = x - hi
    mid = rest.astype(BF).astype(F32)
    return hi, mid, rest - mid


def pack_kernel(
    wout_h, wup_h, wdown_h, cw, bup, ggain, gbias, bqkv, ngain, nbias, obias, logits,
    sp_o, u_o, v_o, wout, wup, wdown, sems,
):
    loads = [
        pltpu.make_async_copy(a, b, sems.at[i])
        for i, (a, b) in enumerate(((wup_h, wup), (wdown_h, wdown), (wout_h, wout)))
    ]
    for c in loads:
        c.start()
    sp_o[...] = jnp.zeros_like(sp_o)
    for b in range(3):
        lanes = slice(b * LANES, (b + 1) * LANES)
        at = b * BLOCK_ROWS
        sp_o[at : at + TAPS, :] = cw[:, lanes]
        sp_o[at + ROW_UP0 : at + ROW_UP0 + 2, :] = bup[:, lanes]
        sp_o[at + ROW_GAIN : at + ROW_GAIN + 1, :] = ggain[:, lanes]
        sp_o[at + ROW_GB0 : at + ROW_GB0 + 2, :] = gbias[:, lanes]
    sp_o[ROW_QKV : ROW_QKV + 3, :] = bqkv[...]
    for i in range(4):
        lanes = slice(i * LANES, (i + 1) * LANES)
        for n in range(3):
            sp_o[ROW_NG + 4 * n + i : ROW_NG + 4 * n + i + 1, :] = ngain[n : n + 1, lanes]
            sp_o[ROW_NB + 4 * n + i : ROW_NB + 4 * n + i + 1, :] = nbias[n : n + 1, lanes]
        for n in range(2):
            sp_o[ROW_OB + 4 * n + i : ROW_OB + 4 * n + i + 1, :] = obias[n : n + 1, lanes]
    for n in range(2):
        sp_o[ROW_LOGIT + n : ROW_LOGIT + n + 1, :] = jnp.full((1, LANES), logits[n], F32)
    for c in loads:
        c.wait()
    model, shard = wup.shape[1], wup.shape[2]
    for lb in range(4):
        lanes = slice(lb * LANES, (lb + 1) * LANES)
        u_o[lb * LANES : (lb + 1) * LANES, :] = wout[:, lanes]
        v_o[lb * shard : (lb + 1) * shard, :] = wdown[:, lanes]
    for hh in range(2):
        for b in range(3):
            at = W_UP + (hh * 3 + b) * model
            u_o[at : at + model, :] = wup[hh, :, b * LANES : (b + 1) * LANES]


def prologue_kernel(scal, frames, cotangent, own_o, oth_o, g_o, buf, sems):
    rows = own_o.shape[0]
    u, half = scal[0], scal[1]
    mine = pl.ds(pl.multiple_of(half * rows, rows), rows)
    other = pl.ds(pl.multiple_of((1 - half) * rows, rows), rows)
    copies = [
        pltpu.make_async_copy(frames.at[u, 0, mine, :], buf.at[0], sems.at[0]),
        pltpu.make_async_copy(frames.at[u, 0, other, :], buf.at[1], sems.at[1]),
        pltpu.make_async_copy(cotangent.at[u, 0, mine, :], buf.at[2], sems.at[2]),
    ]
    for c in copies:
        c.start()
    order = order_matrix(rows, False)
    for c, i, out in zip(copies, range(3), (own_o, oth_o, g_o)):
        c.wait()
        out[...] = dot(order, buf[i], NN).astype(BF)


def attention_forward_kernel(layer, scal, sp, cos_t, sin_t, h_own, h_oth, *refs):
    sets, refs = refs[:8], refs[8:]
    q_h, k_h, v_h, mix_h, lse_h, mix_o, w_s, cs, sn, norm, lse_s, q_o, k_o, v_o, lse_o, wsem, tsem, osem = refs
    sp = sp.at[pl.ds(layer, 1)]
    rows, model = h_own.shape
    half, length = scal[1], scal[2]
    here, there = shard_copies(sets, w_s)
    fetch(scal[3] == layer, here, there, wsem)
    tables = [
        pltpu.make_async_copy(cos_t.at[half], cs, tsem.at[0]),
        pltpu.make_async_copy(sin_t.at[half], sn, tsem.at[1]),
    ]
    for c in tables:
        c.start()
    gain, bias = wide(sp, ROW_NG), wide(sp, ROW_NB)
    step = 64
    for src, base in ((h_own, 0), (h_oth, rows)):
        for r in range(0, rows, step):
            hat, unused = normalized(src[r : r + step, :].astype(F32))
            norm[base + r : base + r + step, :] = (hat * gain + bias).astype(BF)
    lse_s[...] = jnp.zeros_like(lse_s)
    for c in tables:
        c.wait()
    landed(here, wsem)
    total = 2 * rows
    row = lax.broadcasted_iota(jnp.int32, (total, LANES), 0)
    part = jnp.where(row < rows, half, 1 - half)
    position = frame_of(row & (rows - 1), part, rows)
    mask = jnp.where(position < length, 0.0, NEG)
    lane_k = lax.broadcasted_iota(jnp.int32, (total, LANES), 1)
    lane_q = lax.broadcasted_iota(jnp.int32, (rows, LANES), 1)

    def stores(j):
        pairs = ((q_o, q_h), (k_o, k_h), (v_o, v_h), (mix_o, mix_h))
        return [pltpu.make_async_copy(a.at[j], b.at[j], osem.at[j, i]) for i, (a, b) in enumerate(pairs)]

    def shard(j):
        mj = scal[4 + j]
        bq = sp[0, mj, ROW_QKV : ROW_QKV + 1, :]
        bk = sp[0, mj, ROW_QKV + 1 : ROW_QKV + 2, :]
        bv = sp[0, mj, ROW_QKV + 2 : ROW_QKV + 3, :]
        everything = norm[...]
        q = rotate(dot(norm[:rows, :], w_s[j, 0], NN) + bq, cs[:rows, :], sn[:rows, :])
        q = q.astype(BF).astype(F32) * (1.0 / math.sqrt(HEAD))
        k = rotate(dot(everything, w_s[j, 1], NN) + bk, cs[...], sn[...]).astype(BF)
        v = (dot(everything, w_s[j, 2], NN) + bv).astype(BF)
        q_o[j] = q.astype(BF)
        k_o[j] = k
        v_o[j] = v
        kf = k.astype(F32)
        vt = v.astype(F32).T.astype(BF)
        outs = []
        work = []
        for hd in range(2):
            spare = (1 - hd) * HEAD
            qm = jnp.where((lane_q >> 6) == hd, q, jnp.where(lane_q == spare, 1.0, 0.0)).astype(BF)
            km = jnp.where((lane_k >> 6) == hd, kf, jnp.where(lane_k == spare, mask, 0.0)).astype(BF)
            work.append((km, qm))
        score = dot(*work[0], NT)
        for hd in range(2):
            s = score
            if hd == 0:
                score = dot(*work[1], NT)
            top = jnp.max(s, axis=0, keepdims=True)
            p = jnp.exp(s - top)
            den = jnp.sum(p, axis=0, keepdims=True)
            p = (p * (1.0 / den)).astype(BF)
            outs.append(dot(vt[hd * HEAD : (hd + 1) * HEAD, :], p, NN))
            lse_s[2 * j + hd : 2 * j + hd + 1, :] = top + jnp.log(den)
        mix_o[j] = jnp.concatenate(outs, axis=0).T.astype(BF)
        for c in stores(j):
            c.start()

    for j in range(4):
        shard(j)
    lse_o[...] = lse_s[...].T
    last = pltpu.make_async_copy(lse_o, lse_h, osem.at[4, 0])
    last.start()
    for j in range(4):
        for c in stores(j):
            c.wait()
    last.wait()


def gelu_parts(u):
    d = 1.0 + (0.3275911 / math.sqrt(2.0)) * jnp.abs(u)
    t = pl.reciprocal(d, approx=True)
    t = t * (2.0 - d * t)
    e = jnp.exp2((-0.5 / math.log(2.0)) * (u * u))
    half = [0.5 * c for c in (1.061405429, -1.453152027, 1.421413741, -0.284496736, 0.254829592)]
    poly = ((((half[0] * t + half[1]) * t + half[2]) * t + half[3]) * t + half[4]) * t
    tail = poly * e
    phi = jnp.where(u >= 0, 1.0 - tail, tail)
    return u * phi, phi + (u * e) * (1.0 / math.sqrt(2.0 * math.pi))


PHASES = ((0,), (2,), (2, 4), (1,), (3,), (3, 5), (1, 2), (3, 4), (3, 4, 5, 6))
TAP_PHASES = ((0,), (2,), (0, 2), (1,), (3,), (1, 3), (0, 1), (2, 3), (0, 1, 2, 3))


def phase(ref, rows, n):
    out = ref[4 * n + rows[0]]
    for r in rows[1:]:
        out = out + ref[4 * n + r]
    return out


def correlate(taps, xs, count):
    accs = [None] * count
    for m, tap in enumerate(taps):
        for n in range(count):
            term = tap * xs[n + m]
            accs[n] = term if accs[n] is None else accs[n] + term
    return accs


def unfold(q0, q1, q2):
    out = []
    for n in range(len(q2)):
        out.append(q0[n] + q1[n])
        out.append(q2[n] - (q0[n + 1] + q1[n]))
    if len(q1) > len(q2):
        out.append(q0[len(q2)] + q1[len(q2)])
    return out


def fill_filters(filt, row):
    for m in range(8):
        w = [
            jnp.broadcast_to(row(4 * m + r), (SEGS, LANES)) if 4 * m + r < TAPS else jnp.zeros((SEGS, LANES), F32)
            for r in range(4)
        ]
        for i, rows in enumerate(TAP_PHASES):
            out = w[rows[0]]
            for r in rows[1:]:
                out = out + w[r]
            filt[i * 8 + m] = out


def fast_fir(pad, filt, out, keep):
    count = out.shape[0]
    half = count // 2
    for g in range(3):
        qs = []
        for i in range(3):
            n = half // 2 + 1 if i == 0 or (i == 1 and g == 0) else half // 2
            xs = [phase(pad, PHASES[3 * g + i], x) for x in range(n + 7)]
            qs.append(correlate([filt[(3 * g + i) * 8 + m] for m in range(8)], xs, n))
        p = unfold(*qs)
        for n in range(len(p)):
            if g == 0:
                keep[n] = p[n]
            elif g == 1:
                out[2 * n] = keep[n] + p[n]
                out[2 * n + 1] = keep[n + 1] + p[n]
            else:
                out[2 * n + 1] = p[n] - out[2 * n + 1]


def tap_sums(gpad, xpad, count):
    ps = []
    for g in range(3):
        qs = []
        for i in range(3):
            rows = [15 + r for r in TAP_PHASES[3 * g + i]]
            n = 9 if i == 0 else 8
            steps = count // 4
            xs = [phase(xpad, PHASES[3 * g + i], x) for x in range(n + steps - 1)]
            qs.append(correlate([phase(gpad, rows, x) for x in range(steps)], xs, n))
        ps.append(unfold(*qs))
    out = []
    for m in range(16):
        out.append(ps[0][m] + ps[1][m])
        if m < 15:
            out.append(ps[2][m] - (ps[0][m + 1] + ps[1][m]))
    return out


def halo_pads(pad, block, halo_ref, half, right_is_even):
    count = block.shape[0]
    pad[15 : 15 + count] = block
    pad[30 + count : 32 + count] = jnp.zeros((2, SEGS, LANES), F32)
    seg = lax.broadcasted_iota(jnp.int32, (SEGS, LANES), 0)
    from_left = half.astype(F32)
    from_right = 1.0 - from_left
    for i in range(15):
        tail = pltpu.roll(block[count - 15 + i], 1, 0)
        edge = jnp.broadcast_to(halo_ref[i + 1 : i + 2, :], (SEGS, LANES)) * from_left
        pad[i] = jnp.where(seg == 0, edge, tail)
        head = pltpu.roll(block[i], SEGS - 1, 0)
        edge = jnp.broadcast_to(halo_ref[i : i + 1, :], (SEGS, LANES)) * from_right
        pad[15 + count + i] = jnp.where(seg == SEGS - 1, edge, head)


def mlp_forward_kernel(layer, scal, sp, h_own, h_oth, *refs):
    sets, refs = refs[:10], refs[10:]
    (act0_h, dact0_h, dact1_h, ghat_h, conv_h, gated_h, ginv_h, norm_h, gated_o,
     ws, act0, act1, sums, gmean, ginv, pad, filt, fir, keep, halo, act0_o, dact0_o, dact1_o, ghat_o, conv_o, norm_o, wsem, osem) = refs
    sp = sp.at[pl.ds(layer, 1)]
    rows, model = h_own.shape
    every = rows + HALO
    hidden = act0.shape[1]
    shard = hidden // 4
    half, length = scal[1], scal[2]
    here, there = slab_copies(sets, ws, W_UP, W_ROWS)
    fetch(scal[3] == layer, here, there, wsem)
    gain, bias = wide(sp, ROW_NG + 4), wide(sp, ROW_NB + 4)
    step = 64
    for r in range(0, rows, step):
        hat, unused = normalized(h_own[r : r + step, :].astype(F32))
        norm_o[r : r + step, :] = (hat * gain + bias).astype(BF)
    i = lax.broadcasted_iota(jnp.int32, (HALO, rows), 0)
    r = lax.broadcasted_iota(jnp.int32, (HALO, rows), 1)
    wanted = jnp.where(half == 0, i * SEGS, (i + rows // SEGS - HALO) * SEGS + SEGS - 1)
    pick = jnp.where(r == wanted, 1.0, 0.0).astype(BF)
    hat, unused = normalized(dot(pick, h_oth[...], NN))
    norm_o[rows:every, :] = (hat * gain + bias).astype(BF)
    sums[...] = jnp.zeros_like(sums)

    width = 256
    chunk = 48

    def up(i, carry):
        lanes = pl.ds(pl.multiple_of(i * width, width), width)
        rows_of = []
        for hh, base in ((0, ROW_UP0), (1, ROW_UP1)):
            got = []
            for t in range(2):
                c = 2 * i + t
                got.append(sp[0, scal[8 + c], pl.ds(lax.rem(c, 3) * BLOCK_ROWS + base, 1), :])
            rows_of.append(jnp.concatenate(got, axis=1))
        slabs = []
        for hh in range(2):
            pair = []
            for t in range(2):
                c = 2 * i + t
                at = (hh * 3 + lax.rem(c, 3)) * model
                pair.append(ws[lax.div(c, 3), pl.ds(pl.multiple_of(at, model), model), :])
            slabs.append(jnp.concatenate(pair, axis=1))
        u0 = dot(norm_o[...], slabs[0], NN)
        u1 = dot(norm_o[...], slabs[1], NN)
        for r in range(0, every, chunk):
            a, d = gelu_parts(u0[r : r + chunk] + rows_of[0])
            act0[r : r + chunk, lanes] = a
            act0_o[r : r + chunk, lanes] = a.astype(BF)
            dact0_o[r : r + chunk, lanes] = d.astype(BF)
        for r in range(0, every, chunk):
            a, d = gelu_parts(u1[r : r + chunk] + rows_of[1])
            act1[r : r + chunk, lanes] = a
            dact1_o[r : r + chunk, lanes] = d.astype(BF)
            sums[r : r + chunk, :] += a[:, :LANES] + a[:, LANES:]
        return carry

    middle = hidden // width // 2
    for n in range(2):
        for i in range(4 * n, 4 * n + 4):
            pltpu.make_async_copy(*here[i], wsem.at[i]).wait()
        lax.fori_loop(n * middle, (n + 1) * middle, up, 0)
    for r in range(0, every, chunk):
        center = jnp.sum(sums[r : r + chunk, :], axis=1, keepdims=True) * (1.0 / hidden)
        d = act1[r : r + chunk, :] - center
        spread = jnp.sum(d * d, axis=1, keepdims=True) * (1.0 / hidden)
        gmean[r : r + chunk, :] = jnp.broadcast_to(center, (chunk, LANES))
        ginv[r : r + chunk, :] = jnp.broadcast_to(lax.rsqrt(spread + EPS), (chunk, LANES))
    stores = [
        pltpu.make_async_copy(a, b, osem.at[i])
        for i, (a, b) in enumerate(
            ((act0_o, act0_h), (dact0_o, dact0_h), (dact1_o, dact1_h), (norm_o, norm_h), (ginv.at[pl.ds(0, rows)], ginv_h))
        )
    ]
    for c in stores:
        c.start()

    def column_stores(c):
        lanes = pl.ds(pl.multiple_of(c * LANES, LANES), LANES)
        pairs = ((ghat_o, ghat_h), (conv_o, conv_h), (gated_o, gated_h))
        return [
            pltpu.make_async_copy(a.at[:, lanes], b.at[:, lanes], osem.at[5 + 3 * c + i]) for i, (a, b) in enumerate(pairs)
        ]


    row = lax.broadcasted_iota(jnp.int32, (rows, LANES), 0)
    valid = jnp.where(frame_of(row, half, rows) < length, 1.0, 0.0)
    hrow = lax.broadcasted_iota(jnp.int32, (HALO, LANES), 0)
    valid_halo = jnp.where(jnp.where(half == 0, rows, rows - HALO) + hrow < length, 1.0, 0.0)
    count = rows // SEGS

    def gate(c, carry):
        lanes = pl.ds(pl.multiple_of(c * LANES, LANES), LANES)
        mj = scal[8 + c]
        base = lax.rem(c, 3) * BLOCK_ROWS
        ggain = sp[0, mj, pl.ds(base + ROW_GAIN, 1), :]
        gb0 = sp[0, mj, pl.ds(base + ROW_GB0, 1), :]
        gb1 = sp[0, mj, pl.ds(base + ROW_GB1, 1), :]
        hat = (act1[rows:every, lanes] - gmean[rows:every, :]) * ginv[rows:every, :]
        ghat_o[rows:every, lanes] = hat.astype(BF)
        halo[...] = (hat * ggain + gb0) * valid_halo
        hat = (act1[0:rows, lanes] - gmean[0:rows, :]) * ginv[0:rows, :]
        ghat_o[0:rows, lanes] = hat.astype(BF)
        normed = (hat * ggain + gb0) * valid
        halo_pads(pad, normed.reshape(count, SEGS, LANES), halo, half, True)
        fill_filters(filt, lambda k: sp[0, mj, pl.ds(base + k, 1), :])
        fast_fir(pad, filt, fir, keep)
        for t in range(0, count, 8):
            at = t * SEGS
            cv = fir[t : t + 8].reshape(64, LANES) + gb1
            conv_o[at : at + 64, lanes] = cv.astype(BF)
            gated_o[at : at + 64, lanes] = (act0[at : at + 64, lanes] * cv).astype(BF)
        for store in column_stores(c):
            store.start()
        return carry

    lax.fori_loop(0, hidden // LANES, gate, 0)
    for c in range(hidden // LANES):
        stores.extend(column_stores(c))
    for c in stores:
        c.wait()


def attention_rows(mix, ws, r, block):
    mixed = jnp.concatenate([mix[j, r : r + block, :] for j in range(4)], axis=1)
    out = []
    for lb in range(0, 4, 2):
        w = [
            jnp.concatenate([ws[j, (lb + t) * LANES : (lb + t + 1) * LANES, :] for j in range(4)], axis=0)
            for t in range(2)
        ]
        out.append(dot(mixed, jnp.concatenate(w, axis=1), NN))
    return jnp.concatenate(out, axis=1)


def perceptron_rows(gated, wv, r, block):
    shard = wv.shape[1] // 4
    out = []
    for lb in range(0, 4, 2):
        w = [
            jnp.concatenate([wv[j, (lb + t) * shard : (lb + t + 1) * shard, :] for j in range(4)], axis=0)
            for t in range(2)
        ]
        out.append(dot(gated[r : r + block, :], jnp.concatenate(w, axis=1), NN))
    return jnp.concatenate(out, axis=1)


def merge_forward_kernel(layer, scal, sp, h_own, mix, gated, *refs):
    u_sets, v_sets, refs = refs[:10], refs[10:18], refs[18:]
    o_o, nat_o, rhat_h, rstd_h, diff_h, ws, wv, rhat_o, rstd_o, diff_o, usem, vsem, osem = refs
    sp = sp.at[pl.ds(layer, 1)]
    rows, model = h_own.shape
    shard = wv.shape[1] // 4
    here, there = slab_copies(u_sets, ws, 0, W_UP)
    fetch(scal[3] == layer, here, there, usem)
    here_v, there_v = down_copies(v_sets, wv)
    fetch(scal[3] == layer, here_v, there_v, vsem)
    landed(here, usem)
    block = 256
    atts = [attention_rows(mix, ws, r, block) for r in range(0, rows, block)]
    landed(here_v, vsem)
    step = 64

    def stores(r, n):
        part = pl.ds(r, n)
        pairs = ((rhat_o, rhat_h), (rstd_o, rstd_h), (diff_o, diff_h))
        return [
            pltpu.make_async_copy(a.at[part], b.at[part], osem.at[r // n, i]) for i, (a, b) in enumerate(pairs)
        ]

    w0, w1 = branch_weights(sp)
    gain, bias = wide(sp, ROW_NG + 8), wide(sp, ROW_NB + 8)
    b0, b1 = wide(sp, ROW_OB), wide(sp, ROW_OB + 4)
    for r in range(0, rows, block):
        att, br = atts[r // block], perceptron_rows(gated, wv, r, block)
        for q in range(0, block, step):
            at = att[q : q + step] + b0
            bt = br[q : q + step] + b1
            res = h_own[r + q : r + q + step, :].astype(F32) + w0 * at + w1 * bt
            hat, inverse = normalized(res)
            diff_o[r + q : r + q + step, :] = at - bt
            rhat_o[r + q : r + q + step, :] = hat
            rstd_o[r + q : r + q + step, :] = jnp.broadcast_to(inverse, (step, LANES))
            o_o[r + q : r + q + step, :] = (hat * gain + bias).astype(BF)
        for c in stores(r, block):
            c.start()
    nat_o[...] = dot(order_matrix(rows, True), o_o[...], NN).astype(BF)
    for r in range(0, rows, block):
        for c in stores(r, block):
            c.wait()


def binary_weights(down):
    lane = lax.broadcasted_iota(jnp.int32, (1, LANES), 1)
    out = jnp.full((1, LANES), 2.0 ** (63 if down else -63), F32)
    for b in range(7):
        out = jnp.where(((lane >> b) & 1) == 1, out * 2.0 ** (-(2**b) if down else 2**b), out)
    return out


def merge_finish(half, sums, slope, mix, gated, gatt_o, gbr_o, halo_o, keep_o, send_o, small, late):
    rows = gbr_o.shape[0]
    i = lax.broadcasted_iota(jnp.int32, (HALO, rows), 0)
    r = lax.broadcasted_iota(jnp.int32, (HALO, rows), 1)
    wanted = jnp.where(half == 0, (i + rows // SEGS - HALO) * SEGS + SEGS - 1, i * SEGS)
    pick = jnp.where(r == wanted, 1.0, 0.0).astype(BF)
    halo_o[...] = dot(pick, gbr_o[...], NN).astype(BF)
    slope = jnp.sum(slope, axis=1, keepdims=True)
    small[...] = jnp.zeros_like(small)
    for n, v in enumerate(sums):
        for i in range(4):
            small[4 * n + i : 4 * n + i + 1, :] = v[:, i * LANES : (i + 1) * LANES]
    scaled = jnp.abs(slope) * binary_weights(False)
    digits = jnp.floor(scaled) - 2.0 * jnp.floor(0.5 * scaled)
    small[16:17, :] = jnp.where(slope < 0, -digits, digits)
    shards = (keep_o.at[0], send_o.at[0], keep_o.at[1], send_o.at[1])
    shard = gated.shape[1] // 4
    late()
    for j in range(4):
        shards[j][D_SMALL:D_ROWS, :] = small[...].astype(BF)
    for j in range(4):
        w = dot(mix[j], gatt_o[...], TN).astype(BF)
        for i in range(4):
            shards[j][i * LANES : (i + 1) * LANES, :] = w[:, i * LANES : (i + 1) * LANES]
        w = dot(gated[:, j * shard : (j + 1) * shard], gbr_o[...], TN).astype(BF)
        for i in range(4):
            at = OUT_ROWS + i * shard
            shards[j][at : at + shard, :] = w[:, i * LANES : (i + 1) * LANES]


def merge_backward_kernel(
    layer, scal, sp, g, rhat_h, rstd_h, diff_h, mix_h, gated_h,
    gres_o, gatt_o, gbr_o, halo_o, keep_o, send_o, rhat, rstd, diff, mix, gated, small, sems,
):
    sp = sp.at[pl.ds(layer, 1)]
    rows, model = g.shape
    half = scal[1]
    step = 64
    parts = [pl.ds(r, 2 * step) for r in range(0, rows, 2 * step)]
    loads = [
        [
            pltpu.make_async_copy(a.at[part], b.at[part], sems.at[i, n])
            for i, (a, b) in enumerate(((rstd_h, rstd), (rhat_h, rhat), (diff_h, diff)))
        ]
        for n, part in enumerate(parts)
    ]
    late = [
        pltpu.make_async_copy(a, b, sems.at[3, i]) for i, (a, b) in enumerate(((mix_h, mix), (gated_h, gated)))
    ]
    for c in sum(loads, []) + late:
        c.start()
    gain = wide(sp, ROW_NG + 8)
    w0, w1 = branch_weights(sp)
    dgain = dbias = slope = jnp.zeros((1, model), F32)
    db = jnp.zeros((1, model), F32)
    for r in range(0, rows, step):
        if r % (2 * step) == 0:
            for c in loads[r // (2 * step)]:
                c.wait()
        gg = g[r : r + step, :].astype(F32)
        hat = rhat[r : r + step, :]
        dgain = dgain + jnp.sum(gg * hat, axis=0, keepdims=True)
        dbias = dbias + jnp.sum(gg, axis=0, keepdims=True)
        gg = gg * gain
        gr = rstd[r : r + step, 0:1] * (
            gg - jnp.mean(gg, axis=1, keepdims=True) - hat * jnp.mean(gg * hat, axis=1, keepdims=True)
        )
        gres_o[r : r + step, :] = gr
        gatt_o[r : r + step, :] = (w0 * gr).astype(BF)
        gbr_o[r : r + step, :] = (w1 * gr).astype(BF)
        db = db + jnp.sum(gr, axis=0, keepdims=True)
        slope = slope + jnp.sum(gr * diff[r : r + step, :], axis=0, keepdims=True)
    merge_finish(
        half, (dgain, dbias, w0 * db, w1 * db), slope, mix, gated, gatt_o, gbr_o, halo_o, keep_o, send_o, small,
        lambda: [c.wait() for c in late],
    )


def merge_turn_kernel(layer, scal, sp, h_own, mix, gated, g, *refs):
    u_sets, v_sets, refs = refs[:10], refs[10:18], refs[18:]
    nat_o, gres_o, gatt_o, gbr_o, halo_o, keep_o, send_o, ws, wv, o_s, small, usem, vsem = refs
    sp = sp.at[pl.ds(layer, 1)]
    rows, model = h_own.shape
    here, there = slab_copies(u_sets, ws, 0, W_UP)
    fetch(scal[3] == layer, here, there, usem)
    here_v, there_v = down_copies(v_sets, wv)
    fetch(scal[3] == layer, here_v, there_v, vsem)
    landed(here, usem)
    block = 256
    atts = [attention_rows(mix, ws, r, block) for r in range(0, rows, block)]
    landed(here_v, vsem)
    w0, w1 = branch_weights(sp)
    gain, bias = wide(sp, ROW_NG + 8), wide(sp, ROW_NB + 8)
    b0, b1 = wide(sp, ROW_OB), wide(sp, ROW_OB + 4)
    dgain = dbias = slope = db = jnp.zeros((1, model), F32)
    step = 64
    for r in range(0, rows, block):
        att, br = atts[r // block], perceptron_rows(gated, wv, r, block)
        for q in range(0, block, step):
            at = att[q : q + step] + b0
            bt = br[q : q + step] + b1
            lo, hi = r + q, r + q + step
            hat, inverse = normalized(h_own[lo:hi, :].astype(F32) + w0 * at + w1 * bt)
            o_s[lo:hi, :] = (hat * gain + bias).astype(BF)
            gg = g[lo:hi, :].astype(F32)
            dgain = dgain + jnp.sum(gg * hat, axis=0, keepdims=True)
            dbias = dbias + jnp.sum(gg, axis=0, keepdims=True)
            gg = gg * gain
            gr = inverse * (
                gg - jnp.mean(gg, axis=1, keepdims=True) - hat * jnp.mean(gg * hat, axis=1, keepdims=True)
            )
            gres_o[lo:hi, :] = gr
            gatt_o[lo:hi, :] = (w0 * gr).astype(BF)
            gbr_o[lo:hi, :] = (w1 * gr).astype(BF)
            db = db + jnp.sum(gr, axis=0, keepdims=True)
            slope = slope + jnp.sum(gr * (at - bt), axis=0, keepdims=True)
    nat_o[...] = dot(order_matrix(rows, True), o_s[...], NN).astype(BF)
    merge_finish(
        scal[1], (dgain, dbias, w0 * db, w1 * db), slope, mix, gated, gatt_o, gbr_o, halo_o, keep_o, send_o, small,
        lambda: None,
    )


def attention_backward_kernel(layer, scal, gatt_h, q_h, k_h, v_h, mix_h, lse_h, *refs):
    sets, refs = refs[:10], refs[10:]
    cos_t, sin_t, dq_o, own_o, oth_o, w_s, cs, sn, pbuf, dsbuf, dom, qm2, q_r, k_r, v_r, mix, lse, gatt, wsem, tsem = refs
    rows = gatt.shape[0]
    total = 2 * rows
    half, length = scal[1], scal[2]
    here, there = slab_copies(sets, w_s, 0, W_UP)
    fetch(scal[3] == layer, here, there, wsem)
    tables = [
        pltpu.make_async_copy(cos_t.at[half, pl.ds(0, rows), :], cs, tsem.at[0]),
        pltpu.make_async_copy(sin_t.at[half, pl.ds(0, rows), :], sn, tsem.at[1]),
    ]
    for i, (a, b) in enumerate(((q_h, q_r), (k_h, k_r), (v_h, v_r), (mix_h, mix), (lse_h, lse), (gatt_h, gatt))):
        tables.append(pltpu.make_async_copy(a, b, tsem.at[2 + i]))
    for c in tables:
        c.start()
    row = lax.broadcasted_iota(jnp.int32, (total, LANES), 0)
    part = jnp.where(row < rows, half, 1 - half)
    position = frame_of(row & (rows - 1), part, rows)
    mask = jnp.where(position < length, 0.0, NEG)
    lane_k = lax.broadcasted_iota(jnp.int32, (total, LANES), 1)
    lane_q = lax.broadcasted_iota(jnp.int32, (rows, LANES), 1)
    for c in tables:
        c.wait()
    landed(here, wsem)

    def shard(j):
        wo = jnp.concatenate([w_s[j, lb * LANES : (lb + 1) * LANES, :] for lb in range(4)], axis=1)
        dm = dot(gatt[...], wo, NT).astype(BF).astype(F32)
        prod = dm * mix[j].astype(F32)
        q = q_r[j].astype(F32)
        k = k_r[j].astype(F32)
        v = v_r[j].astype(F32)
        kt = k.T.astype(BF)
        dqs = []
        for hd in range(2):
            spare = (1 - hd) * HEAD
            in_q, in_k = (lane_q >> 6) == hd, (lane_k >> 6) == hd
            minus_lse = -jnp.sum(jnp.where(lane_q == 2 * j + hd, lse[...], 0.0), axis=1, keepdims=True)
            minus_delta = -jnp.sum(jnp.where(in_q, prod, 0.0), axis=1, keepdims=True)
            l0, l1, l2 = pieces(minus_lse)
            e0, e1, e2 = pieces(minus_delta)
            qx = jnp.where(lane_q == spare, 1.0, 0.0)
            dx = jnp.zeros_like(qx)
            for n, (lp, ep) in enumerate(((l0, e0), (l1, e1), (l2, e2))):
                here = lane_q == spare + 1 + n
                qx = jnp.where(here, lp, qx)
                dx = jnp.where(here, ep, dx)
            one = jnp.where((lane_k > spare) & (lane_k < spare + 4), 1.0, 0.0)
            qh = jnp.where(in_q, q, qx).astype(BF)
            dh = jnp.where(in_q, dm, dx).astype(BF)
            kh = jnp.where(in_k, k, jnp.where(lane_k == spare, mask, one)).astype(BF)
            vh = jnp.where(in_k, v, one).astype(BF)
            dom[hd * rows : (hd + 1) * rows, :] = jnp.where(in_q, dm, 0.0).astype(BF)
            qm2[hd * rows : (hd + 1) * rows, :] = jnp.where(in_q, q, 0.0).astype(BF)
            p = jnp.exp(dot(kh, qh, NT))
            dp = dot(vh, dh, NT)
            ds = (p * dp).astype(BF)
            pbuf[:, hd * rows : (hd + 1) * rows] = p.astype(BF)
            dsbuf[:, hd * rows : (hd + 1) * rows] = ds
            dqs.append(dot(kt[hd * HEAD : (hd + 1) * HEAD, :], ds, NN))
        dq = jnp.concatenate(dqs, axis=0).T * (1.0 / math.sqrt(HEAD))
        dq_o[j] = rotate_back(dq, cs[...], sn[...]).astype(BF)
        dk = dot(dsbuf[...], qm2[...], NN)
        dv = dot(pbuf[...], dom[...], NN)
        own_o[j, :, 0:LANES] = dk[:rows]
        own_o[j, :, LANES:] = dv[:rows]
        oth_o[j, :, 0:LANES] = dk[rows:].astype(BF)
        oth_o[j, :, LANES:] = dv[rows:].astype(BF)

    for j in range(4):
        shard(j)


def conv_backward_kernel(layer, scal, sp, gbr, ghalo, act0_h, dact0_h, ghat_h, conv_h, *refs):
    v_sets, refs = refs[:8], refs[8:]
    (dup_o, hgrad, hs, xs, small, wv, act0, dact0, ghat, conv, gpad, xpad, filt, fir, keep, halo, gcv, gbuf, vsem, asem) = refs
    sp = sp.at[pl.ds(layer, 1)]
    rows, model = gbr.shape
    every = rows + HALO
    hidden = gcv.shape[1]
    shard = hidden // 4
    half, length = scal[1], scal[2]
    here_v, there_v = down_copies(v_sets, wv)
    fetch(scal[3] == layer, here_v, there_v, vsem)
    width = 256

    def loads(i):
        lanes = pl.ds(pl.multiple_of(i * width, width), width)
        pairs = ((act0_h, act0), (conv_h, conv), (dact0_h, dact0))
        return [
            pltpu.make_async_copy(a.at[:, lanes], b.at[:, lanes], asem.at[n, i]) for n, (a, b) in enumerate(pairs)
        ]

    for i in range(hidden // width):
        for c in loads(i):
            c.start()
    last = pltpu.make_async_copy(ghat_h, ghat, asem.at[3, 0])
    last.start()
    gbuf[0:rows, :] = gbr[...]
    gbuf[rows:every, :] = ghalo[...]
    hs[...] = jnp.zeros_like(hs)
    xs[...] = jnp.zeros_like(xs)
    small[...] = jnp.zeros_like(small)
    landed(here_v, vsem)
    count = rows // SEGS
    chunk = 48

    def down(i, carry):
        for c in loads(i):
            c.wait()
        lanes = pl.ds(pl.multiple_of(i * width, width), width)
        pair = []
        for t in range(2):
            c = 2 * i + t
            base = lax.rem(c, 3) * LANES
            pair.append(
                jnp.concatenate(
                    [
                        wv[lax.div(c, 3), pl.ds(pl.multiple_of(base + lb * shard, LANES), LANES), :]
                        for lb in range(4)
                    ],
                    axis=1,
                )
            )
        g = dot(gbuf[...], jnp.concatenate(pair, axis=0), NT)
        for r in range(0, every, chunk):
            gr = g[r : r + chunk].astype(BF).astype(F32)
            gcv[r : r + chunk, lanes] = gr * act0[r : r + chunk, lanes].astype(F32)
        for r in range(0, rows, 64):
            gr = g[r : r + 64].astype(BF).astype(F32)
            keep = gr * conv[r : r + 64, lanes].astype(F32) * dact0[r : r + 64, lanes].astype(F32)
            dup_o[r : r + 64, lanes] = keep.astype(BF)
        return carry

    lax.fori_loop(0, hidden // width, down, 0)
    last.wait()
    row = lax.broadcasted_iota(jnp.int32, (rows, LANES), 0)
    valid = jnp.where(frame_of(row, half, rows) < length, 1.0, 0.0)
    hrow = lax.broadcasted_iota(jnp.int32, (HALO, LANES), 0)
    valid_halo = jnp.where(jnp.where(half == 0, rows, rows - HALO) + hrow < length, 1.0, 0.0)

    def fold(x):
        return jnp.sum(x, axis=0, keepdims=True)

    def conv_back(c, carry):
        lanes = pl.ds(pl.multiple_of(c * LANES, LANES), LANES)
        mj = scal[8 + c]
        b = lax.rem(c, 3)
        j = lax.div(c, 3)
        base = b * BLOCK_ROWS
        ggain = sp[0, mj, pl.ds(base + ROW_GAIN, 1), :]
        gb0 = sp[0, mj, pl.ds(base + ROW_GB0, 1), :]
        halo[...] = (ghat[rows:every, lanes].astype(F32) * ggain + gb0) * valid_halo
        normed = (ghat[0:rows, lanes].astype(F32) * ggain + gb0) * valid
        halo_pads(xpad, normed.reshape(count, SEGS, LANES), halo, half, True)
        halo[...] = gcv[rows:every, lanes]
        gown = gcv[0:rows, lanes]
        halo_pads(gpad, gown.reshape(count, SEGS, LANES), halo, half, True)
        small[j, pl.ds(base + ROW_GB1, 1), :] = fold(gown)
        for k, t in enumerate(tap_sums(gpad, xpad, count)):
            small[j, pl.ds(base + k, 1), :] = fold(t)
        fill_filters(filt, lambda k: sp[0, mj, pl.ds(base + TAPS - 1 - k, 1), :])
        fast_fir(gpad, filt, fir, keep)
        dgain = jnp.zeros((SEGS, LANES), F32)
        dbias = jnp.zeros((SEGS, LANES), F32)
        for t in range(0, count, 8):
            at = t * SEGS
            gn = fir[t : t + 8].reshape(64, LANES) * valid[at : at + 64]
            hat = ghat[at : at + 64, lanes].astype(F32)
            dgain = dgain + jnp.sum((gn * hat).reshape(8, SEGS, LANES), axis=0)
            dbias = dbias + jnp.sum(gn.reshape(8, SEGS, LANES), axis=0)
            gn = gn * ggain
            hgrad[at : at + 64, lanes] = gn
            hs[at : at + 64, :] += gn
            xs[at : at + 64, :] += gn * hat
        small[j, pl.ds(base + ROW_GAIN, 1), :] = fold(dgain)
        small[j, pl.ds(base + ROW_GB0, 1), :] = fold(dbias)
        return carry

    lax.fori_loop(0, hidden // LANES, conv_back, 0)
    for r in range(0, rows, 64):
        a = jnp.sum(hs[r : r + 64, :], axis=1, keepdims=True) * (1.0 / hidden)
        x = jnp.sum(xs[r : r + 64, :], axis=1, keepdims=True) * (1.0 / hidden)
        hs[r : r + 64, :] = jnp.broadcast_to(a, (64, LANES))
        xs[r : r + 64, :] = jnp.broadcast_to(x, (64, LANES))


def up_backward_kernel(layer, scal, dup0, hgrad, hs, xs, small_i, ghat_h, dact1_h, ginv_h, norm_h, *refs):
    sets, refs = refs[:10], refs[10:]
    dn_o, keep_o, send_o, ws, ghat, dact1, ginv, norm, dup1, small, wsem, asem = refs
    rows, hidden = hgrad.shape
    model = norm.shape[1]
    width = 256
    here, there = slab_copies(sets, ws, W_UP, W_ROWS)
    fetch(scal[3] == layer, here, there, wsem)
    own = pl.ds(0, rows)
    blocks = hidden // LANES

    def columns(c):
        lanes = pl.ds(pl.multiple_of(c * LANES, LANES), LANES)
        return [
            pltpu.make_async_copy(ghat_h.at[own, lanes], ghat.at[:, lanes], asem.at[0, c]),
            pltpu.make_async_copy(dact1_h.at[own, lanes], dact1.at[:, lanes], asem.at[1, c]),
        ]

    first = pltpu.make_async_copy(ginv_h, ginv, asem.at[2, 0])
    first.start()
    for c in range(blocks):
        for load in columns(c):
            load.start()
    last = pltpu.make_async_copy(norm_h, norm, asem.at[2, 1])
    last.start()
    small[...] = small_i[...]

    def fold(x):
        return jnp.sum(x, axis=0, keepdims=True)

    first.wait()

    def gate_back(c, carry):
        for load in columns(c):
            load.wait()
        lanes = pl.ds(pl.multiple_of(c * LANES, LANES), LANES)
        b = lax.rem(c, 3)
        j = lax.div(c, 3)
        base = b * BLOCK_ROWS
        s0 = jnp.zeros((1, LANES), F32)
        s1 = jnp.zeros((1, LANES), F32)
        for r in range(0, rows, 64):
            hat = ghat[r : r + 64, lanes].astype(F32)
            gi = ginv[r : r + 64, :] * (hgrad[r : r + 64, lanes] - hs[r : r + 64, :] - hat * xs[r : r + 64, :])
            d1 = (gi * dact1[r : r + 64, lanes].astype(F32)).astype(BF)
            dup1[r : r + 64, lanes] = d1
            s1 = s1 + fold(d1.astype(F32))
            s0 = s0 + fold(dup0[r : r + 64, lanes].astype(F32))
        small[j, pl.ds(base + ROW_UP0, 1), :] = s0
        small[j, pl.ds(base + ROW_UP1, 1), :] = s1
        return carry

    lax.fori_loop(0, hidden // LANES, gate_back, 0)
    landed(here, wsem)
    last.wait()
    dups = (dup0, dup1)
    for hh in range(2):
        w = jnp.concatenate(
            [ws[j, (hh * 3 + b) * model : (hh * 3 + b + 1) * model, :] for j in range(4) for b in range(3)], axis=1
        )
        if hh == 0:
            dn_o[...] = dot(dups[hh][...], w, NT)
        else:
            dn_o[...] += dot(dups[hh][...], w, NT)
    shards = (keep_o.at[0], send_o.at[0], keep_o.at[1], send_o.at[1])
    own_norm = norm[0:rows, :]
    for i in range(hidden // width):
        lo = i * width
        for hh in range(2):
            w = dot(own_norm, dups[hh][:, lo : lo + width], TN).astype(BF)
            for t in range(2):
                j, b = divmod(2 * i + t, 3)
                at = (hh * 3 + b) * model
                shards[j][at : at + model, :] = w[:, t * LANES : (t + 1) * LANES]
    for j in range(4):
        shards[j][UP_ROWS:M_ROWS, :] = small[j].astype(BF)


def input_backward_kernel(layer, scal, sp, h_h, gres_h, dn_h, dq, dkv_own, dkv_got, *refs):
    sets, refs = refs[:8], refs[8:]
    cos_t, sin_t, g_o, nat_o, keep_o, send_o, wq, cs, sn, dall, norm, xhat, xinv, small, h_own, gres, dn_mlp, wsem, tsem = refs
    sp = sp.at[pl.ds(layer, 1)]
    rows, model = h_own.shape
    half = scal[1]
    here, there = shard_copies(sets, wq)
    fetch(scal[3] == layer, here, there, wsem)
    shards = (keep_o.at[0], send_o.at[0], keep_o.at[1], send_o.at[1])
    tables = [
        pltpu.make_async_copy(cos_t.at[half, pl.ds(0, rows), :], cs, tsem.at[0]),
        pltpu.make_async_copy(sin_t.at[half, pl.ds(0, rows), :], sn, tsem.at[1]),
    ]
    tables.append(pltpu.make_async_copy(gres_h, gres, tsem.at[2]))
    tables.append(pltpu.make_async_copy(dn_h, dn_mlp, tsem.at[4]))
    first = pltpu.make_async_copy(h_h, h_own, tsem.at[3])
    first.start()
    for c in tables:
        c.start()
    first.wait()
    gain, bias = wide(sp, ROW_NG), wide(sp, ROW_NB)
    gain_mlp = wide(sp, ROW_NG + 4)
    step = 64
    for r in range(0, rows, step):
        hat, inverse = normalized(h_own[r : r + step, :].astype(F32))
        xhat[r : r + step, :] = hat
        xinv[r : r + step, :] = jnp.broadcast_to(inverse, (step, LANES))
        norm[r : r + step, :] = (hat * gain + bias).astype(BF)
    for c in tables:
        c.wait()
    for j in range(4):
        at = j * 3 * LANES
        dall[:, at : at + LANES] = dq[j]
        dk = dkv_own[j, :, 0:LANES] + dkv_got[j ^ 1, :, 0:LANES].astype(F32)
        dall[:, at + LANES : at + 2 * LANES] = rotate_back(dk, cs[...], sn[...]).astype(BF)
        dv = dkv_own[j, :, LANES:] + dkv_got[j ^ 1, :, LANES:].astype(F32)
        dall[:, at + 2 * LANES : at + 3 * LANES] = dv.astype(BF)
    landed(here, wsem)
    small[...] = jnp.zeros_like(small)
    dn = dot(dall[...], jnp.concatenate([wq[j, i] for j in range(4) for i in range(3)], axis=1), NT)
    dg0 = db0 = dg1 = db1 = jnp.zeros((1, model), F32)
    for r in range(0, rows, step):
        hat = xhat[r : r + step, :]
        a = dn[r : r + step]
        m = dn_mlp[r : r + step, :]
        dg0 = dg0 + jnp.sum(a * hat, axis=0, keepdims=True)
        db0 = db0 + jnp.sum(a, axis=0, keepdims=True)
        dg1 = dg1 + jnp.sum(m * hat, axis=0, keepdims=True)
        db1 = db1 + jnp.sum(m, axis=0, keepdims=True)
        gg = a * gain + m * gain_mlp
        dx = xinv[r : r + step, 0:1] * (
            gg - jnp.mean(gg, axis=1, keepdims=True) - hat * jnp.mean(gg * hat, axis=1, keepdims=True)
        )
        g_o[r : r + step, :] = (gres[r : r + step, :] + dx).astype(BF)
    nat_o[...] = dot(order_matrix(rows, True), g_o[...], NN).astype(BF)
    for j in range(4):
        for n, v in enumerate((dg0, dg1, db0, db1)):
            for i in range(4):
                small[j, 8 + 4 * n + i : 9 + 4 * n + i, :] = v[:, i * LANES : (i + 1) * LANES]
    for j in range(4):
        at = j * 3 * LANES
        d = dall[:, at : at + 3 * LANES]
        w = dot(norm[...], d, TN).astype(BF)
        s = jnp.sum(d.astype(F32), axis=0, keepdims=True)
        for i in range(3):
            lo = i * model
            shards[j][lo : lo + model, :] = w[:, i * LANES : (i + 1) * LANES]
            small[j, i : i + 1, :] = s[:, i * LANES : (i + 1) * LANES]
        shards[j][QKV_ROWS:A_ROWS, :] = small[j].astype(BF)


def assemble_kernel(scal, here, there, out):
    rows = here.shape[1]
    for n in range(8):
        place, half = scal[24 + n], scal[32 + n]
        part = there if n & 1 else here
        out[place, pl.ds(pl.multiple_of(half * rows, rows), rows), :] = part[n >> 1]


def finale_kernel(
    dm_lo, d_hi, m_hi, a, logits,
    qkv_o, out_o, up_o, down_o, bqkv_o, bup_o, gain_o, gbias_o, conv_o, ng_o, nb_o, ob_o, logit_o,
):
    cut = D_ROWS // 2

    def rows_of(lo, hi, at, n, a, b):
        if b <= n:
            return lo[at + a : at + b, :].astype(F32)
        if a >= n:
            return hi[a - n : b - n, :].astype(F32)
        return jnp.concatenate([lo[at + a : at + n, :], hi[0 : b - n, :]], axis=0).astype(F32)

    d_of = functools.partial(rows_of, dm_lo, d_hi, 0, cut)
    m_of = functools.partial(rows_of, dm_lo, m_hi, cut, M_ROWS // 2)
    def a_of(lo, hi):
        return a[lo:hi, :].astype(F32)

    model, shard = up_o.shape[1], up_o.shape[2]
    for i in range(3):
        qkv_o[i] = a_of(i * model, (i + 1) * model)
    for lb in range(4):
        lanes = slice(lb * LANES, (lb + 1) * LANES)
        out_o[:, lanes] = d_of(lb * LANES, (lb + 1) * LANES)
        down_o[:, lanes] = d_of(OUT_ROWS + lb * shard, OUT_ROWS + (lb + 1) * shard)
    for hh in range(2):
        for b in range(3):
            at = (hh * 3 + b) * model
            up_o[hh, :, b * LANES : (b + 1) * LANES] = m_of(at, at + model)
    small = m_of(UP_ROWS, M_ROWS)
    for b in range(3):
        lanes = slice(b * LANES, (b + 1) * LANES)
        at = b * BLOCK_ROWS
        for k in range(TAPS):
            conv_o[k, :, lanes] = small[at + k : at + k + 1]
        bup_o[:, lanes] = small[at + ROW_UP0 : at + ROW_UP0 + 2]
        gain_o[:, lanes] = small[at + ROW_GAIN : at + ROW_GAIN + 1]
        gbias_o[:, lanes] = small[at + ROW_GB0 : at + ROW_GB0 + 2]
    small = a_of(QKV_ROWS, A_ROWS)
    for n in range(3):
        bqkv_o[n] = small[n : n + 1]
    for n in range(2):
        for i in range(4):
            lanes = slice(i * LANES, (i + 1) * LANES)
            ng_o[n, :, lanes] = small[8 + 4 * n + i : 9 + 4 * n + i]
            nb_o[n, :, lanes] = small[16 + 4 * n + i : 17 + 4 * n + i]
    small = d_of(D_SMALL, D_ROWS)
    for i in range(4):
        lanes = slice(i * LANES, (i + 1) * LANES)
        ng_o[2, :, lanes] = small[i : i + 1]
        nb_o[2, :, lanes] = small[4 + i : 5 + i]
        ob_o[0:1, lanes] = small[8 + i : 9 + i]
        ob_o[1:2, lanes] = small[12 + i : 13 + i]
    total_slope = jnp.sum(small[16:17] * binary_weights(True), axis=1, keepdims=True)
    l0, l1 = jnp.full((1, LANES), logits[0], F32), jnp.full((1, LANES), logits[1], F32)
    top = jnp.maximum(l0, l1)
    e0, e1 = jnp.exp(l0 - top), jnp.exp(l1 - top)
    slope = e0 * e1 / ((e0 + e1) * (e0 + e1)) * total_slope
    logit_o[0:1, :] = slope
    logit_o[1:2, :] = -slope


def exchange(x, axis, bit):
    n = lax.axis_size(axis)
    return lax.ppermute(x, axis, [(i, i ^ bit) for i in range(n)])


def fence(*xs):
    return lax.optimization_barrier(xs)


def total(*xs):
    out = xs[0].astype(F32)
    for x in xs[1:]:
        out = out + x.astype(F32)
    return out


def scatter_over_dp(x):
    n = lax.axis_size("dp")
    if n != 4:
        return (lax.psum(x.astype(F32), "dp").astype(BF),)
    d = lax.axis_index("dp")
    x = x.reshape(n, x.shape[0] // n, LANES)
    own = lax.dynamic_index_in_dim(x, d, 0, keepdims=False)
    return (own, *[exchange(lax.dynamic_index_in_dim(x, d ^ k, 0, keepdims=False), "dp", k) for k in range(1, n)])


def gather_over_dp(x):
    n = lax.axis_size("dp")
    return (x, *[exchange(x, "dp", k) for k in range(1, n)]) if n == 4 else (x,)


def in_order(parts):
    if len(parts) == 1:
        return parts[0]
    d = lax.axis_index("dp")
    low, high = (d & 1) == 0, (d & 2) == 0
    pairs = [
        (jnp.where(low, parts[k], parts[k + 1]), jnp.where(low, parts[k + 1], parts[k])) for k in (0, 2)
    ]
    return jnp.concatenate([jnp.where(high, pairs[i][t], pairs[1 - i][t]) for i in range(2) for t in range(2)], axis=0)


def halves(x, owner):
    rows = x.shape[0] // 2
    return jnp.where(owner, x[:rows], x[rows:]), jnp.where(owner, x[rows:], x[:rows])


def rotary_constants(length):
    half_width = HEAD // 2
    freq = np.exp(np.arange(half_width, dtype=np.float32) * np.float32(-math.log(10000.0) / half_width))
    rows = length // 2
    r = np.arange(rows)
    place = (r % SEGS) * (rows // SEGS) + r // SEGS
    cosines, sines = [], []
    for half in range(2):
        t = np.concatenate([half * rows + place, (1 - half) * rows + place]).astype(np.float32)
        angle = (t[:, None] * freq.astype(np.float32)[None, :]).astype(np.float32)
        c, s = np.cos(angle.astype(np.float64)), np.sin(angle.astype(np.float64))
        cosines.append(np.concatenate([c, c, c, c], axis=1))
        sines.append(np.concatenate([-s, s, -s, s], axis=1))
    return np.stack(cosines).astype(np.float32), np.stack(sines).astype(np.float32)


def per_device(frames, lengths, out_grad, *weights):
    (norm_gains, norm_biases, wqkv, bqkv, wout, wup, bup, ggain, gbias, cw, wdown, obias, logits) = [
        w[0] for w in weights
    ]
    micro, utterances, length, model = frames.shape
    n_sec, n_mp = lax.axis_size("section"), lax.axis_size("mp")
    assert utterances == 1 and n_sec == 2 and n_mp == 4 and micro == 4
    rows = length // 2
    shard = wdown.shape[0]
    hidden = shard * n_mp
    every = rows + HALO
    s, m = lax.axis_index("section"), lax.axis_index("mp")
    u = s * 2 + (m >> 1)
    half = m & 1
    own_length = lax.dynamic_index_in_dim(lengths[:, 0], u, 0, keepdims=False)
    ns = np.arange(40)
    xors = np.zeros(40, np.int32)
    xors[4:8] = np.arange(4)
    xors[8:20] = np.arange(12) // 3
    xors[24:32] = ns[:8] >> 1 & 1
    xors[32:40] = ns[:8] & 1
    sec_bits = np.zeros(40, np.int32)
    sec_bits[24:32] = ns[:8] >> 2
    idx = jnp.asarray(ns)
    by_shard = jnp.asarray(xors)
    by_place = (s ^ jnp.asarray(sec_bits)) * 2 + ((m >> 1) ^ jnp.asarray(xors))
    by_half = half ^ jnp.asarray(xors)
    scal = jnp.where(idx < 24, by_shard, jnp.where(idx < 32, by_place, by_half))
    for i, v in enumerate((u, half, own_length, s)):
        scal = jnp.where(idx == i, v, scal)
    scal = scal.astype(jnp.int32)

    x_of = lambda v: exchange(v, "section", 1)
    y_of = lambda v: exchange(v, "mp", 2)
    core_of = lambda v: exchange(v, "mp", 1)
    flat = shape((rows, model), BF)
    rows_f32 = shape((rows, model), F32)
    stat = shape((rows, LANES), F32)
    wide_bf = shape((rows, hidden), BF)
    halo_bf = shape((every, hidden), BF)

    def head_pack(n):
        return shape((4, n, LANES), BF)

    first = s == 0

    q_x, q_y, q_sib = x_of(wqkv), y_of(wqkv), core_of(wqkv)
    packed, u_own, v_own = call(
        pack_kernel,
        [wout, wup, wdown, cw, bup, ggain[None], gbias, bqkv, norm_gains, norm_biases, obias, logits],
        [ANY] * 3 + [VMEM] * 8 + [SMEM],
        [shape((PACK_ROWS, LANES), F32), shape((W_ROWS, LANES), BF), shape((DOWN_ROWS, LANES), BF)],
        [
            pltpu.VMEM(wout.shape, BF),
            pltpu.VMEM(wup.shape, BF),
            pltpu.VMEM(wdown.shape, BF),
            pltpu.SemaphoreType.DMA((3,)),
        ],
        0,
        12,
    )
    packed, q_x, q_y, scal, u_own, v_own = fence(packed, q_x, q_y, scal, u_own, v_own)
    packed_x = x_of(packed)
    q_d = x_of(q_y)
    packed_x, packed = fence(packed_x, packed)
    sections = jnp.stack([jnp.where(first, packed, packed_x), jnp.where(first, packed_x, packed)])
    sc, sections = fence(scal, sections)
    sections_y = y_of(sections)
    h_own, h_oth, g_last = call(
        prologue_kernel,
        [sc, frames, out_grad],
        [SMEM] + [ANY] * 2,
        [flat, flat, flat],
        [pltpu.VMEM((3, rows, model), BF), pltpu.SemaphoreType.DMA((3,))],
        0,
        12,
    )
    h_own, q_d, sections_y, u_own = fence(h_own, q_d, sections_y, u_own)
    u_x, u_y = x_of(u_own), y_of(u_own)
    q_xs, q_ys = core_of(q_x), core_of(q_y)
    sp_a = jnp.stack([sections, sections_y], axis=1)
    sp_b = core_of(sp_a)
    sp = jnp.stack([sp_a, sp_b], axis=2).reshape(2, n_mp, PACK_ROWS, LANES)
    q_ds = core_of(q_d)
    w_qkv = [wqkv, q_sib, q_y, q_ys, q_x, q_xs, q_d, q_ds]

    cos_np, sin_np = rotary_constants(length)
    cos_t, sin_t = jnp.asarray(cos_np), jnp.asarray(sin_np)

    def attention_forward(layer, scal, h_own, h_oth):
        return call(
            functools.partial(attention_forward_kernel, layer),
            [scal, sp, cos_t, sin_t, h_own, h_oth, *w_qkv],
            [SMEM, VMEM, ANY, ANY, VMEM, VMEM] + [ANY] * 8,
            [head_pack(rows), head_pack(length), head_pack(length), head_pack(rows), stat, head_pack(rows)],
            [
                pltpu.VMEM((4, 3, model, LANES), BF),
                pltpu.VMEM((length, LANES), F32),
                pltpu.VMEM((length, LANES), F32),
                pltpu.VMEM((length, model), BF),
                pltpu.VMEM((LANES, rows), F32),
                pltpu.VMEM((4, rows, LANES), BF),
                pltpu.VMEM((4, length, LANES), BF),
                pltpu.VMEM((4, length, LANES), BF),
                pltpu.VMEM((rows, LANES), F32),
                pltpu.SemaphoreType.DMA((4,)),
                pltpu.SemaphoreType.DMA((2,)),
                pltpu.SemaphoreType.DMA((5, 4)),
            ],
            10 * rows * length * model, 24, range(5))

    def mlp_forward(layer, scal, h_own, h_oth):
        return call(
            functools.partial(mlp_forward_kernel, layer),
            [scal, sp, h_own, h_oth, *w_u],
            [SMEM, VMEM, VMEM, VMEM] + [ANY] * 10,
            [halo_bf, halo_bf, halo_bf, halo_bf, wide_bf, wide_bf, stat, shape((every, model), BF), wide_bf],
            [
                pltpu.VMEM((4, W_ROWS - W_UP, LANES), BF),
                pltpu.VMEM((every, hidden), F32),
                pltpu.VMEM((every, hidden), F32),
                pltpu.VMEM((every, LANES), F32),
                pltpu.VMEM((every, LANES), F32),
                pltpu.VMEM((every, LANES), F32),
                pltpu.VMEM((rows // SEGS + 32, SEGS, LANES), F32),
                pltpu.VMEM((72, SEGS, LANES), F32),
                pltpu.VMEM((rows // SEGS, SEGS, LANES), F32),
                pltpu.VMEM((rows // SEGS // 2 + 1, SEGS, LANES), F32),
                pltpu.VMEM((HALO, LANES), F32),
                pltpu.VMEM((every, hidden), BF),
                pltpu.VMEM((every, hidden), BF),
                pltpu.VMEM((every, hidden), BF),
                pltpu.VMEM((every, hidden), BF),
                pltpu.VMEM((rows, hidden), BF),
                pltpu.VMEM((every, model), BF),
                pltpu.SemaphoreType.DMA((8,)),
                pltpu.SemaphoreType.DMA((5 + 3 * hidden // LANES,)),
            ],
            8 * rows * model * hidden, 34, range(8))

    def merge_forward(layer, scal, h_own, mix, gated):
        return call(
            functools.partial(merge_forward_kernel, layer),
            [scal, sp, h_own, mix, gated, *w_u, *w_v],
            [SMEM, VMEM, VMEM, VMEM, VMEM] + [ANY] * 18,
            [flat, flat, rows_f32, stat, rows_f32],
            [
                pltpu.VMEM((4, W_UP, LANES), BF),
                pltpu.VMEM((4, DOWN_ROWS, LANES), BF),
                pltpu.VMEM((rows, model), F32),
                pltpu.VMEM((rows, LANES), F32),
                pltpu.VMEM((rows, model), F32),
                pltpu.SemaphoreType.DMA((8,)),
                pltpu.SemaphoreType.DMA((4,)),
                pltpu.SemaphoreType.DMA((2, 3)),
            ],
            2 * rows * model * hidden, 18, (2, 3, 4))

    att = attention_forward(0, scal, h_own, h_oth)
    att, u_x, u_y, v_late = fence(att, u_x, u_y, v_own)
    cut = W_ROWS - SPLIT
    d1, both = y_of(u_x[:SPLIT]), x_of(jnp.concatenate([u_y[SPLIT:], v_late], axis=0))
    u_sib, u_xs, u_ys = core_of(u_own), core_of(u_x), core_of(u_y)
    d1, both, v_late = fence(d1, both, v_late)
    d1s, both_s = core_of(d1), core_of(both)
    v_x = both[cut:]
    v_y = y_of(v_late)
    v_d = y_of(v_x)
    v_sib = core_of(v_late)
    w_u = [u_own, u_sib, u_y, u_ys, u_x, u_xs, d1, d1s, both, both_s]
    mlp0 = mlp_forward(0, scal, h_own, h_oth)
    mlp0, v_y, v_d, v_sib = fence(mlp0, v_y, v_d, v_sib)
    v_ys, v_ds = core_of(v_y), core_of(v_d)
    w_v = [v_own, v_sib, v_y, v_ys, both, both_s, v_d, v_ds]
    top0 = merge_forward(0, scal, h_own, att[5], mlp0[8])
    saved = [(h_own, att, mlp0, top0)]
    h_own, h_oth = top0[0], core_of(top0[0])
    att = attention_forward(1, scal, h_own, h_oth)
    mlp1 = mlp_forward(1, scal, h_own, h_oth)
    top1 = call(
        functools.partial(merge_turn_kernel, 1),
        [scal, sp, h_own, att[5], mlp1[8], g_last, *w_u, *w_v],
        [SMEM] + [VMEM] * 5 + [ANY] * 18,
        [flat, rows_f32, flat, flat, shape((HALO, model), BF), shape((2, D_ROWS, LANES), BF), shape((2, D_ROWS, LANES), BF)],
        [
            pltpu.VMEM((4, W_UP, LANES), BF),
            pltpu.VMEM((4, DOWN_ROWS, LANES), BF),
            pltpu.VMEM((rows, model), BF),
            pltpu.VMEM((64, LANES), F32),
            pltpu.SemaphoreType.DMA((8,)),
            pltpu.SemaphoreType.DMA((4,)),
        ],
        0,
        22,
        (),
        (1, 2, 5, 6),
    )
    saved.append((h_own, att, mlp1, top1))

    def merge_backward(layer, scal, g):
        h, att, mlp, top = saved[layer]
        return call(
            functools.partial(merge_backward_kernel, layer),
            [scal, sp, g, top[2], top[3], top[4], att[3], mlp[5]],
            [SMEM, VMEM, VMEM] + [ANY] * 5,
            [rows_f32, flat, flat, shape((HALO, model), BF),
             shape((2, D_ROWS, LANES), BF), shape((2, D_ROWS, LANES), BF)],
            [
                pltpu.VMEM((rows, model), F32),
                pltpu.VMEM((rows, LANES), F32),
                pltpu.VMEM((rows, model), F32),
                pltpu.VMEM((4, rows, LANES), BF),
                pltpu.VMEM((rows, hidden), BF),
                pltpu.VMEM((64, LANES), F32),
                pltpu.SemaphoreType.DMA((4, 4)),
            ],
            2 * rows * model * (hidden + model), 16, (), (0, 1, 4, 5))

    def conv_backward(layer, scal, gbr, halo_in):
        mlp = saved[layer][2]
        return call(
            functools.partial(conv_backward_kernel, layer),
            [scal, sp, gbr, halo_in, mlp[0], mlp[1], mlp[3], mlp[4], *w_v],
            [SMEM, VMEM, VMEM, VMEM] + [ANY] * 12,
            [wide_bf, shape((rows, hidden), F32), stat, stat, shape((4, LANES, LANES), F32)],
            [
                pltpu.VMEM((4, DOWN_ROWS, LANES), BF),
                pltpu.VMEM((every, hidden), BF),
                pltpu.VMEM((every, hidden), BF),
                pltpu.VMEM((every, hidden), BF),
                pltpu.VMEM((rows, hidden), BF),
                pltpu.VMEM((rows // SEGS + 32, SEGS, LANES), F32),
                pltpu.VMEM((rows // SEGS + 32, SEGS, LANES), F32),
                pltpu.VMEM((72, SEGS, LANES), F32),
                pltpu.VMEM((rows // SEGS, SEGS, LANES), F32),
                pltpu.VMEM((rows // SEGS // 2 + 1, SEGS, LANES), F32),
                pltpu.VMEM((HALO, LANES), F32),
                pltpu.VMEM((every, hidden), F32),
                pltpu.VMEM((every, model), BF),
                pltpu.SemaphoreType.DMA((4,)),
                pltpu.SemaphoreType.DMA((4, hidden // 256)),
            ],
            0,
            30,
        )

    def up_backward(layer, scal, dup0, hgrad, hs, xs, small):
        mlp = saved[layer][2]
        return call(
            functools.partial(up_backward_kernel, layer),
            [scal, dup0, hgrad, hs, xs, small, mlp[3], mlp[2], mlp[6], mlp[7], *w_u],
            [SMEM] + [VMEM] * 5 + [ANY] * 14,
            [rows_f32, shape((2, M_ROWS, LANES), BF), shape((2, M_ROWS, LANES), BF)],
            [
                pltpu.VMEM((4, W_ROWS - W_UP, LANES), BF),
                pltpu.VMEM((rows, hidden), BF),
                pltpu.VMEM((rows, hidden), BF),
                pltpu.VMEM((rows, LANES), F32),
                pltpu.VMEM((every, model), BF),
                pltpu.VMEM((rows, hidden), BF),
                pltpu.VMEM((4, LANES, LANES), F32),
                pltpu.SemaphoreType.DMA((8,)),
                pltpu.SemaphoreType.DMA((3, hidden // LANES)),
            ],
            0,
            30,
            (),
            (0, 1, 2),
        )

    def attention_backward(layer, scal, gatt):
        att = saved[layer][1]
        return call(
            functools.partial(attention_backward_kernel, layer),
            [scal, gatt, *att[:5], *w_u, cos_t, sin_t],
            [SMEM] + [ANY] * 18,
            [head_pack(rows), shape((4, rows, 2 * LANES), F32), shape((4, rows, 2 * LANES), BF)],
            [
                pltpu.VMEM((4, W_UP, LANES), BF),
                pltpu.VMEM((rows, LANES), F32),
                pltpu.VMEM((rows, LANES), F32),
                pltpu.VMEM((length, 2 * rows), BF),
                pltpu.VMEM((length, 2 * rows), BF),
                pltpu.VMEM((2 * rows, LANES), BF),
                pltpu.VMEM((2 * rows, LANES), BF),
                pltpu.VMEM((4, rows, LANES), BF),
                pltpu.VMEM((4, length, LANES), BF),
                pltpu.VMEM((4, length, LANES), BF),
                pltpu.VMEM((4, rows, LANES), BF),
                pltpu.VMEM((rows, LANES), F32),
                pltpu.VMEM((rows, model), BF),
                pltpu.SemaphoreType.DMA((4,)),
                pltpu.SemaphoreType.DMA((8,)),
            ],
            12 * rows * length * model, 26)

    def input_backward(layer, scal, gres, dn_mlp, dq, dkv_own, dkv_got):
        h = saved[layer][0]
        return call(
            functools.partial(input_backward_kernel, layer),
            [scal, sp, h, gres, dn_mlp, dq, dkv_own, dkv_got, *w_qkv, cos_t, sin_t],
            [SMEM, VMEM, ANY, ANY, ANY] + [VMEM] * 3 + [ANY] * 10,
            [flat, flat, shape((2, A_ROWS, LANES), BF), shape((2, A_ROWS, LANES), BF)],
            [
                pltpu.VMEM((4, 3, model, LANES), BF),
                pltpu.VMEM((rows, LANES), F32),
                pltpu.VMEM((rows, LANES), F32),
                pltpu.VMEM((rows, 12 * LANES), BF),
                pltpu.VMEM((rows, model), BF),
                pltpu.VMEM((rows, model), F32),
                pltpu.VMEM((rows, LANES), F32),
                pltpu.VMEM((4, 64, LANES), F32),
                pltpu.VMEM((rows, model), BF),
                pltpu.VMEM((rows, model), F32),
                pltpu.VMEM((rows, model), F32),
                pltpu.SemaphoreType.DMA((4,)),
                pltpu.SemaphoreType.DMA((5,)),
            ],
            14 * rows * model * model, 24, (), (2, 3))

    owner1 = jnp.logical_not(first)
    natural0, natural1 = top0[1], top1[0]
    out_keep = jnp.where(first, natural0, natural1)
    out_send = jnp.where(first, natural1, natural0)
    gres, gatt, gbr, halo_out, d_keep, d_send = top1[1:]
    gbr, halo_out, d_send, out_send, out_keep = fence(gbr, halo_out, d_send, out_send, out_keep)
    halo_in = core_of(halo_out)
    sc, gbr, halo_in, out_send, out_keep, d_send = fence(scal, gbr, halo_in, out_send, out_keep, d_send)
    d_got, out_got, out_y = core_of(d_send), x_of(out_send), y_of(out_keep)
    part = conv_backward(1, sc, gbr, halo_in)
    part, d_got, out_got, out_y = fence(part, d_got, out_got, out_y)
    d_away = total(d_keep[1], d_got[1]).astype(BF)
    sc, d_away = fence(scal, d_away)
    d_y = y_of(d_away)
    dn_mlp, m_keep, m_send = up_backward(1, sc, *part)
    gatt, d_y, m_send = fence(gatt, d_y, m_send)
    m_got = core_of(m_send)
    d1_mine, d_give = halves(total(d_keep[0], d_got[0], d_y), owner1)
    m_away = total(m_keep[1], m_got[1]).astype(BF)
    sc, d_give, m_away = fence(scal, d_give.astype(BF), m_away)
    m_y = y_of(m_away)
    d_x = x_of(d_give)
    dq, dkv_own, dkv_oth = attention_backward(1, sc, gatt)
    dq, dkv_oth, m_y, d_x = fence(dq, dkv_oth, m_y, d_x)
    dkv_got = core_of(dkv_oth)
    m1_mine, m_give = halves(total(m_keep[0], m_got[0], m_y), owner1)
    sc, m_give, out_got = fence(scal, m_give.astype(BF), out_got)
    m_x = x_of(m_give)
    out_yg = y_of(out_got)
    g, ingrad1, a_keep, a_send = input_backward(1, sc, gres, dn_mlp, dq, dkv_own, dkv_got)

    g, a_send, m_x = fence(g, a_send, m_x)
    a_got = core_of(a_send)
    dm1_half = jnp.concatenate([total(d1_mine, d_x), total(m1_mine, m_x)], axis=0).astype(BF)
    sc, dm1_half = fence(scal, dm1_half)
    dm1_half = lax.psum(dm1_half, "dp")
    gres, gatt, gbr, halo_out, d0_keep, d0_send = merge_backward(0, sc, g)
    gbr, halo_out, d0_send, a_got, out_yg = fence(gbr, halo_out, d0_send, a_got, out_yg)
    halo_in, d0_got = core_of(halo_out), core_of(d0_send)
    a_away = total(a_keep[1], a_got[1]).astype(BF)
    gbr, halo_in, d0_got, a_away = fence(gbr, halo_in, d0_got, a_away)
    d_away = total(d0_keep[1], d0_got[1]).astype(BF)
    sc, a_away, d_away = fence(scal, a_away, d_away)
    a_y, d_y = y_of(a_away), y_of(d_away)
    part = conv_backward(0, sc, gbr, halo_in)
    part, a_y, d_y = fence(part, a_y, d_y)
    a_mine, a_give = halves(total(a_keep[0], a_got[0], a_y), owner1)
    d_mine, d_give = halves(total(d0_keep[0], d0_got[0], d_y), first)
    sc, give = fence(scal, jnp.concatenate([a_give, d_give], axis=0).astype(BF))
    got = x_of(give)
    dn_mlp, m0_keep, m0_send = up_backward(0, sc, *part)
    gatt, got, m0_send, dm1_half = fence(gatt, got, m0_send, dm1_half)
    m0_got = core_of(m0_send)
    ad_half = total(jnp.concatenate([a_mine, d_mine], axis=0), got).astype(BF)
    m_away = total(m0_keep[1], m0_got[1]).astype(BF)
    sc, m_away, ad_half = fence(scal, m_away, ad_half)
    m_y = y_of(m_away)
    ad_terms = scatter_over_dp(ad_half)
    dq, dkv_own, dkv_oth = attention_backward(0, sc, gatt)
    dq, dkv_oth, m_y, ad_terms = fence(dq, dkv_oth, m_y, ad_terms)
    dkv_got = core_of(dkv_oth)
    m_mine, m_give = halves(total(m0_keep[0], m0_got[0], m_y), first)
    sc, m_give, ad_half = fence(scal, m_give.astype(BF), total(*ad_terms).astype(BF))
    m_x = x_of(m_give)
    ad_half = gather_over_dp(ad_half)
    g, ingrad0, a_keep, a_send = input_backward(0, sc, gres, dn_mlp, dq, dkv_own, dkv_got)

    ingrad0, a_send, m_x, ad_half, out_yg = fence(ingrad0, a_send, m_x, ad_half, out_yg)
    a_got = core_of(a_send)
    in_keep = jnp.where(first, ingrad0, ingrad1)
    in_got = x_of(jnp.where(first, ingrad1, ingrad0))
    m_terms = scatter_over_dp(total(m_mine, m_x).astype(BF))
    a_away = total(a_keep[1], a_got[1]).astype(BF)
    a_y = y_of(a_away)
    a_y, m_terms, in_keep, in_got = fence(a_y, m_terms, in_keep, in_got)
    a_sum = total(a_keep[0], a_got[0], a_y).astype(BF)
    a_x = x_of(a_sum)
    in_y = y_of(in_keep)
    m_parts = gather_over_dp(total(*m_terms).astype(BF))
    out_half = jnp.stack([out_keep, out_y, out_got, out_yg])
    out_other = core_of(out_half)
    a_x, m_parts, ad_half, in_y, in_got, out_other = fence(a_x, m_parts, ad_half, in_y, in_got, out_other)
    a_terms = scatter_over_dp(total(a_sum, a_x).astype(BF))
    in_yg = y_of(in_got)
    ad_half = in_order(ad_half)
    a1_half = ad_half[: A_ROWS // 2]
    dm0_half = jnp.concatenate([ad_half[A_ROWS // 2 :], in_order(m_parts)], axis=0)
    dm_lo = jnp.where(first, dm0_half, dm1_half)
    cut = D_ROWS // 2
    away = jnp.where(first, dm1_half, dm0_half)
    m_back = x_of(away[cut:])
    d_away = jnp.concatenate([away[:cut], a1_half], axis=0)
    a_terms, in_yg, m_back, d_away = fence(a_terms, in_yg, m_back, d_away)
    d_back = x_of(d_away)
    a_parts = gather_over_dp(total(*a_terms).astype(BF))
    in_half = jnp.stack([in_keep, in_y, in_got, in_yg])
    in_other = core_of(in_half)

    def assemble(here, there):
        return call(
            assemble_kernel, [scal, here, there], [SMEM, VMEM, VMEM], [shape((micro, length, model), BF)], [], 0, 10
        )[0]

    layer_out = assemble(out_half, out_other)
    input_grad = assemble(in_half, in_other)

    a_parts, layer_out, input_grad, d_back = fence(a_parts, layer_out, input_grad, d_back)
    a_whole = jnp.where(first, in_order(a_parts), jnp.concatenate([a1_half, d_back[cut:]], axis=0))
    (g_qkv, g_out, g_up, g_down, g_bqkv, g_bup, g_gain, g_gbias, g_conv, g_ng, g_nb, g_ob, g_logit) = call(
        finale_kernel,
        [dm_lo, d_back, m_back, a_whole, logits],
        [VMEM] * 4 + [SMEM],
        [shape((3, model, LANES), F32), shape((LANES, model), F32), shape((2, model, shard), F32),
         shape((shard, model), F32), shape((3, 1, LANES), F32), shape((2, shard), F32), shape((1, shard), F32),
         shape((2, shard), F32), shape((TAPS, 1, shard), F32), shape((3, 1, model), F32), shape((3, 1, model), F32),
         shape((2, model), F32), shape((2, LANES), F32)],
        [],
        0,
        16,
    )
    outs = (
        layer_out.reshape(micro, 1, length, model),
        input_grad.reshape(micro, 1, length, model),
        g_ng[:, 0],
        g_nb[:, 0],
        g_qkv,
        g_bqkv[:, 0],
        g_out,
        g_up,
        g_bup,
        g_gain[0],
        g_gbias,
        g_conv[:, 0],
        g_down,
        g_ob,
        g_logit[:, 0],
    )
    return tuple(x[None] for x in outs)


def solution(mesh):
    placed = (
        P(None, "dp", None, None),
        P(None, "dp"),
        P(None, "dp", None, None),
        P("section", None, None),
        P("section", None, None),
        P("section", None, None, "mp"),
        P("section", None, "mp"),
        P("section", "mp", None),
        P("section", None, None, "mp"),
        P("section", None, "mp"),
        P("section", "mp"),
        P("section", None, "mp"),
        P("section", None, "mp"),
        P("section", "mp", None),
        P("section", None, None),
        P("section", None),
    )
    return jax.shard_map(
        per_device,
        mesh=mesh,
        in_specs=placed,
        out_specs=(
            P("section", None, "dp", None, None),
            P("section", None, "dp", None, None),
            P("section", None, None),
            P("section", None, None),
            P("section", None, None, "mp"),
            P("section", None, "mp"),
            P("section", "mp", None),
            P("section", None, None, "mp"),
            P("section", None, "mp"),
            P("section", "mp"),
            P("section", None, "mp"),
            P("section", None, "mp"),
            P("section", "mp", None),
            P("section", None, None),
            P("section", None),
        ),
        check_vma=False,
    )
```
